32 devices in a mesh: dp: 8 (over y, x, core), mp: 4 (over z).
Axes of the slice: x: 2, y: 2, z: 4, core: 2. Of those that a mesh axis runs over, the one named last changes fastest.
Arguments:
- hidden_in: bfloat16 [8192, 2048], P(('dp', 'mp')), may hold values from -48 to 48
- output_grad: bfloat16 [8192, 2048], P(('dp', 'mp')), may hold values from -6 to 6
- first_gain: bfloat16 [2048], P('dp'), may hold values from 0.25 to 1.75
- first_shift: bfloat16 [2048], P('dp'), may hold values from -1.75 to 1.75
- query_weight: bfloat16 [2048, 2048], P('dp', 'mp'), may hold values from -0.1875 to 0.1875
- query_bias: bfloat16 [2048], P('dp'), may hold values from -3 to 3
- key_weight: bfloat16 [2048, 2048], P('dp', 'mp'), may hold values from -0.1875 to 0.1875
- value_weight: bfloat16 [2048, 2048], P('dp', 'mp'), may hold values from -0.125 to 0.125
- value_bias: bfloat16 [2048], P('dp'), may hold values from -3 to 3
- out_weight: bfloat16 [2048, 2048], P('dp', 'mp'), may hold values from -0.5 to 0.5
- out_bias: bfloat16 [2048], P('dp'), may hold values from -3 to 3
- second_gain: bfloat16 [2048], P('dp'), may hold values from 0.25 to 1.75
- second_shift: bfloat16 [2048], P('dp'), may hold values from -1.75 to 1.75
- up_weight: bfloat16 [2048, 8192], P('dp', 'mp'), may hold values from -0.125 to 0.125
- up_bias: bfloat16 [8192], P('dp'), may hold values from -3 to 3
- down_weight: bfloat16 [2048, 8192], P('dp', 'mp'), may hold values from -0.0625 to 0.0625
- down_bias: bfloat16 [2048], P('dp'), may hold values from -3 to 3
- seq_lengths: int32 [8], replicated, may hold values from 1 to 4096, as said below
- block_order: int32 [64], replicated, may hold values from 0 to 63, as said below
- block_slot: int32 [64], replicated, may hold values from 0 to 63, as said below
Outputs:
- output: bfloat16 [8192, 2048], P(('dp', 'mp'))
- input_grad: float32 [8192, 2048], P(('dp', 'mp'))
- first_gain_grad: float32 [2048], P('dp')
- first_shift_grad: float32 [2048], P('dp')
- query_weight_grad: float32 [2048, 2048], P('dp', 'mp')
- query_bias_grad: float32 [2048], P('dp')
- key_weight_grad: float32 [2048, 2048], P('dp', 'mp')
- value_weight_grad: float32 [2048, 2048], P('dp', 'mp')
- value_bias_grad: float32 [2048], P('dp')
- out_weight_grad: float32 [2048, 2048], P('dp', 'mp')
- out_bias_grad: float32 [2048], P('dp')
- second_gain_grad: float32 [2048], P('dp')
- second_shift_grad: float32 [2048], P('dp')
- up_weight_grad: float32 [2048, 8192], P('dp', 'mp')
- up_bias_grad: float32 [8192], P('dp')
- down_weight_grad: float32 [2048, 8192], P('dp', 'mp')
- down_bias_grad: float32 [2048], P('dp')
The draws below stay inside these ranges and needn't reach their ends.
Inputs may be any that keep to these rules, and one draw needn't show every extreme that they name: Sequence s covers ceil(seq_lengths[s] / 128) whole blocks, and these block counts add up to 64. `block_order`: a permutation of the blocks; dealt blocks 8 * g to 8 * g + 7 are those of index g of dp. The inverse of block_order: block_slot[block_order[j]] = j.
All inputs are finite; a program needn't handle non-finite values.
Results may differ from the reference program's by a relative error of at most 0.025.
Values may be sent and summed in bfloat16 or wider, within the bound.
A program may use at most 576 MiB of HBM per device.

```python
import jax
import jax.numpy as jnp
from jax import lax

D = 2048
HEADS = 16
HEAD_DIM = 128
FF = 8192
BLOCK = 128
BLK_DP = 8
NSEQ = 8
TOKENS = 8192
NBLK = 64
LONGEST = 32


def sequence_plan(key):
    plan_key = jax.random.fold_in(key, 101)
    subkeys = jax.random.split(plan_key, 7)
    others = NSEQ - 1
    spare = NBLK - LONGEST
    index_others = jnp.arange(others, dtype=jnp.int32)
    shares = (spare // others + (index_others < spare % others).astype(jnp.int32)).astype(jnp.int32)

    def move(step_index, current):
        step_key = jax.random.fold_in(subkeys[0], step_index)
        chosen_pair = jax.random.randint(step_key, (2,), 0, others)
        source = chosen_pair[0]
        target = chosen_pair[1]
        headroom = jnp.minimum(current[source] - 1, LONGEST - current[target])
        headroom = jnp.where(source == target, 0, jnp.maximum(headroom, 0))
        amount = jax.random.randint(jax.random.fold_in(step_key, 7), (), 0, headroom + 1)
        return current.at[source].add(-amount).at[target].add(amount)
    shares = lax.fori_loop(0, 6 * NSEQ, move, shares)
    longest_at = jax.random.randint(subkeys[1], (), 0, NSEQ)
    seq_index = jnp.arange(NSEQ, dtype=jnp.int32)
    shifted = jnp.clip(jnp.where(seq_index < longest_at, seq_index, seq_index - 1), 0, others - 1)
    counts = jnp.where(seq_index == longest_at, LONGEST, shares[shifted]).astype(jnp.int32)
    trim_tokens = jax.random.randint(subkeys[2], (NSEQ,), 0, BLOCK)
    trim_tokens = jnp.where(seq_index == longest_at, 0, trim_tokens)
    lengths = (counts * BLOCK - trim_tokens).astype(jnp.int32)
    starts = (jnp.cumsum(counts) - counts).astype(jnp.int32)
    long_start = jnp.sum(jnp.where(seq_index == longest_at, starts, 0)).astype(jnp.int32)
    groups = NBLK // BLK_DP
    group_index = jnp.arange(groups, dtype=jnp.int32)
    chosen = group_index * BLK_DP + jax.random.randint(subkeys[3], (groups,), 0, BLK_DP)
    slot_index = jnp.arange(NBLK, dtype=jnp.int32)
    special_slot = jnp.zeros((NBLK,), jnp.int32).at[chosen].set(1)
    slot_score = jnp.where(special_slot == 1, slot_index, NBLK + jax.random.permutation(subkeys[4], NBLK))
    order_slots = jnp.argsort(slot_score).astype(jnp.int32)
    offset = slot_index - long_start
    special_block = (offset >= 0) & (offset < groups)
    group_rank = jax.random.permutation(subkeys[5], groups)
    block_score = jnp.where(special_block, group_rank[jnp.clip(offset, 0, groups - 1)], NBLK + jax.random.permutation(subkeys[6], NBLK))
    order_blocks = jnp.argsort(block_score).astype(jnp.int32)
    block_order = jnp.zeros((NBLK,), jnp.int32).at[order_slots].set(order_blocks)
    block_slot = jnp.zeros((NBLK,), jnp.int32).at[order_blocks].set(order_slots)
    return (lengths, block_order, block_slot)


def draw_seq_lengths(key, part):
    return sequence_plan(key)[0]


def draw_block_order(key, part):
    return sequence_plan(key)[1]


def draw_block_slot(key, part):
    return sequence_plan(key)[2]


def draw_hidden_in(key, part):
    key = jax.random.fold_in(key, 3)
    subkeys = jax.random.split(key, 3)
    column_scale = jnp.exp(jax.random.uniform(subkeys[0], (1, D), minval=jnp.log(0.3), maxval=jnp.log(3.0)))
    row_scale = jnp.exp(jax.random.uniform(subkeys[1], (TOKENS, 1), minval=jnp.log(0.4), maxval=jnp.log(4.0)))
    values = jnp.clip(jax.random.normal(subkeys[2], (TOKENS, D)), -4.0, 4.0) * column_scale * row_scale
    return values.astype(jnp.bfloat16)


def strengthened(values, rng, source, target, blocks, factor):
    def block_of(axis_at):
        return (jnp.arange(values.shape[axis_at]) // (values.shape[axis_at] // blocks)).reshape((-1,) + (1,) * (values.ndim - 1 - axis_at))

    first = jax.random.permutation(rng, blocks)[block_of(target)]
    second = (block_of(target) + blocks // 2) % blocks
    return jnp.where((block_of(source) == first) | (block_of(source) == second), factor * values, values)


def level_of(own_key, dims, pieces, smallest, top_value):
    factor_of, own = 1.0, jax.random.fold_in(own_key, 6)
    for position, parts in pieces:
        steps = jnp.exp(jax.random.uniform(jax.random.fold_in(own, position), (parts,), jnp.float32, smallest / len(pieces), top_value / len(pieces)))
        factor_of = factor_of * jnp.repeat(steps, dims[position] // parts).reshape([-1 if axis == position else 1 for axis in range(len(dims))])
    return factor_of


def gaussian(key, shape, width, bound, shards=(), held_as=jnp.bfloat16):
    gain = level_of(key, shape, shards, -0.22, 0.18) if shards else 1.0
    entries = jax.random.normal(key, shape, jnp.float32) * width * gain
    return jnp.minimum(jnp.maximum(entries, -bound), bound).astype(held_as)


def heavy_noise(rng, shape, deviation, reach, cuts, heavy, kind=jnp.bfloat16):
    values = deviation * jax.random.normal(rng, shape, jnp.float32)
    if cuts:
        values = values * level_of(rng, shape, cuts, -0.22, 0.18)
    return jnp.clip(strengthened(values, jax.random.fold_in(rng, 3), *heavy), -reach, reach).astype(kind)


def setup_inputs(seed: int = 0) -> dict:
    key_of = jax.random.split(jax.random.key(seed), 21)
    hidden_in = draw_hidden_in(jax.random.fold_in(key_of[20], 71), 0)
    output_grad = heavy_noise(key_of[1], (TOKENS, D), 1.0, 6.0, ((0, 32),), (0, 1, 32, 2.75))
    first_gain = jnp.clip(1.0 + 0.15 * jax.random.normal(key_of[2], (D,), jnp.float32), 0.25, 1.75).astype(jnp.bfloat16)
    first_shift = gaussian(key_of[3], (D,), 0.3, 1.75, ((0, 8),))
    query_weight = gaussian(key_of[4], (D, D), (D // 2) ** -0.5, 0.1875, ((0, 8), (1, 4)))
    query_bias = gaussian(key_of[5], (D,), 0.5, 3.0, ((0, 8),))
    key_weight = gaussian(key_of[6], (D, D), (D // 2) ** -0.5, 0.1875, ((0, 8), (1, 4)))
    value_weight = gaussian(key_of[7], (D, D), D ** -0.5, 0.125, ((0, 8), (1, 4)))
    value_bias = gaussian(key_of[8], (D,), 0.5, 3.0, ((0, 8),))
    out_weight = gaussian(key_of[9], (D, D), (D // 16) ** -0.5, 0.5, ((0, 8), (1, 4)))
    out_bias = gaussian(key_of[10], (D,), 0.5, 3.0, ((0, 8),))
    second_gain = jnp.clip(1.0 + 0.15 * jax.random.normal(key_of[11], (D,), jnp.float32), 0.25, 1.75).astype(jnp.bfloat16)
    second_shift = gaussian(key_of[12], (D,), 0.3, 1.75, ((0, 8),))
    up_weight = gaussian(key_of[13], (D, FF), D ** -0.5, 0.125, ((0, 8), (1, 4)))
    up_bias = gaussian(key_of[14], (FF,), 0.5, 3.0, ((0, 8),))
    down_weight = gaussian(key_of[15], (D, FF), FF ** -0.5, 0.0625, ((0, 8), (1, 4)))
    down_bias = gaussian(key_of[16], (D,), 0.5, 3.0, ((0, 8),))
    seq_lengths = draw_seq_lengths(jax.random.fold_in(key_of[20], 71), 0)
    block_order = draw_block_order(jax.random.fold_in(key_of[20], 71), 0)
    block_slot = draw_block_slot(jax.random.fold_in(key_of[20], 71), 0)
    return dict(hidden_in=hidden_in, output_grad=output_grad, first_gain=first_gain, first_shift=first_shift, query_weight=query_weight, query_bias=query_bias, key_weight=key_weight, value_weight=value_weight, value_bias=value_bias, out_weight=out_weight, out_bias=out_bias, second_gain=second_gain, second_shift=second_shift, up_weight=up_weight, up_bias=up_bias, down_weight=down_weight, down_bias=down_bias, seq_lengths=seq_lengths, block_order=block_order, block_slot=block_slot)


big_negative = -1e+30
norm_epsilon = 1e-05

@jax.custom_vjp
def low(v):
    return lax.optimization_barrier(v.astype(jnp.bfloat16)).astype(jnp.float32)

@jax.custom_vjp
def low_back(v):
    return v

def low_keep(v):
    return (low(v), None)

def low_pass(kept, grad):
    return (grad,)

def back_keep(v):
    return (v, None)

def back_low(kept, grad):
    return (low(grad),)
low.defvjp(low_keep, low_pass)
low_back.defvjp(back_keep, back_low)

def matmul(left, right):
    return jnp.dot(left, right, precision=lax.Precision.HIGHEST)

def layer_norm(values, gain_row, offset):
    average = lax.optimization_barrier(jnp.mean(values, axis=-1, keepdims=True))
    centred = values - average
    variance = lax.optimization_barrier(jnp.mean(centred * centred, axis=-1, keepdims=True))
    return centred * lax.rsqrt(variance + norm_epsilon) * gain_row + offset

def sequence_layout(seq_lengths):
    block_counts = ((seq_lengths + BLOCK - 1) // BLOCK).astype(jnp.int32)
    starts = (jnp.cumsum(block_counts) - block_counts).astype(jnp.int32)
    block_ids = jnp.arange(NBLK, dtype=jnp.int32)
    seq_of_block = (lax.optimization_barrier(jnp.sum((block_ids[:, None] >= starts[None, :]).astype(jnp.int32), axis=1)) - 1).astype(jnp.int32)
    row_block = jnp.repeat(block_ids, BLOCK).astype(jnp.int32)
    within = jnp.tile(jnp.arange(BLOCK, dtype=jnp.int32), NBLK).astype(jnp.int32)
    row_seq = seq_of_block[row_block]
    row_pos = ((row_block - starts[row_seq]) * BLOCK + within).astype(jnp.int32)
    row_valid = row_pos < seq_lengths[row_seq]
    return (row_seq, row_pos, row_valid)

def reference(hidden_in, output_grad, first_gain, first_shift, query_weight, query_bias, key_weight, value_weight, value_bias, out_weight, out_bias, second_gain, second_shift, up_weight, up_bias, down_weight, down_bias, seq_lengths, block_order, block_slot):
    row_seq, row_pos, row_valid = sequence_layout(seq_lengths)
    window = LONGEST * BLOCK
    score_scale = 1.0 / HEAD_DIM ** 0.5

    def forward(hidden, gain_one, shift_one, weight_query, bias_query, weight_key, weight_value, bias_value, weight_out, bias_out, gain_two, shift_two, weight_up, bias_up, weight_down, bias_down):
        ordered = hidden.reshape(NBLK, BLOCK, D)[block_slot].reshape(TOKENS, D)
        normed_one = low(layer_norm(ordered, gain_one, shift_one))
        queries = low(low_back(matmul(normed_one, weight_query) + bias_query))
        key_rows = low(low_back(matmul(normed_one, weight_key)))
        value_rows = low(low_back(matmul(normed_one, weight_value) + bias_value))

        def attend(block_id):
            first_row = (block_id * BLOCK).astype(jnp.int32)
            key_first = jnp.maximum(first_row + BLOCK - window, 0).astype(jnp.int32)
            query_block = lax.dynamic_slice_in_dim(queries, first_row, BLOCK, 0).reshape(BLOCK, HEADS, HEAD_DIM)
            key_block = lax.dynamic_slice_in_dim(key_rows, key_first, window, 0).reshape(window, HEADS, HEAD_DIM)
            value_block = lax.dynamic_slice_in_dim(value_rows, key_first, window, 0).reshape(window, HEADS, HEAD_DIM)
            query_seq = lax.dynamic_slice_in_dim(row_seq, first_row, BLOCK, 0)
            query_pos = lax.dynamic_slice_in_dim(row_pos, first_row, BLOCK, 0)
            query_valid = lax.dynamic_slice_in_dim(row_valid, first_row, BLOCK, 0)
            key_seq = lax.dynamic_slice_in_dim(row_seq, key_first, window, 0)
            key_pos = lax.dynamic_slice_in_dim(row_pos, key_first, window, 0)
            allowed = ((query_seq[:, None] == key_seq[None, :]) & (key_pos[None, :] <= query_pos[:, None]) & query_valid[:, None])[None]
            scores = low_back(jnp.einsum('qhd,khd->hqk', query_block, key_block, precision=lax.Precision.HIGHEST) * score_scale)
            masked = jnp.where(allowed, scores, big_negative)
            row_top = lax.optimization_barrier(jnp.max(masked, axis=2, keepdims=True))
            weights = jnp.where(allowed, jnp.exp(masked - row_top), 0.0)
            row_total = lax.optimization_barrier(jnp.sum(weights, axis=2, keepdims=True))
            probability = weights / jnp.where(query_valid[None, :, None], row_total, 1.0)
            value_mix = jnp.einsum('hqk,khd->qhd', low(probability), value_block, precision=lax.Precision.HIGHEST)
            return value_mix.reshape(BLOCK, D)
        attended = lax.map(jax.checkpoint(attend), jnp.arange(NBLK, dtype=jnp.int32)).reshape(TOKENS, D)
        mixed_heads = low(low_back(attended))
        residual = ordered + low_back(matmul(mixed_heads, weight_out.T) + bias_out)
        normed_two = low(layer_norm(residual, gain_two, shift_two))
        pre_act = low_back(matmul(normed_two, weight_up) + bias_up)
        hidden_units = low(jax.nn.gelu(pre_act, approximate=False))
        result = residual + low_back(matmul(hidden_units, weight_down.T) + bias_down)
        result = jnp.where(row_valid[:, None], result, 0.0)
        return result.reshape(NBLK, BLOCK, D)[block_order].reshape(TOKENS, D)
    floats = (hidden_in.astype(jnp.float32), first_gain.astype(jnp.float32), first_shift.astype(jnp.float32), query_weight.astype(jnp.float32), query_bias.astype(jnp.float32), key_weight.astype(jnp.float32), value_weight.astype(jnp.float32), value_bias.astype(jnp.float32), out_weight.astype(jnp.float32), out_bias.astype(jnp.float32), second_gain.astype(jnp.float32), second_shift.astype(jnp.float32), up_weight.astype(jnp.float32), up_bias.astype(jnp.float32), down_weight.astype(jnp.float32), down_bias.astype(jnp.float32))
    result, pullback = jax.vjp(forward, *floats)
    gradients = pullback(output_grad.astype(jnp.float32))
    return (result.astype(jnp.bfloat16), gradients[0], gradients[1], gradients[2], gradients[3], gradients[4], gradients[5], gradients[6], gradients[7], gradients[8], gradients[9], gradients[10], gradients[11], gradients[12], gradients[13], gradients[14], gradients[15])
```

```python
import math

import jax
import jax.numpy as jnp
from jax import lax
from jax.experimental import pallas as pl
from jax.experimental.pallas import tpu as pltpu
from jax.sharding import PartitionSpec as P

HEAD_DIM = 128
BLOCK = 128
KEY_BLOCKS = 4
MESH = pl.DeviceIdType.MESH
ANY = pl.BlockSpec(memory_space=pl.ANY)
VMEM = pl.BlockSpec(memory_space=pltpu.VMEM)
SMEM = pl.BlockSpec(memory_space=pltpu.SMEM)
MIB = 1 << 20


big_negative = -1e30
norm_epsilon = 1e-05


def layer_norm(values, gain_row, offset):
    average = jnp.mean(values, axis=-1, keepdims=True)
    centred = values - average
    variance = jnp.mean(centred * centred, axis=-1, keepdims=True)
    inverse = lax.rsqrt(variance + norm_epsilon)
    normed = centred * inverse
    return (normed * gain_row + offset, normed, inverse)


def norm_back(upstream, normed, inverse, gain_row):
    scaled = upstream * gain_row
    mean_grad = jnp.mean(scaled, axis=-1, keepdims=True)
    second = jnp.mean(scaled * normed, axis=-1, keepdims=True)
    return inverse * (scaled - mean_grad - normed * second)


def gelu_exact(values):
    return jax.nn.gelu(values, approximate=False)


def contract_last(left, right):
    return lax.dot_general(
        left, right, (((1,), (1,)), ((), ())), preferred_element_type=jnp.float32
    )


def contract_first(left, right):
    return lax.dot_general(
        left, right, (((0,), (0,)), ((), ())), preferred_element_type=jnp.float32
    )


def row_meta(seq_lengths, block_order, first_row, row_count):
    block_count = block_order.shape[0]
    seq_count = seq_lengths.shape[0]
    row_ids = first_row + jnp.arange(row_count, dtype=jnp.int32)
    slot_ids = row_ids // BLOCK
    within = row_ids % BLOCK
    slot_hit = slot_ids[:, None] == jnp.arange(block_count, dtype=jnp.int32)[None, :]
    initial = jnp.sum(jnp.where(slot_hit, block_order[None, :], 0), axis=1)
    block_counts = (seq_lengths + BLOCK - 1) // BLOCK
    starts = jnp.cumsum(block_counts) - block_counts
    seq_ids = jnp.sum((initial[:, None] >= starts[None, :]).astype(jnp.int32), axis=1) - 1
    seq_hit = seq_ids[:, None] == jnp.arange(seq_count, dtype=jnp.int32)[None, :]
    seq_start = jnp.sum(jnp.where(seq_hit, starts[None, :], 0), axis=1)
    seq_length = jnp.sum(jnp.where(seq_hit, seq_lengths[None, :], 0), axis=1)
    position = (initial - seq_start) * BLOCK + within
    return (seq_ids, position, position < seq_length)


def greet(peers):
    barrier = pltpu.get_barrier_semaphore()
    for peer in peers:
        pl.semaphore_signal(barrier, inc=1, device_id=peer, device_id_type=MESH)
    pl.semaphore_wait(barrier, len(peers))


def remote(src, dst, send_sem, recv_sem, peer):
    return pltpu.make_async_remote_copy(
        src_ref=src, dst_ref=dst, send_sem=send_sem, recv_sem=recv_sem,
        device_id=peer, device_id_type=MESH,
    )


def head_place(heads, members):
    me = lax.axis_index("dp")
    return me, me // members, me % members, lax.axis_index("mp")


def lanes(head):
    return pl.ds(pl.multiple_of(head * HEAD_DIM, HEAD_DIM), HEAD_DIM)


def to_heads(owned, shared, heads, members, collective_id):
    rows = (owned + shared)[0].shape[0]
    n_owned, n_shared = len(owned), len(shared)
    count = n_owned + n_shared

    def kernel(*refs):
        ins, outs = refs[:count], refs[count : 2 * count]
        local_sem, send_sem, recv_sem, fwd_send, fwd_recv = refs[2 * count :]
        me, group, member, mp = head_place(heads, members)

        def dest(array, source):
            place = (source // members) if array < n_owned else source
            return outs[array].at[pl.ds(pl.multiple_of(place * rows, rows), rows)]

        head_peers = [((group ^ o) * members + member, mp) for o in range(1, heads)]
        pair_peers = [(group * members + (member ^ o), mp) for o in range(1, members)]
        greet(head_peers + pair_peers)
        order = list(range(n_owned, count)) + list(range(n_owned))
        sends, locals_, forwards = {}, [], []
        for a in order:
            for o in range(1, heads):
                copy = remote(ins[a].at[:, lanes(group ^ o)], dest(a, me), send_sem.at[a, o],
                              recv_sem.at[a, o], head_peers[o - 1])
                copy.start()
                sends[a, o] = copy
        for a in range(count):
            copy = pltpu.make_async_copy(ins[a].at[:, lanes(group)], dest(a, me), local_sem.at[a])
            copy.start()
            locals_.append(copy)
        for a in range(n_owned, count):
            for o in range(heads):
                source = (group ^ o) * members + member
                if o:
                    sends[a, o].wait_recv()
                for p in range(1, members):
                    piece = ins[a].at[:, lanes(group)] if o == 0 else dest(a, source)
                    copy = remote(piece, dest(a, source), fwd_send.at[a - n_owned, o, p],
                                  fwd_recv.at[a - n_owned, o, p], pair_peers[p - 1])
                    copy.start()
                    forwards.append(copy)
        for copy in locals_:
            copy.wait()
        for (a, o), copy in sends.items():
            copy.wait_send()
            if a < n_owned:
                copy.wait_recv()
        for copy in forwards:
            copy.wait()

    total = rows * lax.axis_size("dp")
    shapes = [jax.ShapeDtypeStruct((heads * rows, HEAD_DIM), a.dtype) for a in owned]
    shapes += [jax.ShapeDtypeStruct((total, HEAD_DIM), a.dtype) for a in shared]
    dma = pltpu.SemaphoreType.DMA
    return pl.pallas_call(
        kernel,
        out_shape=shapes,
        in_specs=[ANY] * count,
        out_specs=[ANY] * count,
        scratch_shapes=[
            dma((count,)), dma((count, heads)), dma((count, heads)),
            dma((max(n_shared, 1), heads, members)), dma((max(n_shared, 1), heads, members)),
        ],
        compiler_params=pltpu.CompilerParams(collective_id=collective_id, has_side_effects=True),
        cost_estimate=pl.CostEstimate(flops=0, bytes_accessed=100 * MIB, transcendentals=0),
    )(*owned, *shared)


def to_rows(owned, shared, heads, members, collective_id):
    rows = owned[0].shape[0] // heads
    n_owned, n_shared = len(owned), len(shared)
    count = n_owned + n_shared

    def kernel(*refs):
        ins, outs = refs[:count], refs[count : 2 * count]
        local_sem, send_sem, recv_sem, own_sem, part_send, part_recv = refs[2 * count : 2 * count + 6]
        me, group, member, mp = head_place(heads, members)
        head_peers = [((group ^ o) * members + member, mp) for o in range(1, heads)]
        pair_peers = [(group * members + (member ^ o), mp) for o in range(1, members)]
        greet(head_peers + pair_peers)
        if n_shared:
            own, parts, total = refs[2 * count + 6 :]
        copies, pending = [], {}

        def part(array, o, who):
            first = pl.multiple_of(((group ^ o) * members + who) * rows, rows)
            return ins[array].at[pl.ds(first, rows)]

        for s in range(n_shared):
            for o in range(heads):
                copy = pltpu.make_async_copy(part(n_owned + s, o, member), own.at[s, o], own_sem.at[s, o])
                copy.start()
                pending[s, o, 0] = copy
                for p in range(1, members):
                    copy = remote(part(n_owned + s, o, member ^ p), parts.at[s, o, p - 1],
                                  part_send.at[s, o, p], part_recv.at[s, o, p], pair_peers[p - 1])
                    copy.start()
                    pending[s, o, p] = copy
        for a in range(n_owned):
            for o in range(heads):
                piece = ins[a].at[pl.ds(pl.multiple_of((group ^ o) * rows, rows), rows)]
                place = outs[a].at[:, lanes(group)]
                if o:
                    copy = remote(piece, place, send_sem.at[a, o], recv_sem.at[a, o], head_peers[o - 1])
                else:
                    copy = pltpu.make_async_copy(piece, place, local_sem.at[a])
                copy.start()
                copies.append(copy)
        for o in list(range(1, heads)) + [0]:
            for s in range(n_shared):
                for p in range(members):
                    if p:
                        pending[s, o, p].wait_recv()
                    else:
                        pending[s, o, p].wait()
                value = own[s, o].astype(jnp.float32)
                for p in range(1, members):
                    value = value + parts[s, o, p - 1].astype(jnp.float32)
                total[s, o] = value.astype(total.dtype)
                a = n_owned + s
                place = outs[a].at[:, lanes(group)]
                if o:
                    copy = remote(total.at[s, o], place, send_sem.at[a, o], recv_sem.at[a, o], head_peers[o - 1])
                else:
                    copy = pltpu.make_async_copy(total.at[s, o], place, local_sem.at[a])
                copy.start()
                copies.append(copy)
        for s in range(n_shared):
            for o in range(heads):
                for p in range(1, members):
                    pending[s, o, p].wait_send()
        for copy in copies:
            copy.wait()

    dma = pltpu.SemaphoreType.DMA
    slots = max(n_shared, 1)
    scratch = [
        dma((count,)), dma((count, heads)), dma((count, heads)),
        dma((slots, heads)), dma((slots, heads, members)), dma((slots, heads, members)),
    ]
    if n_shared:
        kind = shared[0].dtype
        scratch += [
            pltpu.VMEM((n_shared, heads, rows, HEAD_DIM), kind),
            pltpu.VMEM((n_shared, heads, members - 1, rows, HEAD_DIM), kind),
            pltpu.VMEM((n_shared, heads, rows, HEAD_DIM), kind),
        ]
    return pl.pallas_call(
        kernel,
        out_shape=[jax.ShapeDtypeStruct((rows, heads * HEAD_DIM), a.dtype) for a in owned + shared],
        in_specs=[ANY] * count,
        out_specs=[ANY] * count,
        scratch_shapes=scratch,
        compiler_params=pltpu.CompilerParams(
            collective_id=collective_id, has_side_effects=True, vmem_limit_bytes=48 * MIB
        ),
        cost_estimate=pl.CostEstimate(flops=0, bytes_accessed=100 * MIB, transcendentals=0),
    )(*owned, *shared)


def query_block(index, lengths, order, members, blocks_each):
    member = lax.axis_index("dp") % members
    dealt = ((index // blocks_each) * members + member) * blocks_each + index % blocks_each
    place = order[dealt]
    first, length, running = jnp.int32(0), jnp.int32(0), jnp.int32(0)
    for s in range(lengths.shape[0]):
        inside = place >= running
        first = jnp.where(inside, running, first)
        length = jnp.where(inside, lengths[s], length)
        running = running + (lengths[s] + (BLOCK - 1)) // BLOCK
    behind = place - first
    return first, behind, length - behind * BLOCK


def key_blocks(block_count, slot, visit):
    @pl.loop(0, block_count)
    def _(block):
        visit(pl.multiple_of(block * BLOCK, BLOCK), pl.multiple_of(slot[block] * BLOCK, BLOCK))


def allowed_keys(tile, behind):
    width = KEY_BLOCKS * BLOCK
    key_pos = lax.broadcasted_iota(jnp.int32, (width, BLOCK), 0) + tile * width
    query_pos = lax.broadcasted_iota(jnp.int32, (width, BLOCK), 1) + behind * BLOCK
    return key_pos <= query_pos


def attend(queries, key_rows, value_rows, lengths, order, slot, members, blocks_each):
    query_count, key_count = queries.shape[0] // BLOCK, key_rows.shape[0] // BLOCK
    width = KEY_BLOCKS * BLOCK
    padded = (key_count + KEY_BLOCKS - 1) * BLOCK
    scale = math.log2(math.e) / math.sqrt(HEAD_DIM)

    def kernel(lengths_ref, order_ref, slot_ref, q_ref, k_ref, v_ref, out_ref, exact_ref, log_ref, keys, values_t):
        def visit(to, source):
            keys[pl.ds(to, BLOCK)] = k_ref[pl.ds(source, BLOCK)]
            values_t[:, pl.ds(to, BLOCK)] = v_ref[pl.ds(source, BLOCK)].T

        key_blocks(key_count, slot_ref, visit)
        keys[pl.ds(key_count * BLOCK, padded - key_count * BLOCK)] = jnp.zeros(
            (padded - key_count * BLOCK, HEAD_DIM), keys.dtype)
        values_t[:, pl.ds(key_count * BLOCK, padded - key_count * BLOCK)] = jnp.zeros(
            (HEAD_DIM, padded - key_count * BLOCK), keys.dtype)

        @pl.loop(0, query_count)
        def _(index):
            first, behind, valid = query_block(index, lengths_ref, order_ref, members, blocks_each)
            query_t = q_ref[pl.ds(pl.multiple_of(index * BLOCK, BLOCK), BLOCK)].T

            def step(tile, carry):
                top, total, mix = carry
                row = pl.multiple_of((first + tile * KEY_BLOCKS) * BLOCK, BLOCK)
                scores = jnp.dot(keys[pl.ds(row, width)], query_t, preferred_element_type=jnp.float32) * scale
                scores = jnp.where(allowed_keys(tile, behind), scores, big_negative)
                new_top = jnp.maximum(top, jnp.max(scores, axis=0, keepdims=True))
                weights = jnp.exp2(scores - new_top)
                fade = jnp.exp2(top - new_top)
                total = total * fade + jnp.sum(weights, axis=0, keepdims=True)
                mix = mix * fade + jnp.dot(
                    values_t[:, pl.ds(row, width)], weights.astype(jnp.bfloat16), preferred_element_type=jnp.float32)
                return new_top, total, mix

            top, total, mix = lax.fori_loop(
                0, behind // KEY_BLOCKS + 1, step,
                (jnp.full((1, BLOCK), big_negative, jnp.float32), jnp.zeros((1, BLOCK), jnp.float32),
                 jnp.zeros((HEAD_DIM, BLOCK), jnp.float32)))
            live = lax.broadcasted_iota(jnp.int32, (1, BLOCK), 1) < valid
            mix = jnp.where(live, mix / total, 0.0)
            exact_ref[index] = mix
            out_ref[pl.ds(pl.multiple_of(index * BLOCK, BLOCK), BLOCK)] = mix.T.astype(out_ref.dtype)
            log_ref[index] = jnp.where(live, top + jnp.log2(total), -big_negative)

    return pl.pallas_call(
        kernel,
        out_shape=[
            jax.ShapeDtypeStruct(queries.shape, jnp.bfloat16),
            jax.ShapeDtypeStruct((query_count, HEAD_DIM, BLOCK), jnp.float32),
            jax.ShapeDtypeStruct((query_count, 1, BLOCK), jnp.float32),
        ],
        in_specs=[SMEM] * 3 + [VMEM] * 3,
        out_specs=[VMEM] * 3,
        scratch_shapes=[pltpu.VMEM((padded, HEAD_DIM), jnp.bfloat16), pltpu.VMEM((HEAD_DIM, padded), jnp.bfloat16)],
        compiler_params=pltpu.CompilerParams(vmem_limit_bytes=56 * MIB),
        cost_estimate=pl.CostEstimate(flops=8 << 30, bytes_accessed=50 * MIB, transcendentals=8 << 20),
    )(lengths, order, slot, queries, key_rows, value_rows)


def attend_back(queries, key_rows, value_rows, upstream, exact, logs, lengths, order, slot, members, blocks_each):
    query_count, key_count = queries.shape[0] // BLOCK, key_rows.shape[0] // BLOCK
    width = KEY_BLOCKS * BLOCK
    padded = (key_count + KEY_BLOCKS - 1) * BLOCK
    scale = math.log2(math.e) / math.sqrt(HEAD_DIM)
    plain_scale = 1.0 / math.sqrt(HEAD_DIM)

    def kernel(lengths_ref, order_ref, slot_ref, q_ref, k_ref, v_ref, g_ref, exact_ref, log_ref,
               dq_ref, dk_ref, dv_ref, keys, keys_t, values, key_sum, value_sum):
        def visit(to, source):
            block = k_ref[pl.ds(source, BLOCK)]
            keys[pl.ds(to, BLOCK)] = block
            keys_t[:, pl.ds(to, BLOCK)] = block.T
            values[pl.ds(to, BLOCK)] = v_ref[pl.ds(source, BLOCK)]
            key_sum[pl.ds(to, BLOCK)] = jnp.zeros((BLOCK, HEAD_DIM), jnp.float32)
            value_sum[pl.ds(to, BLOCK)] = jnp.zeros((BLOCK, HEAD_DIM), jnp.float32)

        key_blocks(key_count, slot_ref, visit)
        tail = pl.ds(key_count * BLOCK, padded - key_count * BLOCK)
        keys[tail] = jnp.zeros((padded - key_count * BLOCK, HEAD_DIM), keys.dtype)
        values[tail] = jnp.zeros((padded - key_count * BLOCK, HEAD_DIM), keys.dtype)
        keys_t[:, tail] = jnp.zeros((HEAD_DIM, padded - key_count * BLOCK), keys.dtype)
        key_sum[tail] = jnp.zeros((padded - key_count * BLOCK, HEAD_DIM), jnp.float32)
        value_sum[tail] = jnp.zeros((padded - key_count * BLOCK, HEAD_DIM), jnp.float32)

        @pl.loop(0, query_count)
        def _(index):
            first, behind, _ = query_block(index, lengths_ref, order_ref, members, blocks_each)
            mine = pl.ds(pl.multiple_of(index * BLOCK, BLOCK), BLOCK)
            query = q_ref[mine]
            grad = g_ref[mine]
            query_t, grad_t = query.T, grad.T
            delta = jnp.sum(grad_t.astype(jnp.float32) * exact_ref[index], axis=0, keepdims=True)
            log_total = log_ref[index]

            def step(tile, query_grad):
                row = pl.multiple_of((first + tile * KEY_BLOCKS) * BLOCK, BLOCK)
                span = pl.ds(row, width)
                scores = jnp.dot(keys[span], query_t, preferred_element_type=jnp.float32) * scale
                probability = jnp.where(allowed_keys(tile, behind), jnp.exp2(scores - log_total), 0.0)
                prob_grad = jnp.dot(values[span], grad_t, preferred_element_type=jnp.float32)
                score_grad = (probability * (prob_grad - delta)).astype(jnp.bfloat16)
                value_sum[span] += jnp.dot(
                    probability.astype(jnp.bfloat16), grad, preferred_element_type=jnp.float32)
                key_sum[span] += jnp.dot(score_grad, query, preferred_element_type=jnp.float32)
                return query_grad + jnp.dot(keys_t[:, span], score_grad, preferred_element_type=jnp.float32)

            query_grad = lax.fori_loop(
                0, behind // KEY_BLOCKS + 1, step, jnp.zeros((HEAD_DIM, BLOCK), jnp.float32))
            dq_ref[mine] = (query_grad * plain_scale).T.astype(dq_ref.dtype)

        def leave(at, dealt):
            dk_ref[pl.ds(dealt, BLOCK)] = (key_sum[pl.ds(at, BLOCK)] * plain_scale).astype(dk_ref.dtype)
            dv_ref[pl.ds(dealt, BLOCK)] = value_sum[pl.ds(at, BLOCK)].astype(dv_ref.dtype)

        key_blocks(key_count, slot_ref, leave)

    return pl.pallas_call(
        kernel,
        out_shape=[
            jax.ShapeDtypeStruct(queries.shape, jnp.bfloat16),
            jax.ShapeDtypeStruct(key_rows.shape, jnp.bfloat16),
            jax.ShapeDtypeStruct(key_rows.shape, jnp.bfloat16),
        ],
        in_specs=[SMEM] * 3 + [VMEM] * 6,
        out_specs=[VMEM] * 3,
        scratch_shapes=[
            pltpu.VMEM((padded, HEAD_DIM), jnp.bfloat16),
            pltpu.VMEM((HEAD_DIM, padded), jnp.bfloat16),
            pltpu.VMEM((padded, HEAD_DIM), jnp.bfloat16),
            pltpu.VMEM((padded, HEAD_DIM), jnp.float32),
            pltpu.VMEM((padded, HEAD_DIM), jnp.float32),
        ],
        compiler_params=pltpu.CompilerParams(vmem_limit_bytes=60 * MIB),
        cost_estimate=pl.CostEstimate(flops=20 << 30, bytes_accessed=100 * MIB, transcendentals=8 << 20),
    )(lengths, order, slot, queries, key_rows, value_rows, upstream, exact, logs)


def gather_attention(
    query_weight,
    key_weight,
    value_weight,
    out_weight,
    first_gain,
    first_shift,
    query_bias,
    value_bias,
    out_bias,
):
    return (
        lax.all_gather(query_weight, "dp", axis=0, tiled=True),
        lax.all_gather(key_weight, "dp", axis=0, tiled=True),
        lax.all_gather(value_weight, "dp", axis=0, tiled=True),
        lax.all_gather(out_weight, "dp", axis=0, tiled=True),
        lax.all_gather(first_gain, "dp", axis=0, tiled=True),
        lax.all_gather(first_shift, "dp", axis=0, tiled=True),
        lax.all_gather(query_bias, "dp", axis=0, tiled=True),
        lax.all_gather(value_bias, "dp", axis=0, tiled=True),
        lax.all_gather(out_bias, "dp", axis=0, tiled=True),
    )


def gather_feed(up_weight, down_weight, second_gain, second_shift, up_bias, down_bias):
    return (
        lax.all_gather(up_weight, "dp", axis=0, tiled=True),
        lax.all_gather(down_weight, "dp", axis=0, tiled=True),
        lax.all_gather(second_gain, "dp", axis=0, tiled=True),
        lax.all_gather(second_shift, "dp", axis=0, tiled=True),
        lax.all_gather(up_bias, "dp", axis=0, tiled=True),
        lax.all_gather(down_bias, "dp", axis=0, tiled=True),
    )


def whole_rows(local_part):
    return lax.all_gather(local_part, "mp", axis=0, tiled=True)


def row_share(term, local_rows):
    return lax.psum_scatter(
        term(jnp.int32(0), local_rows * lax.axis_size("mp")).astype(jnp.bfloat16),
        "mp",
        scatter_dimension=0,
        tiled=True,
    ).astype(jnp.float32)


def per_device(
    hidden_in,
    output_grad,
    first_gain,
    first_shift,
    query_weight,
    query_bias,
    key_weight,
    value_weight,
    value_bias,
    out_weight,
    out_bias,
    second_gain,
    second_shift,
    up_weight,
    up_bias,
    down_weight,
    down_bias,
    seq_lengths,
    block_order,
    block_slot,
):
    local_rows = hidden_in.shape[0]
    model_width = hidden_in.shape[1]
    mp_count = lax.axis_size("mp")
    mp_index = lax.axis_index("mp")
    dp_index = lax.axis_index("dp")
    group_rows = local_rows * mp_count
    head_width = query_weight.shape[1]
    heads_local = head_width // HEAD_DIM
    hidden_width = up_weight.shape[1]
    _, _, own_valid = row_meta(
        seq_lengths, block_order, dp_index * group_rows + mp_index * local_rows, local_rows
    )

    def project(normed_rows, gathered):
        all_rows = whole_rows(normed_rows.astype(jnp.bfloat16))
        bias_query = lax.dynamic_slice_in_dim(
            gathered[6], mp_index * head_width, head_width, 0
        ).astype(jnp.float32)
        bias_value = lax.dynamic_slice_in_dim(
            gathered[7], mp_index * head_width, head_width, 0
        ).astype(jnp.float32)
        queries = (
            jnp.dot(all_rows, gathered[0], preferred_element_type=jnp.float32) + bias_query
        ).astype(jnp.bfloat16)
        key_rows = jnp.dot(all_rows, gathered[1], preferred_element_type=jnp.float32).astype(
            jnp.bfloat16
        )
        value_rows = (
            jnp.dot(all_rows, gathered[2], preferred_element_type=jnp.float32) + bias_value
        ).astype(jnp.bfloat16)
        return (all_rows, queries, key_rows, value_rows)

    def expand(normed_rows, gathered):
        all_rows = whole_rows(normed_rows.astype(jnp.bfloat16))
        bias_up = lax.dynamic_slice_in_dim(
            gathered[4], mp_index * hidden_width, hidden_width, 0
        ).astype(jnp.float32)
        pre_act = jnp.dot(all_rows, gathered[0], preferred_element_type=jnp.float32) + bias_up
        return (all_rows, pre_act, gelu_exact(pre_act).astype(jnp.bfloat16))

    input_rows = hidden_in.astype(jnp.float32)
    attn_params = gather_attention(
        query_weight,
        key_weight,
        value_weight,
        out_weight,
        first_gain,
        first_shift,
        query_bias,
        value_bias,
        out_bias,
    )
    normed_one, unit_one, inverse_one = layer_norm(
        input_rows, attn_params[4].astype(jnp.float32), attn_params[5].astype(jnp.float32)
    )
    rows_one, queries, key_rows, value_rows = project(normed_one, attn_params)
    members = lax.axis_size("dp") // heads_local
    blocks_each = group_rows // BLOCK
    head_queries, head_keys, head_values = to_heads(
        [queries], [key_rows, value_rows], heads_local, members, 0
    )
    head_mix, exact_mix, log_total = attend(
        head_queries, head_keys, head_values, seq_lengths, block_order, block_slot, members, blocks_each
    )
    (attended_low,) = to_rows([head_mix], [], heads_local, members, 1)

    def attention_term(first_row, row_count):
        return contract_last(attended_low, attn_params[3])

    residual = (
        input_rows + row_share(attention_term, local_rows) + attn_params[8].astype(jnp.float32)
    )
    feed_params = gather_feed(up_weight, down_weight, second_gain, second_shift, up_bias, down_bias)
    normed_two, unit_two, inverse_two = layer_norm(
        residual, feed_params[2].astype(jnp.float32), feed_params[3].astype(jnp.float32)
    )
    rows_two, pre_act, hidden_low = expand(normed_two, feed_params)

    def feed_term(first_row, row_count):
        return contract_last(hidden_low, feed_params[1])

    result = residual + row_share(feed_term, local_rows) + feed_params[5].astype(jnp.float32)
    output = jnp.where(own_valid[:, None], result, 0.0).astype(jnp.bfloat16)
    result_grad = jnp.where(own_valid[:, None], output_grad.astype(jnp.float32), 0.0)
    branch_two = result_grad.astype(jnp.bfloat16)
    down_bias_part = jnp.sum(branch_two.astype(jnp.float32), axis=0)
    feed_now, rows_two_now, pre_now, hidden_now = feed_params, rows_two, pre_act, hidden_low
    branch_rows_two = whole_rows(branch_two)
    down_weight_part = contract_first(branch_rows_two, hidden_now)
    hidden_grad = jnp.dot(branch_rows_two, feed_now[1], preferred_element_type=jnp.float32)
    act_grad = jax.vjp(gelu_exact, pre_now)[1](hidden_grad)[0]
    pre_grad = act_grad.astype(jnp.bfloat16)
    up_bias_local = jnp.sum(pre_grad.astype(jnp.float32), axis=0)
    up_weight_part = contract_first(rows_two_now, pre_grad)

    def feed_back_term(first_row, row_count):
        return contract_last(pre_grad, feed_now[0])

    normed_two_grad = row_share(feed_back_term, local_rows)
    second_gain_part = jnp.sum(normed_two_grad * unit_two, axis=0)
    second_shift_part = jnp.sum(normed_two_grad, axis=0)
    residual_grad = result_grad + norm_back(
        normed_two_grad, unit_two, inverse_two, feed_now[2].astype(jnp.float32)
    )
    branch_one = residual_grad.astype(jnp.bfloat16)
    out_bias_part = jnp.sum(branch_one.astype(jnp.float32), axis=0)
    attn_now, rows_one_now = attn_params, rows_one
    branch_rows_one = whole_rows(branch_one)
    out_weight_part = contract_first(branch_rows_one, attended_low)
    attended_grad = jnp.dot(
        branch_rows_one, attn_now[3], preferred_element_type=jnp.float32
    ).astype(jnp.bfloat16)
    (head_grad,) = to_heads([attended_grad], [], heads_local, members, 2)
    head_query_grad, head_key_grad, head_value_grad = attend_back(
        head_queries, head_keys, head_values, head_grad, exact_mix, log_total,
        seq_lengths, block_order, block_slot, members, blocks_each,
    )
    query_low, key_low, value_low = to_rows(
        [head_query_grad], [head_key_grad, head_value_grad], heads_local, members, 3
    )
    query_weight_part = contract_first(rows_one_now, query_low)
    key_weight_part = contract_first(rows_one_now, key_low)
    value_weight_part = contract_first(rows_one_now, value_low)
    query_bias_local = jnp.sum(query_low.astype(jnp.float32), axis=0)
    value_bias_local = jnp.sum(value_low.astype(jnp.float32), axis=0)

    def attention_back_term(first_row, row_count):
        total_term = contract_last(query_low, attn_now[0])
        total_term = total_term + contract_last(key_low, attn_now[1])
        return total_term + contract_last(value_low, attn_now[2])

    normed_one_grad = row_share(attention_back_term, local_rows)
    first_gain_part = jnp.sum(normed_one_grad * unit_one, axis=0)
    first_shift_part = jnp.sum(normed_one_grad, axis=0)
    input_grad = residual_grad + norm_back(
        normed_one_grad, unit_one, inverse_one, attn_now[4].astype(jnp.float32)
    )
    query_bias_full = lax.dynamic_update_slice_in_dim(
        jnp.zeros((model_width,), jnp.float32), query_bias_local, mp_index * head_width, 0
    )
    value_bias_full = lax.dynamic_update_slice_in_dim(
        jnp.zeros((model_width,), jnp.float32), value_bias_local, mp_index * head_width, 0
    )
    up_bias_full = lax.dynamic_update_slice_in_dim(
        jnp.zeros((hidden_width * mp_count,), jnp.float32),
        up_bias_local,
        mp_index * hidden_width,
        0,
    )
    vector_sums = (
        lax.psum(first_gain_part.astype(jnp.bfloat16), "mp").astype(jnp.float32),
        lax.psum(first_shift_part.astype(jnp.bfloat16), "mp").astype(jnp.float32),
        lax.psum(query_bias_full.astype(jnp.bfloat16), "mp").astype(jnp.float32),
        lax.psum(value_bias_full.astype(jnp.bfloat16), "mp").astype(jnp.float32),
        lax.psum(out_bias_part.astype(jnp.bfloat16), "mp").astype(jnp.float32),
        lax.psum(second_gain_part.astype(jnp.bfloat16), "mp").astype(jnp.float32),
        lax.psum(second_shift_part.astype(jnp.bfloat16), "mp").astype(jnp.float32),
        lax.psum(up_bias_full.astype(jnp.bfloat16), "mp").astype(jnp.float32),
        lax.psum(down_bias_part.astype(jnp.bfloat16), "mp").astype(jnp.float32),
    )
    owned_grads = (
        lax.psum_scatter(
            vector_sums[0].astype(jnp.bfloat16), "dp", scatter_dimension=0, tiled=True
        ).astype(jnp.float32),
        lax.psum_scatter(
            vector_sums[1].astype(jnp.bfloat16), "dp", scatter_dimension=0, tiled=True
        ).astype(jnp.float32),
        lax.psum_scatter(
            query_weight_part.astype(jnp.bfloat16), "dp", scatter_dimension=0, tiled=True
        ).astype(jnp.float32),
        lax.psum_scatter(
            vector_sums[2].astype(jnp.bfloat16), "dp", scatter_dimension=0, tiled=True
        ).astype(jnp.float32),
        lax.psum_scatter(
            key_weight_part.astype(jnp.bfloat16), "dp", scatter_dimension=0, tiled=True
        ).astype(jnp.float32),
        lax.psum_scatter(
            value_weight_part.astype(jnp.bfloat16), "dp", scatter_dimension=0, tiled=True
        ).astype(jnp.float32),
        lax.psum_scatter(
            vector_sums[3].astype(jnp.bfloat16), "dp", scatter_dimension=0, tiled=True
        ).astype(jnp.float32),
        lax.psum_scatter(
            out_weight_part.astype(jnp.bfloat16), "dp", scatter_dimension=0, tiled=True
        ).astype(jnp.float32),
        lax.psum_scatter(
            vector_sums[4].astype(jnp.bfloat16), "dp", scatter_dimension=0, tiled=True
        ).astype(jnp.float32),
        lax.psum_scatter(
            vector_sums[5].astype(jnp.bfloat16), "dp", scatter_dimension=0, tiled=True
        ).astype(jnp.float32),
        lax.psum_scatter(
            vector_sums[6].astype(jnp.bfloat16), "dp", scatter_dimension=0, tiled=True
        ).astype(jnp.float32),
        lax.psum_scatter(
            up_weight_part.astype(jnp.bfloat16), "dp", scatter_dimension=0, tiled=True
        ).astype(jnp.float32),
        lax.psum_scatter(
            vector_sums[7].astype(jnp.bfloat16), "dp", scatter_dimension=0, tiled=True
        ).astype(jnp.float32),
        lax.psum_scatter(
            down_weight_part.astype(jnp.bfloat16), "dp", scatter_dimension=0, tiled=True
        ).astype(jnp.float32),
        lax.psum_scatter(
            vector_sums[8].astype(jnp.bfloat16), "dp", scatter_dimension=0, tiled=True
        ).astype(jnp.float32),
    )
    return (
        output,
        input_grad,
        owned_grads[0],
        owned_grads[1],
        owned_grads[2],
        owned_grads[3],
        owned_grads[4],
        owned_grads[5],
        owned_grads[6],
        owned_grads[7],
        owned_grads[8],
        owned_grads[9],
        owned_grads[10],
        owned_grads[11],
        owned_grads[12],
        owned_grads[13],
        owned_grads[14],
    )


def solution(mesh):
    return jax.shard_map(
        per_device,
        mesh=mesh,
        in_specs=(
            P(("dp", "mp"), None),
            P(("dp", "mp"), None),
            P("dp"),
            P("dp"),
            P("dp", "mp"),
            P("dp"),
            P("dp", "mp"),
            P("dp", "mp"),
            P("dp"),
            P("dp", "mp"),
            P("dp"),
            P("dp"),
            P("dp"),
            P("dp", "mp"),
            P("dp"),
            P("dp", "mp"),
            P("dp"),
            P(),
            P(),
            P(),
        ),
        out_specs=(
            P(("dp", "mp"), None),
            P(("dp", "mp"), None),
            P("dp"),
            P("dp"),
            P("dp", "mp"),
            P("dp"),
            P("dp", "mp"),
            P("dp", "mp"),
            P("dp"),
            P("dp", "mp"),
            P("dp"),
            P("dp"),
            P("dp"),
            P("dp", "mp"),
            P("dp"),
            P("dp", "mp"),
            P("dp"),
        ),
        check_vma=False,
    )
```

```python
import math

import jax
import jax.numpy as jnp
from jax import lax
from jax.experimental import pallas as pl
from jax.experimental.pallas import tpu as pltpu
from jax.sharding import PartitionSpec as P

HEAD_DIM = 128
BLOCK = 128
KEY_BLOCKS = 4
MESH = pl.DeviceIdType.MESH
ANY = pl.BlockSpec(memory_space=pl.ANY)
VMEM = pl.BlockSpec(memory_space=pltpu.VMEM)
SMEM = pl.BlockSpec(memory_space=pltpu.SMEM)
MIB = 1 << 20


big_negative = -1e30
norm_epsilon = 1e-05


def norm_back(upstream, normed, inverse, gain_row):
    scaled = upstream * gain_row
    mean_grad = jnp.mean(scaled, axis=-1, keepdims=True)
    second = jnp.mean(scaled * normed, axis=-1, keepdims=True)
    return inverse * (scaled - mean_grad - normed * second)


def gelu_exact(values):
    return jax.nn.gelu(values, approximate=False)


def contract_last(left, right):
    return lax.dot_general(
        left, right, (((1,), (1,)), ((), ())), preferred_element_type=jnp.float32
    )


def contract_first(left, right):
    return lax.dot_general(
        left, right, (((0,), (0,)), ((), ())), preferred_element_type=jnp.float32
    )


def valid_rows(seq_lengths, block_order, first_row, row_count):
    row_ids = first_row + jnp.arange(row_count, dtype=jnp.int32)
    slot_hit = (row_ids // BLOCK)[:, None] == jnp.arange(block_order.shape[0], dtype=jnp.int32)[None, :]
    initial = jnp.sum(jnp.where(slot_hit, block_order[None, :], 0), axis=1)
    block_counts = (seq_lengths + BLOCK - 1) // BLOCK
    ends = jnp.cumsum(block_counts)
    starts = ends - block_counts
    inside = (initial[:, None] >= starts[None, :]) & (initial[:, None] < ends[None, :])
    left = seq_lengths[None, :] - (initial[:, None] - starts[None, :]) * BLOCK
    return (row_ids % BLOCK) < jnp.sum(jnp.where(inside, left, 0), axis=1)


def whole_rows(local_part):
    return lax.all_gather(local_part, "mp", axis=0, tiled=True)


def row_share(term):
    term = term.astype(jnp.bfloat16)
    return lax.psum_scatter(term, "mp", scatter_dimension=0, tiled=True).astype(jnp.float32)


def owner_share(term):
    term = term.astype(jnp.bfloat16)
    return lax.psum_scatter(term, "dp", scatter_dimension=0, tiled=True).astype(jnp.float32)


def greet(peers):
    barrier = pltpu.get_barrier_semaphore()
    for peer in peers:
        pl.semaphore_signal(barrier, inc=1, device_id=peer, device_id_type=MESH)
    pl.semaphore_wait(barrier, len(peers))


def remote(src, dst, send_sem, recv_sem, peer):
    return pltpu.make_async_remote_copy(
        src_ref=src, dst_ref=dst, send_sem=send_sem, recv_sem=recv_sem,
        device_id=peer, device_id_type=MESH,
    )


def head_place(heads, members):
    me = lax.axis_index("dp")
    return me, me // members, me % members, lax.axis_index("mp")


def lanes(head):
    return pl.ds(pl.multiple_of(head * HEAD_DIM, HEAD_DIM), HEAD_DIM)


def to_heads(owned, shared, heads, members, collective_id):
    rows = (owned + shared)[0].shape[0]
    n_owned, n_shared = len(owned), len(shared)
    count = n_owned + n_shared

    def kernel(*refs):
        ins, outs = refs[:count], refs[count : 2 * count]
        local_sem, send_sem, recv_sem, fwd_send, fwd_recv = refs[2 * count :]
        me, group, member, mp = head_place(heads, members)

        def dest(array, source):
            place = (source // members) if array < n_owned else source
            return outs[array].at[pl.ds(pl.multiple_of(place * rows, rows), rows)]

        head_peers = [((group ^ o) * members + member, mp) for o in range(1, heads)]
        pair_peers = [(group * members + (member ^ o), mp) for o in range(1, members)]
        greet(head_peers + pair_peers)
        order = list(range(n_owned, count)) + list(range(n_owned))
        sends, locals_, forwards = {}, [], []
        for a in order:
            for o in range(1, heads):
                copy = remote(ins[a].at[:, lanes(group ^ o)], dest(a, me), send_sem.at[a, o],
                              recv_sem.at[a, o], head_peers[o - 1])
                copy.start()
                sends[a, o] = copy
        for a in range(count):
            copy = pltpu.make_async_copy(ins[a].at[:, lanes(group)], dest(a, me), local_sem.at[a])
            copy.start()
            locals_.append(copy)
        for a in range(n_owned, count):
            for o in range(heads):
                source = (group ^ o) * members + member
                if o:
                    sends[a, o].wait_recv()
                for p in range(1, members):
                    piece = ins[a].at[:, lanes(group)] if o == 0 else dest(a, source)
                    copy = remote(piece, dest(a, source), fwd_send.at[a - n_owned, o, p],
                                  fwd_recv.at[a - n_owned, o, p], pair_peers[p - 1])
                    copy.start()
                    forwards.append(copy)
        for copy in locals_:
            copy.wait()
        for (a, o), copy in sends.items():
            copy.wait_send()
            if a < n_owned:
                copy.wait_recv()
        for copy in forwards:
            copy.wait()

    total = rows * lax.axis_size("dp")
    shapes = [jax.ShapeDtypeStruct((heads * rows, HEAD_DIM), a.dtype) for a in owned]
    shapes += [jax.ShapeDtypeStruct((total, HEAD_DIM), a.dtype) for a in shared]
    dma = pltpu.SemaphoreType.DMA
    return pl.pallas_call(
        kernel,
        out_shape=shapes,
        in_specs=[ANY] * count,
        out_specs=[ANY] * count,
        scratch_shapes=[
            dma((count,)), dma((count, heads)), dma((count, heads)),
            dma((max(n_shared, 1), heads, members)), dma((max(n_shared, 1), heads, members)),
        ],
        compiler_params=pltpu.CompilerParams(collective_id=collective_id, has_side_effects=True),
        cost_estimate=pl.CostEstimate(flops=0, bytes_accessed=100 * MIB, transcendentals=0),
    )(*owned, *shared)


def to_rows(owned, shared, heads, members, collective_id):
    rows = owned[0].shape[0] // heads
    n_owned, n_shared = len(owned), len(shared)
    count = n_owned + n_shared

    def kernel(*refs):
        ins, outs = refs[:count], refs[count : 2 * count]
        local_sem, send_sem, recv_sem, own_sem, part_send, part_recv = refs[2 * count : 2 * count + 6]
        me, group, member, mp = head_place(heads, members)
        head_peers = [((group ^ o) * members + member, mp) for o in range(1, heads)]
        pair_peers = [(group * members + (member ^ o), mp) for o in range(1, members)]
        greet(head_peers + pair_peers)
        if n_shared:
            own, parts, total = refs[2 * count + 6 :]
        copies, pending = [], {}

        def part(array, o, who):
            first = pl.multiple_of(((group ^ o) * members + who) * rows, rows)
            return ins[array].at[pl.ds(first, rows)]

        for s in range(n_shared):
            for o in range(heads):
                copy = pltpu.make_async_copy(part(n_owned + s, o, member), own.at[s, o], own_sem.at[s, o])
                copy.start()
                pending[s, o, 0] = copy
                for p in range(1, members):
                    copy = remote(part(n_owned + s, o, member ^ p), parts.at[s, o, p - 1],
                                  part_send.at[s, o, p], part_recv.at[s, o, p], pair_peers[p - 1])
                    copy.start()
                    pending[s, o, p] = copy
        for a in range(n_owned):
            for o in range(heads):
                piece = ins[a].at[pl.ds(pl.multiple_of((group ^ o) * rows, rows), rows)]
                place = outs[a].at[:, lanes(group)]
                if o:
                    copy = remote(piece, place, send_sem.at[a, o], recv_sem.at[a, o], head_peers[o - 1])
                else:
                    copy = pltpu.make_async_copy(piece, place, local_sem.at[a])
                copy.start()
                copies.append(copy)
        for o in list(range(1, heads)) + [0]:
            for s in range(n_shared):
                for p in range(members):
                    if p:
                        pending[s, o, p].wait_recv()
                    else:
                        pending[s, o, p].wait()
                value = own[s, o].astype(jnp.float32)
                for p in range(1, members):
                    value = value + parts[s, o, p - 1].astype(jnp.float32)
                total[s, o] = value.astype(total.dtype)
                a = n_owned + s
                place = outs[a].at[:, lanes(group)]
                if o:
                    copy = remote(total.at[s, o], place, send_sem.at[a, o], recv_sem.at[a, o], head_peers[o - 1])
                else:
                    copy = pltpu.make_async_copy(total.at[s, o], place, local_sem.at[a])
                copy.start()
                copies.append(copy)
        for s in range(n_shared):
            for o in range(heads):
                for p in range(1, members):
                    pending[s, o, p].wait_send()
        for copy in copies:
            copy.wait()

    dma = pltpu.SemaphoreType.DMA
    slots = max(n_shared, 1)
    scratch = [
        dma((count,)), dma((count, heads)), dma((count, heads)),
        dma((slots, heads)), dma((slots, heads, members)), dma((slots, heads, members)),
    ]
    if n_shared:
        kind = shared[0].dtype
        scratch += [
            pltpu.VMEM((n_shared, heads, rows, HEAD_DIM), kind),
            pltpu.VMEM((n_shared, heads, members - 1, rows, HEAD_DIM), kind),
            pltpu.VMEM((n_shared, heads, rows, HEAD_DIM), kind),
        ]
    return pl.pallas_call(
        kernel,
        out_shape=[jax.ShapeDtypeStruct((rows, heads * HEAD_DIM), a.dtype) for a in owned + shared],
        in_specs=[ANY] * count,
        out_specs=[ANY] * count,
        scratch_shapes=scratch,
        compiler_params=pltpu.CompilerParams(
            collective_id=collective_id, has_side_effects=True, vmem_limit_bytes=48 * MIB
        ),
        cost_estimate=pl.CostEstimate(flops=0, bytes_accessed=100 * MIB, transcendentals=0),
    )(*owned, *shared)


def query_block(index, lengths, order, members, blocks_each):
    member = lax.axis_index("dp") % members
    dealt = ((index // blocks_each) * members + member) * blocks_each + index % blocks_each
    place = order[dealt]
    first, length, running = jnp.int32(0), jnp.int32(0), jnp.int32(0)
    for s in range(lengths.shape[0]):
        inside = place >= running
        first = jnp.where(inside, running, first)
        length = jnp.where(inside, lengths[s], length)
        running = running + (lengths[s] + (BLOCK - 1)) // BLOCK
    behind = place - first
    return first, behind, length - behind * BLOCK


def key_blocks(block_count, slot, visit):
    @pl.loop(0, block_count)
    def _(block):
        visit(pl.multiple_of(block * BLOCK, BLOCK), pl.multiple_of(slot[block] * BLOCK, BLOCK))


def allowed_keys(tile, behind):
    width = KEY_BLOCKS * BLOCK
    key_pos = lax.broadcasted_iota(jnp.int32, (width, BLOCK), 0) + tile * width
    query_pos = lax.broadcasted_iota(jnp.int32, (width, BLOCK), 1) + behind * BLOCK
    return key_pos <= query_pos


def attend(queries, key_rows, value_rows, lengths, order, slot, members, blocks_each):
    query_count, key_count = queries.shape[0] // BLOCK, key_rows.shape[0] // BLOCK
    width = KEY_BLOCKS * BLOCK
    padded = (key_count + KEY_BLOCKS - 1) * BLOCK
    scale = math.log2(math.e) / math.sqrt(HEAD_DIM)

    def kernel(lengths_ref, order_ref, slot_ref, q_ref, k_ref, v_ref, out_ref, exact_ref, log_ref, keys, values_t):
        def visit(to, source):
            keys[pl.ds(to, BLOCK)] = k_ref[pl.ds(source, BLOCK)]
            values_t[:, pl.ds(to, BLOCK)] = v_ref[pl.ds(source, BLOCK)].T

        key_blocks(key_count, slot_ref, visit)
        keys[pl.ds(key_count * BLOCK, padded - key_count * BLOCK)] = jnp.zeros(
            (padded - key_count * BLOCK, HEAD_DIM), keys.dtype)
        values_t[:, pl.ds(key_count * BLOCK, padded - key_count * BLOCK)] = jnp.zeros(
            (HEAD_DIM, padded - key_count * BLOCK), keys.dtype)

        @pl.loop(0, query_count)
        def _(index):
            first, behind, valid = query_block(index, lengths_ref, order_ref, members, blocks_each)
            query_t = q_ref[pl.ds(pl.multiple_of(index * BLOCK, BLOCK), BLOCK)].T

            def step(tile, carry):
                top, total, mix = carry
                row = pl.multiple_of((first + tile * KEY_BLOCKS) * BLOCK, BLOCK)
                scores = jnp.dot(keys[pl.ds(row, width)], query_t, preferred_element_type=jnp.float32) * scale
                scores = jnp.where(allowed_keys(tile, behind), scores, big_negative)
                new_top = jnp.maximum(top, jnp.max(scores, axis=0, keepdims=True))
                weights = jnp.exp2(scores - new_top)
                fade = jnp.exp2(top - new_top)
                total = total * fade + jnp.sum(weights, axis=0, keepdims=True)
                mix = mix * fade + jnp.dot(
                    values_t[:, pl.ds(row, width)], weights.astype(jnp.bfloat16), preferred_element_type=jnp.float32)
                return new_top, total, mix

            top, total, mix = lax.fori_loop(
                0, behind // KEY_BLOCKS + 1, step,
                (jnp.full((1, BLOCK), big_negative, jnp.float32), jnp.zeros((1, BLOCK), jnp.float32),
                 jnp.zeros((HEAD_DIM, BLOCK), jnp.float32)))
            live = lax.broadcasted_iota(jnp.int32, (1, BLOCK), 1) < valid
            mix = jnp.where(live, mix / total, 0.0)
            exact_ref[index] = mix
            out_ref[pl.ds(pl.multiple_of(index * BLOCK, BLOCK), BLOCK)] = mix.T.astype(out_ref.dtype)
            log_ref[index] = jnp.where(live, top + jnp.log2(total), -big_negative)

    return pl.pallas_call(
        kernel,
        out_shape=[
            jax.ShapeDtypeStruct(queries.shape, jnp.bfloat16),
            jax.ShapeDtypeStruct((query_count, HEAD_DIM, BLOCK), jnp.float32),
            jax.ShapeDtypeStruct((query_count, 1, BLOCK), jnp.float32),
        ],
        in_specs=[SMEM] * 3 + [VMEM] * 3,
        out_specs=[VMEM] * 3,
        scratch_shapes=[pltpu.VMEM((padded, HEAD_DIM), jnp.bfloat16), pltpu.VMEM((HEAD_DIM, padded), jnp.bfloat16)],
        compiler_params=pltpu.CompilerParams(vmem_limit_bytes=56 * MIB),
        cost_estimate=pl.CostEstimate(flops=8 << 30, bytes_accessed=50 * MIB, transcendentals=8 << 20),
    )(lengths, order, slot, queries, key_rows, value_rows)


def attend_back(queries, key_rows, value_rows, upstream, exact, logs, lengths, order, slot, members, blocks_each):
    query_count, key_count = queries.shape[0] // BLOCK, key_rows.shape[0] // BLOCK
    width = KEY_BLOCKS * BLOCK
    padded = (key_count + KEY_BLOCKS - 1) * BLOCK
    scale = math.log2(math.e) / math.sqrt(HEAD_DIM)
    plain_scale = 1.0 / math.sqrt(HEAD_DIM)

    def kernel(lengths_ref, order_ref, slot_ref, q_ref, k_ref, v_ref, g_ref, exact_ref, log_ref,
               dq_ref, dk_ref, dv_ref, keys, keys_t, values, key_sum, value_sum):
        def visit(to, source):
            block = k_ref[pl.ds(source, BLOCK)]
            keys[pl.ds(to, BLOCK)] = block
            keys_t[:, pl.ds(to, BLOCK)] = block.T
            values[pl.ds(to, BLOCK)] = v_ref[pl.ds(source, BLOCK)]
            key_sum[pl.ds(to, BLOCK)] = jnp.zeros((BLOCK, HEAD_DIM), jnp.float32)
            value_sum[pl.ds(to, BLOCK)] = jnp.zeros((BLOCK, HEAD_DIM), jnp.float32)

        key_blocks(key_count, slot_ref, visit)
        tail = pl.ds(key_count * BLOCK, padded - key_count * BLOCK)
        keys[tail] = jnp.zeros((padded - key_count * BLOCK, HEAD_DIM), keys.dtype)
        values[tail] = jnp.zeros((padded - key_count * BLOCK, HEAD_DIM), keys.dtype)
        keys_t[:, tail] = jnp.zeros((HEAD_DIM, padded - key_count * BLOCK), keys.dtype)
        key_sum[tail] = jnp.zeros((padded - key_count * BLOCK, HEAD_DIM), jnp.float32)
        value_sum[tail] = jnp.zeros((padded - key_count * BLOCK, HEAD_DIM), jnp.float32)

        @pl.loop(0, query_count)
        def _(index):
            first, behind, _ = query_block(index, lengths_ref, order_ref, members, blocks_each)
            mine = pl.ds(pl.multiple_of(index * BLOCK, BLOCK), BLOCK)
            query = q_ref[mine]
            grad = g_ref[mine]
            query_t, grad_t = query.T, grad.T
            delta = jnp.sum(grad_t.astype(jnp.float32) * exact_ref[index], axis=0, keepdims=True)
            log_total = log_ref[index]

            def step(tile, query_grad):
                row = pl.multiple_of((first + tile * KEY_BLOCKS) * BLOCK, BLOCK)
                span = pl.ds(row, width)
                scores = jnp.dot(keys[span], query_t, preferred_element_type=jnp.float32) * scale
                probability = jnp.where(allowed_keys(tile, behind), jnp.exp2(scores - log_total), 0.0)
                prob_grad = jnp.dot(values[span], grad_t, preferred_element_type=jnp.float32)
                score_grad = (probability * (prob_grad - delta)).astype(jnp.bfloat16)
                value_sum[span] += jnp.dot(
                    probability.astype(jnp.bfloat16), grad, preferred_element_type=jnp.float32)
                key_sum[span] += jnp.dot(score_grad, query, preferred_element_type=jnp.float32)
                return query_grad + jnp.dot(keys_t[:, span], score_grad, preferred_element_type=jnp.float32)

            query_grad = lax.fori_loop(
                0, behind // KEY_BLOCKS + 1, step, jnp.zeros((HEAD_DIM, BLOCK), jnp.float32))
            dq_ref[mine] = (query_grad * plain_scale).T.astype(dq_ref.dtype)

        def leave(at, dealt):
            dk_ref[pl.ds(dealt, BLOCK)] = (key_sum[pl.ds(at, BLOCK)] * plain_scale).astype(dk_ref.dtype)
            dv_ref[pl.ds(dealt, BLOCK)] = value_sum[pl.ds(at, BLOCK)].astype(dv_ref.dtype)

        key_blocks(key_count, slot_ref, leave)

    return pl.pallas_call(
        kernel,
        out_shape=[
            jax.ShapeDtypeStruct(queries.shape, jnp.bfloat16),
            jax.ShapeDtypeStruct(key_rows.shape, jnp.bfloat16),
            jax.ShapeDtypeStruct(key_rows.shape, jnp.bfloat16),
        ],
        in_specs=[SMEM] * 3 + [VMEM] * 6,
        out_specs=[VMEM] * 3,
        scratch_shapes=[
            pltpu.VMEM((padded, HEAD_DIM), jnp.bfloat16),
            pltpu.VMEM((HEAD_DIM, padded), jnp.bfloat16),
            pltpu.VMEM((padded, HEAD_DIM), jnp.bfloat16),
            pltpu.VMEM((padded, HEAD_DIM), jnp.float32),
            pltpu.VMEM((padded, HEAD_DIM), jnp.float32),
        ],
        compiler_params=pltpu.CompilerParams(vmem_limit_bytes=60 * MIB),
        cost_estimate=pl.CostEstimate(flops=20 << 30, bytes_accessed=100 * MIB, transcendentals=8 << 20),
    )(lengths, order, slot, queries, key_rows, value_rows, upstream, exact, logs)


def line_neighbours(mp, count):
    return ((1, mp + 1 < count, jnp.minimum(mp + 1, count - 1)), (-1, mp >= 1, jnp.maximum(mp - 1, 0)))


def greet_all(fixed, dp, mp, count):
    barrier = pltpu.get_barrier_semaphore()
    for peer in fixed:
        pl.semaphore_signal(barrier, inc=1, device_id=peer, device_id_type=MESH)
    expected = jnp.int32(len(fixed))
    for _, there, place in line_neighbours(mp, count):

        @pl.when(there)
        def _():
            pl.semaphore_signal(barrier, inc=1, device_id=(dp, place), device_id_type=MESH)

        expected = expected + there.astype(jnp.int32)
    pl.semaphore_wait(barrier, expected)


class LineGather:
    def __init__(self, own, full, rows, pieces, send_sem, recv_sem, dp, mp, count):
        self.own, self.full, self.rows, self.pieces = own, full, rows, pieces
        self.send_sem, self.recv_sem, self.dp, self.mp, self.count = send_sem, recv_sem, dp, mp, count
        self.size = rows // pieces

    def place(self, block, piece):
        return self.full.at[pl.ds(pl.multiple_of(block * self.rows + piece * self.size, self.size), self.size)]

    def hop(self, way, step, piece):
        sign, there, neighbour = line_neighbours(self.mp, self.count)[way]
        origin = self.mp - sign * step
        exists = (origin >= 0) & (origin < self.count)
        origin = jnp.clip(origin, 0, self.count - 1)
        if step == 0:
            source = self.own.at[pl.ds(pl.multiple_of(piece * self.size, self.size), self.size)]
        else:
            source = self.place(origin, piece)
        def copy():
            return remote(source, self.place(origin, piece), self.send_sem.at[way, step, piece],
                          self.recv_sem.at[way, step, piece], (self.dp, neighbour))

        return exists, exists & there, copy

    def advance(self, step, piece, also=True):
        for way in range(2):
            if step:
                exists, _, _ = self.hop(way, step, piece)
                _, _, earlier = self.hop(way, step - 1, piece)

                @pl.when(exists & also)
                def _():
                    earlier().wait_recv()

            if step < self.count - 1:
                _, sends, copy = self.hop(way, step, piece)

                @pl.when(sends & also)
                def _():
                    copy().start()

    def finish(self):
        @pl.loop(0, self.pieces)
        def _(piece):
            for way in range(2):
                for step in range(self.count - 1):
                    _, sends, copy = self.hop(way, step, piece)

                    @pl.when(sends)
                    def _():
                        copy().wait_send()

    @staticmethod
    def semaphores(count, pieces):
        return [pltpu.SemaphoreType.DMA((2, count, pieces)), pltpu.SemaphoreType.DMA((2, count, pieces))]


class LineReduce:
    def __init__(self, part, flows, rows, pieces, send_sem, recv_sem, dp, mp, count):
        self.part, self.flows, self.rows, self.pieces = part, flows, rows, pieces
        self.send_sem, self.recv_sem, self.dp, self.mp, self.count = send_sem, recv_sem, dp, mp, count
        self.size = rows // pieces

    def span(self, block, piece):
        return pl.ds(pl.multiple_of(block * self.rows + piece * self.size, self.size), self.size)

    def hop(self, way, block, piece, first=False):
        neighbour = line_neighbours(self.mp, self.count)[way][2]
        span = self.span(block, piece)
        source = self.part.at[span] if first else self.flows.at[way, span]
        return remote(source, self.flows.at[way, span], self.send_sem.at[way, block, piece],
                      self.recv_sem.at[way, block, piece], (self.dp, neighbour))

    def roles(self, way, block):
        if way == 0:
            behind, ahead = self.mp >= 1, self.mp < block
            ends = self.mp <= block
        else:
            behind, ahead = self.mp < self.count - 1, self.mp > block
            ends = self.mp >= block
        return ahead & jnp.logical_not(behind), ahead & behind, ends & behind

    def targets(self):
        for index in range(self.count - 1):
            yield 0, self.count - 1 - index
            yield 1, index

    def begin(self):
        @pl.loop(0, self.pieces)
        def _(piece):
            for way, block in self.targets():
                begins, _, _ = self.roles(way, block)

                @pl.when(begins)
                def _():
                    self.hop(way, block, piece, True).start()

    def advance(self, piece):
        for way, block in self.targets():
            _, hands_on, receives = self.roles(way, block)

            @pl.when(receives)
            def _():
                self.hop(way, block, piece).wait_recv()

            @pl.when(hands_on)
            def _():
                span = self.span(block, piece)
                value = self.flows[way, span].astype(jnp.float32) + self.part[span].astype(jnp.float32)
                self.flows[way, span] = value.astype(self.flows.dtype)
                self.hop(way, block, piece).start()

    def total(self, piece, result):
        span = self.span(self.mp, piece)
        result[...] = self.part[span].astype(jnp.float32)
        for way in range(2):

            @pl.when(self.mp >= 1 if way == 0 else self.mp < self.count - 1)
            def _():
                result[...] += self.flows[way, span].astype(jnp.float32)

    def finish(self):
        @pl.loop(0, self.pieces)
        def _(piece):
            for way, block in self.targets():
                begins, hands_on, _ = self.roles(way, block)

                @pl.when(begins)
                def _():
                    self.hop(way, block, piece, True).wait_send()

                @pl.when(hands_on)
                def _():
                    self.hop(way, block, piece).wait_send()

    @staticmethod
    def scratch(count, rows, width, pieces):
        return [pltpu.VMEM((2, count * rows, width), jnp.bfloat16),
                pltpu.SemaphoreType.DMA((2, count, pieces)), pltpu.SemaphoreType.DMA((2, count, pieces))]


PIECES = 8


def gather_first(hidden, vectors, weights, collective_id):
    rows, width = hidden.shape
    dp_count, mp_count = lax.axis_size("dp"), lax.axis_size("mp")
    chips = dp_count // 2
    arrays = [vectors] + list(weights)
    count = len(arrays)
    depth = [a.shape[0] for a in arrays]

    def kernel(*refs):
        own_rows, ins = refs[0], refs[1 : 1 + count]
        full_rows, outs = refs[1 + count], refs[2 + count : 2 + 2 * count]
        row_sem, local_sem, line_send, line_recv, send_sem, recv_sem, fwd_send, fwd_recv = refs[2 + 2 * count :]
        dp, mp = lax.axis_index("dp"), lax.axis_index("mp")
        peers = [(dp ^ (2 * o), mp) for o in range(1, chips)]
        partner = (dp ^ 1, mp)
        greet_all(peers + [partner], dp, mp, mp_count)
        line = LineGather(own_rows, full_rows, rows, PIECES, line_send, line_recv, dp, mp, mp_count)

        def place(array, owner):
            return outs[array].at[pl.ds(pl.multiple_of(owner * depth[array], depth[array]), depth[array])]

        def cross(array, o):
            return remote(ins[array], place(array, dp), send_sem.at[array, o], recv_sem.at[array, o], peers[o - 1])

        def forward(array, o):
            owner = dp ^ (2 * o)
            source = place(array, owner) if o else ins[array]
            return remote(source, place(array, owner), fwd_send.at[array, o], fwd_recv.at[array, o], partner)

        @pl.loop(0, PIECES)
        def _(piece):
            line.advance(0, piece)

        for a in range(count):
            for o in range(1, chips):
                cross(a, o).start()
            forward(a, 0).start()
        own_copy = pltpu.make_async_copy(own_rows, full_rows.at[pl.ds(pl.multiple_of(mp * rows, rows), rows)], row_sem)
        own_copy.start()
        locals_ = [pltpu.make_async_copy(ins[a], place(a, dp), local_sem.at[a]) for a in range(count)]
        for copy in locals_:
            copy.start()
        for step in range(1, mp_count - 1):

            @pl.loop(0, PIECES)
            def _(piece):
                line.advance(step, piece)

        for a in range(count):
            for o in range(1, chips):
                cross(a, o).wait_recv()
                forward(a, o).start()

        @pl.loop(0, PIECES)
        def _(piece):
            line.advance(mp_count - 1, piece)

        line.finish()
        own_copy.wait()
        for a in range(count):
            locals_[a].wait()
            for o in range(chips):
                if o:
                    cross(a, o).wait_send()
                forward(a, o).wait()

    dma = pltpu.SemaphoreType.DMA
    return pl.pallas_call(
        kernel,
        out_shape=[jax.ShapeDtypeStruct((mp_count * rows, width), hidden.dtype)]
        + [jax.ShapeDtypeStruct((dp_count * a.shape[0], a.shape[1]), a.dtype) for a in arrays],
        in_specs=[ANY] * (1 + count),
        out_specs=[ANY] * (1 + count),
        scratch_shapes=[dma(()), dma((count,))] + LineGather.semaphores(mp_count, PIECES)
        + [dma((count, chips)) for _ in range(4)],
        compiler_params=pltpu.CompilerParams(collective_id=collective_id, has_side_effects=True),
        cost_estimate=pl.CostEstimate(flops=0, bytes_accessed=200 * MIB, transcendentals=0),
    )(hidden, *arrays)


def unit_rows(values):
    average = jnp.mean(values, axis=-1, keepdims=True)
    centred = values - average
    inverse = lax.rsqrt(jnp.mean(centred * centred, axis=-1, keepdims=True) + norm_epsilon)
    return centred * inverse, inverse


def reduce_norm_gather(part, hidden, out_bias, gain, shift, collective_id):
    mp_count = lax.axis_size("mp")
    rows, width = hidden.shape
    size = rows // PIECES

    def kernel(part_ref, hidden_ref, bias_ref, gain_ref, shift_ref, residual_ref, full_ref,
               total, normed, flows, red_send, red_recv, line_send, line_recv, own_sem):
        dp, mp = lax.axis_index("dp"), lax.axis_index("mp")
        greet_all([], dp, mp, mp_count)
        reduce = LineReduce(part_ref, flows, rows, PIECES, red_send, red_recv, dp, mp, mp_count)
        gather = LineGather(normed, full_ref, rows, PIECES, line_send, line_recv, dp, mp, mp_count)
        reduce.begin()

        @pl.loop(0, PIECES + mp_count - 1)
        def _(turn):
            @pl.when(turn < PIECES)
            def _():
                reduce.advance(turn)
                reduce.total(turn, total)
                span = pl.ds(pl.multiple_of(turn * size, size), size)
                residual = hidden_ref[span].astype(jnp.float32) + total[...] + bias_ref[...]
                residual_ref[span] = residual
                unit, _ = unit_rows(residual)
                normed[span] = (unit * gain_ref[...] + shift_ref[...]).astype(normed.dtype)
                gather.advance(0, turn)

            for step in range(1, mp_count):
                piece = jnp.clip(turn - step, 0, PIECES - 1)
                gather.advance(step, piece, (turn >= step) & (turn - step < PIECES))

        own = pltpu.make_async_copy(normed, full_ref.at[pl.ds(pl.multiple_of(mp * rows, rows), rows)], own_sem)
        own.start()
        reduce.finish()
        gather.finish()
        own.wait()

    return pl.pallas_call(
        kernel,
        out_shape=[
            jax.ShapeDtypeStruct((rows, width), jnp.float32),
            jax.ShapeDtypeStruct((mp_count * rows, width), jnp.bfloat16),
        ],
        in_specs=[VMEM] * 5,
        out_specs=[VMEM, ANY],
        scratch_shapes=[pltpu.VMEM((size, width), jnp.float32), pltpu.VMEM((rows, width), jnp.bfloat16)]
        + LineReduce.scratch(mp_count, rows, width, PIECES) + LineGather.semaphores(mp_count, PIECES)
        + [pltpu.SemaphoreType.DMA(())],
        compiler_params=pltpu.CompilerParams(
            collective_id=collective_id, has_side_effects=True, vmem_limit_bytes=48 * MIB),
        cost_estimate=pl.CostEstimate(flops=0, bytes_accessed=300 * MIB, transcendentals=0),
    )(part, hidden, out_bias, gain, shift)


def reduce_back_gather(part, residual, branch_two, gain, collective_id):
    mp_count = lax.axis_size("mp")
    rows, width = residual.shape
    size = rows // PIECES

    def kernel(part_ref, residual_ref, branch_ref, gain_ref, grad_ref, sums_ref, full_ref,
               total, low, flows, red_send, red_recv, line_send, line_recv, own_sem):
        dp, mp = lax.axis_index("dp"), lax.axis_index("mp")
        greet_all([], dp, mp, mp_count)
        reduce = LineReduce(part_ref, flows, rows, PIECES, red_send, red_recv, dp, mp, mp_count)
        gather = LineGather(low, full_ref, rows, PIECES, line_send, line_recv, dp, mp, mp_count)
        reduce.begin()
        sums_ref[...] = jnp.zeros_like(sums_ref)

        @pl.loop(0, PIECES + mp_count - 1)
        def _(turn):
            @pl.when(turn < PIECES)
            def _():
                reduce.advance(turn)
                reduce.total(turn, total)
                span = pl.ds(pl.multiple_of(turn * size, size), size)
                unit, inverse = unit_rows(residual_ref[span])
                upstream = total[...]
                sums_ref[0:1] += jnp.sum(upstream * unit, axis=0, keepdims=True)
                sums_ref[1:2] += jnp.sum(upstream, axis=0, keepdims=True)
                grad = branch_ref[span].astype(jnp.float32) + norm_back(upstream, unit, inverse, gain_ref[...])
                grad_ref[span] = grad
                rounded = grad.astype(low.dtype)
                low[span] = rounded
                sums_ref[2:3] += jnp.sum(rounded.astype(jnp.float32), axis=0, keepdims=True)
                gather.advance(0, turn)

            for step in range(1, mp_count):
                piece = jnp.clip(turn - step, 0, PIECES - 1)
                gather.advance(step, piece, (turn >= step) & (turn - step < PIECES))

        own = pltpu.make_async_copy(low, full_ref.at[pl.ds(pl.multiple_of(mp * rows, rows), rows)], own_sem)
        own.start()
        reduce.finish()
        gather.finish()
        own.wait()

    return pl.pallas_call(
        kernel,
        out_shape=[
            jax.ShapeDtypeStruct((rows, width), jnp.float32),
            jax.ShapeDtypeStruct((8, width), jnp.float32),
            jax.ShapeDtypeStruct((mp_count * rows, width), jnp.bfloat16),
        ],
        in_specs=[VMEM] * 4,
        out_specs=[VMEM, VMEM, ANY],
        scratch_shapes=[pltpu.VMEM((size, width), jnp.float32), pltpu.VMEM((rows, width), jnp.bfloat16)]
        + LineReduce.scratch(mp_count, rows, width, PIECES) + LineGather.semaphores(mp_count, PIECES)
        + [pltpu.SemaphoreType.DMA(())],
        compiler_params=pltpu.CompilerParams(
            collective_id=collective_id, has_side_effects=True, vmem_limit_bytes=48 * MIB),
        cost_estimate=pl.CostEstimate(flops=0, bytes_accessed=300 * MIB, transcendentals=0),
    )(part, residual, branch_two, gain)


def reduce_last(part, residual_grad, hidden, gain, weight_parts, collective_id):
    dp_count, mp_count = lax.axis_size("dp"), lax.axis_size("mp")
    chips = dp_count // 2
    rows, width = hidden.shape
    size = rows // PIECES
    count = len(weight_parts)
    depth, columns = weight_parts[0].shape[0] // dp_count, weight_parts[0].shape[1]

    def kernel(*refs):
        part_ref, residual_ref, hidden_ref, gain_ref = refs[:4]
        weights = refs[4 : 4 + count]
        grad_ref, sums_ref = refs[4 + count : 6 + count]
        outs = refs[6 + count : 6 + 2 * count]
        (total, flows, red_send, red_recv, from_partner, chip_sum, from_chips,
         pair_send, pair_recv, send_sem, recv_sem) = refs[6 + 2 * count :]
        dp, mp = lax.axis_index("dp"), lax.axis_index("mp")
        peers = [(dp ^ (2 * o), mp) for o in range(1, chips)]
        partner = (dp ^ 1, mp)
        greet_all(peers + [partner], dp, mp, mp_count)
        reduce = LineReduce(part_ref, flows, rows, PIECES, red_send, red_recv, dp, mp, mp_count)
        reduce.begin()

        def piece_of(weight, owner):
            return weights[weight].at[pl.ds(pl.multiple_of(owner * depth, depth), depth)]

        def pair(weight, o):
            return remote(piece_of(weight, dp ^ (2 * o) ^ 1), from_partner.at[weight, o],
                          pair_send.at[weight, o], pair_recv.at[weight, o], partner)

        def cross(weight, o):
            return remote(chip_sum.at[weight, o], from_chips.at[weight, o - 1],
                          send_sem.at[weight, o], recv_sem.at[weight, o], peers[o - 1])

        order = list(range(1, chips)) + [0]
        for w in range(count):
            for o in order:
                pair(w, o).start()
        for w in range(count):
            for o in order:
                pair(w, o).wait_recv()
                value = piece_of(w, dp ^ (2 * o))[...].astype(jnp.float32)
                value = value + from_partner[w, o].astype(jnp.float32)
                if o:
                    chip_sum[w, o] = value.astype(chip_sum.dtype)
                    cross(w, o).start()
                else:
                    outs[w][...] = value
        sums_ref[...] = jnp.zeros_like(sums_ref)

        @pl.loop(0, PIECES)
        def _(turn):
            reduce.advance(turn)
            reduce.total(turn, total)
            span = pl.ds(pl.multiple_of(turn * size, size), size)
            unit, inverse = unit_rows(hidden_ref[span].astype(jnp.float32))
            upstream = total[...]
            sums_ref[0:1] += jnp.sum(upstream * unit, axis=0, keepdims=True)
            sums_ref[1:2] += jnp.sum(upstream, axis=0, keepdims=True)
            grad_ref[span] = residual_ref[span] + norm_back(upstream, unit, inverse, gain_ref[...])

        reduce.finish()
        for w in range(count):
            for o in range(1, chips):
                cross(w, o).wait()
                outs[w][...] += from_chips[w, o - 1].astype(jnp.float32)
            for o in range(chips):
                pair(w, o).wait_send()

    dma = pltpu.SemaphoreType.DMA
    kind = weight_parts[0].dtype
    return pl.pallas_call(
        kernel,
        out_shape=[jax.ShapeDtypeStruct((rows, width), jnp.float32), jax.ShapeDtypeStruct((8, width), jnp.float32)]
        + [jax.ShapeDtypeStruct((depth, columns), jnp.float32)] * count,
        in_specs=[VMEM] * (4 + count),
        out_specs=[VMEM] * (2 + count),
        scratch_shapes=[pltpu.VMEM((size, width), jnp.float32)]
        + LineReduce.scratch(mp_count, rows, width, PIECES)
        + [pltpu.VMEM((count, chips, depth, columns), kind), pltpu.VMEM((count, chips, depth, columns), kind),
           pltpu.VMEM((count, chips - 1, depth, columns), kind)]
        + [dma((count, chips)) for _ in range(4)],
        compiler_params=pltpu.CompilerParams(
            collective_id=collective_id, has_side_effects=True, vmem_limit_bytes=60 * MIB),
        cost_estimate=pl.CostEstimate(flops=0, bytes_accessed=300 * MIB, transcendentals=0),
    )(part, residual_grad, hidden, gain, *weight_parts)


def sum_vectors(packed, collective_id):
    dp_count, mp_count = lax.axis_size("dp"), lax.axis_size("mp")
    depth, width = packed.shape[1:]

    def kernel(in_ref, out_ref, landed, mine, others, send_sem, recv_sem, line_send, line_recv):
        dp, mp = lax.axis_index("dp"), lax.axis_index("mp")
        peers = [(dp ^ o, mp) for o in range(1, dp_count)]
        along = [(dp, mp ^ o) for o in range(1, mp_count)]
        greet(peers + along)
        copies = []
        for o in range(1, dp_count):
            copies.append(remote(in_ref.at[dp ^ o], landed.at[o - 1], send_sem.at[o], recv_sem.at[o], peers[o - 1]))
            copies[-1].start()
        value = in_ref[dp]
        for o in range(1, dp_count):
            copies[o - 1].wait()
            value = value + landed[o - 1]
        mine[...] = value
        others[mp] = value
        copies = []
        for o in range(1, mp_count):
            copies.append(remote(mine, others.at[mp], line_send.at[o], line_recv.at[o], along[o - 1]))
            copies[-1].start()
        for copy in copies:
            copy.wait()
        value = others[0]
        for index in range(1, mp_count):
            value = value + others[index]
        out_ref[...] = value

    dma = pltpu.SemaphoreType.DMA
    return pl.pallas_call(
        kernel,
        out_shape=jax.ShapeDtypeStruct((depth, width), jnp.float32),
        in_specs=[VMEM],
        out_specs=VMEM,
        scratch_shapes=[
            pltpu.VMEM((dp_count - 1, depth, width), jnp.float32), pltpu.VMEM((depth, width), jnp.float32),
            pltpu.VMEM((mp_count, depth, width), jnp.float32),
            dma((dp_count,)), dma((dp_count,)), dma((mp_count,)), dma((mp_count,)),
        ],
        compiler_params=pltpu.CompilerParams(collective_id=collective_id, has_side_effects=True),
        cost_estimate=pl.CostEstimate(flops=0, bytes_accessed=20 * MIB, transcendentals=0),
    )(packed)


def packed_rows(vectors):
    flat = jnp.concatenate([v.astype(jnp.float32) for v in vectors])
    rows = flat.shape[0] // 128
    return jnp.pad(flat.reshape(rows, 128), ((0, -rows % 8), (0, 0)))


def per_device(
    hidden_in,
    output_grad,
    first_gain,
    first_shift,
    query_weight,
    query_bias,
    key_weight,
    value_weight,
    value_bias,
    out_weight,
    out_bias,
    second_gain,
    second_shift,
    up_weight,
    up_bias,
    down_weight,
    down_bias,
    seq_lengths,
    block_order,
    block_slot,
):
    local_rows, model_width = hidden_in.shape
    mp_count, dp_count = lax.axis_size("mp"), lax.axis_size("dp")
    mp_index, dp_index = lax.axis_index("mp"), lax.axis_index("dp")
    group_rows = local_rows * mp_count
    head_width = query_weight.shape[1]
    heads_local = head_width // HEAD_DIM
    hidden_width = up_weight.shape[1]
    members = dp_count // heads_local
    blocks_each = group_rows // BLOCK
    plan = (seq_lengths, block_order, block_slot)

    own_valid = valid_rows(seq_lengths, block_order, dp_index * group_rows + mp_index * local_rows, local_rows)

    vectors = (first_gain, first_shift, query_bias, value_bias, out_bias, second_gain, second_shift, down_bias, up_bias)
    rows_in, vector_rows, query_all, key_all, value_all, out_all = gather_first(
        hidden_in, packed_rows(vectors), (query_weight, key_weight, value_weight, out_weight), 0
    )
    vector_rows = vector_rows.reshape(dp_count, -1, 128)
    each = model_width // dp_count // 128
    (gain_one, shift_one, bias_query, bias_value, bias_out, gain_two, shift_two, bias_down) = (
        vector_rows[:, k * each : (k + 1) * each].reshape(1, model_width) for k in range(8)
    )
    up_each = up_bias.shape[0] // 128
    bias_up = vector_rows[:, 8 * each : 8 * each + up_each].reshape(1, up_bias.shape[0] * dp_count)

    def heads_of(vector):
        return lax.dynamic_slice_in_dim(vector, mp_index * head_width, head_width, 1)

    unit_one, _ = unit_rows(rows_in.astype(jnp.float32))
    rows_one = (unit_one * gain_one + shift_one).astype(jnp.bfloat16)

    def project(weight, bias):
        return (jnp.dot(rows_one, weight, preferred_element_type=jnp.float32) + bias).astype(jnp.bfloat16)

    key_rows = project(key_all, 0.0)
    value_rows = project(value_all, heads_of(bias_value))
    queries = project(query_all, heads_of(bias_query))
    head_queries, head_keys, head_values = to_heads([queries], [key_rows, value_rows], heads_local, members, 1)
    head_mix, exact_mix, log_total = attend(head_queries, head_keys, head_values, *plan, members, blocks_each)
    (attended_low,) = to_rows([head_mix], [], heads_local, members, 2)
    out_part = contract_last(attended_low, out_all).astype(jnp.bfloat16)
    residual, rows_two = reduce_norm_gather(out_part, hidden_in, bias_out, gain_two, shift_two, 3)

    up_all = lax.all_gather(up_weight, "dp", axis=0, tiled=True)
    down_all = lax.all_gather(down_weight, "dp", axis=0, tiled=True)
    branch_two = jnp.where(own_valid[:, None], output_grad, 0).astype(jnp.bfloat16)
    branch_rows_two = whole_rows(branch_two)

    bias_hidden = lax.dynamic_slice_in_dim(bias_up, mp_index * hidden_width, hidden_width, 1)
    pre_act = jnp.dot(rows_two, up_all, preferred_element_type=jnp.float32) + bias_hidden
    hidden_low = gelu_exact(pre_act).astype(jnp.bfloat16)
    hidden_grad = jnp.dot(branch_rows_two, down_all, preferred_element_type=jnp.float32)
    pre_grad = jax.vjp(gelu_exact, pre_act)[1](hidden_grad)[0].astype(jnp.bfloat16)
    up_part = contract_last(pre_grad, up_all).astype(jnp.bfloat16)
    residual_grad, sums_two, branch_rows_one = reduce_back_gather(up_part, residual, branch_two, gain_two, 4)

    feed = row_share(contract_last(hidden_low, down_all))
    result = residual + feed + bias_down
    output = jnp.where(own_valid[:, None], result, 0.0).astype(jnp.bfloat16)
    down_weight_grad = owner_share(contract_first(branch_rows_two, hidden_low))
    up_weight_grad = owner_share(contract_first(rows_two, pre_grad))

    attended_grad = jnp.dot(branch_rows_one, out_all, preferred_element_type=jnp.float32).astype(jnp.bfloat16)
    (head_grad,) = to_heads([attended_grad], [], heads_local, members, 5)
    head_query_grad, head_key_grad, head_value_grad = attend_back(
        head_queries, head_keys, head_values, head_grad, exact_mix, log_total, *plan, members, blocks_each
    )
    query_low, key_low, value_low = to_rows(
        [head_query_grad], [head_key_grad, head_value_grad], heads_local, members, 6
    )
    last_part = contract_last(query_low, query_all)
    last_part = last_part + contract_last(key_low, key_all)
    last_part = (last_part + contract_last(value_low, value_all)).astype(jnp.bfloat16)
    weight_parts = [
        contract_first(left, right).astype(jnp.bfloat16)
        for left, right in (
            (rows_one, query_low), (rows_one, key_low), (rows_one, value_low), (branch_rows_one, attended_low)
        )
    ]
    input_grad, sums_one, query_weight_grad, key_weight_grad, value_weight_grad, out_weight_grad = reduce_last(
        last_part, residual_grad, hidden_in, gain_one, weight_parts, 7
    )

    def column_sums(values):
        return jnp.sum(values.astype(jnp.float32), axis=0)

    def placed(values):
        whole = jnp.zeros((values.shape[0] * mp_count,), jnp.float32)
        return lax.dynamic_update_slice_in_dim(whole, values, mp_index * values.shape[0], 0)

    sums = (
        sums_one[0], sums_one[1], placed(column_sums(query_low)), placed(column_sums(value_low)), sums_two[2],
        sums_two[0], sums_two[1], column_sums(branch_two), placed(column_sums(pre_grad)),
    )
    packed = jnp.concatenate([v.reshape(dp_count, -1, 128) for v in sums], axis=1)
    packed = jnp.pad(packed, ((0, 0), (0, -packed.shape[1] % 8), (0, 0)))
    summed = sum_vectors(packed, 8)
    vector_grads = [summed[k * each : (k + 1) * each].reshape(-1) for k in range(8)]
    up_bias_grad = summed[8 * each : 8 * each + up_each].reshape(-1)
    return (
        output,
        input_grad,
        vector_grads[0],
        vector_grads[1],
        query_weight_grad,
        vector_grads[2],
        key_weight_grad,
        value_weight_grad,
        vector_grads[3],
        out_weight_grad,
        vector_grads[4],
        vector_grads[5],
        vector_grads[6],
        up_weight_grad,
        up_bias_grad,
        down_weight_grad,
        vector_grads[7],
    )


def solution(mesh):
    return jax.shard_map(
        per_device,
        mesh=mesh,
        in_specs=(
            P(("dp", "mp"), None),
            P(("dp", "mp"), None),
            P("dp"),
            P("dp"),
            P("dp", "mp"),
            P("dp"),
            P("dp", "mp"),
            P("dp", "mp"),
            P("dp"),
            P("dp", "mp"),
            P("dp"),
            P("dp"),
            P("dp"),
            P("dp", "mp"),
            P("dp"),
            P("dp", "mp"),
            P("dp"),
            P(),
            P(),
            P(),
        ),
        out_specs=(
            P(("dp", "mp"), None),
            P(("dp", "mp"), None),
            P("dp"),
            P("dp"),
            P("dp", "mp"),
            P("dp"),
            P("dp", "mp"),
            P("dp", "mp"),
            P("dp"),
            P("dp", "mp"),
            P("dp"),
            P("dp"),
            P("dp"),
            P("dp", "mp"),
            P("dp"),
            P("dp", "mp"),
            P("dp"),
        ),
        check_vma=False,
    )
```

```python
import math

import jax
import jax.numpy as jnp
from jax import lax
from jax.experimental import pallas as pl
from jax.experimental.pallas import tpu as pltpu
from jax.sharding import PartitionSpec as P

HEAD_DIM = 128
BLOCK = 128
KEY_BLOCKS = 4
MESH = pl.DeviceIdType.MESH
ANY = pl.BlockSpec(memory_space=pl.ANY)
VMEM = pl.BlockSpec(memory_space=pltpu.VMEM)
SMEM = pl.BlockSpec(memory_space=pltpu.SMEM)
MIB = 1 << 20


big_negative = -1e30
norm_epsilon = 1e-05


def norm_back(upstream, normed, inverse, gain_row):
    scaled = upstream * gain_row
    mean_grad = jnp.mean(scaled, axis=-1, keepdims=True)
    second = jnp.mean(scaled * normed, axis=-1, keepdims=True)
    return inverse * (scaled - mean_grad - normed * second)


def gelu_exact(values):
    return jax.nn.gelu(values, approximate=False)


def contract_last(left, right):
    return lax.dot_general(
        left, right, (((1,), (1,)), ((), ())), preferred_element_type=jnp.float32
    )


def contract_first(left, right):
    return lax.dot_general(
        left, right, (((0,), (0,)), ((), ())), preferred_element_type=jnp.float32
    )


def valid_rows(seq_lengths, block_order, first_row, row_count):
    row_ids = first_row + jnp.arange(row_count, dtype=jnp.int32)
    slot_hit = (row_ids // BLOCK)[:, None] == jnp.arange(block_order.shape[0], dtype=jnp.int32)[None, :]
    initial = jnp.sum(jnp.where(slot_hit, block_order[None, :], 0), axis=1)
    block_counts = (seq_lengths + BLOCK - 1) // BLOCK
    ends = jnp.cumsum(block_counts)
    starts = ends - block_counts
    inside = (initial[:, None] >= starts[None, :]) & (initial[:, None] < ends[None, :])
    left = seq_lengths[None, :] - (initial[:, None] - starts[None, :]) * BLOCK
    return (row_ids % BLOCK) < jnp.sum(jnp.where(inside, left, 0), axis=1)


def whole_rows(local_part):
    return lax.all_gather(local_part, "mp", axis=0, tiled=True)


def row_share(term):
    term = term.astype(jnp.bfloat16)
    return lax.psum_scatter(term, "mp", scatter_dimension=0, tiled=True).astype(jnp.float32)


def owner_share(term):
    term = term.astype(jnp.bfloat16)
    return lax.psum_scatter(term, "dp", scatter_dimension=0, tiled=True).astype(jnp.float32)


def greet(peers):
    barrier = pltpu.get_barrier_semaphore()
    for peer in peers:
        pl.semaphore_signal(barrier, inc=1, device_id=peer, device_id_type=MESH)
    pl.semaphore_wait(barrier, len(peers))


def remote(src, dst, send_sem, recv_sem, peer):
    return pltpu.make_async_remote_copy(
        src_ref=src, dst_ref=dst, send_sem=send_sem, recv_sem=recv_sem,
        device_id=peer, device_id_type=MESH,
    )


def head_place(heads, members):
    me = lax.axis_index("dp")
    return me, me // members, me % members, lax.axis_index("mp")


def lanes(head):
    return pl.ds(pl.multiple_of(head * HEAD_DIM, HEAD_DIM), HEAD_DIM)


def to_heads(owned, shared, heads, members, collective_id):
    rows = (owned + shared)[0].shape[0]
    n_owned, n_shared = len(owned), len(shared)
    count = n_owned + n_shared

    def kernel(*refs):
        ins, outs = refs[:count], refs[count : 2 * count]
        local_sem, send_sem, recv_sem, fwd_send, fwd_recv = refs[2 * count :]
        me, group, member, mp = head_place(heads, members)

        def dest(array, source):
            place = (source // members) if array < n_owned else source
            return outs[array].at[pl.ds(pl.multiple_of(place * rows, rows), rows)]

        head_peers = [((group ^ o) * members + member, mp) for o in range(1, heads)]
        pair_peers = [(group * members + (member ^ o), mp) for o in range(1, members)]
        greet(head_peers + pair_peers)
        order = list(range(n_owned, count)) + list(range(n_owned))
        sends, locals_, forwards = {}, [], []
        for a in order:
            for o in range(1, heads):
                copy = remote(ins[a].at[:, lanes(group ^ o)], dest(a, me), send_sem.at[a, o],
                              recv_sem.at[a, o], head_peers[o - 1])
                copy.start()
                sends[a, o] = copy
        for a in range(count):
            copy = pltpu.make_async_copy(ins[a].at[:, lanes(group)], dest(a, me), local_sem.at[a])
            copy.start()
            locals_.append(copy)
        for a in range(n_owned, count):
            for o in range(heads):
                source = (group ^ o) * members + member
                if o:
                    sends[a, o].wait_recv()
                for p in range(1, members):
                    piece = ins[a].at[:, lanes(group)] if o == 0 else dest(a, source)
                    copy = remote(piece, dest(a, source), fwd_send.at[a - n_owned, o, p],
                                  fwd_recv.at[a - n_owned, o, p], pair_peers[p - 1])
                    copy.start()
                    forwards.append(copy)
        for copy in locals_:
            copy.wait()
        for (a, o), copy in sends.items():
            copy.wait_send()
            if a < n_owned:
                copy.wait_recv()
        for copy in forwards:
            copy.wait()

    total = rows * lax.axis_size("dp")
    shapes = [jax.ShapeDtypeStruct((heads * rows, HEAD_DIM), a.dtype) for a in owned]
    shapes += [jax.ShapeDtypeStruct((total, HEAD_DIM), a.dtype) for a in shared]
    dma = pltpu.SemaphoreType.DMA
    return pl.pallas_call(
        kernel,
        out_shape=shapes,
        in_specs=[ANY] * count,
        out_specs=[ANY] * count,
        scratch_shapes=[
            dma((count,)), dma((count, heads)), dma((count, heads)),
            dma((max(n_shared, 1), heads, members)), dma((max(n_shared, 1), heads, members)),
        ],
        compiler_params=pltpu.CompilerParams(collective_id=collective_id, has_side_effects=True),
        cost_estimate=pl.CostEstimate(flops=0, bytes_accessed=100 * MIB, transcendentals=0),
    )(*owned, *shared)


def to_rows(owned, shared, heads, members, collective_id):
    rows = owned[0].shape[0] // heads
    n_owned, n_shared = len(owned), len(shared)
    count = n_owned + n_shared

    def kernel(*refs):
        ins, outs = refs[:count], refs[count : 2 * count]
        local_sem, send_sem, recv_sem, own_sem, part_send, part_recv = refs[2 * count : 2 * count + 6]
        me, group, member, mp = head_place(heads, members)
        head_peers = [((group ^ o) * members + member, mp) for o in range(1, heads)]
        pair_peers = [(group * members + (member ^ o), mp) for o in range(1, members)]
        greet(head_peers + pair_peers)
        if n_shared:
            own, parts, total = refs[2 * count + 6 :]
        copies, pending = [], {}

        def part(array, o, who):
            first = pl.multiple_of(((group ^ o) * members + who) * rows, rows)
            return ins[array].at[pl.ds(first, rows)]

        for s in range(n_shared):
            for o in range(heads):
                copy = pltpu.make_async_copy(part(n_owned + s, o, member), own.at[s, o], own_sem.at[s, o])
                copy.start()
                pending[s, o, 0] = copy
                for p in range(1, members):
                    copy = remote(part(n_owned + s, o, member ^ p), parts.at[s, o, p - 1],
                                  part_send.at[s, o, p], part_recv.at[s, o, p], pair_peers[p - 1])
                    copy.start()
                    pending[s, o, p] = copy
        for a in range(n_owned):
            for o in range(heads):
                piece = ins[a].at[pl.ds(pl.multiple_of((group ^ o) * rows, rows), rows)]
                place = outs[a].at[:, lanes(group)]
                if o:
                    copy = remote(piece, place, send_sem.at[a, o], recv_sem.at[a, o], head_peers[o - 1])
                else:
                    copy = pltpu.make_async_copy(piece, place, local_sem.at[a])
                copy.start()
                copies.append(copy)
        for o in list(range(1, heads)) + [0]:
            for s in range(n_shared):
                for p in range(members):
                    if p:
                        pending[s, o, p].wait_recv()
                    else:
                        pending[s, o, p].wait()
                value = own[s, o].astype(jnp.float32)
                for p in range(1, members):
                    value = value + parts[s, o, p - 1].astype(jnp.float32)
                total[s, o] = value.astype(total.dtype)
                a = n_owned + s
                place = outs[a].at[:, lanes(group)]
                if o:
                    copy = remote(total.at[s, o], place, send_sem.at[a, o], recv_sem.at[a, o], head_peers[o - 1])
                else:
                    copy = pltpu.make_async_copy(total.at[s, o], place, local_sem.at[a])
                copy.start()
                copies.append(copy)
        for s in range(n_shared):
            for o in range(heads):
                for p in range(1, members):
                    pending[s, o, p].wait_send()
        for copy in copies:
            copy.wait()

    dma = pltpu.SemaphoreType.DMA
    slots = max(n_shared, 1)
    scratch = [
        dma((count,)), dma((count, heads)), dma((count, heads)),
        dma((slots, heads)), dma((slots, heads, members)), dma((slots, heads, members)),
    ]
    if n_shared:
        kind = shared[0].dtype
        scratch += [
            pltpu.VMEM((n_shared, heads, rows, HEAD_DIM), kind),
            pltpu.VMEM((n_shared, heads, members - 1, rows, HEAD_DIM), kind),
            pltpu.VMEM((n_shared, heads, rows, HEAD_DIM), kind),
        ]
    return pl.pallas_call(
        kernel,
        out_shape=[jax.ShapeDtypeStruct((rows, heads * HEAD_DIM), a.dtype) for a in owned + shared],
        in_specs=[ANY] * count,
        out_specs=[ANY] * count,
        scratch_shapes=scratch,
        compiler_params=pltpu.CompilerParams(
            collective_id=collective_id, has_side_effects=True, vmem_limit_bytes=48 * MIB
        ),
        cost_estimate=pl.CostEstimate(flops=0, bytes_accessed=100 * MIB, transcendentals=0),
    )(*owned, *shared)


def query_block(index, lengths, order, members, blocks_each):
    member = lax.axis_index("dp") % members
    dealt = ((index // blocks_each) * members + member) * blocks_each + index % blocks_each
    place = order[dealt]
    first, length, running = jnp.int32(0), jnp.int32(0), jnp.int32(0)
    for s in range(lengths.shape[0]):
        inside = place >= running
        first = jnp.where(inside, running, first)
        length = jnp.where(inside, lengths[s], length)
        running = running + (lengths[s] + (BLOCK - 1)) // BLOCK
    behind = place - first
    return first, behind, length - behind * BLOCK


def key_blocks(block_count, slot, visit):
    @pl.loop(0, block_count)
    def _(block):
        visit(pl.multiple_of(block * BLOCK, BLOCK), pl.multiple_of(slot[block] * BLOCK, BLOCK))


def allowed_keys(tile, behind):
    width = KEY_BLOCKS * BLOCK
    key_pos = lax.broadcasted_iota(jnp.int32, (width, BLOCK), 0) + tile * width
    query_pos = lax.broadcasted_iota(jnp.int32, (width, BLOCK), 1) + behind * BLOCK
    return key_pos <= query_pos


def attend(queries, key_rows, value_rows, lengths, order, slot, members, blocks_each):
    query_count, key_count = queries.shape[0] // BLOCK, key_rows.shape[0] // BLOCK
    width = KEY_BLOCKS * BLOCK
    padded = (key_count + KEY_BLOCKS - 1) * BLOCK
    scale = math.log2(math.e) / math.sqrt(HEAD_DIM)

    def kernel(lengths_ref, order_ref, slot_ref, q_ref, k_ref, v_ref, out_ref, exact_ref, log_ref, keys, values_t):
        def visit(to, source):
            keys[pl.ds(to, BLOCK)] = k_ref[pl.ds(source, BLOCK)]
            values_t[:, pl.ds(to, BLOCK)] = v_ref[pl.ds(source, BLOCK)].T

        key_blocks(key_count, slot_ref, visit)
        keys[pl.ds(key_count * BLOCK, padded - key_count * BLOCK)] = jnp.zeros(
            (padded - key_count * BLOCK, HEAD_DIM), keys.dtype)
        values_t[:, pl.ds(key_count * BLOCK, padded - key_count * BLOCK)] = jnp.zeros(
            (HEAD_DIM, padded - key_count * BLOCK), keys.dtype)

        @pl.loop(0, query_count)
        def _(index):
            first, behind, valid = query_block(index, lengths_ref, order_ref, members, blocks_each)
            query_t = q_ref[pl.ds(pl.multiple_of(index * BLOCK, BLOCK), BLOCK)].T

            def step(tile, carry):
                top, total, mix = carry
                row = pl.multiple_of((first + tile * KEY_BLOCKS) * BLOCK, BLOCK)
                scores = jnp.dot(keys[pl.ds(row, width)], query_t, preferred_element_type=jnp.float32) * scale
                scores = jnp.where(allowed_keys(tile, behind), scores, big_negative)
                new_top = jnp.maximum(top, jnp.max(scores, axis=0, keepdims=True))
                weights = jnp.exp2(scores - new_top)
                fade = jnp.exp2(top - new_top)
                total = total * fade + jnp.sum(weights, axis=0, keepdims=True)
                mix = mix * fade + jnp.dot(
                    values_t[:, pl.ds(row, width)], weights.astype(jnp.bfloat16), preferred_element_type=jnp.float32)
                return new_top, total, mix

            top, total, mix = lax.fori_loop(
                0, behind // KEY_BLOCKS + 1, step,
                (jnp.full((1, BLOCK), big_negative, jnp.float32), jnp.zeros((1, BLOCK), jnp.float32),
                 jnp.zeros((HEAD_DIM, BLOCK), jnp.float32)))
            live = lax.broadcasted_iota(jnp.int32, (1, BLOCK), 1) < valid
            mix = jnp.where(live, mix / total, 0.0)
            exact_ref[index] = mix
            out_ref[pl.ds(pl.multiple_of(index * BLOCK, BLOCK), BLOCK)] = mix.T.astype(out_ref.dtype)
            log_ref[index] = jnp.where(live, top + jnp.log2(total), -big_negative)

    return pl.pallas_call(
        kernel,
        out_shape=[
            jax.ShapeDtypeStruct(queries.shape, jnp.bfloat16),
            jax.ShapeDtypeStruct((query_count, HEAD_DIM, BLOCK), jnp.float32),
            jax.ShapeDtypeStruct((query_count, 1, BLOCK), jnp.float32),
        ],
        in_specs=[SMEM] * 3 + [VMEM] * 3,
        out_specs=[VMEM] * 3,
        scratch_shapes=[pltpu.VMEM((padded, HEAD_DIM), jnp.bfloat16), pltpu.VMEM((HEAD_DIM, padded), jnp.bfloat16)],
        compiler_params=pltpu.CompilerParams(vmem_limit_bytes=56 * MIB),
        cost_estimate=pl.CostEstimate(flops=8 << 30, bytes_accessed=50 * MIB, transcendentals=8 << 20),
    )(lengths, order, slot, queries, key_rows, value_rows)


def attend_back(queries, key_rows, value_rows, upstream, exact, logs, lengths, order, slot, members, blocks_each):
    query_count, key_count = queries.shape[0] // BLOCK, key_rows.shape[0] // BLOCK
    width = KEY_BLOCKS * BLOCK
    padded = (key_count + KEY_BLOCKS - 1) * BLOCK
    scale = math.log2(math.e) / math.sqrt(HEAD_DIM)
    plain_scale = 1.0 / math.sqrt(HEAD_DIM)

    def kernel(lengths_ref, order_ref, slot_ref, q_ref, k_ref, v_ref, g_ref, exact_ref, log_ref,
               dq_ref, dk_ref, dv_ref, keys, keys_t, values, key_sum, value_sum):
        def visit(to, source):
            block = k_ref[pl.ds(source, BLOCK)]
            keys[pl.ds(to, BLOCK)] = block
            keys_t[:, pl.ds(to, BLOCK)] = block.T
            values[pl.ds(to, BLOCK)] = v_ref[pl.ds(source, BLOCK)]
            key_sum[pl.ds(to, BLOCK)] = jnp.zeros((BLOCK, HEAD_DIM), jnp.float32)
            value_sum[pl.ds(to, BLOCK)] = jnp.zeros((BLOCK, HEAD_DIM), jnp.float32)

        key_blocks(key_count, slot_ref, visit)
        tail = pl.ds(key_count * BLOCK, padded - key_count * BLOCK)
        keys[tail] = jnp.zeros((padded - key_count * BLOCK, HEAD_DIM), keys.dtype)
        values[tail] = jnp.zeros((padded - key_count * BLOCK, HEAD_DIM), keys.dtype)
        keys_t[:, tail] = jnp.zeros((HEAD_DIM, padded - key_count * BLOCK), keys.dtype)
        key_sum[tail] = jnp.zeros((padded - key_count * BLOCK, HEAD_DIM), jnp.float32)
        value_sum[tail] = jnp.zeros((padded - key_count * BLOCK, HEAD_DIM), jnp.float32)

        @pl.loop(0, query_count)
        def _(index):
            first, behind, _ = query_block(index, lengths_ref, order_ref, members, blocks_each)
            mine = pl.ds(pl.multiple_of(index * BLOCK, BLOCK), BLOCK)
            query = q_ref[mine]
            grad = g_ref[mine]
            query_t, grad_t = query.T, grad.T
            delta = jnp.sum(grad_t.astype(jnp.float32) * exact_ref[index], axis=0, keepdims=True)
            log_total = log_ref[index]

            def step(tile, query_grad):
                row = pl.multiple_of((first + tile * KEY_BLOCKS) * BLOCK, BLOCK)
                span = pl.ds(row, width)
                scores = jnp.dot(keys[span], query_t, preferred_element_type=jnp.float32) * scale
                probability = jnp.where(allowed_keys(tile, behind), jnp.exp2(scores - log_total), 0.0)
                prob_grad = jnp.dot(values[span], grad_t, preferred_element_type=jnp.float32)
                score_grad = (probability * (prob_grad - delta)).astype(jnp.bfloat16)
                value_sum[span] += jnp.dot(
                    probability.astype(jnp.bfloat16), grad, preferred_element_type=jnp.float32)
                key_sum[span] += jnp.dot(score_grad, query, preferred_element_type=jnp.float32)
                return query_grad + jnp.dot(keys_t[:, span], score_grad, preferred_element_type=jnp.float32)

            query_grad = lax.fori_loop(
                0, behind // KEY_BLOCKS + 1, step, jnp.zeros((HEAD_DIM, BLOCK), jnp.float32))
            dq_ref[mine] = (query_grad * plain_scale).T.astype(dq_ref.dtype)

        def leave(at, dealt):
            dk_ref[pl.ds(dealt, BLOCK)] = (key_sum[pl.ds(at, BLOCK)] * plain_scale).astype(dk_ref.dtype)
            dv_ref[pl.ds(dealt, BLOCK)] = value_sum[pl.ds(at, BLOCK)].astype(dv_ref.dtype)

        key_blocks(key_count, slot_ref, leave)

    return pl.pallas_call(
        kernel,
        out_shape=[
            jax.ShapeDtypeStruct(queries.shape, jnp.bfloat16),
            jax.ShapeDtypeStruct(key_rows.shape, jnp.bfloat16),
            jax.ShapeDtypeStruct(key_rows.shape, jnp.bfloat16),
        ],
        in_specs=[SMEM] * 3 + [VMEM] * 6,
        out_specs=[VMEM] * 3,
        scratch_shapes=[
            pltpu.VMEM((padded, HEAD_DIM), jnp.bfloat16),
            pltpu.VMEM((HEAD_DIM, padded), jnp.bfloat16),
            pltpu.VMEM((padded, HEAD_DIM), jnp.bfloat16),
            pltpu.VMEM((padded, HEAD_DIM), jnp.float32),
            pltpu.VMEM((padded, HEAD_DIM), jnp.float32),
        ],
        compiler_params=pltpu.CompilerParams(vmem_limit_bytes=60 * MIB),
        cost_estimate=pl.CostEstimate(flops=20 << 30, bytes_accessed=100 * MIB, transcendentals=8 << 20),
    )(lengths, order, slot, queries, key_rows, value_rows, upstream, exact, logs)


def line_neighbours(mp, count):
    return ((1, mp + 1 < count, jnp.minimum(mp + 1, count - 1)), (-1, mp >= 1, jnp.maximum(mp - 1, 0)))


def greet_all(fixed, dp, mp, count):
    barrier = pltpu.get_barrier_semaphore()
    for peer in fixed:
        pl.semaphore_signal(barrier, inc=1, device_id=peer, device_id_type=MESH)
    expected = jnp.int32(len(fixed))
    for _, there, place in line_neighbours(mp, count):

        @pl.when(there)
        def _():
            pl.semaphore_signal(barrier, inc=1, device_id=(dp, place), device_id_type=MESH)

        expected = expected + there.astype(jnp.int32)
    pl.semaphore_wait(barrier, expected)


class LineGather:
    def __init__(self, own, full, rows, pieces, send_sem, recv_sem, dp, mp, count):
        self.own, self.full, self.rows, self.pieces = own, full, rows, pieces
        self.send_sem, self.recv_sem, self.dp, self.mp, self.count = send_sem, recv_sem, dp, mp, count
        self.size = rows // pieces

    def place(self, block, piece):
        return self.full.at[pl.ds(pl.multiple_of(block * self.rows + piece * self.size, self.size), self.size)]

    def hop(self, way, step, piece):
        sign, there, neighbour = line_neighbours(self.mp, self.count)[way]
        origin = self.mp - sign * step
        exists = (origin >= 0) & (origin < self.count)
        origin = jnp.clip(origin, 0, self.count - 1)
        if step == 0:
            source = self.own.at[pl.ds(pl.multiple_of(piece * self.size, self.size), self.size)]
        else:
            source = self.place(origin, piece)
        def copy():
            return remote(source, self.place(origin, piece), self.send_sem.at[way, step, piece],
                          self.recv_sem.at[way, step, piece], (self.dp, neighbour))

        return exists, exists & there, copy

    def advance(self, step, piece, also=True):
        for way in range(2):
            if step:
                exists, _, _ = self.hop(way, step, piece)
                _, _, earlier = self.hop(way, step - 1, piece)

                @pl.when(exists & also)
                def _():
                    earlier().wait_recv()

            if step < self.count - 1:
                _, sends, copy = self.hop(way, step, piece)

                @pl.when(sends & also)
                def _():
                    copy().start()

    def finish(self):
        @pl.loop(0, self.pieces)
        def _(piece):
            for way in range(2):
                for step in range(self.count - 1):
                    _, sends, copy = self.hop(way, step, piece)

                    @pl.when(sends)
                    def _():
                        copy().wait_send()

    @staticmethod
    def semaphores(count, pieces):
        return [pltpu.SemaphoreType.DMA((2, count, pieces)), pltpu.SemaphoreType.DMA((2, count, pieces))]


class LineReduce:
    def __init__(self, part, flows, rows, pieces, send_sem, recv_sem, dp, mp, count):
        self.part, self.flows, self.rows, self.pieces = part, flows, rows, pieces
        self.send_sem, self.recv_sem, self.dp, self.mp, self.count = send_sem, recv_sem, dp, mp, count
        self.size = rows // pieces

    def span(self, block, piece):
        return pl.ds(pl.multiple_of(block * self.rows + piece * self.size, self.size), self.size)

    def hop(self, way, block, piece, first=False):
        neighbour = line_neighbours(self.mp, self.count)[way][2]
        span = self.span(block, piece)
        source = self.part.at[span] if first else self.flows.at[way, span]
        return remote(source, self.flows.at[way, span], self.send_sem.at[way, block, piece],
                      self.recv_sem.at[way, block, piece], (self.dp, neighbour))

    def roles(self, way, block):
        if way == 0:
            behind, ahead = self.mp >= 1, self.mp < block
        else:
            behind, ahead = self.mp < self.count - 1, self.mp > block
        return ahead & jnp.logical_not(behind), ahead & behind

    def targets(self):
        for index in range(self.count - 1):
            yield 0, self.count - 1 - index
            yield 1, index

    def begin(self, piece, also=True):
        for way, block in self.targets():
            begins, _ = self.roles(way, block)

            @pl.when(begins & also)
            def _():
                self.hop(way, block, piece, True).start()

    def advance(self, turn):
        for way, block in self.targets():
            _, hands_on = self.roles(way, block)
            passed = SKEW * (self.mp - 1 if way == 0 else self.count - 2 - self.mp)
            piece = jnp.clip(turn - passed, 0, self.pieces - 1)

            @pl.when(hands_on & (turn >= passed) & (turn - passed < self.pieces))
            def _():
                self.hop(way, block, piece).wait_recv()
                span = self.span(block, piece)
                value = self.flows[way, span].astype(jnp.float32) + self.part[span].astype(jnp.float32)
                self.flows[way, span] = value.astype(self.flows.dtype)
                self.hop(way, block, piece).start()

    def arrive(self, piece):
        for way in range(2):

            @pl.when(self.mp >= 1 if way == 0 else self.mp < self.count - 1)
            def _():
                self.hop(way, self.mp, piece).wait_recv()

    def total(self, piece, result):
        span = self.span(self.mp, piece)
        result[...] = self.part[span].astype(jnp.float32)
        for way in range(2):

            @pl.when(self.mp >= 1 if way == 0 else self.mp < self.count - 1)
            def _():
                result[...] += self.flows[way, span].astype(jnp.float32)

    def finish(self):
        @pl.loop(0, self.pieces)
        def _(piece):
            for way, block in self.targets():
                begins, hands_on = self.roles(way, block)

                @pl.when(begins)
                def _():
                    self.hop(way, block, piece, True).wait_send()

                @pl.when(hands_on)
                def _():
                    self.hop(way, block, piece).wait_send()

    @staticmethod
    def scratch(count, rows, width, pieces):
        return [pltpu.VMEM((2, count * rows, width), jnp.bfloat16),
                pltpu.SemaphoreType.DMA((2, count, pieces)), pltpu.SemaphoreType.DMA((2, count, pieces))]


AHEAD = 1
MAX_PIECES = 16
SKEW = 1


def pieces_of(rows):
    return min(MAX_PIECES, rows // 16)


def gather_first(hidden, vectors, weights, collective_id):
    rows, width = hidden.shape
    pieces = pieces_of(rows)
    dp_count, mp_count = lax.axis_size("dp"), lax.axis_size("mp")
    chips = dp_count // 2
    arrays = [vectors] + list(weights)
    count = len(arrays)
    depth = [a.shape[0] for a in arrays]

    def kernel(*refs):
        own_rows, ins = refs[0], refs[1 : 1 + count]
        full_rows, outs = refs[1 + count], refs[2 + count : 2 + 2 * count]
        row_sem, local_sem, line_send, line_recv, send_sem, recv_sem, fwd_send, fwd_recv = refs[2 + 2 * count :]
        dp, mp = lax.axis_index("dp"), lax.axis_index("mp")
        peers = [(dp ^ (2 * o), mp) for o in range(1, chips)]
        partner = (dp ^ 1, mp)
        greet_all(peers + [partner], dp, mp, mp_count)
        line = LineGather(own_rows, full_rows, rows, pieces, line_send, line_recv, dp, mp, mp_count)

        def place(array, owner):
            return outs[array].at[pl.ds(pl.multiple_of(owner * depth[array], depth[array]), depth[array])]

        def cross(array, o):
            return remote(ins[array], place(array, dp), send_sem.at[array, o], recv_sem.at[array, o], peers[o - 1])

        def forward(array, o):
            owner = dp ^ (2 * o)
            source = place(array, owner) if o else ins[array]
            return remote(source, place(array, owner), fwd_send.at[array, o], fwd_recv.at[array, o], partner)

        @pl.loop(0, pieces)
        def _(piece):
            line.advance(0, piece)

        for a in range(count):
            for o in range(1, chips):
                cross(a, o).start()
            forward(a, 0).start()
        own_copy = pltpu.make_async_copy(own_rows, full_rows.at[pl.ds(pl.multiple_of(mp * rows, rows), rows)], row_sem)
        own_copy.start()
        locals_ = [pltpu.make_async_copy(ins[a], place(a, dp), local_sem.at[a]) for a in range(count)]
        for copy in locals_:
            copy.start()
        for step in range(1, mp_count - 1):

            @pl.loop(0, pieces)
            def _(piece):
                line.advance(step, piece)

        for a in range(count):
            for o in range(1, chips):
                cross(a, o).wait_recv()
                forward(a, o).start()

        @pl.loop(0, pieces)
        def _(piece):
            line.advance(mp_count - 1, piece)

        line.finish()
        own_copy.wait()
        for a in range(count):
            locals_[a].wait()
            for o in range(chips):
                if o:
                    cross(a, o).wait_send()
                forward(a, o).wait()

    dma = pltpu.SemaphoreType.DMA
    return pl.pallas_call(
        kernel,
        out_shape=[jax.ShapeDtypeStruct((mp_count * rows, width), hidden.dtype)]
        + [jax.ShapeDtypeStruct((dp_count * a.shape[0], a.shape[1]), a.dtype) for a in arrays],
        in_specs=[ANY] * (1 + count),
        out_specs=[ANY] * (1 + count),
        scratch_shapes=[dma(()), dma((count,))] + LineGather.semaphores(mp_count, pieces)
        + [dma((count, chips)) for _ in range(4)],
        compiler_params=pltpu.CompilerParams(collective_id=collective_id, has_side_effects=True),
        cost_estimate=pl.CostEstimate(flops=0, bytes_accessed=200 * MIB, transcendentals=0),
    )(hidden, *arrays)


def unit_rows(values):
    average = jnp.mean(values, axis=-1, keepdims=True)
    centred = values - average
    inverse = lax.rsqrt(jnp.mean(centred * centred, axis=-1, keepdims=True) + norm_epsilon)
    return centred * inverse, inverse


def reduce_norm_gather(part, hidden, out_bias, gain, shift, collective_id):
    mp_count = lax.axis_size("mp")
    rows, width = hidden.shape
    pieces = pieces_of(rows)
    size = rows // pieces

    def kernel(part_ref, hidden_ref, bias_ref, gain_ref, shift_ref, residual_ref, full_ref,
               total, normed, flows, red_send, red_recv, line_send, line_recv, own_sem):
        dp, mp = lax.axis_index("dp"), lax.axis_index("mp")
        greet_all([], dp, mp, mp_count)
        reduce = LineReduce(part_ref, flows, rows, pieces, red_send, red_recv, dp, mp, mp_count)
        gather = LineGather(normed, full_ref, rows, pieces, line_send, line_recv, dp, mp, mp_count)
        for piece in range(AHEAD):
            reduce.begin(piece)

        @pl.loop(0, pieces + 2 * SKEW * (mp_count - 1))
        def _(turn):
            reduce.begin(jnp.minimum(turn + AHEAD, pieces - 1), turn + AHEAD < pieces)
            reduce.advance(turn)
            done = turn - SKEW * (mp_count - 1)

            @pl.when((done >= 0) & (done < pieces))
            def _():
                reduce.arrive(done)
                reduce.total(done, total)
                span = pl.ds(pl.multiple_of(done * size, size), size)
                residual = hidden_ref[span].astype(jnp.float32) + total[...] + bias_ref[...]
                residual_ref[span] = residual
                unit, _ = unit_rows(residual)
                normed[span] = (unit * gain_ref[...] + shift_ref[...]).astype(normed.dtype)
                gather.advance(0, done)

            for step in range(1, mp_count):
                late = done - SKEW * step
                gather.advance(step, jnp.clip(late, 0, pieces - 1), (late >= 0) & (late < pieces))

        own = pltpu.make_async_copy(normed, full_ref.at[pl.ds(pl.multiple_of(mp * rows, rows), rows)], own_sem)
        own.start()
        reduce.finish()
        gather.finish()
        own.wait()

    return pl.pallas_call(
        kernel,
        out_shape=[
            jax.ShapeDtypeStruct((rows, width), jnp.float32),
            jax.ShapeDtypeStruct((mp_count * rows, width), jnp.bfloat16),
        ],
        in_specs=[VMEM] * 5,
        out_specs=[VMEM, ANY],
        scratch_shapes=[pltpu.VMEM((size, width), jnp.float32), pltpu.VMEM((rows, width), jnp.bfloat16)]
        + LineReduce.scratch(mp_count, rows, width, pieces) + LineGather.semaphores(mp_count, pieces)
        + [pltpu.SemaphoreType.DMA(())],
        compiler_params=pltpu.CompilerParams(
            collective_id=collective_id, has_side_effects=True, vmem_limit_bytes=48 * MIB),
        cost_estimate=pl.CostEstimate(flops=0, bytes_accessed=300 * MIB, transcendentals=0),
    )(part, hidden, out_bias, gain, shift)


def reduce_back_gather(part, residual, branch_two, gain, collective_id):
    mp_count = lax.axis_size("mp")
    rows, width = residual.shape
    pieces = pieces_of(rows)
    size = rows // pieces

    def kernel(part_ref, residual_ref, branch_ref, gain_ref, grad_ref, sums_ref, full_ref,
               total, low, flows, red_send, red_recv, line_send, line_recv, own_sem):
        dp, mp = lax.axis_index("dp"), lax.axis_index("mp")
        greet_all([], dp, mp, mp_count)
        reduce = LineReduce(part_ref, flows, rows, pieces, red_send, red_recv, dp, mp, mp_count)
        gather = LineGather(low, full_ref, rows, pieces, line_send, line_recv, dp, mp, mp_count)
        for piece in range(AHEAD):
            reduce.begin(piece)
        sums_ref[...] = jnp.zeros_like(sums_ref)

        @pl.loop(0, pieces + 2 * SKEW * (mp_count - 1))
        def _(turn):
            reduce.begin(jnp.minimum(turn + AHEAD, pieces - 1), turn + AHEAD < pieces)
            reduce.advance(turn)
            done = turn - SKEW * (mp_count - 1)

            @pl.when((done >= 0) & (done < pieces))
            def _():
                reduce.arrive(done)
                reduce.total(done, total)
                span = pl.ds(pl.multiple_of(done * size, size), size)
                unit, inverse = unit_rows(residual_ref[span])
                upstream = total[...]
                sums_ref[0:1] += jnp.sum(upstream * unit, axis=0, keepdims=True)
                sums_ref[1:2] += jnp.sum(upstream, axis=0, keepdims=True)
                grad = branch_ref[span].astype(jnp.float32) + norm_back(upstream, unit, inverse, gain_ref[...])
                grad_ref[span] = grad
                rounded = grad.astype(low.dtype)
                low[span] = rounded
                sums_ref[2:3] += jnp.sum(rounded.astype(jnp.float32), axis=0, keepdims=True)
                gather.advance(0, done)

            for step in range(1, mp_count):
                late = done - SKEW * step
                gather.advance(step, jnp.clip(late, 0, pieces - 1), (late >= 0) & (late < pieces))

        own = pltpu.make_async_copy(low, full_ref.at[pl.ds(pl.multiple_of(mp * rows, rows), rows)], own_sem)
        own.start()
        reduce.finish()
        gather.finish()
        own.wait()

    return pl.pallas_call(
        kernel,
        out_shape=[
            jax.ShapeDtypeStruct((rows, width), jnp.float32),
            jax.ShapeDtypeStruct((8, width), jnp.float32),
            jax.ShapeDtypeStruct((mp_count * rows, width), jnp.bfloat16),
        ],
        in_specs=[VMEM] * 4,
        out_specs=[VMEM, VMEM, ANY],
        scratch_shapes=[pltpu.VMEM((size, width), jnp.float32), pltpu.VMEM((rows, width), jnp.bfloat16)]
        + LineReduce.scratch(mp_count, rows, width, pieces) + LineGather.semaphores(mp_count, pieces)
        + [pltpu.SemaphoreType.DMA(())],
        compiler_params=pltpu.CompilerParams(
            collective_id=collective_id, has_side_effects=True, vmem_limit_bytes=48 * MIB),
        cost_estimate=pl.CostEstimate(flops=0, bytes_accessed=300 * MIB, transcendentals=0),
    )(part, residual, branch_two, gain)


def reduce_last(part, residual_grad, hidden, gain, weight_parts, collective_id):
    dp_count, mp_count = lax.axis_size("dp"), lax.axis_size("mp")
    chips = dp_count // 2
    rows, width = hidden.shape
    pieces = pieces_of(rows)
    size = rows // pieces
    count = len(weight_parts)
    depth, columns = weight_parts[0].shape[0] // dp_count, weight_parts[0].shape[1]

    def kernel(*refs):
        part_ref, residual_ref, hidden_ref, gain_ref = refs[:4]
        weights = refs[4 : 4 + count]
        grad_ref, sums_ref = refs[4 + count : 6 + count]
        outs = refs[6 + count : 6 + 2 * count]
        (total, flows, red_send, red_recv, from_partner, chip_sum, from_chips,
         pair_send, pair_recv, send_sem, recv_sem) = refs[6 + 2 * count :]
        dp, mp = lax.axis_index("dp"), lax.axis_index("mp")
        peers = [(dp ^ (2 * o), mp) for o in range(1, chips)]
        partner = (dp ^ 1, mp)
        greet_all(peers + [partner], dp, mp, mp_count)
        reduce = LineReduce(part_ref, flows, rows, pieces, red_send, red_recv, dp, mp, mp_count)
        for piece in range(AHEAD):
            reduce.begin(piece)

        def piece_of(weight, owner):
            return weights[weight].at[pl.ds(pl.multiple_of(owner * depth, depth), depth)]

        def pair(weight, o):
            return remote(piece_of(weight, dp ^ (2 * o) ^ 1), from_partner.at[weight, o],
                          pair_send.at[weight, o], pair_recv.at[weight, o], partner)

        def cross(weight, o):
            return remote(chip_sum.at[weight, o], from_chips.at[weight, o - 1],
                          send_sem.at[weight, o], recv_sem.at[weight, o], peers[o - 1])

        order = list(range(1, chips)) + [0]
        for w in range(count):
            for o in order:
                pair(w, o).start()
        for w in range(count):
            for o in order:
                pair(w, o).wait_recv()
                value = piece_of(w, dp ^ (2 * o))[...].astype(jnp.float32)
                value = value + from_partner[w, o].astype(jnp.float32)
                if o:
                    chip_sum[w, o] = value.astype(chip_sum.dtype)
                    cross(w, o).start()
                else:
                    outs[w][...] = value
        sums_ref[...] = jnp.zeros_like(sums_ref)

        @pl.loop(0, pieces + SKEW * (mp_count - 1))
        def _(turn):
            reduce.begin(jnp.minimum(turn + AHEAD, pieces - 1), turn + AHEAD < pieces)
            reduce.advance(turn)
            done = turn - SKEW * (mp_count - 1)

            @pl.when(done >= 0)
            def _():
                reduce.arrive(done)
                reduce.total(done, total)
                span = pl.ds(pl.multiple_of(done * size, size), size)
                unit, inverse = unit_rows(hidden_ref[span].astype(jnp.float32))
                upstream = total[...]
                sums_ref[0:1] += jnp.sum(upstream * unit, axis=0, keepdims=True)
                sums_ref[1:2] += jnp.sum(upstream, axis=0, keepdims=True)
                grad_ref[span] = residual_ref[span] + norm_back(upstream, unit, inverse, gain_ref[...])

        reduce.finish()
        for w in range(count):
            for o in range(1, chips):
                cross(w, o).wait()
                outs[w][...] += from_chips[w, o - 1].astype(jnp.float32)
            for o in range(chips):
                pair(w, o).wait_send()

    dma = pltpu.SemaphoreType.DMA
    kind = weight_parts[0].dtype
    return pl.pallas_call(
        kernel,
        out_shape=[jax.ShapeDtypeStruct((rows, width), jnp.float32), jax.ShapeDtypeStruct((8, width), jnp.float32)]
        + [jax.ShapeDtypeStruct((depth, columns), jnp.float32)] * count,
        in_specs=[VMEM] * (4 + count),
        out_specs=[VMEM] * (2 + count),
        scratch_shapes=[pltpu.VMEM((size, width), jnp.float32)]
        + LineReduce.scratch(mp_count, rows, width, pieces)
        + [pltpu.VMEM((count, chips, depth, columns), kind), pltpu.VMEM((count, chips, depth, columns), kind),
           pltpu.VMEM((count, chips - 1, depth, columns), kind)]
        + [dma((count, chips)) for _ in range(4)],
        compiler_params=pltpu.CompilerParams(
            collective_id=collective_id, has_side_effects=True, vmem_limit_bytes=60 * MIB),
        cost_estimate=pl.CostEstimate(flops=0, bytes_accessed=300 * MIB, transcendentals=0),
    )(part, residual_grad, hidden, gain, *weight_parts)


def sum_vectors(packed, collective_id):
    dp_count, mp_count = lax.axis_size("dp"), lax.axis_size("mp")
    depth, width = packed.shape[1:]

    def kernel(in_ref, out_ref, landed, mine, others, send_sem, recv_sem, line_send, line_recv):
        dp, mp = lax.axis_index("dp"), lax.axis_index("mp")
        peers = [(dp ^ o, mp) for o in range(1, dp_count)]
        along = [(dp, mp ^ o) for o in range(1, mp_count)]
        greet(peers + along)
        copies = []
        for o in range(1, dp_count):
            copies.append(remote(in_ref.at[dp ^ o], landed.at[o - 1], send_sem.at[o], recv_sem.at[o], peers[o - 1]))
            copies[-1].start()
        value = in_ref[dp]
        for o in range(1, dp_count):
            copies[o - 1].wait()
            value = value + landed[o - 1]
        mine[...] = value
        others[mp] = value
        copies = []
        for o in range(1, mp_count):
            copies.append(remote(mine, others.at[mp], line_send.at[o], line_recv.at[o], along[o - 1]))
            copies[-1].start()
        for copy in copies:
            copy.wait()
        value = others[0]
        for index in range(1, mp_count):
            value = value + others[index]
        out_ref[...] = value

    dma = pltpu.SemaphoreType.DMA
    return pl.pallas_call(
        kernel,
        out_shape=jax.ShapeDtypeStruct((depth, width), jnp.float32),
        in_specs=[VMEM],
        out_specs=VMEM,
        scratch_shapes=[
            pltpu.VMEM((dp_count - 1, depth, width), jnp.float32), pltpu.VMEM((depth, width), jnp.float32),
            pltpu.VMEM((mp_count, depth, width), jnp.float32),
            dma((dp_count,)), dma((dp_count,)), dma((mp_count,)), dma((mp_count,)),
        ],
        compiler_params=pltpu.CompilerParams(collective_id=collective_id, has_side_effects=True),
        cost_estimate=pl.CostEstimate(flops=0, bytes_accessed=20 * MIB, transcendentals=0),
    )(packed)


def packed_rows(vectors):
    flat = jnp.concatenate([v.astype(jnp.float32) for v in vectors])
    rows = flat.shape[0] // 128
    return jnp.pad(flat.reshape(rows, 128), ((0, -rows % 8), (0, 0)))


def per_device(
    hidden_in,
    output_grad,
    first_gain,
    first_shift,
    query_weight,
    query_bias,
    key_weight,
    value_weight,
    value_bias,
    out_weight,
    out_bias,
    second_gain,
    second_shift,
    up_weight,
    up_bias,
    down_weight,
    down_bias,
    seq_lengths,
    block_order,
    block_slot,
):
    local_rows, model_width = hidden_in.shape
    mp_count, dp_count = lax.axis_size("mp"), lax.axis_size("dp")
    mp_index, dp_index = lax.axis_index("mp"), lax.axis_index("dp")
    group_rows = local_rows * mp_count
    head_width = query_weight.shape[1]
    heads_local = head_width // HEAD_DIM
    hidden_width = up_weight.shape[1]
    members = dp_count // heads_local
    blocks_each = group_rows // BLOCK
    plan = (seq_lengths, block_order, block_slot)

    own_valid = valid_rows(seq_lengths, block_order, dp_index * group_rows + mp_index * local_rows, local_rows)

    vectors = (first_gain, first_shift, query_bias, value_bias, out_bias, second_gain, second_shift, down_bias, up_bias)
    rows_in, vector_rows, query_all, key_all, value_all, out_all = gather_first(
        hidden_in, packed_rows(vectors), (query_weight, key_weight, value_weight, out_weight), 0
    )
    vector_rows = vector_rows.reshape(dp_count, -1, 128)
    each = model_width // dp_count // 128
    (gain_one, shift_one, bias_query, bias_value, bias_out, gain_two, shift_two, bias_down) = (
        vector_rows[:, k * each : (k + 1) * each].reshape(1, model_width) for k in range(8)
    )
    up_each = up_bias.shape[0] // 128
    bias_up = vector_rows[:, 8 * each : 8 * each + up_each].reshape(1, up_bias.shape[0] * dp_count)

    def heads_of(vector):
        return lax.dynamic_slice_in_dim(vector, mp_index * head_width, head_width, 1)

    unit_one, _ = unit_rows(rows_in.astype(jnp.float32))
    rows_one = (unit_one * gain_one + shift_one).astype(jnp.bfloat16)

    def project(weight, bias):
        return (jnp.dot(rows_one, weight, preferred_element_type=jnp.float32) + bias).astype(jnp.bfloat16)

    key_rows = project(key_all, 0.0)
    value_rows = project(value_all, heads_of(bias_value))
    queries = project(query_all, heads_of(bias_query))
    head_queries, head_keys, head_values = to_heads([queries], [key_rows, value_rows], heads_local, members, 1)
    head_mix, exact_mix, log_total = attend(head_queries, head_keys, head_values, *plan, members, blocks_each)
    (attended_low,) = to_rows([head_mix], [], heads_local, members, 2)
    out_part = contract_last(attended_low, out_all).astype(jnp.bfloat16)
    residual, rows_two = reduce_norm_gather(out_part, hidden_in, bias_out, gain_two, shift_two, 3)

    up_all = lax.all_gather(up_weight, "dp", axis=0, tiled=True)
    down_all = lax.all_gather(down_weight, "dp", axis=0, tiled=True)
    branch_two = jnp.where(own_valid[:, None], output_grad, 0).astype(jnp.bfloat16)
    branch_rows_two = whole_rows(branch_two)

    bias_hidden = lax.dynamic_slice_in_dim(bias_up, mp_index * hidden_width, hidden_width, 1)
    pre_act = jnp.dot(rows_two, up_all, preferred_element_type=jnp.float32) + bias_hidden
    hidden_low = gelu_exact(pre_act).astype(jnp.bfloat16)
    hidden_grad = jnp.dot(branch_rows_two, down_all, preferred_element_type=jnp.float32)
    pre_grad = jax.vjp(gelu_exact, pre_act)[1](hidden_grad)[0].astype(jnp.bfloat16)
    up_part = contract_last(pre_grad, up_all).astype(jnp.bfloat16)
    residual_grad, sums_two, branch_rows_one = reduce_back_gather(up_part, residual, branch_two, gain_two, 4)

    feed = row_share(contract_last(hidden_low, down_all))
    result = residual + feed + bias_down
    output = jnp.where(own_valid[:, None], result, 0.0).astype(jnp.bfloat16)
    down_weight_grad = owner_share(contract_first(branch_rows_two, hidden_low))
    up_weight_grad = owner_share(contract_first(rows_two, pre_grad))

    attended_grad = jnp.dot(branch_rows_one, out_all, preferred_element_type=jnp.float32).astype(jnp.bfloat16)
    (head_grad,) = to_heads([attended_grad], [], heads_local, members, 5)
    head_query_grad, head_key_grad, head_value_grad = attend_back(
        head_queries, head_keys, head_values, head_grad, exact_mix, log_total, *plan, members, blocks_each
    )
    query_low, key_low, value_low = to_rows(
        [head_query_grad], [head_key_grad, head_value_grad], heads_local, members, 6
    )
    last_part = contract_last(query_low, query_all)
    last_part = last_part + contract_last(key_low, key_all)
    last_part = (last_part + contract_last(value_low, value_all)).astype(jnp.bfloat16)
    weight_parts = [
        contract_first(left, right).astype(jnp.bfloat16)
        for left, right in (
            (rows_one, query_low), (rows_one, key_low), (rows_one, value_low), (branch_rows_one, attended_low)
        )
    ]
    input_grad, sums_one, query_weight_grad, key_weight_grad, value_weight_grad, out_weight_grad = reduce_last(
        last_part, residual_grad, hidden_in, gain_one, weight_parts, 7
    )

    def column_sums(values):
        return jnp.sum(values.astype(jnp.float32), axis=0)

    def placed(values):
        whole = jnp.zeros((values.shape[0] * mp_count,), jnp.float32)
        return lax.dynamic_update_slice_in_dim(whole, values, mp_index * values.shape[0], 0)

    sums = (
        sums_one[0], sums_one[1], placed(column_sums(query_low)), placed(column_sums(value_low)), sums_two[2],
        sums_two[0], sums_two[1], column_sums(branch_two), placed(column_sums(pre_grad)),
    )
    packed = jnp.concatenate([v.reshape(dp_count, -1, 128) for v in sums], axis=1)
    packed = jnp.pad(packed, ((0, 0), (0, -packed.shape[1] % 8), (0, 0)))
    summed = sum_vectors(packed, 8)
    vector_grads = [summed[k * each : (k + 1) * each].reshape(-1) for k in range(8)]
    up_bias_grad = summed[8 * each : 8 * each + up_each].reshape(-1)
    return (
        output,
        input_grad,
        vector_grads[0],
        vector_grads[1],
        query_weight_grad,
        vector_grads[2],
        key_weight_grad,
        value_weight_grad,
        vector_grads[3],
        out_weight_grad,
        vector_grads[4],
        vector_grads[5],
        vector_grads[6],
        up_weight_grad,
        up_bias_grad,
        down_weight_grad,
        vector_grads[7],
    )


def solution(mesh):
    return jax.shard_map(
        per_device,
        mesh=mesh,
        in_specs=(
            P(("dp", "mp"), None),
            P(("dp", "mp"), None),
            P("dp"),
            P("dp"),
            P("dp", "mp"),
            P("dp"),
            P("dp", "mp"),
            P("dp", "mp"),
            P("dp"),
            P("dp", "mp"),
            P("dp"),
            P("dp"),
            P("dp"),
            P("dp", "mp"),
            P("dp"),
            P("dp", "mp"),
            P("dp"),
            P(),
            P(),
            P(),
        ),
        out_specs=(
            P(("dp", "mp"), None),
            P(("dp", "mp"), None),
            P("dp"),
            P("dp"),
            P("dp", "mp"),
            P("dp"),
            P("dp", "mp"),
            P("dp", "mp"),
            P("dp"),
            P("dp", "mp"),
            P("dp"),
            P("dp"),
            P("dp"),
            P("dp", "mp"),
            P("dp"),
            P("dp", "mp"),
            P("dp"),
        ),
        check_vma=False,
    )
```

```python
import math

import jax
import jax.numpy as jnp
from jax import lax
from jax.experimental import pallas as pl
from jax.experimental.pallas import tpu as pltpu
from jax.sharding import PartitionSpec as P

HEAD_DIM = 128
BLOCK = 128
KEY_BLOCKS = 8
MESH = pl.DeviceIdType.MESH
ANY = pl.BlockSpec(memory_space=pl.ANY)
VMEM = pl.BlockSpec(memory_space=pltpu.VMEM)
SMEM = pl.BlockSpec(memory_space=pltpu.SMEM)
MIB = 1 << 20


big_negative = -1e30
norm_epsilon = 1e-05


def norm_back(upstream, normed, inverse, gain_row):
    scaled = upstream * gain_row
    mean_grad = jnp.mean(scaled, axis=-1, keepdims=True)
    second = jnp.mean(scaled * normed, axis=-1, keepdims=True)
    return inverse * (scaled - mean_grad - normed * second)


def gelu_exact(values):
    return jax.nn.gelu(values, approximate=False)


def contract_last(left, right):
    return lax.dot_general(
        left, right, (((1,), (1,)), ((), ())), preferred_element_type=jnp.float32
    )


def contract_first(left, right):
    return lax.dot_general(
        left, right, (((0,), (0,)), ((), ())), preferred_element_type=jnp.float32
    )


def whole_rows(local_part):
    return lax.all_gather(local_part, "mp", axis=0, tiled=True)


def row_share(term):
    term = term.astype(jnp.bfloat16)
    return lax.psum_scatter(term, "mp", scatter_dimension=0, tiled=True).astype(jnp.float32)


def owner_share(term):
    term = term.astype(jnp.bfloat16)
    return lax.psum_scatter(term, "dp", scatter_dimension=0, tiled=True).astype(jnp.float32)


def greet(peers):
    barrier = pltpu.get_barrier_semaphore()
    for peer in peers:
        pl.semaphore_signal(barrier, inc=1, device_id=peer, device_id_type=MESH)
    pl.semaphore_wait(barrier, len(peers))


def remote(src, dst, send_sem, recv_sem, peer):
    return pltpu.make_async_remote_copy(
        src_ref=src, dst_ref=dst, send_sem=send_sem, recv_sem=recv_sem,
        device_id=peer, device_id_type=MESH,
    )


def head_place(heads, members):
    me = lax.axis_index("dp")
    return me, me // members, me % members, lax.axis_index("mp")


def lanes(head):
    return pl.ds(pl.multiple_of(head * HEAD_DIM, HEAD_DIM), HEAD_DIM)


def to_heads(owned, shared, heads, members, collective_id):
    rows = (owned + shared)[0].shape[0]
    n_owned, n_shared = len(owned), len(shared)
    count = n_owned + n_shared

    def kernel(*refs):
        ins, outs = refs[:count], refs[count : 2 * count]
        local_sem, send_sem, recv_sem, fwd_send, fwd_recv = refs[2 * count :]
        me, group, member, mp = head_place(heads, members)

        def dest(array, source):
            place = (source // members) if array < n_owned else source
            return outs[array].at[pl.ds(pl.multiple_of(place * rows, rows), rows)]

        head_peers = [((group ^ o) * members + member, mp) for o in range(1, heads)]
        pair_peers = [(group * members + (member ^ o), mp) for o in range(1, members)]
        greet(head_peers + pair_peers)
        order = list(range(n_owned, count)) + list(range(n_owned))
        sends, locals_, forwards = {}, [], []
        for a in order:
            for o in range(1, heads):
                copy = remote(ins[a].at[:, lanes(group ^ o)], dest(a, me), send_sem.at[a, o],
                              recv_sem.at[a, o], head_peers[o - 1])
                copy.start()
                sends[a, o] = copy
        for a in range(count):
            copy = pltpu.make_async_copy(ins[a].at[:, lanes(group)], dest(a, me), local_sem.at[a])
            copy.start()
            locals_.append(copy)
        for a in range(n_owned, count):
            for o in range(heads):
                source = (group ^ o) * members + member
                if o:
                    sends[a, o].wait_recv()
                for p in range(1, members):
                    piece = ins[a].at[:, lanes(group)] if o == 0 else dest(a, source)
                    copy = remote(piece, dest(a, source), fwd_send.at[a - n_owned, o, p],
                                  fwd_recv.at[a - n_owned, o, p], pair_peers[p - 1])
                    copy.start()
                    forwards.append(copy)
        for copy in locals_:
            copy.wait()
        for (a, o), copy in sends.items():
            copy.wait_send()
            if a < n_owned:
                copy.wait_recv()
        for copy in forwards:
            copy.wait()

    total = rows * lax.axis_size("dp")
    shapes = [jax.ShapeDtypeStruct((heads * rows, HEAD_DIM), a.dtype) for a in owned]
    shapes += [jax.ShapeDtypeStruct((total, HEAD_DIM), a.dtype) for a in shared]
    dma = pltpu.SemaphoreType.DMA
    return pl.pallas_call(
        kernel,
        out_shape=shapes,
        in_specs=[ANY] * count,
        out_specs=[ANY] * count,
        scratch_shapes=[
            dma((count,)), dma((count, heads)), dma((count, heads)),
            dma((max(n_shared, 1), heads, members)), dma((max(n_shared, 1), heads, members)),
        ],
        compiler_params=pltpu.CompilerParams(collective_id=collective_id, has_side_effects=True),
        cost_estimate=pl.CostEstimate(flops=0, bytes_accessed=100 * MIB, transcendentals=0),
    )(*owned, *shared)


def to_rows(owned, shared, heads, members, collective_id):
    rows = owned[0].shape[0] // heads
    n_owned, n_shared = len(owned), len(shared)
    count = n_owned + n_shared

    def kernel(*refs):
        ins, outs = refs[:count], refs[count : 2 * count]
        local_sem, send_sem, recv_sem, own_sem, part_send, part_recv = refs[2 * count : 2 * count + 6]
        me, group, member, mp = head_place(heads, members)
        head_peers = [((group ^ o) * members + member, mp) for o in range(1, heads)]
        pair_peers = [(group * members + (member ^ o), mp) for o in range(1, members)]
        greet(head_peers + pair_peers)
        if n_shared:
            own, parts, total = refs[2 * count + 6 :]
        copies, pending = [], {}

        def part(array, o, who):
            first = pl.multiple_of(((group ^ o) * members + who) * rows, rows)
            return ins[array].at[pl.ds(first, rows)]

        for s in range(n_shared):
            for o in range(heads):
                copy = pltpu.make_async_copy(part(n_owned + s, o, member), own.at[s, o], own_sem.at[s, o])
                copy.start()
                pending[s, o, 0] = copy
                for p in range(1, members):
                    copy = remote(part(n_owned + s, o, member ^ p), parts.at[s, o, p - 1],
                                  part_send.at[s, o, p], part_recv.at[s, o, p], pair_peers[p - 1])
                    copy.start()
                    pending[s, o, p] = copy
        for a in range(n_owned):
            for o in range(heads):
                piece = ins[a].at[pl.ds(pl.multiple_of((group ^ o) * rows, rows), rows)]
                place = outs[a].at[:, lanes(group)]
                if o:
                    copy = remote(piece, place, send_sem.at[a, o], recv_sem.at[a, o], head_peers[o - 1])
                else:
                    copy = pltpu.make_async_copy(piece, place, local_sem.at[a])
                copy.start()
                copies.append(copy)
        for o in list(range(1, heads)) + [0]:
            for s in range(n_shared):
                for p in range(members):
                    if p:
                        pending[s, o, p].wait_recv()
                    else:
                        pending[s, o, p].wait()
                value = own[s, o].astype(jnp.float32)
                for p in range(1, members):
                    value = value + parts[s, o, p - 1].astype(jnp.float32)
                total[s, o] = value.astype(total.dtype)
                a = n_owned + s
                place = outs[a].at[:, lanes(group)]
                if o:
                    copy = remote(total.at[s, o], place, send_sem.at[a, o], recv_sem.at[a, o], head_peers[o - 1])
                else:
                    copy = pltpu.make_async_copy(total.at[s, o], place, local_sem.at[a])
                copy.start()
                copies.append(copy)
        for s in range(n_shared):
            for o in range(heads):
                for p in range(1, members):
                    pending[s, o, p].wait_send()
        for copy in copies:
            copy.wait()

    dma = pltpu.SemaphoreType.DMA
    slots = max(n_shared, 1)
    scratch = [
        dma((count,)), dma((count, heads)), dma((count, heads)),
        dma((slots, heads)), dma((slots, heads, members)), dma((slots, heads, members)),
    ]
    if n_shared:
        kind = shared[0].dtype
        scratch += [
            pltpu.VMEM((n_shared, heads, rows, HEAD_DIM), kind),
            pltpu.VMEM((n_shared, heads, members - 1, rows, HEAD_DIM), kind),
            pltpu.VMEM((n_shared, heads, rows, HEAD_DIM), kind),
        ]
    return pl.pallas_call(
        kernel,
        out_shape=[jax.ShapeDtypeStruct((rows, heads * HEAD_DIM), a.dtype) for a in owned + shared],
        in_specs=[ANY] * count,
        out_specs=[ANY] * count,
        scratch_shapes=scratch,
        compiler_params=pltpu.CompilerParams(
            collective_id=collective_id, has_side_effects=True, vmem_limit_bytes=48 * MIB
        ),
        cost_estimate=pl.CostEstimate(flops=0, bytes_accessed=100 * MIB, transcendentals=0),
    )(*owned, *shared)


def sequence_of(place, lengths):
    first, length, running = jnp.int32(0), jnp.int32(0), jnp.int32(0)
    for s in range(lengths.shape[0]):
        inside = place >= running
        first = jnp.where(inside, running, first)
        length = jnp.where(inside, lengths[s], length)
        running = running + (lengths[s] + (BLOCK - 1)) // BLOCK
    return first, length - (place - first) * BLOCK


def list_queries(slot, index_list, place_list, members, blocks_each):
    member = lax.axis_index("dp") % members

    def visit(block, count):
        dealt = slot[block]
        owner = dealt // blocks_each

        @pl.when(owner % members == member)
        def _():
            index_list[count] = (owner // members) * blocks_each + dealt % blocks_each
            place_list[count] = block

        return count + (owner % members == member).astype(jnp.int32)

    lax.fori_loop(0, slot.shape[0], visit, jnp.int32(0))


def block_rows(block):
    return pl.ds(pl.multiple_of(block * BLOCK, BLOCK), BLOCK)


class QueryPair:
    def __init__(self, pair, lengths, index_list, place_list):
        self.index = [index_list[2 * pair + i] for i in range(2)]
        self.place = [place_list[2 * pair + i] for i in range(2)]
        found = [sequence_of(place, lengths) for place in self.place]
        self.start = found[0][0]
        lane = lax.broadcasted_iota(jnp.int32, (1, 2 * BLOCK), 1)
        right = lane >= BLOCK

        def lanes_of(left_value, right_value):
            return jnp.where(right, right_value, left_value)

        within = lane - lanes_of(0, BLOCK)
        base = self.start * BLOCK
        self.position = lanes_of(self.place[0], self.place[1]) * BLOCK + within - base
        self.lowest = lanes_of(found[0][0], found[1][0]) * BLOCK - base
        self.live = within < lanes_of(found[0][1], found[1][1])
        self.tiles = (self.place[1] - self.start) // KEY_BLOCKS + 1
        self.open_tiles = jnp.where(found[0][0] == found[1][0], (self.place[0] - self.start) // KEY_BLOCKS, 0)

    def row(self, tile):
        return pl.multiple_of((self.start + tile * KEY_BLOCKS) * BLOCK, BLOCK)

    def allowed(self, tile):
        width = KEY_BLOCKS * BLOCK
        key = lax.broadcasted_iota(jnp.int32, (width, 2 * BLOCK), 0)
        return (key <= self.position - tile * width) & (key >= self.lowest - tile * width)

    def load_t(self, ref):
        return jnp.concatenate([ref[block_rows(index)].T for index in self.index], axis=1)

    def load(self, ref):
        return jnp.concatenate([ref[block_rows(index)] for index in self.index], axis=0)

    def store_t(self, ref, value_t):
        for i, index in enumerate(self.index):
            ref[block_rows(index)] = value_t[:, i * BLOCK : (i + 1) * BLOCK].T.astype(ref.dtype)


def attend(queries, shared, lengths, order, slot, members, blocks_each):
    pairs, key_count = queries.shape[0] // (2 * BLOCK), shared.shape[1] // BLOCK
    width = KEY_BLOCKS * BLOCK
    padded = (key_count + KEY_BLOCKS - 1) * BLOCK
    scale = math.log2(math.e) / math.sqrt(HEAD_DIM)

    def kernel(lengths_ref, slot_ref, q_ref, shared_ref, out_ref, exact_ref, log_ref,
               index_list, place_list, keys, values_t):
        list_queries(slot_ref, index_list, place_list, members, blocks_each)

        @pl.loop(0, key_count)
        def _(block):
            source = block_rows(slot_ref[block])
            keys[block_rows(block)] = shared_ref[0, source]
            values_t[:, block_rows(block)] = shared_ref[1, source].T

        tail = pl.ds(key_count * BLOCK, padded - key_count * BLOCK)
        keys[tail] = jnp.zeros((padded - key_count * BLOCK, HEAD_DIM), keys.dtype)
        values_t[:, tail] = jnp.zeros((HEAD_DIM, padded - key_count * BLOCK), keys.dtype)

        @pl.loop(0, pairs)
        def _(index):
            pair = QueryPair(index, lengths_ref, index_list, place_list)
            query_t = pair.load_t(q_ref)

            def step(tile, carry, masked):
                top, total, mix = carry
                span = pl.ds(pair.row(tile), width)
                scores = jnp.dot(keys[span], query_t, preferred_element_type=jnp.float32)
                if masked:
                    scores = jnp.where(pair.allowed(tile), scores, big_negative)
                new_top = jnp.maximum(top, jnp.max(scores, axis=0, keepdims=True))
                weights = jnp.exp2((scores - new_top) * scale)
                fade = jnp.exp2((top - new_top) * scale)
                total = total * fade + jnp.sum(weights, axis=0, keepdims=True)
                mix = mix * fade + jnp.dot(
                    values_t[:, span], weights.astype(jnp.bfloat16), preferred_element_type=jnp.float32)
                return new_top, total, mix

            carry = (jnp.full((1, 2 * BLOCK), big_negative, jnp.float32), jnp.zeros((1, 2 * BLOCK), jnp.float32),
                     jnp.zeros((HEAD_DIM, 2 * BLOCK), jnp.float32))
            carry = lax.fori_loop(0, pair.open_tiles, lambda tile, c: step(tile, c, False), carry)
            top, total, mix = lax.fori_loop(pair.open_tiles, pair.tiles, lambda tile, c: step(tile, c, True), carry)
            mix = jnp.where(pair.live, mix / total, 0.0)
            exact_ref[index] = mix
            pair.store_t(out_ref, mix)
            log_ref[index] = jnp.where(pair.live, top * scale + jnp.log2(total), -big_negative)

    return pl.pallas_call(
        kernel,
        out_shape=[
            jax.ShapeDtypeStruct(queries.shape, jnp.bfloat16),
            jax.ShapeDtypeStruct((pairs, HEAD_DIM, 2 * BLOCK), jnp.float32),
            jax.ShapeDtypeStruct((pairs, 1, 2 * BLOCK), jnp.float32),
        ],
        in_specs=[SMEM] * 2 + [VMEM] * 2,
        out_specs=[VMEM] * 3,
        scratch_shapes=[
            pltpu.SMEM((2 * pairs,), jnp.int32), pltpu.SMEM((2 * pairs,), jnp.int32),
            pltpu.VMEM((padded, HEAD_DIM), jnp.bfloat16), pltpu.VMEM((HEAD_DIM, padded), jnp.bfloat16),
        ],
        compiler_params=pltpu.CompilerParams(vmem_limit_bytes=56 * MIB),
        cost_estimate=pl.CostEstimate(flops=8 << 30, bytes_accessed=50 * MIB, transcendentals=8 << 20),
    )(lengths, slot, queries, shared)


def attend_back(queries, shared, upstream, exact, logs, lengths, order, slot, members, blocks_each):
    pairs, key_count = queries.shape[0] // (2 * BLOCK), shared.shape[1] // BLOCK
    width = KEY_BLOCKS * BLOCK
    padded = (key_count + KEY_BLOCKS - 1) * BLOCK
    scale = math.log2(math.e) / math.sqrt(HEAD_DIM)
    plain_scale = 1.0 / math.sqrt(HEAD_DIM)

    def kernel(lengths_ref, slot_ref, q_ref, shared_ref, g_ref, exact_ref, log_ref, dq_ref, dk_ref, dv_ref,
               index_list, place_list, keys, keys_t, values, key_sum, value_sum):
        list_queries(slot_ref, index_list, place_list, members, blocks_each)

        @pl.loop(0, key_count)
        def _(block):
            source, to = block_rows(slot_ref[block]), block_rows(block)
            rows = shared_ref[0, source]
            keys[to] = rows
            keys_t[:, to] = rows.T
            values[to] = shared_ref[1, source]
            key_sum[to] = jnp.zeros((BLOCK, HEAD_DIM), jnp.float32)
            value_sum[to] = jnp.zeros((BLOCK, HEAD_DIM), jnp.float32)

        tail = pl.ds(key_count * BLOCK, padded - key_count * BLOCK)
        keys[tail] = jnp.zeros((padded - key_count * BLOCK, HEAD_DIM), keys.dtype)
        values[tail] = jnp.zeros((padded - key_count * BLOCK, HEAD_DIM), keys.dtype)
        keys_t[:, tail] = jnp.zeros((HEAD_DIM, padded - key_count * BLOCK), keys.dtype)
        key_sum[tail] = jnp.zeros((padded - key_count * BLOCK, HEAD_DIM), jnp.float32)
        value_sum[tail] = jnp.zeros((padded - key_count * BLOCK, HEAD_DIM), jnp.float32)

        @pl.loop(0, pairs)
        def _(index):
            pair = QueryPair(index, lengths_ref, index_list, place_list)
            query, grad = pair.load(q_ref), pair.load(g_ref)
            query_t, grad_t = pair.load_t(q_ref), pair.load_t(g_ref)
            delta = jnp.sum(grad_t.astype(jnp.float32) * exact_ref[index], axis=0, keepdims=True)
            log_total = log_ref[index]

            def step(tile, query_grad, masked):
                span = pl.ds(pair.row(tile), width)
                scores = jnp.dot(keys[span], query_t, preferred_element_type=jnp.float32)
                probability = jnp.exp2(scores * scale - log_total)
                if masked:
                    probability = jnp.where(pair.allowed(tile), probability, 0.0)
                prob_grad = jnp.dot(values[span], grad_t, preferred_element_type=jnp.float32)
                score_grad = (probability * (prob_grad - delta)).astype(jnp.bfloat16)
                value_sum[span] += jnp.dot(
                    probability.astype(jnp.bfloat16), grad, preferred_element_type=jnp.float32)
                key_sum[span] += jnp.dot(score_grad, query, preferred_element_type=jnp.float32)
                return query_grad + jnp.dot(keys_t[:, span], score_grad, preferred_element_type=jnp.float32)

            query_grad = jnp.zeros((HEAD_DIM, 2 * BLOCK), jnp.float32)
            query_grad = lax.fori_loop(0, pair.open_tiles, lambda tile, c: step(tile, c, False), query_grad)
            query_grad = lax.fori_loop(pair.open_tiles, pair.tiles, lambda tile, c: step(tile, c, True), query_grad)
            pair.store_t(dq_ref, query_grad * plain_scale)

        @pl.loop(0, key_count)
        def _(block):
            at, dealt = block_rows(block), block_rows(slot_ref[block])
            dk_ref[dealt] = (key_sum[at] * plain_scale).astype(dk_ref.dtype)
            dv_ref[dealt] = value_sum[at].astype(dv_ref.dtype)

    return pl.pallas_call(
        kernel,
        out_shape=[
            jax.ShapeDtypeStruct(queries.shape, jnp.bfloat16),
            jax.ShapeDtypeStruct(shared.shape[1:], jnp.bfloat16),
            jax.ShapeDtypeStruct(shared.shape[1:], jnp.bfloat16),
        ],
        in_specs=[SMEM] * 2 + [VMEM] * 5,
        out_specs=[VMEM] * 3,
        scratch_shapes=[
            pltpu.SMEM((2 * pairs,), jnp.int32), pltpu.SMEM((2 * pairs,), jnp.int32),
            pltpu.VMEM((padded, HEAD_DIM), jnp.bfloat16),
            pltpu.VMEM((HEAD_DIM, padded), jnp.bfloat16),
            pltpu.VMEM((padded, HEAD_DIM), jnp.bfloat16),
            pltpu.VMEM((padded, HEAD_DIM), jnp.float32),
            pltpu.VMEM((padded, HEAD_DIM), jnp.float32),
        ],
        compiler_params=pltpu.CompilerParams(vmem_limit_bytes=60 * MIB),
        cost_estimate=pl.CostEstimate(flops=20 << 30, bytes_accessed=100 * MIB, transcendentals=8 << 20),
    )(lengths, slot, queries, shared, upstream, exact, logs)


def line_neighbours(mp, count):
    return ((1, mp + 1 < count, jnp.minimum(mp + 1, count - 1)), (-1, mp >= 1, jnp.maximum(mp - 1, 0)))


def greet_all(fixed, dp, mp, count):
    barrier = pltpu.get_barrier_semaphore()
    for peer in fixed:
        pl.semaphore_signal(barrier, inc=1, device_id=peer, device_id_type=MESH)
    expected = jnp.int32(len(fixed))
    for _, there, place in line_neighbours(mp, count):

        @pl.when(there)
        def _():
            pl.semaphore_signal(barrier, inc=1, device_id=(dp, place), device_id_type=MESH)

        expected = expected + there.astype(jnp.int32)
    pl.semaphore_wait(barrier, expected)


class LineGather:
    def __init__(self, own, full, rows, pieces, send_sem, recv_sem, dp, mp, count):
        self.own, self.full, self.rows, self.pieces = own, full, rows, pieces
        self.send_sem, self.recv_sem, self.dp, self.mp, self.count = send_sem, recv_sem, dp, mp, count
        self.size = rows // pieces

    def place(self, block, piece):
        return self.full.at[pl.ds(pl.multiple_of(block * self.rows + piece * self.size, self.size), self.size)]

    def hop(self, way, step, piece):
        sign, there, neighbour = line_neighbours(self.mp, self.count)[way]
        origin = self.mp - sign * step
        exists = (origin >= 0) & (origin < self.count)
        origin = jnp.clip(origin, 0, self.count - 1)
        if step == 0:
            source = self.own.at[pl.ds(pl.multiple_of(piece * self.size, self.size), self.size)]
        else:
            source = self.place(origin, piece)
        def copy():
            return remote(source, self.place(origin, piece), self.send_sem.at[way, step, piece],
                          self.recv_sem.at[way, step, piece], (self.dp, neighbour))

        return exists, exists & there, copy

    def advance(self, step, piece, also=True):
        for way in range(2):
            if step:
                exists, _, _ = self.hop(way, step, piece)
                _, _, earlier = self.hop(way, step - 1, piece)

                @pl.when(exists & also)
                def _():
                    earlier().wait_recv()

            if step < self.count - 1:
                _, sends, copy = self.hop(way, step, piece)

                @pl.when(sends & also)
                def _():
                    copy().start()

    def finish(self):
        @pl.loop(0, self.pieces)
        def _(piece):
            for way in range(2):
                for step in range(self.count - 1):
                    _, sends, copy = self.hop(way, step, piece)

                    @pl.when(sends)
                    def _():
                        copy().wait_send()

    @staticmethod
    def semaphores(count, pieces):
        return [pltpu.SemaphoreType.DMA((2, count, pieces)), pltpu.SemaphoreType.DMA((2, count, pieces))]


class ShardGather:
    def __init__(self, shards, wholes, depth, cross_send, cross_recv, core_send, core_recv, own_sem, dp, mp, chips):
        self.shards, self.wholes, self.depth, self.own_sem = shards, wholes, depth, own_sem
        self.cross_send, self.cross_recv, self.core_send, self.core_recv = cross_send, cross_recv, core_send, core_recv
        self.dp, self.mp, self.chips = dp, mp, chips

    def place(self, array, owner):
        return self.wholes[array].at[pl.ds(pl.multiple_of(owner * self.depth, self.depth), self.depth)]

    def cross(self, array, o):
        return remote(self.shards[array], self.place(array, self.dp), self.cross_send.at[array, o],
                      self.cross_recv.at[array, o], (self.dp ^ (2 * o), self.mp))

    def core(self, array, o):
        owner = self.dp ^ (2 * o)
        source = self.place(array, owner) if o else self.shards[array]
        return remote(source, self.place(array, owner), self.core_send.at[array, o], self.core_recv.at[array, o],
                      (self.dp ^ 1, self.mp))

    def own(self, array):
        return pltpu.make_async_copy(self.shards[array], self.place(array, self.dp), self.own_sem.at[array])

    def begin(self):
        for array in range(len(self.shards)):
            for o in range(1, self.chips):
                self.cross(array, o).start()
        for array in range(len(self.shards)):
            self.own(array).start()
            self.core(array, 0).start()

    def spread(self, array):
        for o in range(1, self.chips):
            self.cross(array, o).wait_recv()
            self.core(array, o).start()

    def finish(self):
        for array in range(len(self.shards)):
            self.own(array).wait()
            for o in range(self.chips):
                self.core(array, o).wait()
                if o:
                    self.cross(array, o).wait_send()

    @staticmethod
    def semaphores(count, chips):
        return [pltpu.SemaphoreType.DMA((count, chips)) for _ in range(4)] + [pltpu.SemaphoreType.DMA((count,))]


class LineReduce:
    def __init__(self, part, flows, rows, pieces, send_sem, recv_sem, dp, mp, count):
        self.part, self.flows, self.rows, self.pieces = part, flows, rows, pieces
        self.send_sem, self.recv_sem, self.dp, self.mp, self.count = send_sem, recv_sem, dp, mp, count
        self.size = rows // pieces

    def span(self, block, piece):
        return pl.ds(pl.multiple_of(block * self.rows + piece * self.size, self.size), self.size)

    def hop(self, way, block, piece, first=False):
        neighbour = line_neighbours(self.mp, self.count)[way][2]
        span = self.span(block, piece)
        source = self.part.at[span] if first else self.flows.at[way, span]
        return remote(source, self.flows.at[way, span], self.send_sem.at[way, block, piece],
                      self.recv_sem.at[way, block, piece], (self.dp, neighbour))

    def roles(self, way, block):
        if way == 0:
            behind, ahead = self.mp >= 1, self.mp < block
        else:
            behind, ahead = self.mp < self.count - 1, self.mp > block
        return ahead & jnp.logical_not(behind), ahead & behind

    def targets(self):
        for index in range(self.count - 1):
            yield 0, self.count - 1 - index
            yield 1, index

    def begin(self, piece, also=True):
        for way, block in self.targets():
            begins, _ = self.roles(way, block)

            @pl.when(begins & also)
            def _():
                self.hop(way, block, piece, True).start()

    def advance(self, turn):
        for way, block in self.targets():
            _, hands_on = self.roles(way, block)
            passed = SKEW * (self.mp - 1 if way == 0 else self.count - 2 - self.mp)
            piece = jnp.clip(turn - passed, 0, self.pieces - 1)

            @pl.when(hands_on & (turn >= passed) & (turn - passed < self.pieces))
            def _():
                self.hop(way, block, piece).wait_recv()
                span = self.span(block, piece)
                value = self.flows[way, span].astype(jnp.float32) + self.part[span].astype(jnp.float32)
                self.flows[way, span] = value.astype(self.flows.dtype)
                self.hop(way, block, piece).start()

    def arrive(self, piece):
        for way in range(2):

            @pl.when(self.mp >= 1 if way == 0 else self.mp < self.count - 1)
            def _():
                self.hop(way, self.mp, piece).wait_recv()

    def total(self, piece, result):
        span = self.span(self.mp, piece)
        result[...] = self.part[span].astype(jnp.float32)
        for way in range(2):

            @pl.when(self.mp >= 1 if way == 0 else self.mp < self.count - 1)
            def _():
                result[...] += self.flows[way, span].astype(jnp.float32)

    def finish(self):
        @pl.loop(0, self.pieces)
        def _(piece):
            for way, block in self.targets():
                begins, hands_on = self.roles(way, block)

                @pl.when(begins)
                def _():
                    self.hop(way, block, piece, True).wait_send()

                @pl.when(hands_on)
                def _():
                    self.hop(way, block, piece).wait_send()

    @staticmethod
    def scratch(count, rows, width, pieces):
        return [pltpu.VMEM((2, count * rows, width), jnp.bfloat16),
                pltpu.SemaphoreType.DMA((2, count, pieces)), pltpu.SemaphoreType.DMA((2, count, pieces))]


AHEAD = 1
MAX_PIECES = 16
SKEW = 1


def pieces_of(rows):
    return min(MAX_PIECES, rows // 16)


def unit_rows(values):
    average = jnp.mean(values, axis=-1, keepdims=True)
    centred = values - average
    inverse = lax.rsqrt(jnp.mean(centred * centred, axis=-1, keepdims=True) + norm_epsilon)
    return centred * inverse, inverse


def project_first(
    hidden, output_grad, lengths, order, vectors, projections, out_weight, heads, members, collective_id
):
    rows, width = hidden.shape
    dp_count, mp_count = lax.axis_size("dp"), lax.axis_size("mp")
    chips, pieces = dp_count // 2, pieces_of(rows)
    group_rows, depth, columns = mp_count * rows, projections[0].shape[0], projections[0].shape[1]
    each = width // dp_count // 128
    tall = [v.shape[1] // 128 for v in vectors]
    slab = sum(tall) + -sum(tall) % 8
    halves, kinds = heads // 2, 3
    arrays = kinds + 2
    offsets = sorted({2 * o for o in range(1, chips)} | {o for o in range(1, members)} | {o * members for o in range(1, heads)})

    def kernel(lengths_ref, order_ref, hidden_ref, upstream_ref, *refs):
        parts, refs = refs[: len(vectors)], refs[len(vectors) :]
        weight_refs, out_weight_ref = refs[:kinds], refs[kinds]
        normed, all_vectors, weights, all_out, shared, queries, branch, live = refs[kinds + 1 : kinds + 9]
        (vector_ref, raw, stage, gains, biases, line_send, line_recv, row_sem, own_sem, cross_send, cross_recv, core_send, core_recv,
         head_local, head_send, head_recv, pair_send, pair_recv) = refs[kinds + 9 :]
        dp, mp = lax.axis_index("dp"), lax.axis_index("mp")
        vector_ref[...] = jnp.zeros_like(vector_ref)
        first = 0
        for part, count in zip(parts, tall):
            for r in range(count):
                vector_ref[first + r : first + r + 1] = part[:, r * 128 : (r + 1) * 128].astype(jnp.float32)
            first += count
        group, member = dp // members, dp % members
        partner = (dp ^ 1, mp)
        greet_all([(dp ^ o, mp) for o in offsets], dp, mp, mp_count)
        line = LineGather(hidden_ref, raw, rows, pieces, line_send, line_recv, dp, mp, mp_count)

        def source(array):
            return (list(weight_refs) + [out_weight_ref, vector_ref])[array]

        def place(array, owner):
            if array < kinds:
                return weights.at[array, pl.ds(pl.multiple_of(owner * depth, depth), depth)]
            if array == kinds:
                return all_out.at[pl.ds(pl.multiple_of(owner * depth, depth), depth)]
            return all_vectors.at[pl.ds(pl.multiple_of(owner * slab, slab), slab)]

        def cross(array, o):
            return remote(source(array), place(array, dp), cross_send.at[array, o], cross_recv.at[array, o],
                          (dp ^ (2 * o), mp))

        def core(array, o):
            owner = dp ^ (2 * o)
            return remote(place(array, owner) if o else source(array), place(array, owner),
                          core_send.at[array, o], core_recv.at[array, o], partner)

        def own(array):
            return pltpu.make_async_copy(source(array), place(array, dp), own_sem.at[array])

        def block_span(block):
            return pl.ds(pl.multiple_of(block * rows, rows), rows)

        first_to_last = [kinds + 1] + list(range(kinds + 1))
        for array in first_to_last:
            for o in range(1, chips):
                cross(array, o).start()
            if array == first_to_last[0]:

                @pl.loop(0, pieces)
                def _(piece):
                    line.advance(0, piece)

        for block in range(rows // BLOCK):
            found = order_ref[(dp * group_rows + mp * rows) // BLOCK + block]
            valid = sequence_of(found, lengths_ref)[1]
            span = slice(block * BLOCK, (block + 1) * BLOCK)
            live[span] = (lax.broadcasted_iota(jnp.int32, (BLOCK, 128), 0) < valid).astype(jnp.float32)
            keep = lax.broadcasted_iota(jnp.int32, (BLOCK, width), 0) < valid
            branch[span] = jnp.where(keep, upstream_ref[span].astype(jnp.float32), 0.0).astype(branch.dtype)
        own_rows = pltpu.make_async_copy(hidden_ref, raw.at[block_span(mp)], row_sem)
        own_rows.start()
        for array in first_to_last:
            own(array).start()
            core(array, 0).start()

        def spread(array):
            for o in range(1, chips):
                cross(array, o).wait_recv()
                core(array, o).start()

        def settle(array):
            own(array).wait()
            for o in range(chips):
                core(array, o).wait_recv()

        def norm(block):
            chunk = 64

            @pl.loop(0, rows // chunk)
            def _(part):
                span = pl.ds(pl.multiple_of(block * rows + part * chunk, chunk), chunk)
                unit, _ = unit_rows(raw[span].astype(jnp.float32))
                normed[span] = (unit * gains[0:1] + gains[1:2]).astype(normed.dtype)

        def each_block(low, high, visit):
            @pl.loop(0, mp_count)
            def _(block):
                distance = jnp.abs(block - mp)

                @pl.when((distance >= low) & (distance <= high))
                def _():
                    visit(block)

        def rows_of(kind_ref, owner, block):
            return kind_ref.at[pl.ds(pl.multiple_of(owner * group_rows + block * rows, rows), rows)]

        def pass_on(kind, o, block, piece):
            giver = (group ^ o) * members + member
            return [remote(piece, rows_of(shared.at[kind], giver, block), pair_send.at[kind, o, block, p - 1],
                           pair_recv.at[kind, o, block, p - 1], (group * members + (member ^ p), mp))
                    for p in range(1, members)]

        def head_copy(kind, o, block, to_shared):
            target = group ^ o
            piece = stage.at[kind, block, target]
            landing = rows_of(shared.at[kind], dp, block) if to_shared else rows_of(queries, group, block)
            return remote(piece, landing, head_send.at[kind, o, block], head_recv.at[kind, o, block],
                          (target * members + member, mp))

        def local_copy(kind, block, to_shared):
            landing = rows_of(shared.at[kind], dp, block) if to_shared else rows_of(queries, group, block)
            return pltpu.make_async_copy(stage.at[kind, block, group], landing, head_local.at[kind, block])

        def project(tile, block):
            kind, half = tile // halves, tile % halves
            span = pl.ds(pl.multiple_of(half * 256, 256), 256)
            value = jnp.dot(normed[block_span(block)], weights[kind, :, span], preferred_element_type=jnp.float32)
            value = (value + biases[pl.ds(kind, 1), span]).astype(stage.dtype)
            for h in range(2):
                head = 2 * half + h
                stage[kind, block, head] = value[:, h * HEAD_DIM : (h + 1) * HEAD_DIM]
            for h in range(2):
                o = (2 * half + h) ^ group
                for to_shared in (True, False):
                    chosen = (kind < 2) if to_shared else (kind == 2)

                    @pl.when(chosen & (o != 0))
                    def _():
                        head_copy(kind, o, block, to_shared).start()

                    @pl.when(chosen & (o == 0))
                    def _():
                        local_copy(kind, block, to_shared).start()
                        if to_shared:
                            for copy in pass_on(kind, 0, block, stage.at[kind, block, group]):
                                copy.start()

        def hand_on(block):
            @pl.loop(0, 2)
            def _(kind):
                for o in range(1, heads):
                    head_copy(kind, o, block, True).wait_recv()
                    giver = (group ^ o) * members + member
                    for copy in pass_on(kind, o, block, rows_of(shared.at[kind], giver, block)):
                        copy.start()

        last = mp_count - 1
        for step in range(1, last):

            @pl.loop(0, pieces)
            def _(piece):
                line.advance(step, piece)

            if step == 1:
                spread(kinds + 1)
                settle(kinds + 1)
                for owner in range(dp_count):
                    for r in range(each):
                        at = pl.ds((owner * each + r) * 128, 128)
                        for k in range(2):
                            gains[k : k + 1, at] = all_vectors[owner * slab + k * each + r : owner * slab + k * each + r + 1]
                biases[...] = jnp.zeros_like(biases)
                for head in range(heads):
                    feature = mp * heads + head
                    first = (feature // each) * slab + feature % each
                    for kind, k in ((1, 3), (2, 2)):
                        biases[kind : kind + 1, head * 128 : (head + 1) * 128] = all_vectors[pl.ds(first + k * each, 1)]
                own_rows.wait()
                each_block(0, 1, norm)
            else:
                each_block(step, step, norm)
        for array in range(kinds + 1):
            spread(array)
        for array in range(kinds):
            settle(array)
        tiles = kinds * halves

        @pl.loop(0, pieces)
        def _(piece):
            line.advance(last - 1 if last == 1 else last, piece)

            @pl.when(piece < tiles)
            def _():
                each_block(0, last - 1, lambda block: project(piece, block))

        each_block(last, last, norm)

        @pl.loop(0, tiles)
        def _(tile):
            each_block(last, last, lambda block: project(tile, block))

        each_block(0, last - 1, hand_on)
        each_block(last, last, hand_on)
        line.finish()
        settle(kinds)
        for array in first_to_last:
            for o in range(chips):
                core(array, o).wait_send()
                if o:
                    cross(array, o).wait_send()

        @pl.loop(0, mp_count)
        def _(block):
            for kind in range(kinds):
                to_shared = kind < 2
                local_copy(kind, block, to_shared).wait()
                for o in range(1, heads):
                    head_copy(kind, o, block, to_shared).wait_send()
                    if not to_shared:
                        head_copy(kind, o, block, to_shared).wait_recv()
                if to_shared:
                    for o in range(heads):
                        giver = (group ^ o) * members + member
                        for copy in pass_on(kind, o, block, rows_of(shared.at[kind], giver, block)):
                            copy.wait()

    dma = pltpu.SemaphoreType.DMA
    bf16, f32 = jnp.bfloat16, jnp.float32
    return pl.pallas_call(
        kernel,
        out_shape=[
            jax.ShapeDtypeStruct((group_rows, width), bf16),
            jax.ShapeDtypeStruct((dp_count * slab, 128), f32),
            jax.ShapeDtypeStruct((kinds, width, columns), bf16),
            jax.ShapeDtypeStruct((width, columns), bf16),
            jax.ShapeDtypeStruct((2, dp_count * group_rows, HEAD_DIM), bf16),
            jax.ShapeDtypeStruct((heads * group_rows, HEAD_DIM), bf16),
            jax.ShapeDtypeStruct((rows, width), bf16),
            jax.ShapeDtypeStruct((rows, 128), f32),
        ],
        in_specs=[SMEM, SMEM, VMEM, VMEM] + [VMEM] * len(vectors) + [ANY] * (kinds + 1),
        out_specs=[VMEM, VMEM, VMEM, ANY, ANY, ANY, VMEM, VMEM],
        scratch_shapes=[
            pltpu.VMEM((slab, 128), f32),
            pltpu.VMEM((group_rows, width), bf16),
            pltpu.VMEM((kinds, mp_count, heads, rows, HEAD_DIM), bf16),
            pltpu.VMEM((8, width), f32),
            pltpu.VMEM((8, columns), f32),
        ]
        + LineGather.semaphores(mp_count, pieces)
        + [dma(()), dma((arrays,))]
        + [dma((arrays, chips)) for _ in range(4)]
        + [dma((kinds, mp_count)), dma((kinds, heads, mp_count)), dma((kinds, heads, mp_count))]
        + [dma((2, heads, mp_count, members)) for _ in range(2)],
        compiler_params=pltpu.CompilerParams(
            collective_id=collective_id, has_side_effects=True, vmem_limit_bytes=48 * MIB),
        cost_estimate=pl.CostEstimate(flops=8 << 30, bytes_accessed=250 * MIB, transcendentals=0),
    )(lengths, order, hidden, output_grad, *vectors, *projections, out_weight)


def reduce_norm_gather(part, hidden, out_bias, gain, shift, shards, collective_id):
    dp_count, mp_count = lax.axis_size("dp"), lax.axis_size("mp")
    chips, count = dp_count // 2, len(shards)
    rows, width = hidden.shape
    pieces = pieces_of(rows)
    size = rows // pieces

    turns = pieces + 2 * SKEW * (mp_count - 1)

    def kernel(part_ref, hidden_ref, bias_ref, gain_ref, shift_ref, *refs):
        shard_refs, (residual_ref, full_ref), whole_refs = refs[:count], refs[count : count + 2], refs[count + 2 : 2 * count + 2]
        total, normed, flows, red_send, red_recv, line_send, line_recv, own_sem, *weight_sems = refs[2 * count + 2 :]
        dp, mp = lax.axis_index("dp"), lax.axis_index("mp")
        greet_all([(dp ^ (2 * o), mp) for o in range(1, chips)] + [(dp ^ 1, mp)], dp, mp, mp_count)
        weights = ShardGather(shard_refs, whole_refs, shards[0].shape[0], *weight_sems, dp, mp, chips)
        weights.begin()
        reduce = LineReduce(part_ref, flows, rows, pieces, red_send, red_recv, dp, mp, mp_count)
        gather = LineGather(normed, full_ref, rows, pieces, line_send, line_recv, dp, mp, mp_count)
        for piece in range(AHEAD):
            reduce.begin(piece)

        @pl.loop(0, turns)
        def _(turn):
            for array in range(count):

                @pl.when(turn == turns - 1 - 6 * (count - 1 - array))
                def _():
                    weights.spread(array)

            reduce.begin(jnp.minimum(turn + AHEAD, pieces - 1), turn + AHEAD < pieces)
            reduce.advance(turn)
            done = turn - SKEW * (mp_count - 1)

            @pl.when((done >= 0) & (done < pieces))
            def _():
                reduce.arrive(done)
                reduce.total(done, total)
                span = pl.ds(pl.multiple_of(done * size, size), size)
                residual = hidden_ref[span].astype(jnp.float32) + total[...] + bias_ref[...]
                residual_ref[span] = residual
                unit, _ = unit_rows(residual)
                normed[span] = (unit * gain_ref[...] + shift_ref[...]).astype(normed.dtype)
                gather.advance(0, done)

            for step in range(1, mp_count):
                late = done - SKEW * step
                gather.advance(step, jnp.clip(late, 0, pieces - 1), (late >= 0) & (late < pieces))

        own = pltpu.make_async_copy(normed, full_ref.at[pl.ds(pl.multiple_of(mp * rows, rows), rows)], own_sem)
        own.start()
        reduce.finish()
        gather.finish()
        own.wait()
        weights.finish()

    return pl.pallas_call(
        kernel,
        out_shape=[
            jax.ShapeDtypeStruct((rows, width), jnp.float32),
            jax.ShapeDtypeStruct((mp_count * rows, width), jnp.bfloat16),
        ]
        + [jax.ShapeDtypeStruct((dp_count * a.shape[0], a.shape[1]), a.dtype) for a in shards],
        in_specs=[VMEM] * 5 + [ANY] * count,
        out_specs=[VMEM, ANY] + [ANY] * count,
        scratch_shapes=[pltpu.VMEM((size, width), jnp.float32), pltpu.VMEM((rows, width), jnp.bfloat16)]
        + LineReduce.scratch(mp_count, rows, width, pieces) + LineGather.semaphores(mp_count, pieces)
        + [pltpu.SemaphoreType.DMA(())] + ShardGather.semaphores(count, chips),
        compiler_params=pltpu.CompilerParams(
            collective_id=collective_id, has_side_effects=True, vmem_limit_bytes=48 * MIB),
        cost_estimate=pl.CostEstimate(flops=0, bytes_accessed=300 * MIB, transcendentals=0),
    )(part, hidden, out_bias, gain, shift, *shards)


def reduce_back_gather(part, residual, branch_two, gain, collective_id):
    mp_count = lax.axis_size("mp")
    rows, width = residual.shape
    pieces = pieces_of(rows)
    size = rows // pieces

    def kernel(part_ref, residual_ref, branch_ref, gain_ref, grad_ref, sums_ref, full_ref,
               total, low, flows, red_send, red_recv, line_send, line_recv, own_sem):
        dp, mp = lax.axis_index("dp"), lax.axis_index("mp")
        greet_all([], dp, mp, mp_count)
        reduce = LineReduce(part_ref, flows, rows, pieces, red_send, red_recv, dp, mp, mp_count)
        gather = LineGather(low, full_ref, rows, pieces, line_send, line_recv, dp, mp, mp_count)
        for piece in range(AHEAD):
            reduce.begin(piece)
        sums_ref[...] = jnp.zeros_like(sums_ref)

        @pl.loop(0, pieces + 2 * SKEW * (mp_count - 1))
        def _(turn):
            reduce.begin(jnp.minimum(turn + AHEAD, pieces - 1), turn + AHEAD < pieces)
            reduce.advance(turn)
            done = turn - SKEW * (mp_count - 1)

            @pl.when((done >= 0) & (done < pieces))
            def _():
                reduce.arrive(done)
                reduce.total(done, total)
                span = pl.ds(pl.multiple_of(done * size, size), size)
                unit, inverse = unit_rows(residual_ref[span])
                upstream = total[...]
                sums_ref[0:1] += jnp.sum(upstream * unit, axis=0, keepdims=True)
                sums_ref[1:2] += jnp.sum(upstream, axis=0, keepdims=True)
                grad = branch_ref[span].astype(jnp.float32) + norm_back(upstream, unit, inverse, gain_ref[...])
                grad_ref[span] = grad
                rounded = grad.astype(low.dtype)
                low[span] = rounded
                sums_ref[2:3] += jnp.sum(rounded.astype(jnp.float32), axis=0, keepdims=True)
                gather.advance(0, done)

            for step in range(1, mp_count):
                late = done - SKEW * step
                gather.advance(step, jnp.clip(late, 0, pieces - 1), (late >= 0) & (late < pieces))

        own = pltpu.make_async_copy(low, full_ref.at[pl.ds(pl.multiple_of(mp * rows, rows), rows)], own_sem)
        own.start()
        reduce.finish()
        gather.finish()
        own.wait()

    return pl.pallas_call(
        kernel,
        out_shape=[
            jax.ShapeDtypeStruct((rows, width), jnp.float32),
            jax.ShapeDtypeStruct((8, width), jnp.float32),
            jax.ShapeDtypeStruct((mp_count * rows, width), jnp.bfloat16),
        ],
        in_specs=[VMEM] * 4,
        out_specs=[VMEM, VMEM, ANY],
        scratch_shapes=[pltpu.VMEM((size, width), jnp.float32), pltpu.VMEM((rows, width), jnp.bfloat16)]
        + LineReduce.scratch(mp_count, rows, width, pieces) + LineGather.semaphores(mp_count, pieces)
        + [pltpu.SemaphoreType.DMA(())],
        compiler_params=pltpu.CompilerParams(
            collective_id=collective_id, has_side_effects=True, vmem_limit_bytes=48 * MIB),
        cost_estimate=pl.CostEstimate(flops=0, bytes_accessed=300 * MIB, transcendentals=0),
    )(part, residual, branch_two, gain)


def reduce_last(part, residual_grad, hidden, gain, weight_parts, collective_id):
    dp_count, mp_count = lax.axis_size("dp"), lax.axis_size("mp")
    chips = dp_count // 2
    rows, width = hidden.shape
    pieces = pieces_of(rows)
    size = rows // pieces
    count = len(weight_parts)
    depth, columns = weight_parts[0].shape[0] // dp_count, weight_parts[0].shape[1]

    def kernel(*refs):
        part_ref, residual_ref, hidden_ref, gain_ref = refs[:4]
        weights = refs[4 : 4 + count]
        grad_ref, sums_ref = refs[4 + count : 6 + count]
        outs = refs[6 + count : 6 + 2 * count]
        (total, flows, red_send, red_recv, from_partner, chip_sum, from_chips,
         pair_send, pair_recv, send_sem, recv_sem) = refs[6 + 2 * count :]
        dp, mp = lax.axis_index("dp"), lax.axis_index("mp")
        peers = [(dp ^ (2 * o), mp) for o in range(1, chips)]
        partner = (dp ^ 1, mp)
        greet_all(peers + [partner], dp, mp, mp_count)
        reduce = LineReduce(part_ref, flows, rows, pieces, red_send, red_recv, dp, mp, mp_count)
        for piece in range(AHEAD):
            reduce.begin(piece)

        def piece_of(weight, owner):
            return weights[weight].at[pl.ds(pl.multiple_of(owner * depth, depth), depth)]

        def pair(weight, o):
            return remote(piece_of(weight, dp ^ (2 * o) ^ 1), from_partner.at[weight, o],
                          pair_send.at[weight, o], pair_recv.at[weight, o], partner)

        def cross(weight, o):
            return remote(chip_sum.at[weight, o], from_chips.at[weight, o - 1],
                          send_sem.at[weight, o], recv_sem.at[weight, o], peers[o - 1])

        order = list(range(1, chips)) + [0]
        for w in range(count):
            for o in order:
                pair(w, o).start()
        for w in range(count):
            for o in order:
                pair(w, o).wait_recv()
                value = piece_of(w, dp ^ (2 * o))[...].astype(jnp.float32)
                value = value + from_partner[w, o].astype(jnp.float32)
                if o:
                    chip_sum[w, o] = value.astype(chip_sum.dtype)
                    cross(w, o).start()
                else:
                    outs[w][...] = value
        sums_ref[...] = jnp.zeros_like(sums_ref)

        @pl.loop(0, pieces + SKEW * (mp_count - 1))
        def _(turn):
            reduce.begin(jnp.minimum(turn + AHEAD, pieces - 1), turn + AHEAD < pieces)
            reduce.advance(turn)
            done = turn - SKEW * (mp_count - 1)

            @pl.when(done >= 0)
            def _():
                reduce.arrive(done)
                reduce.total(done, total)
                span = pl.ds(pl.multiple_of(done * size, size), size)
                unit, inverse = unit_rows(hidden_ref[span].astype(jnp.float32))
                upstream = total[...]
                sums_ref[0:1] += jnp.sum(upstream * unit, axis=0, keepdims=True)
                sums_ref[1:2] += jnp.sum(upstream, axis=0, keepdims=True)
                grad_ref[span] = residual_ref[span] + norm_back(upstream, unit, inverse, gain_ref[...])

        reduce.finish()
        for w in range(count):
            for o in range(1, chips):
                cross(w, o).wait()
                outs[w][...] += from_chips[w, o - 1].astype(jnp.float32)
            for o in range(chips):
                pair(w, o).wait_send()

    dma = pltpu.SemaphoreType.DMA
    kind = weight_parts[0].dtype
    return pl.pallas_call(
        kernel,
        out_shape=[jax.ShapeDtypeStruct((rows, width), jnp.float32), jax.ShapeDtypeStruct((8, width), jnp.float32)]
        + [jax.ShapeDtypeStruct((depth, columns), jnp.float32)] * count,
        in_specs=[VMEM] * (4 + count),
        out_specs=[VMEM] * (2 + count),
        scratch_shapes=[pltpu.VMEM((size, width), jnp.float32)]
        + LineReduce.scratch(mp_count, rows, width, pieces)
        + [pltpu.VMEM((count, chips, depth, columns), kind), pltpu.VMEM((count, chips, depth, columns), kind),
           pltpu.VMEM((count, chips - 1, depth, columns), kind)]
        + [dma((count, chips)) for _ in range(4)],
        compiler_params=pltpu.CompilerParams(
            collective_id=collective_id, has_side_effects=True, vmem_limit_bytes=60 * MIB),
        cost_estimate=pl.CostEstimate(flops=0, bytes_accessed=300 * MIB, transcendentals=0),
    )(part, residual_grad, hidden, gain, *weight_parts)


def sum_vectors(packed, collective_id):
    dp_count, mp_count = lax.axis_size("dp"), lax.axis_size("mp")
    depth, width = packed.shape[1:]

    def kernel(in_ref, out_ref, landed, mine, others, send_sem, recv_sem, line_send, line_recv):
        dp, mp = lax.axis_index("dp"), lax.axis_index("mp")
        peers = [(dp ^ o, mp) for o in range(1, dp_count)]
        along = [(dp, mp ^ o) for o in range(1, mp_count)]
        greet(peers + along)
        copies = []
        for o in range(1, dp_count):
            copies.append(remote(in_ref.at[dp ^ o], landed.at[o - 1], send_sem.at[o], recv_sem.at[o], peers[o - 1]))
            copies[-1].start()
        value = in_ref[dp]
        for o in range(1, dp_count):
            copies[o - 1].wait()
            value = value + landed[o - 1]
        mine[...] = value
        others[mp] = value
        copies = []
        for o in range(1, mp_count):
            copies.append(remote(mine, others.at[mp], line_send.at[o], line_recv.at[o], along[o - 1]))
            copies[-1].start()
        for copy in copies:
            copy.wait()
        value = others[0]
        for index in range(1, mp_count):
            value = value + others[index]
        out_ref[...] = value

    dma = pltpu.SemaphoreType.DMA
    return pl.pallas_call(
        kernel,
        out_shape=jax.ShapeDtypeStruct((depth, width), jnp.float32),
        in_specs=[VMEM],
        out_specs=VMEM,
        scratch_shapes=[
            pltpu.VMEM((dp_count - 1, depth, width), jnp.float32), pltpu.VMEM((depth, width), jnp.float32),
            pltpu.VMEM((mp_count, depth, width), jnp.float32),
            dma((dp_count,)), dma((dp_count,)), dma((mp_count,)), dma((mp_count,)),
        ],
        compiler_params=pltpu.CompilerParams(collective_id=collective_id, has_side_effects=True),
        cost_estimate=pl.CostEstimate(flops=0, bytes_accessed=20 * MIB, transcendentals=0),
    )(packed)


def per_device(
    hidden_in,
    output_grad,
    first_gain,
    first_shift,
    query_weight,
    query_bias,
    key_weight,
    value_weight,
    value_bias,
    out_weight,
    out_bias,
    second_gain,
    second_shift,
    up_weight,
    up_bias,
    down_weight,
    down_bias,
    seq_lengths,
    block_order,
    block_slot,
):
    local_rows, model_width = hidden_in.shape
    mp_count, dp_count = lax.axis_size("mp"), lax.axis_size("dp")
    mp_index, dp_index = lax.axis_index("mp"), lax.axis_index("dp")
    group_rows = local_rows * mp_count
    head_width = query_weight.shape[1]
    heads_local = head_width // HEAD_DIM
    hidden_width = up_weight.shape[1]
    members = dp_count // heads_local
    blocks_each = group_rows // BLOCK
    plan = (seq_lengths, block_order, block_slot)

    vectors = (first_gain, first_shift, query_bias, value_bias, out_bias, second_gain, second_shift, down_bias, up_bias)
    rows_one, vector_rows, projections, out_all, head_shared, head_queries, branch_two, live = project_first(
        hidden_in, output_grad, seq_lengths, block_order, [v.reshape(1, -1) for v in vectors],
        (key_weight, value_weight, query_weight), out_weight, heads_local, members, 0,
    )
    own_valid = live[:, :1] > 0
    key_all, value_all, query_all = projections
    vector_rows = vector_rows.reshape(dp_count, -1, 128)
    each = model_width // dp_count // 128
    gain_one, _, _, _, bias_out, gain_two, shift_two, bias_down = (
        vector_rows[:, k * each : (k + 1) * each].reshape(1, model_width) for k in range(8)
    )
    up_each = up_bias.shape[0] // 128
    bias_up = vector_rows[:, 8 * each : 8 * each + up_each].reshape(1, up_bias.shape[0] * dp_count)

    branch_rows_two = whole_rows(branch_two)
    head_mix, exact_mix, log_total = attend(head_queries, head_shared, *plan, members, blocks_each)
    (attended_low,) = to_rows([head_mix], [], heads_local, members, 2)
    out_part = contract_last(attended_low, out_all).astype(jnp.bfloat16)
    residual, rows_two, up_all, down_all = reduce_norm_gather(
        out_part, hidden_in, bias_out, gain_two, shift_two, (up_weight, down_weight), 3
    )

    bias_hidden = lax.dynamic_slice_in_dim(bias_up, mp_index * hidden_width, hidden_width, 1)
    pre_act = jnp.dot(rows_two, up_all, preferred_element_type=jnp.float32) + bias_hidden
    hidden_low = gelu_exact(pre_act).astype(jnp.bfloat16)
    hidden_grad = jnp.dot(branch_rows_two, down_all, preferred_element_type=jnp.float32)
    pre_grad = jax.vjp(gelu_exact, pre_act)[1](hidden_grad)[0].astype(jnp.bfloat16)
    up_part = contract_last(pre_grad, up_all).astype(jnp.bfloat16)
    down_weight_grad = owner_share(contract_first(branch_rows_two, hidden_low))
    up_weight_grad = owner_share(contract_first(rows_two, pre_grad))
    residual_grad, sums_two, branch_rows_one = reduce_back_gather(up_part, residual, branch_two, gain_two, 4)

    hidden_low, branch_rows_one = lax.optimization_barrier((hidden_low, branch_rows_one))
    feed = row_share(contract_last(hidden_low, down_all))
    result = residual + feed + bias_down
    output = jnp.where(own_valid, result, 0.0).astype(jnp.bfloat16)

    attended_grad = jnp.dot(branch_rows_one, out_all, preferred_element_type=jnp.float32).astype(jnp.bfloat16)
    (head_grad,) = to_heads([attended_grad], [], heads_local, members, 5)
    head_query_grad, head_key_grad, head_value_grad = attend_back(
        head_queries, head_shared, head_grad, exact_mix, log_total, *plan, members, blocks_each
    )
    query_low, key_low, value_low = to_rows(
        [head_query_grad], [head_key_grad, head_value_grad], heads_local, members, 6
    )
    last_part = contract_last(query_low, query_all)
    last_part = last_part + contract_last(key_low, key_all)
    last_part = (last_part + contract_last(value_low, value_all)).astype(jnp.bfloat16)
    weight_parts = [
        contract_first(left, right).astype(jnp.bfloat16)
        for left, right in (
            (rows_one, query_low), (rows_one, key_low), (rows_one, value_low), (branch_rows_one, attended_low)
        )
    ]
    input_grad, sums_one, query_weight_grad, key_weight_grad, value_weight_grad, out_weight_grad = reduce_last(
        last_part, residual_grad, hidden_in, gain_one, weight_parts, 7
    )

    def column_sums(values):
        return jnp.sum(values.astype(jnp.float32), axis=0)

    def placed(values):
        whole = jnp.zeros((values.shape[0] * mp_count,), jnp.float32)
        return lax.dynamic_update_slice_in_dim(whole, values, mp_index * values.shape[0], 0)

    sums = (
        sums_one[0], sums_one[1], placed(column_sums(query_low)), placed(column_sums(value_low)), sums_two[2],
        sums_two[0], sums_two[1], column_sums(branch_two), placed(column_sums(pre_grad)),
    )
    packed = jnp.concatenate([v.reshape(dp_count, -1, 128) for v in sums], axis=1)
    packed = jnp.pad(packed, ((0, 0), (0, -packed.shape[1] % 8), (0, 0)))
    summed = sum_vectors(packed, 8)
    vector_grads = [summed[k * each : (k + 1) * each].reshape(-1) for k in range(8)]
    up_bias_grad = summed[8 * each : 8 * each + up_each].reshape(-1)
    return (
        output,
        input_grad,
        vector_grads[0],
        vector_grads[1],
        query_weight_grad,
        vector_grads[2],
        key_weight_grad,
        value_weight_grad,
        vector_grads[3],
        out_weight_grad,
        vector_grads[4],
        vector_grads[5],
        vector_grads[6],
        up_weight_grad,
        up_bias_grad,
        down_weight_grad,
        vector_grads[7],
    )


def solution(mesh):
    return jax.shard_map(
        per_device,
        mesh=mesh,
        in_specs=(
            P(("dp", "mp"), None),
            P(("dp", "mp"), None),
            P("dp"),
            P("dp"),
            P("dp", "mp"),
            P("dp"),
            P("dp", "mp"),
            P("dp", "mp"),
            P("dp"),
            P("dp", "mp"),
            P("dp"),
            P("dp"),
            P("dp"),
            P("dp", "mp"),
            P("dp"),
            P("dp", "mp"),
            P("dp"),
            P(),
            P(),
            P(),
        ),
        out_specs=(
            P(("dp", "mp"), None),
            P(("dp", "mp"), None),
            P("dp"),
            P("dp"),
            P("dp", "mp"),
            P("dp"),
            P("dp", "mp"),
            P("dp", "mp"),
            P("dp"),
            P("dp", "mp"),
            P("dp"),
            P("dp"),
            P("dp"),
            P("dp", "mp"),
            P("dp"),
            P("dp", "mp"),
            P("dp"),
        ),
        check_vma=False,
    )
```

```python
import math

import jax
import jax.numpy as jnp
from jax import lax
from jax.experimental import pallas as pl
from jax.experimental.pallas import tpu as pltpu
from jax.sharding import PartitionSpec as P

HEAD_DIM = 128
BLOCK = 128
KEY_BLOCKS = 8
MESH = pl.DeviceIdType.MESH
ANY = pl.BlockSpec(memory_space=pl.ANY)
VMEM = pl.BlockSpec(memory_space=pltpu.VMEM)
SMEM = pl.BlockSpec(memory_space=pltpu.SMEM)
MIB = 1 << 20


big_negative = -1e30
norm_epsilon = 1e-05


def norm_back(upstream, normed, inverse, gain_row):
    scaled = upstream * gain_row
    mean_grad = jnp.mean(scaled, axis=-1, keepdims=True)
    second = jnp.mean(scaled * normed, axis=-1, keepdims=True)
    return inverse * (scaled - mean_grad - normed * second)


def gelu_exact(values):
    return jax.nn.gelu(values, approximate=False)


def contract_last(left, right):
    return lax.dot_general(
        left, right, (((1,), (1,)), ((), ())), preferred_element_type=jnp.float32
    )


def contract_first(left, right):
    return lax.dot_general(
        left, right, (((0,), (0,)), ((), ())), preferred_element_type=jnp.float32
    )


def whole_rows(local_part):
    return lax.all_gather(local_part, "mp", axis=0, tiled=True)


def row_share(term):
    term = term.astype(jnp.bfloat16)
    return lax.psum_scatter(term, "mp", scatter_dimension=0, tiled=True).astype(jnp.float32)


def greet(peers):
    barrier = pltpu.get_barrier_semaphore()
    for peer in peers:
        pl.semaphore_signal(barrier, inc=1, device_id=peer, device_id_type=MESH)
    pl.semaphore_wait(barrier, len(peers))


def remote(src, dst, send_sem, recv_sem, peer):
    return pltpu.make_async_remote_copy(
        src_ref=src, dst_ref=dst, send_sem=send_sem, recv_sem=recv_sem,
        device_id=peer, device_id_type=MESH,
    )


def head_place(heads, members):
    me = lax.axis_index("dp")
    return me, me // members, me % members, lax.axis_index("mp")


def lanes(head):
    return pl.ds(pl.multiple_of(head * HEAD_DIM, HEAD_DIM), HEAD_DIM)


def to_heads(owned, shared, heads, members, collective_id):
    rows = (owned + shared)[0].shape[0]
    n_owned, n_shared = len(owned), len(shared)
    count = n_owned + n_shared

    def kernel(*refs):
        ins, outs = refs[:count], refs[count : 2 * count]
        local_sem, send_sem, recv_sem, fwd_send, fwd_recv = refs[2 * count :]
        me, group, member, mp = head_place(heads, members)

        def dest(array, source):
            place = (source // members) if array < n_owned else source
            return outs[array].at[pl.ds(pl.multiple_of(place * rows, rows), rows)]

        head_peers = [((group ^ o) * members + member, mp) for o in range(1, heads)]
        pair_peers = [(group * members + (member ^ o), mp) for o in range(1, members)]
        greet(head_peers + pair_peers)
        order = list(range(n_owned, count)) + list(range(n_owned))
        sends, locals_, forwards = {}, [], []
        for a in order:
            for o in range(1, heads):
                copy = remote(ins[a].at[:, lanes(group ^ o)], dest(a, me), send_sem.at[a, o],
                              recv_sem.at[a, o], head_peers[o - 1])
                copy.start()
                sends[a, o] = copy
        for a in range(count):
            copy = pltpu.make_async_copy(ins[a].at[:, lanes(group)], dest(a, me), local_sem.at[a])
            copy.start()
            locals_.append(copy)
        for a in range(n_owned, count):
            for o in range(heads):
                source = (group ^ o) * members + member
                if o:
                    sends[a, o].wait_recv()
                for p in range(1, members):
                    piece = ins[a].at[:, lanes(group)] if o == 0 else dest(a, source)
                    copy = remote(piece, dest(a, source), fwd_send.at[a - n_owned, o, p],
                                  fwd_recv.at[a - n_owned, o, p], pair_peers[p - 1])
                    copy.start()
                    forwards.append(copy)
        for copy in locals_:
            copy.wait()
        for (a, o), copy in sends.items():
            copy.wait_send()
            if a < n_owned:
                copy.wait_recv()
        for copy in forwards:
            copy.wait()

    total = rows * lax.axis_size("dp")
    shapes = [jax.ShapeDtypeStruct((heads * rows, HEAD_DIM), a.dtype) for a in owned]
    shapes += [jax.ShapeDtypeStruct((total, HEAD_DIM), a.dtype) for a in shared]
    dma = pltpu.SemaphoreType.DMA
    return pl.pallas_call(
        kernel,
        out_shape=shapes,
        in_specs=[ANY] * count,
        out_specs=[ANY] * count,
        scratch_shapes=[
            dma((count,)), dma((count, heads)), dma((count, heads)),
            dma((max(n_shared, 1), heads, members)), dma((max(n_shared, 1), heads, members)),
        ],
        compiler_params=pltpu.CompilerParams(collective_id=collective_id, has_side_effects=True),
        cost_estimate=pl.CostEstimate(flops=0, bytes_accessed=100 * MIB, transcendentals=0),
    )(*owned, *shared)


def to_rows(owned, shared, heads, members, collective_id):
    rows = owned[0].shape[0] // heads
    n_owned, n_shared = len(owned), len(shared)
    count = n_owned + n_shared

    def kernel(*refs):
        ins, outs = refs[:count], refs[count : 2 * count]
        local_sem, send_sem, recv_sem, own_sem, part_send, part_recv = refs[2 * count : 2 * count + 6]
        me, group, member, mp = head_place(heads, members)
        head_peers = [((group ^ o) * members + member, mp) for o in range(1, heads)]
        pair_peers = [(group * members + (member ^ o), mp) for o in range(1, members)]
        greet(head_peers + pair_peers)
        if n_shared:
            own, parts, total = refs[2 * count + 6 :]
        copies, pending = [], {}

        def part(array, o, who):
            first = pl.multiple_of(((group ^ o) * members + who) * rows, rows)
            return ins[array].at[pl.ds(first, rows)]

        for s in range(n_shared):
            for o in range(heads):
                copy = pltpu.make_async_copy(part(n_owned + s, o, member), own.at[s, o], own_sem.at[s, o])
                copy.start()
                pending[s, o, 0] = copy
                for p in range(1, members):
                    copy = remote(part(n_owned + s, o, member ^ p), parts.at[s, o, p - 1],
                                  part_send.at[s, o, p], part_recv.at[s, o, p], pair_peers[p - 1])
                    copy.start()
                    pending[s, o, p] = copy
        for a in range(n_owned):
            for o in range(heads):
                piece = ins[a].at[pl.ds(pl.multiple_of((group ^ o) * rows, rows), rows)]
                place = outs[a].at[:, lanes(group)]
                if o:
                    copy = remote(piece, place, send_sem.at[a, o], recv_sem.at[a, o], head_peers[o - 1])
                else:
                    copy = pltpu.make_async_copy(piece, place, local_sem.at[a])
                copy.start()
                copies.append(copy)
        for o in list(range(1, heads)) + [0]:
            for s in range(n_shared):
                for p in range(members):
                    if p:
                        pending[s, o, p].wait_recv()
                    else:
                        pending[s, o, p].wait()
                value = own[s, o].astype(jnp.float32)
                for p in range(1, members):
                    value = value + parts[s, o, p - 1].astype(jnp.float32)
                total[s, o] = value.astype(total.dtype)
                a = n_owned + s
                place = outs[a].at[:, lanes(group)]
                if o:
                    copy = remote(total.at[s, o], place, send_sem.at[a, o], recv_sem.at[a, o], head_peers[o - 1])
                else:
                    copy = pltpu.make_async_copy(total.at[s, o], place, local_sem.at[a])
                copy.start()
                copies.append(copy)
        for s in range(n_shared):
            for o in range(heads):
                for p in range(1, members):
                    pending[s, o, p].wait_send()
        for copy in copies:
            copy.wait()

    dma = pltpu.SemaphoreType.DMA
    slots = max(n_shared, 1)
    scratch = [
        dma((count,)), dma((count, heads)), dma((count, heads)),
        dma((slots, heads)), dma((slots, heads, members)), dma((slots, heads, members)),
    ]
    if n_shared:
        kind = shared[0].dtype
        scratch += [
            pltpu.VMEM((n_shared, heads, rows, HEAD_DIM), kind),
            pltpu.VMEM((n_shared, heads, members - 1, rows, HEAD_DIM), kind),
            pltpu.VMEM((n_shared, heads, rows, HEAD_DIM), kind),
        ]
    return pl.pallas_call(
        kernel,
        out_shape=[jax.ShapeDtypeStruct((rows, heads * HEAD_DIM), a.dtype) for a in owned + shared],
        in_specs=[ANY] * count,
        out_specs=[ANY] * count,
        scratch_shapes=scratch,
        compiler_params=pltpu.CompilerParams(
            collective_id=collective_id, has_side_effects=True, vmem_limit_bytes=48 * MIB
        ),
        cost_estimate=pl.CostEstimate(flops=0, bytes_accessed=100 * MIB, transcendentals=0),
    )(*owned, *shared)


def sequence_of(place, lengths):
    first, length, running = jnp.int32(0), jnp.int32(0), jnp.int32(0)
    for s in range(lengths.shape[0]):
        inside = place >= running
        first = jnp.where(inside, running, first)
        length = jnp.where(inside, lengths[s], length)
        running = running + (lengths[s] + (BLOCK - 1)) // BLOCK
    return first, length - (place - first) * BLOCK


def list_queries(slot, index_list, place_list, members, blocks_each):
    member = lax.axis_index("dp") % members

    def visit(block, count):
        dealt = slot[block]
        owner = dealt // blocks_each

        @pl.when(owner % members == member)
        def _():
            index_list[count] = (owner // members) * blocks_each + dealt % blocks_each
            place_list[count] = block

        return count + (owner % members == member).astype(jnp.int32)

    lax.fori_loop(0, slot.shape[0], visit, jnp.int32(0))


def block_rows(block):
    return pl.ds(pl.multiple_of(block * BLOCK, BLOCK), BLOCK)


class QueryPair:
    def __init__(self, pair, lengths, index_list, place_list):
        self.index = [index_list[2 * pair + i] for i in range(2)]
        self.place = [place_list[2 * pair + i] for i in range(2)]
        found = [sequence_of(place, lengths) for place in self.place]
        self.start = found[0][0]
        lane = lax.broadcasted_iota(jnp.int32, (1, 2 * BLOCK), 1)
        right = lane >= BLOCK

        def lanes_of(left_value, right_value):
            return jnp.where(right, right_value, left_value)

        within = lane - lanes_of(0, BLOCK)
        base = self.start * BLOCK
        self.position = lanes_of(self.place[0], self.place[1]) * BLOCK + within - base
        self.lowest = lanes_of(found[0][0], found[1][0]) * BLOCK - base
        self.live = within < lanes_of(found[0][1], found[1][1])
        self.tiles = (self.place[1] - self.start) // KEY_BLOCKS + 1
        self.open_tiles = jnp.where(found[0][0] == found[1][0], (self.place[0] - self.start) // KEY_BLOCKS, 0)

    def row(self, tile):
        return pl.multiple_of((self.start + tile * KEY_BLOCKS) * BLOCK, BLOCK)

    def allowed(self, tile):
        width = KEY_BLOCKS * BLOCK
        key = lax.broadcasted_iota(jnp.int32, (width, 2 * BLOCK), 0)
        return (key <= self.position - tile * width) & (key >= self.lowest - tile * width)

    def load_t(self, ref):
        return jnp.concatenate([ref[block_rows(index)].T for index in self.index], axis=1)

    def load(self, ref):
        return jnp.concatenate([ref[block_rows(index)] for index in self.index], axis=0)

    def store_t(self, ref, value_t):
        for i, index in enumerate(self.index):
            ref[block_rows(index)] = value_t[:, i * BLOCK : (i + 1) * BLOCK].T.astype(ref.dtype)


def attend(queries, shared, lengths, order, slot, members, blocks_each):
    pairs, key_count = queries.shape[0] // (2 * BLOCK), shared.shape[1] // BLOCK
    width = KEY_BLOCKS * BLOCK
    padded = (key_count + KEY_BLOCKS - 1) * BLOCK
    scale = math.log2(math.e) / math.sqrt(HEAD_DIM)

    def kernel(lengths_ref, slot_ref, q_ref, shared_ref, out_ref, exact_ref, log_ref,
               index_list, place_list, keys, values_t):
        list_queries(slot_ref, index_list, place_list, members, blocks_each)

        @pl.loop(0, key_count)
        def _(block):
            source = block_rows(slot_ref[block])
            keys[block_rows(block)] = shared_ref[0, source]
            values_t[:, block_rows(block)] = shared_ref[1, source].T

        tail = pl.ds(key_count * BLOCK, padded - key_count * BLOCK)
        keys[tail] = jnp.zeros((padded - key_count * BLOCK, HEAD_DIM), keys.dtype)
        values_t[:, tail] = jnp.zeros((HEAD_DIM, padded - key_count * BLOCK), keys.dtype)

        @pl.loop(0, pairs)
        def _(index):
            pair = QueryPair(index, lengths_ref, index_list, place_list)
            query_t = pair.load_t(q_ref)

            def step(tile, carry, masked):
                top, total, mix = carry
                span = pl.ds(pair.row(tile), width)
                scores = jnp.dot(keys[span], query_t, preferred_element_type=jnp.float32)
                if masked:
                    scores = jnp.where(pair.allowed(tile), scores, big_negative)
                new_top = jnp.maximum(top, jnp.max(scores, axis=0, keepdims=True))
                weights = jnp.exp2((scores - new_top) * scale)
                fade = jnp.exp2((top - new_top) * scale)
                total = total * fade + jnp.sum(weights, axis=0, keepdims=True)
                mix = mix * fade + jnp.dot(
                    values_t[:, span], weights.astype(jnp.bfloat16), preferred_element_type=jnp.float32)
                return new_top, total, mix

            carry = (jnp.full((1, 2 * BLOCK), big_negative, jnp.float32), jnp.zeros((1, 2 * BLOCK), jnp.float32),
                     jnp.zeros((HEAD_DIM, 2 * BLOCK), jnp.float32))
            carry = lax.fori_loop(0, pair.open_tiles, lambda tile, c: step(tile, c, False), carry)
            top, total, mix = lax.fori_loop(pair.open_tiles, pair.tiles, lambda tile, c: step(tile, c, True), carry)
            mix = jnp.where(pair.live, mix / total, 0.0)
            exact_ref[index] = mix
            pair.store_t(out_ref, mix)
            log_ref[index] = jnp.where(pair.live, top * scale + jnp.log2(total), -big_negative)

    return pl.pallas_call(
        kernel,
        out_shape=[
            jax.ShapeDtypeStruct(queries.shape, jnp.bfloat16),
            jax.ShapeDtypeStruct((pairs, HEAD_DIM, 2 * BLOCK), jnp.float32),
            jax.ShapeDtypeStruct((pairs, 1, 2 * BLOCK), jnp.float32),
        ],
        in_specs=[SMEM] * 2 + [VMEM] * 2,
        out_specs=[VMEM] * 3,
        scratch_shapes=[
            pltpu.SMEM((2 * pairs,), jnp.int32), pltpu.SMEM((2 * pairs,), jnp.int32),
            pltpu.VMEM((padded, HEAD_DIM), jnp.bfloat16), pltpu.VMEM((HEAD_DIM, padded), jnp.bfloat16),
        ],
        compiler_params=pltpu.CompilerParams(vmem_limit_bytes=56 * MIB),
        cost_estimate=pl.CostEstimate(flops=8 << 30, bytes_accessed=50 * MIB, transcendentals=8 << 20),
    )(lengths, slot, queries, shared)


def attend_back(queries, shared, upstream, exact, logs, lengths, order, slot, members, blocks_each):
    pairs, key_count = queries.shape[0] // (2 * BLOCK), shared.shape[1] // BLOCK
    width = KEY_BLOCKS * BLOCK
    padded = (key_count + KEY_BLOCKS - 1) * BLOCK
    scale = math.log2(math.e) / math.sqrt(HEAD_DIM)
    plain_scale = 1.0 / math.sqrt(HEAD_DIM)

    def kernel(lengths_ref, slot_ref, q_ref, shared_ref, g_ref, exact_ref, log_ref, dq_ref, dk_ref, dv_ref,
               index_list, place_list, keys, keys_t, values, key_sum, value_sum):
        list_queries(slot_ref, index_list, place_list, members, blocks_each)

        @pl.loop(0, key_count)
        def _(block):
            source, to = block_rows(slot_ref[block]), block_rows(block)
            rows = shared_ref[0, source]
            keys[to] = rows
            keys_t[:, to] = rows.T
            values[to] = shared_ref[1, source]
            key_sum[to] = jnp.zeros((BLOCK, HEAD_DIM), jnp.float32)
            value_sum[to] = jnp.zeros((BLOCK, HEAD_DIM), jnp.float32)

        tail = pl.ds(key_count * BLOCK, padded - key_count * BLOCK)
        keys[tail] = jnp.zeros((padded - key_count * BLOCK, HEAD_DIM), keys.dtype)
        values[tail] = jnp.zeros((padded - key_count * BLOCK, HEAD_DIM), keys.dtype)
        keys_t[:, tail] = jnp.zeros((HEAD_DIM, padded - key_count * BLOCK), keys.dtype)
        key_sum[tail] = jnp.zeros((padded - key_count * BLOCK, HEAD_DIM), jnp.float32)
        value_sum[tail] = jnp.zeros((padded - key_count * BLOCK, HEAD_DIM), jnp.float32)

        @pl.loop(0, pairs)
        def _(index):
            pair = QueryPair(index, lengths_ref, index_list, place_list)
            query, grad = pair.load(q_ref), pair.load(g_ref)
            query_t, grad_t = pair.load_t(q_ref), pair.load_t(g_ref)
            delta = jnp.sum(grad_t.astype(jnp.float32) * exact_ref[index], axis=0, keepdims=True)
            log_total = log_ref[index]

            def step(tile, query_grad, masked):
                span = pl.ds(pair.row(tile), width)
                scores = jnp.dot(keys[span], query_t, preferred_element_type=jnp.float32)
                probability = jnp.exp2(scores * scale - log_total)
                if masked:
                    probability = jnp.where(pair.allowed(tile), probability, 0.0)
                prob_grad = jnp.dot(values[span], grad_t, preferred_element_type=jnp.float32)
                score_grad = (probability * (prob_grad - delta)).astype(jnp.bfloat16)
                value_sum[span] += jnp.dot(
                    probability.astype(jnp.bfloat16), grad, preferred_element_type=jnp.float32)
                key_sum[span] += jnp.dot(score_grad, query, preferred_element_type=jnp.float32)
                return query_grad + jnp.dot(keys_t[:, span], score_grad, preferred_element_type=jnp.float32)

            query_grad = jnp.zeros((HEAD_DIM, 2 * BLOCK), jnp.float32)
            query_grad = lax.fori_loop(0, pair.open_tiles, lambda tile, c: step(tile, c, False), query_grad)
            query_grad = lax.fori_loop(pair.open_tiles, pair.tiles, lambda tile, c: step(tile, c, True), query_grad)
            pair.store_t(dq_ref, query_grad * plain_scale)

        @pl.loop(0, key_count)
        def _(block):
            at, dealt = block_rows(block), block_rows(slot_ref[block])
            dk_ref[dealt] = (key_sum[at] * plain_scale).astype(dk_ref.dtype)
            dv_ref[dealt] = value_sum[at].astype(dv_ref.dtype)

    return pl.pallas_call(
        kernel,
        out_shape=[
            jax.ShapeDtypeStruct(queries.shape, jnp.bfloat16),
            jax.ShapeDtypeStruct(shared.shape[1:], jnp.bfloat16),
            jax.ShapeDtypeStruct(shared.shape[1:], jnp.bfloat16),
        ],
        in_specs=[SMEM] * 2 + [VMEM] * 5,
        out_specs=[VMEM] * 3,
        scratch_shapes=[
            pltpu.SMEM((2 * pairs,), jnp.int32), pltpu.SMEM((2 * pairs,), jnp.int32),
            pltpu.VMEM((padded, HEAD_DIM), jnp.bfloat16),
            pltpu.VMEM((HEAD_DIM, padded), jnp.bfloat16),
            pltpu.VMEM((padded, HEAD_DIM), jnp.bfloat16),
            pltpu.VMEM((padded, HEAD_DIM), jnp.float32),
            pltpu.VMEM((padded, HEAD_DIM), jnp.float32),
        ],
        compiler_params=pltpu.CompilerParams(vmem_limit_bytes=60 * MIB),
        cost_estimate=pl.CostEstimate(flops=20 << 30, bytes_accessed=100 * MIB, transcendentals=8 << 20),
    )(lengths, slot, queries, shared, upstream, exact, logs)


def line_neighbours(mp, count):
    return ((1, mp + 1 < count, jnp.minimum(mp + 1, count - 1)), (-1, mp >= 1, jnp.maximum(mp - 1, 0)))


def greet_all(fixed, dp, mp, count):
    barrier = pltpu.get_barrier_semaphore()
    for peer in fixed:
        pl.semaphore_signal(barrier, inc=1, device_id=peer, device_id_type=MESH)
    expected = jnp.int32(len(fixed))
    for _, there, place in line_neighbours(mp, count):

        @pl.when(there)
        def _():
            pl.semaphore_signal(barrier, inc=1, device_id=(dp, place), device_id_type=MESH)

        expected = expected + there.astype(jnp.int32)
    pl.semaphore_wait(barrier, expected)


class LineGather:
    def __init__(self, own, full, rows, pieces, send_sem, recv_sem, dp, mp, count):
        self.own, self.full, self.rows, self.pieces = own, full, rows, pieces
        self.send_sem, self.recv_sem, self.dp, self.mp, self.count = send_sem, recv_sem, dp, mp, count
        self.size = rows // pieces

    def place(self, block, piece):
        return self.full.at[pl.ds(pl.multiple_of(block * self.rows + piece * self.size, self.size), self.size)]

    def hop(self, way, step, piece):
        sign, there, neighbour = line_neighbours(self.mp, self.count)[way]
        origin = self.mp - sign * step
        exists = (origin >= 0) & (origin < self.count)
        origin = jnp.clip(origin, 0, self.count - 1)
        if step == 0:
            source = self.own.at[pl.ds(pl.multiple_of(piece * self.size, self.size), self.size)]
        else:
            source = self.place(origin, piece)
        def copy():
            return remote(source, self.place(origin, piece), self.send_sem.at[way, step, piece],
                          self.recv_sem.at[way, step, piece], (self.dp, neighbour))

        return exists, exists & there, copy

    def advance(self, step, piece, also=True):
        for way in range(2):
            if step:
                exists, _, _ = self.hop(way, step, piece)
                _, _, earlier = self.hop(way, step - 1, piece)

                @pl.when(exists & also)
                def _():
                    earlier().wait_recv()

            if step < self.count - 1:
                _, sends, copy = self.hop(way, step, piece)

                @pl.when(sends & also)
                def _():
                    copy().start()

    def finish(self):
        @pl.loop(0, self.pieces)
        def _(piece):
            for way in range(2):
                for step in range(self.count - 1):
                    _, sends, copy = self.hop(way, step, piece)

                    @pl.when(sends)
                    def _():
                        copy().wait_send()

    @staticmethod
    def semaphores(count, pieces):
        return [pltpu.SemaphoreType.DMA((2, count, pieces)), pltpu.SemaphoreType.DMA((2, count, pieces))]


class ShardGather:
    def __init__(self, shards, wholes, depth, cross_send, cross_recv, core_send, core_recv, own_sem, dp, mp, chips):
        self.shards, self.wholes, self.depth, self.own_sem = shards, wholes, depth, own_sem
        self.cross_send, self.cross_recv, self.core_send, self.core_recv = cross_send, cross_recv, core_send, core_recv
        self.dp, self.mp, self.chips = dp, mp, chips

    def place(self, array, owner):
        return self.wholes[array].at[pl.ds(pl.multiple_of(owner * self.depth, self.depth), self.depth)]

    def cross(self, array, o):
        return remote(self.shards[array], self.place(array, self.dp), self.cross_send.at[array, o],
                      self.cross_recv.at[array, o], (self.dp ^ (2 * o), self.mp))

    def core(self, array, o):
        owner = self.dp ^ (2 * o)
        source = self.place(array, owner) if o else self.shards[array]
        return remote(source, self.place(array, owner), self.core_send.at[array, o], self.core_recv.at[array, o],
                      (self.dp ^ 1, self.mp))

    def own(self, array):
        return pltpu.make_async_copy(self.shards[array], self.place(array, self.dp), self.own_sem.at[array])

    def begin(self):
        for array in range(len(self.shards)):
            for o in range(1, self.chips):
                self.cross(array, o).start()
        for array in range(len(self.shards)):
            self.own(array).start()
            self.core(array, 0).start()

    def spread(self, array):
        for o in range(1, self.chips):
            self.cross(array, o).wait_recv()
            self.core(array, o).start()

    def finish(self):
        for array in range(len(self.shards)):
            self.own(array).wait()
            for o in range(self.chips):
                self.core(array, o).wait()
                if o:
                    self.cross(array, o).wait_send()

    @staticmethod
    def semaphores(count, chips):
        return [pltpu.SemaphoreType.DMA((count, chips)) for _ in range(4)] + [pltpu.SemaphoreType.DMA((count,))]


class LineReduce:
    def __init__(self, part, flows, rows, pieces, send_sem, recv_sem, dp, mp, count):
        self.part, self.flows, self.rows, self.pieces = part, flows, rows, pieces
        self.send_sem, self.recv_sem, self.dp, self.mp, self.count = send_sem, recv_sem, dp, mp, count
        self.size = rows // pieces

    def span(self, block, piece):
        return pl.ds(pl.multiple_of(block * self.rows + piece * self.size, self.size), self.size)

    def hop(self, way, block, piece, first=False):
        neighbour = line_neighbours(self.mp, self.count)[way][2]
        span = self.span(block, piece)
        source = self.part.at[span] if first else self.flows.at[way, span]
        return remote(source, self.flows.at[way, span], self.send_sem.at[way, block, piece],
                      self.recv_sem.at[way, block, piece], (self.dp, neighbour))

    def roles(self, way, block):
        if way == 0:
            behind, ahead = self.mp >= 1, self.mp < block
        else:
            behind, ahead = self.mp < self.count - 1, self.mp > block
        return ahead & jnp.logical_not(behind), ahead & behind

    def targets(self):
        for index in range(self.count - 1):
            yield 0, self.count - 1 - index
            yield 1, index

    def begin(self, piece, also=True):
        for way, block in self.targets():
            begins, _ = self.roles(way, block)

            @pl.when(begins & also)
            def _():
                self.hop(way, block, piece, True).start()

    def advance(self, turn):
        for way, block in self.targets():
            _, hands_on = self.roles(way, block)
            passed = SKEW * (self.mp - 1 if way == 0 else self.count - 2 - self.mp)
            piece = jnp.clip(turn - passed, 0, self.pieces - 1)

            @pl.when(hands_on & (turn >= passed) & (turn - passed < self.pieces))
            def _():
                self.hop(way, block, piece).wait_recv()
                span = self.span(block, piece)
                value = self.flows[way, span].astype(jnp.float32) + self.part[span].astype(jnp.float32)
                self.flows[way, span] = value.astype(self.flows.dtype)
                self.hop(way, block, piece).start()

    def arrive(self, piece):
        for way in range(2):

            @pl.when(self.mp >= 1 if way == 0 else self.mp < self.count - 1)
            def _():
                self.hop(way, self.mp, piece).wait_recv()

    def total(self, piece, result):
        span = self.span(self.mp, piece)
        result[...] = self.part[span].astype(jnp.float32)
        for way in range(2):

            @pl.when(self.mp >= 1 if way == 0 else self.mp < self.count - 1)
            def _():
                result[...] += self.flows[way, span].astype(jnp.float32)

    def finish(self):
        @pl.loop(0, self.pieces)
        def _(piece):
            for way, block in self.targets():
                begins, hands_on = self.roles(way, block)

                @pl.when(begins)
                def _():
                    self.hop(way, block, piece, True).wait_send()

                @pl.when(hands_on)
                def _():
                    self.hop(way, block, piece).wait_send()

    @staticmethod
    def scratch(count, rows, width, pieces):
        return [pltpu.VMEM((2, count * rows, width), jnp.bfloat16),
                pltpu.SemaphoreType.DMA((2, count, pieces)), pltpu.SemaphoreType.DMA((2, count, pieces))]


AHEAD = 1
MAX_PIECES = 16
SKEW = 1


def pieces_of(rows):
    return min(MAX_PIECES, rows // 16)


def unit_rows(values):
    average = jnp.mean(values, axis=-1, keepdims=True)
    centred = values - average
    inverse = lax.rsqrt(jnp.mean(centred * centred, axis=-1, keepdims=True) + norm_epsilon)
    return centred * inverse, inverse


def project_first(
    hidden, output_grad, lengths, order, vectors, projections, out_weight, heads, members, collective_id
):
    rows, width = hidden.shape
    dp_count, mp_count = lax.axis_size("dp"), lax.axis_size("mp")
    chips, pieces = dp_count // 2, pieces_of(rows)
    group_rows, depth, columns = mp_count * rows, projections[0].shape[0], projections[0].shape[1]
    each = width // dp_count // 128
    tall = [v.shape[1] // 128 for v in vectors]
    slab = sum(tall) + -sum(tall) % 8
    halves, kinds = heads // 2, 3
    arrays = kinds + 2
    offsets = sorted({2 * o for o in range(1, chips)} | {o for o in range(1, members)} | {o * members for o in range(1, heads)})

    def kernel(lengths_ref, order_ref, hidden_ref, upstream_ref, *refs):
        parts, refs = refs[: len(vectors)], refs[len(vectors) :]
        weight_refs, out_weight_ref = refs[:kinds], refs[kinds]
        normed, all_vectors, weights, all_out, shared, queries, branch, live = refs[kinds + 1 : kinds + 9]
        (vector_ref, raw, stage, gains, biases, line_send, line_recv, row_sem, own_sem, cross_send, cross_recv, core_send, core_recv,
         head_local, head_send, head_recv, pair_send, pair_recv) = refs[kinds + 9 :]
        dp, mp = lax.axis_index("dp"), lax.axis_index("mp")
        vector_ref[...] = jnp.zeros_like(vector_ref)
        first = 0
        for part, count in zip(parts, tall):
            for r in range(count):
                vector_ref[first + r : first + r + 1] = part[:, r * 128 : (r + 1) * 128].astype(jnp.float32)
            first += count
        group, member = dp // members, dp % members
        partner = (dp ^ 1, mp)
        greet_all([(dp ^ o, mp) for o in offsets], dp, mp, mp_count)
        line = LineGather(hidden_ref, raw, rows, pieces, line_send, line_recv, dp, mp, mp_count)

        def source(array):
            return (list(weight_refs) + [out_weight_ref, vector_ref])[array]

        def place(array, owner):
            if array < kinds:
                return weights.at[pl.ds(pl.multiple_of(owner * depth, depth), depth), pl.ds(array * columns, columns)]
            if array == kinds:
                return all_out.at[pl.ds(pl.multiple_of(owner * depth, depth), depth)]
            return all_vectors.at[pl.ds(pl.multiple_of(owner * slab, slab), slab)]

        def cross(array, o):
            return remote(source(array), place(array, dp), cross_send.at[array, o], cross_recv.at[array, o],
                          (dp ^ (2 * o), mp))

        def core(array, o):
            owner = dp ^ (2 * o)
            return remote(place(array, owner) if o else source(array), place(array, owner),
                          core_send.at[array, o], core_recv.at[array, o], partner)

        def own(array):
            return pltpu.make_async_copy(source(array), place(array, dp), own_sem.at[array])

        def block_span(block):
            return pl.ds(pl.multiple_of(block * rows, rows), rows)

        first_to_last = [kinds + 1] + list(range(kinds + 1))
        for array in first_to_last:
            for o in range(1, chips):
                cross(array, o).start()
            if array == first_to_last[0]:

                @pl.loop(0, pieces)
                def _(piece):
                    line.advance(0, piece)

        for block in range(rows // BLOCK):
            found = order_ref[(dp * group_rows + mp * rows) // BLOCK + block]
            valid = sequence_of(found, lengths_ref)[1]
            span = slice(block * BLOCK, (block + 1) * BLOCK)
            live[span] = (lax.broadcasted_iota(jnp.int32, (BLOCK, 128), 0) < valid).astype(jnp.float32)
            keep = lax.broadcasted_iota(jnp.int32, (BLOCK, width), 0) < valid
            branch[span] = jnp.where(keep, upstream_ref[span].astype(jnp.float32), 0.0).astype(branch.dtype)
        own_rows = pltpu.make_async_copy(hidden_ref, raw.at[block_span(mp)], row_sem)
        own_rows.start()
        for array in first_to_last:
            own(array).start()
            core(array, 0).start()

        def spread(array):
            for o in range(1, chips):
                cross(array, o).wait_recv()
                core(array, o).start()

        def settle(array):
            own(array).wait()
            for o in range(chips):
                core(array, o).wait_recv()

        def norm(block):
            chunk = 64

            @pl.loop(0, rows // chunk)
            def _(part):
                span = pl.ds(pl.multiple_of(block * rows + part * chunk, chunk), chunk)
                unit, _ = unit_rows(raw[span].astype(jnp.float32))
                normed[span] = (unit * gains[0:1] + gains[1:2]).astype(normed.dtype)

        def each_block(low, high, visit):
            @pl.loop(0, mp_count)
            def _(block):
                distance = jnp.abs(block - mp)

                @pl.when((distance >= low) & (distance <= high))
                def _():
                    visit(block)

        def rows_of(kind_ref, owner, block):
            return kind_ref.at[pl.ds(pl.multiple_of(owner * group_rows + block * rows, rows), rows)]

        def pass_on(kind, o, block, piece):
            giver = (group ^ o) * members + member
            return [remote(piece, rows_of(shared.at[kind], giver, block), pair_send.at[kind, o, block, p - 1],
                           pair_recv.at[kind, o, block, p - 1], (group * members + (member ^ p), mp))
                    for p in range(1, members)]

        def head_copy(kind, o, block, to_shared):
            target = group ^ o
            piece = stage.at[kind, block, target]
            landing = rows_of(shared.at[kind], dp, block) if to_shared else rows_of(queries, group, block)
            return remote(piece, landing, head_send.at[kind, o, block], head_recv.at[kind, o, block],
                          (target * members + member, mp))

        def local_copy(kind, block, to_shared):
            landing = rows_of(shared.at[kind], dp, block) if to_shared else rows_of(queries, group, block)
            return pltpu.make_async_copy(stage.at[kind, block, group], landing, head_local.at[kind, block])

        def project(tile, block):
            kind, half = tile // halves, tile % halves
            span = pl.ds(pl.multiple_of(half * 256, 256), 256)
            across = pl.ds(pl.multiple_of(kind * columns + half * 256, 256), 256)
            value = jnp.dot(normed[block_span(block)], weights[:, across], preferred_element_type=jnp.float32)
            value = (value + biases[pl.ds(kind, 1), span]).astype(stage.dtype)
            for h in range(2):
                head = 2 * half + h
                stage[kind, block, head] = value[:, h * HEAD_DIM : (h + 1) * HEAD_DIM]
            for h in range(2):
                o = (2 * half + h) ^ group
                for to_shared in (True, False):
                    chosen = (kind < 2) if to_shared else (kind == 2)

                    @pl.when(chosen & (o != 0))
                    def _():
                        head_copy(kind, o, block, to_shared).start()

                    @pl.when(chosen & (o == 0))
                    def _():
                        local_copy(kind, block, to_shared).start()
                        if to_shared:
                            for copy in pass_on(kind, 0, block, stage.at[kind, block, group]):
                                copy.start()

        def hand_on(block):
            @pl.loop(0, 2)
            def _(kind):
                for o in range(1, heads):
                    head_copy(kind, o, block, True).wait_recv()
                    giver = (group ^ o) * members + member
                    for copy in pass_on(kind, o, block, rows_of(shared.at[kind], giver, block)):
                        copy.start()

        last = mp_count - 1
        for step in range(1, last):

            @pl.loop(0, pieces)
            def _(piece):
                line.advance(step, piece)

            if step == 1:
                spread(kinds + 1)
                settle(kinds + 1)
                for owner in range(dp_count):
                    for r in range(each):
                        at = pl.ds((owner * each + r) * 128, 128)
                        for k in range(2):
                            gains[k : k + 1, at] = all_vectors[owner * slab + k * each + r : owner * slab + k * each + r + 1]
                biases[...] = jnp.zeros_like(biases)
                for head in range(heads):
                    feature = mp * heads + head
                    first = (feature // each) * slab + feature % each
                    for kind, k in ((1, 3), (2, 2)):
                        biases[kind : kind + 1, head * 128 : (head + 1) * 128] = all_vectors[pl.ds(first + k * each, 1)]
                own_rows.wait()
                each_block(0, 1, norm)
            else:
                each_block(step, step, norm)
        for array in range(kinds + 1):
            spread(array)
        for array in range(kinds):
            settle(array)
        tiles = kinds * halves

        @pl.loop(0, pieces)
        def _(piece):
            line.advance(last - 1 if last == 1 else last, piece)

            @pl.when(piece < tiles)
            def _():
                each_block(0, last - 1, lambda block: project(piece, block))

        each_block(last, last, norm)

        @pl.loop(0, tiles)
        def _(tile):
            each_block(last, last, lambda block: project(tile, block))

        each_block(0, last - 1, hand_on)
        each_block(last, last, hand_on)
        line.finish()
        settle(kinds)
        for array in first_to_last:
            for o in range(chips):
                core(array, o).wait_send()
                if o:
                    cross(array, o).wait_send()

        @pl.loop(0, mp_count)
        def _(block):
            for kind in range(kinds):
                to_shared = kind < 2
                local_copy(kind, block, to_shared).wait()
                for o in range(1, heads):
                    head_copy(kind, o, block, to_shared).wait_send()
                    if not to_shared:
                        head_copy(kind, o, block, to_shared).wait_recv()
                if to_shared:
                    for o in range(heads):
                        giver = (group ^ o) * members + member
                        for copy in pass_on(kind, o, block, rows_of(shared.at[kind], giver, block)):
                            copy.wait()

    dma = pltpu.SemaphoreType.DMA
    bf16, f32 = jnp.bfloat16, jnp.float32
    return pl.pallas_call(
        kernel,
        out_shape=[
            jax.ShapeDtypeStruct((group_rows, width), bf16),
            jax.ShapeDtypeStruct((dp_count * slab, 128), f32),
            jax.ShapeDtypeStruct((width, kinds * columns), bf16),
            jax.ShapeDtypeStruct((width, columns), bf16),
            jax.ShapeDtypeStruct((2, dp_count * group_rows, HEAD_DIM), bf16),
            jax.ShapeDtypeStruct((heads * group_rows, HEAD_DIM), bf16),
            jax.ShapeDtypeStruct((rows, width), bf16),
            jax.ShapeDtypeStruct((rows, 128), f32),
        ],
        in_specs=[SMEM, SMEM, VMEM, VMEM] + [VMEM] * len(vectors) + [ANY] * (kinds + 1),
        out_specs=[VMEM, VMEM, VMEM, ANY, ANY, ANY, VMEM, VMEM],
        scratch_shapes=[
            pltpu.VMEM((slab, 128), f32),
            pltpu.VMEM((group_rows, width), bf16),
            pltpu.VMEM((kinds, mp_count, heads, rows, HEAD_DIM), bf16),
            pltpu.VMEM((8, width), f32),
            pltpu.VMEM((8, columns), f32),
        ]
        + LineGather.semaphores(mp_count, pieces)
        + [dma(()), dma((arrays,))]
        + [dma((arrays, chips)) for _ in range(4)]
        + [dma((kinds, mp_count)), dma((kinds, heads, mp_count)), dma((kinds, heads, mp_count))]
        + [dma((2, heads, mp_count, members)) for _ in range(2)],
        compiler_params=pltpu.CompilerParams(
            collective_id=collective_id, has_side_effects=True, vmem_limit_bytes=48 * MIB),
        cost_estimate=pl.CostEstimate(flops=8 << 30, bytes_accessed=250 * MIB, transcendentals=0),
    )(lengths, order, hidden, output_grad, *vectors, *projections, out_weight)


def reduce_norm_gather(part, hidden, out_bias, gain, shift, shards, collective_id):
    dp_count, mp_count = lax.axis_size("dp"), lax.axis_size("mp")
    chips, count = dp_count // 2, len(shards)
    rows, width = hidden.shape
    pieces = pieces_of(rows)
    size = rows // pieces

    turns = pieces + 2 * SKEW * (mp_count - 1)

    def kernel(part_ref, hidden_ref, bias_ref, gain_ref, shift_ref, *refs):
        shard_refs, (residual_ref, full_ref), whole_refs = refs[:count], refs[count : count + 2], refs[count + 2 : 2 * count + 2]
        total, normed, flows, red_send, red_recv, line_send, line_recv, own_sem, *weight_sems = refs[2 * count + 2 :]
        dp, mp = lax.axis_index("dp"), lax.axis_index("mp")
        greet_all([(dp ^ (2 * o), mp) for o in range(1, chips)] + [(dp ^ 1, mp)], dp, mp, mp_count)
        weights = ShardGather(shard_refs, whole_refs, shards[0].shape[0], *weight_sems, dp, mp, chips)
        weights.begin()
        reduce = LineReduce(part_ref, flows, rows, pieces, red_send, red_recv, dp, mp, mp_count)
        gather = LineGather(normed, full_ref, rows, pieces, line_send, line_recv, dp, mp, mp_count)
        for piece in range(AHEAD):
            reduce.begin(piece)

        @pl.loop(0, turns)
        def _(turn):
            for array in range(count):

                @pl.when(turn == turns - 1 - 6 * (count - 1 - array))
                def _():
                    weights.spread(array)

            reduce.begin(jnp.minimum(turn + AHEAD, pieces - 1), turn + AHEAD < pieces)
            reduce.advance(turn)
            done = turn - SKEW * (mp_count - 1)

            @pl.when((done >= 0) & (done < pieces))
            def _():
                reduce.arrive(done)
                reduce.total(done, total)
                span = pl.ds(pl.multiple_of(done * size, size), size)
                residual = hidden_ref[span].astype(jnp.float32) + total[...] + bias_ref[...]
                residual_ref[span] = residual
                unit, _ = unit_rows(residual)
                normed[span] = (unit * gain_ref[...] + shift_ref[...]).astype(normed.dtype)
                gather.advance(0, done)

            for step in range(1, mp_count):
                late = done - SKEW * step
                gather.advance(step, jnp.clip(late, 0, pieces - 1), (late >= 0) & (late < pieces))

        own = pltpu.make_async_copy(normed, full_ref.at[pl.ds(pl.multiple_of(mp * rows, rows), rows)], own_sem)
        own.start()
        reduce.finish()
        gather.finish()
        own.wait()
        weights.finish()

    return pl.pallas_call(
        kernel,
        out_shape=[
            jax.ShapeDtypeStruct((rows, width), jnp.float32),
            jax.ShapeDtypeStruct((mp_count * rows, width), jnp.bfloat16),
        ]
        + [jax.ShapeDtypeStruct((dp_count * a.shape[0], a.shape[1]), a.dtype) for a in shards],
        in_specs=[VMEM] * 5 + [ANY] * count,
        out_specs=[VMEM, ANY] + [ANY] * count,
        scratch_shapes=[pltpu.VMEM((size, width), jnp.float32), pltpu.VMEM((rows, width), jnp.bfloat16)]
        + LineReduce.scratch(mp_count, rows, width, pieces) + LineGather.semaphores(mp_count, pieces)
        + [pltpu.SemaphoreType.DMA(())] + ShardGather.semaphores(count, chips),
        compiler_params=pltpu.CompilerParams(
            collective_id=collective_id, has_side_effects=True, vmem_limit_bytes=48 * MIB),
        cost_estimate=pl.CostEstimate(flops=0, bytes_accessed=300 * MIB, transcendentals=0),
    )(part, hidden, out_bias, gain, shift, *shards)


def reduce_back_gather(part, residual, branch_two, gain, pairs, collective_id):
    dp_count, mp_count = lax.axis_size("dp"), lax.axis_size("mp")
    chips, count = dp_count // 2, len(pairs)
    rows, width = residual.shape
    pieces = pieces_of(rows)
    size, depth = rows // pieces, width // dp_count
    units = pairs[0][1].shape[1]
    turns = pieces + 2 * SKEW * (mp_count - 1)
    each = dp_count // 4
    busy = count * dp_count // each
    assert 1 + busy <= turns

    def kernel(part_ref, residual_ref, branch_ref, gain_ref, *refs):
        operands, refs = refs[: 2 * count], refs[2 * count :]
        (grad_ref, sums_ref, full_ref), terms, refs = refs[:3], refs[3 : 3 + count], refs[3 + count :]
        loaded, refs = refs[: 2 * count], refs[2 * count :]
        (total, low, kept, slices, from_partner, chip_sum, load_sem, keep_sem, pair_send, pair_recv, cross_send, cross_recv,
         flows, red_send, red_recv, line_send, line_recv, own_sem) = refs
        dp, mp = lax.axis_index("dp"), lax.axis_index("mp")
        partner = (dp ^ 1, mp)
        greet_all([(dp ^ (2 * o), mp) for o in range(1, chips)] + [partner], dp, mp, mp_count)
        reduce = LineReduce(part_ref, flows, rows, pieces, red_send, red_recv, dp, mp, mp_count)
        gather = LineGather(low, full_ref, rows, pieces, line_send, line_recv, dp, mp, mp_count)
        for piece in range(AHEAD):
            reduce.begin(piece)
        loads = [pltpu.make_async_copy(operands[k], loaded[k], load_sem.at[k]) for k in range(2 * count)]
        for copy in loads:
            copy.start()
        sums_ref[...] = jnp.zeros_like(sums_ref)

        def pair(mat, o):
            return remote(slices.at[o], from_partner.at[mat, o], pair_send.at[mat, o], pair_recv.at[mat, o], partner)

        def cross(mat, o, peer):
            return remote(chip_sum.at[mat, o - 1], terms[mat].at[o], cross_send.at[mat, o], cross_recv.at[mat, o],
                          (peer, mp))

        def weight_slice(mat, index):
            o = (index + 1) % chips
            mine = index >= chips
            owner = dp ^ (2 * o) ^ jnp.where(mine, 0, 1)
            left = loaded[2 * mat][:, pl.ds(pl.multiple_of(owner * depth, depth), depth)]
            value = contract_first(left, loaded[2 * mat + 1][...])

            @pl.when(jnp.logical_not(mine))
            def _():
                if mat:
                    pair(mat - 1, o).wait_send()
                slices[o] = value.astype(slices.dtype)
                pair(mat, o).start()

            @pl.when(mine)
            def _():
                pair(mat, o).wait_recv()
                both = (value + from_partner[mat, o].astype(jnp.float32)).astype(slices.dtype)

                @pl.when(o == 0)
                def _():
                    kept[mat] = both
                    pltpu.make_async_copy(kept.at[mat], terms[mat].at[0], keep_sem.at[mat]).start()

                @pl.when(o != 0)
                def _():
                    chip_sum[mat, o - 1] = both
                    cross(mat, o, owner).start()

        @pl.loop(0, turns)
        def _(turn):
            reduce.begin(jnp.minimum(turn + AHEAD, pieces - 1), turn + AHEAD < pieces)
            reduce.advance(turn)
            done = turn - SKEW * (mp_count - 1)

            @pl.when((done >= 0) & (done < pieces))
            def _():
                reduce.arrive(done)
                reduce.total(done, total)
                span = pl.ds(pl.multiple_of(done * size, size), size)
                unit, inverse = unit_rows(residual_ref[span])
                upstream = total[...]
                sums_ref[0:1] += jnp.sum(upstream * unit, axis=0, keepdims=True)
                sums_ref[1:2] += jnp.sum(upstream, axis=0, keepdims=True)
                grad = branch_ref[span].astype(jnp.float32) + norm_back(upstream, unit, inverse, gain_ref[...])
                grad_ref[span] = grad
                rounded = grad.astype(low.dtype)
                low[span] = rounded
                sums_ref[2:3] += jnp.sum(rounded.astype(jnp.float32), axis=0, keepdims=True)
                gather.advance(0, done)

            for step in range(1, mp_count):
                late = done - SKEW * step
                gather.advance(step, jnp.clip(late, 0, pieces - 1), (late >= 0) & (late < pieces))
            for mat in range(count):

                @pl.when(turn == 1 + mat * busy // count)
                def _():
                    for copy in loads[2 * mat : 2 * mat + 2]:
                        copy.wait()

                first = turn - 1 - mat * busy // count

                @pl.when((first >= 0) & (first < busy // count))
                def _():
                    for i in range(each):
                        weight_slice(mat, first * each + i)

        own = pltpu.make_async_copy(low, full_ref.at[pl.ds(pl.multiple_of(mp * rows, rows), rows)], own_sem)
        own.start()
        reduce.finish()
        gather.finish()
        own.wait()
        for mat in range(count):
            pltpu.make_async_copy(kept.at[mat], terms[mat].at[0], keep_sem.at[mat]).wait()
            for o in range(chips):
                if mat == count - 1:
                    pair(mat, o).wait_send()
                if o:
                    cross(mat, o, dp ^ (2 * o)).wait()

    bf16, f32 = jnp.bfloat16, jnp.float32
    dma = pltpu.SemaphoreType.DMA
    flat = [array for two in pairs for array in two]
    return pl.pallas_call(
        kernel,
        out_shape=[
            jax.ShapeDtypeStruct((rows, width), f32),
            jax.ShapeDtypeStruct((8, width), f32),
            jax.ShapeDtypeStruct((mp_count * rows, width), bf16),
        ]
        + [jax.ShapeDtypeStruct((chips, depth, units), bf16)] * count,
        in_specs=[VMEM] * 4 + [ANY] * (2 * count),
        out_specs=[VMEM, VMEM] + [ANY] * (1 + count),
        scratch_shapes=[pltpu.VMEM(a.shape, a.dtype) for a in flat]
        + [
            pltpu.VMEM((size, width), f32),
            pltpu.VMEM((rows, width), bf16),
            pltpu.VMEM((count, depth, units), bf16),
            pltpu.VMEM((chips, depth, units), bf16),
            pltpu.VMEM((count, chips, depth, units), bf16),
            pltpu.VMEM((count, chips - 1, depth, units), bf16),
            dma((2 * count,)), dma((count,)),
        ]
        + [dma((count, chips)) for _ in range(4)]
        + LineReduce.scratch(mp_count, rows, width, pieces) + LineGather.semaphores(mp_count, pieces)
        + [dma(())],
        compiler_params=pltpu.CompilerParams(
            collective_id=collective_id, has_side_effects=True, vmem_limit_bytes=63 * MIB),
        cost_estimate=pl.CostEstimate(flops=40 << 30, bytes_accessed=300 * MIB, transcendentals=0),
    )(part, residual, branch_two, gain, *flat)


QUARTERS = 4


def finish_back(query_grad, key_part, value_part, weights, normed, residual_grad, hidden, gain, out_part, heads, members,
                collective_id):
    rows, width = hidden.shape
    dp_count, mp_count = lax.axis_size("dp"), lax.axis_size("mp")
    chips, pieces = dp_count // 2, pieces_of(rows)
    size, depth, columns = rows // pieces, width // dp_count, heads * HEAD_DIM
    kinds, quarter = 3, rows // QUARTERS
    per_quarter = pieces // QUARTERS
    slice_rows = width // per_quarter
    turns = pieces + SKEW * (mp_count - 1)
    slices_each = max(dp_count // 8, 1)
    slice_turn = turns // 3
    group_rows = mp_count * rows
    offsets = sorted({2 * o for o in range(1, chips)} | {o for o in range(1, members)} | {o * members for o in range(1, heads)})
    query_grad = query_grad.reshape(heads, mp_count, rows, HEAD_DIM)
    shared = [v.reshape(dp_count, mp_count, rows, HEAD_DIM) for v in (key_part, value_part)]

    def kernel(query_ref, key_ref, value_ref, weights_hbm, normed_hbm, residual_ref, hidden_ref, gain_ref, out_ref,
               grad_ref, sums_ref, weight_grad_ref, out_grad_ref, column_ref,
               weights, normed, landed, own, parts, stage, part, total, flows, red_send, red_recv,
               slices, from_partner, chip_sum, from_chips, out_partner, out_sum, out_chips,
               load_sem, own_sem, part_send, part_recv, local_sem, head_send, head_recv,
               pair_send, pair_recv, cross_send, cross_recv):
        dp, mp = lax.axis_index("dp"), lax.axis_index("mp")
        group, member = dp // members, dp % members
        partner = (dp ^ 1, mp)
        greet_all([(dp ^ o, mp) for o in offsets], dp, mp, mp_count)
        reduce = LineReduce(part, flows, rows, pieces, red_send, red_recv, dp, mp, mp_count)
        loads = [pltpu.make_async_copy(weights_hbm, weights, load_sem.at[0]),
                 pltpu.make_async_copy(normed_hbm, normed, load_sem.at[1])]
        shared_refs = (key_ref, value_ref)

        def rows_of(k):
            return pl.ds(k * quarter, quarter)

        def lane_span(kind, head):
            return pl.ds(pl.multiple_of(kind * columns + head * HEAD_DIM, HEAD_DIM), HEAD_DIM)

        def landing(kind, k, head):
            return landed.at[:, rows_of(k), lane_span(kind, head)]

        def own_copy(kind, o):
            return pltpu.make_async_copy(shared_refs[kind].at[(group ^ o) * members + member], own.at[kind, o],
                                         own_sem.at[kind, o])

        def part_copy(kind, o, p, k):
            return remote(shared_refs[kind].at[(group ^ o) * members + (member ^ p), :, rows_of(k)],
                          parts.at[kind, o, p - 1, :, rows_of(k)], part_send.at[kind, o, p - 1, k],
                          part_recv.at[kind, o, p - 1, k], (group * members + (member ^ p), mp))

        def head_copy(kind, o, k):
            source = query_ref.at[group ^ o, :, rows_of(k)] if kind == 2 else stage.at[kind, o, :, rows_of(k)]
            return remote(source, landing(kind, k, group), head_send.at[kind, o, k], head_recv.at[kind, o, k],
                          ((group ^ o) * members + member, mp))

        def local_copy(k):
            return pltpu.make_async_copy(query_ref.at[group, :, rows_of(k)], landing(2, k, group), local_sem.at[k])

        for k in range(QUARTERS):
            for kind in range(2):
                for o in range(heads):
                    for p in range(1, members):
                        part_copy(kind, o, p, k).start()
            if k == 0:
                for kind in range(2):
                    for o in range(heads):
                        own_copy(kind, o).start()
                for copy in loads:
                    copy.start()
            for o in range(1, heads):
                head_copy(2, o, k).start()
            local_copy(k).start()
        for k in range(QUARTERS):
            for kind in range(2):
                for o in list(range(1, heads)) + [0]:
                    if k == 0:
                        own_copy(kind, o).wait()
                    value = own[kind, o, :, k * quarter : (k + 1) * quarter].astype(jnp.float32)
                    for p in range(1, members):
                        part_copy(kind, o, p, k).wait_recv()
                        value = value + parts[kind, o, p - 1, :, k * quarter : (k + 1) * quarter].astype(jnp.float32)
                    if o:
                        stage[kind, o, :, k * quarter : (k + 1) * quarter] = value.astype(stage.dtype)
                        head_copy(kind, o, k).start()
                    else:
                        landed[:, k * quarter : (k + 1) * quarter, lane_span(kind, group)] = value.astype(landed.dtype)

        def arrived(k):
            for kind in range(kinds):
                for o in range(1, heads):
                    head_copy(kind, o, k).wait_recv()
            local_copy(k).wait()

        def project(k, first, count):
            span = pl.ds(pl.multiple_of(k * quarter, quarter), quarter)
            left = landed[:, span].reshape(mp_count * quarter, kinds * columns)
            features = pl.ds(pl.multiple_of(first, count), count)
            value = contract_last(left, weights[features]).astype(part.dtype)
            for block in range(mp_count):
                at = pl.ds(pl.multiple_of(block * rows + k * quarter, quarter), quarter)
                part[at, features] = value[block * quarter : (block + 1) * quarter]

        def slab(owner):
            return pl.ds(pl.multiple_of(owner * depth, depth), depth)

        def pair(o):
            return remote(slices.at[o], from_partner.at[o], pair_send.at[0, o], pair_recv.at[0, o], partner)

        def cross(o, peer):
            return remote(chip_sum.at[o], from_chips.at[o], cross_send.at[0, o], cross_recv.at[0, o], (peer, mp))

        def out_pair(o):
            return remote(out_ref.at[slab(dp ^ (2 * o) ^ 1)], out_partner.at[o], pair_send.at[1, o], pair_recv.at[1, o],
                          partner)

        def out_cross(o):
            return remote(out_sum.at[o], out_chips.at[o], cross_send.at[1, o], cross_recv.at[1, o], (dp ^ (2 * o), mp))

        def weight_slice(index):
            o = (index + 1) % chips
            mine = index >= chips
            owner = dp ^ (2 * o) ^ jnp.where(mine, 0, 1)
            rows_all = landed[...].reshape(group_rows, kinds * columns)
            value = contract_first(normed[:, slab(owner)], rows_all)

            @pl.when(jnp.logical_not(mine))
            def _():
                slices[o] = value.astype(slices.dtype)
                pair(o).start()

            @pl.when(mine)
            def _():
                pair(o).wait_recv()
                both = value + from_partner[o].astype(jnp.float32)

                @pl.when(o == 0)
                def _():
                    weight_grad_ref[...] = both

                @pl.when(o != 0)
                def _():
                    chip_sum[o] = both.astype(chip_sum.dtype)
                    cross(o, owner).start()

        for copy in loads:
            copy.wait()
        arrived(0)
        for part_index in range(per_quarter):
            project(0, part_index * slice_rows, slice_rows)
        for o in range(chips):
            out_pair(o).start()
        sums_ref[...] = jnp.zeros_like(sums_ref)

        @pl.loop(0, turns)
        def _(turn):
            @pl.when(turn < pieces)
            def _():
                reduce.begin(jnp.minimum(turn, pieces - 1))

            reduce.advance(turn)
            done = turn - SKEW * (mp_count - 1)

            @pl.when(done >= 0)
            def _():
                reduce.arrive(done)
                reduce.total(done, total)
                span = pl.ds(pl.multiple_of(done * size, size), size)
                unit, inverse = unit_rows(hidden_ref[span].astype(jnp.float32))
                upstream = total[...]
                sums_ref[0:1] += jnp.sum(upstream * unit, axis=0, keepdims=True)
                sums_ref[1:2] += jnp.sum(upstream, axis=0, keepdims=True)
                grad_ref[span] = residual_ref[span] + norm_back(upstream, unit, inverse, gain_ref[...])

            for k in range(1, QUARTERS):

                @pl.when(turn == (k - 1) * per_quarter)
                def _():
                    arrived(k)

            @pl.when(turn < (QUARTERS - 1) * per_quarter)
            def _():
                k, portion = turn // per_quarter + 1, turn % per_quarter
                project(k, portion * slice_rows, slice_rows)

            @pl.when(turn == slice_turn)
            def _():
                for o in list(range(1, chips)) + [0]:
                    out_pair(o).wait_recv()
                    value = out_ref[slab(dp ^ (2 * o))].astype(jnp.float32) + out_partner[o].astype(jnp.float32)
                    if o:
                        out_sum[o] = value.astype(out_sum.dtype)
                        out_cross(o).start()
                    else:
                        out_grad_ref[...] = value

            @pl.when((turn >= late_turn) & (turn < late_turn + dp_count // slices_each))
            def _():
                for i in range(slices_each):
                    weight_slice((turn - late_turn) * slices_each + i)

        reduce.finish()
        column_ref[...] = jnp.zeros_like(column_ref)
        column_ref[0:1] = jnp.sum(
            landed[...].reshape(group_rows, kinds * columns).astype(jnp.float32), axis=0, keepdims=True)
        for o in range(chips):
            pair(o).wait_send()
            out_pair(o).wait_send()
            if o:
                cross(o, dp ^ (2 * o)).wait()
                weight_grad_ref[...] += from_chips[o].astype(jnp.float32)
                out_cross(o).wait()
                out_grad_ref[...] += out_chips[o].astype(jnp.float32)
        for k in range(QUARTERS):
            for o in range(heads):
                for kind in range(2):
                    for p in range(1, members):
                        part_copy(kind, o, p, k).wait_send()
                if o:
                    for kind in range(kinds):
                        head_copy(kind, o, k).wait_send()

    late_turn = max(slice_turn, (QUARTERS - 2) * per_quarter + 1)
    assert late_turn + dp_count // slices_each <= turns
    dma = pltpu.SemaphoreType.DMA
    bf16, f32 = jnp.bfloat16, jnp.float32
    own_columns = out_part.shape[1]
    return pl.pallas_call(
        kernel,
        out_shape=[
            jax.ShapeDtypeStruct((rows, width), f32),
            jax.ShapeDtypeStruct((8, width), f32),
            jax.ShapeDtypeStruct((depth, kinds * columns), f32),
            jax.ShapeDtypeStruct((depth, own_columns), f32),
            jax.ShapeDtypeStruct((8, kinds * columns), f32),
        ],
        in_specs=[ANY] * 5 + [VMEM] * 4,
        out_specs=[VMEM] * 5,
        scratch_shapes=[
            pltpu.VMEM((width, kinds * columns), bf16),
            pltpu.VMEM((group_rows, width), bf16),
            pltpu.VMEM((mp_count, rows, kinds * columns), bf16),
            pltpu.VMEM((2, heads, mp_count, rows, HEAD_DIM), bf16),
            pltpu.VMEM((2, heads, members - 1, mp_count, rows, HEAD_DIM), bf16),
            pltpu.VMEM((2, heads, mp_count, rows, HEAD_DIM), bf16),
            pltpu.VMEM((group_rows, width), bf16),
            pltpu.VMEM((size, width), f32),
        ]
        + LineReduce.scratch(mp_count, rows, width, pieces)
        + [pltpu.VMEM((chips, depth, kinds * columns), bf16) for _ in range(4)]
        + [pltpu.VMEM((chips, depth, own_columns), bf16) for _ in range(3)]
        + [dma((2,)), dma((2, heads))]
        + [dma((2, heads, members - 1, QUARTERS)) for _ in range(2)]
        + [dma((QUARTERS,)), dma((kinds, heads, QUARTERS)), dma((kinds, heads, QUARTERS))]
        + [dma((2, chips)) for _ in range(4)],
        compiler_params=pltpu.CompilerParams(
            collective_id=collective_id, has_side_effects=True, vmem_limit_bytes=63 * MIB),
        cost_estimate=pl.CostEstimate(flops=20 << 30, bytes_accessed=300 * MIB, transcendentals=0),
    )(query_grad, *shared, weights, normed, residual_grad, hidden, gain, out_part)


def sum_vectors(packed, collective_id):
    dp_count, mp_count = lax.axis_size("dp"), lax.axis_size("mp")
    depth, width = packed.shape[1:]

    def kernel(in_ref, out_ref, landed, mine, others, send_sem, recv_sem, line_send, line_recv):
        dp, mp = lax.axis_index("dp"), lax.axis_index("mp")
        peers = [(dp ^ o, mp) for o in range(1, dp_count)]
        along = [(dp, mp ^ o) for o in range(1, mp_count)]
        greet(peers + along)
        copies = []
        for o in range(1, dp_count):
            copies.append(remote(in_ref.at[dp ^ o], landed.at[o - 1], send_sem.at[o], recv_sem.at[o], peers[o - 1]))
            copies[-1].start()
        value = in_ref[dp]
        for o in range(1, dp_count):
            copies[o - 1].wait()
            value = value + landed[o - 1]
        mine[...] = value
        others[mp] = value
        copies = []
        for o in range(1, mp_count):
            copies.append(remote(mine, others.at[mp], line_send.at[o], line_recv.at[o], along[o - 1]))
            copies[-1].start()
        for copy in copies:
            copy.wait()
        value = others[0]
        for index in range(1, mp_count):
            value = value + others[index]
        out_ref[...] = value

    dma = pltpu.SemaphoreType.DMA
    return pl.pallas_call(
        kernel,
        out_shape=jax.ShapeDtypeStruct((depth, width), jnp.float32),
        in_specs=[VMEM],
        out_specs=VMEM,
        scratch_shapes=[
            pltpu.VMEM((dp_count - 1, depth, width), jnp.float32), pltpu.VMEM((depth, width), jnp.float32),
            pltpu.VMEM((mp_count, depth, width), jnp.float32),
            dma((dp_count,)), dma((dp_count,)), dma((mp_count,)), dma((mp_count,)),
        ],
        compiler_params=pltpu.CompilerParams(collective_id=collective_id, has_side_effects=True),
        cost_estimate=pl.CostEstimate(flops=0, bytes_accessed=20 * MIB, transcendentals=0),
    )(packed)


def per_device(
    hidden_in,
    output_grad,
    first_gain,
    first_shift,
    query_weight,
    query_bias,
    key_weight,
    value_weight,
    value_bias,
    out_weight,
    out_bias,
    second_gain,
    second_shift,
    up_weight,
    up_bias,
    down_weight,
    down_bias,
    seq_lengths,
    block_order,
    block_slot,
):
    local_rows, model_width = hidden_in.shape
    mp_count, dp_count = lax.axis_size("mp"), lax.axis_size("dp")
    mp_index, dp_index = lax.axis_index("mp"), lax.axis_index("dp")
    group_rows = local_rows * mp_count
    head_width = query_weight.shape[1]
    heads_local = head_width // HEAD_DIM
    hidden_width = up_weight.shape[1]
    members = dp_count // heads_local
    blocks_each = group_rows // BLOCK
    plan = (seq_lengths, block_order, block_slot)

    vectors = (first_gain, first_shift, query_bias, value_bias, out_bias, second_gain, second_shift, down_bias, up_bias)
    rows_one, vector_rows, projections, out_all, head_shared, head_queries, branch_two, live = project_first(
        hidden_in, output_grad, seq_lengths, block_order, [v.reshape(1, -1) for v in vectors],
        (key_weight, value_weight, query_weight), out_weight, heads_local, members, 0,
    )
    own_valid = live[:, :1] > 0
    vector_rows = vector_rows.reshape(dp_count, -1, 128)
    each = model_width // dp_count // 128
    gain_one, _, _, _, bias_out, gain_two, shift_two, bias_down = (
        vector_rows[:, k * each : (k + 1) * each].reshape(1, model_width) for k in range(8)
    )
    up_each = up_bias.shape[0] // 128
    bias_up = vector_rows[:, 8 * each : 8 * each + up_each].reshape(1, up_bias.shape[0] * dp_count)

    branch_rows_two = whole_rows(branch_two)
    head_mix, exact_mix, log_total = attend(head_queries, head_shared, *plan, members, blocks_each)
    (attended_low,) = to_rows([head_mix], [], heads_local, members, 2)
    out_part = contract_last(attended_low, out_all).astype(jnp.bfloat16)
    residual, rows_two, up_all, down_all = reduce_norm_gather(
        out_part, hidden_in, bias_out, gain_two, shift_two, (up_weight, down_weight), 3
    )

    bias_hidden = lax.dynamic_slice_in_dim(bias_up, mp_index * hidden_width, hidden_width, 1)
    pre_act = jnp.dot(rows_two, up_all, preferred_element_type=jnp.float32) + bias_hidden
    hidden_low = gelu_exact(pre_act).astype(jnp.bfloat16)
    hidden_grad = jnp.dot(branch_rows_two, down_all, preferred_element_type=jnp.float32)
    pre_grad = jax.vjp(gelu_exact, pre_act)[1](hidden_grad)[0].astype(jnp.bfloat16)
    up_part = contract_last(pre_grad, up_all).astype(jnp.bfloat16)
    residual_grad, sums_two, branch_rows_one, down_terms, up_terms = reduce_back_gather(
        up_part, residual, branch_two, gain_two, ((branch_rows_two, hidden_low), (rows_two, pre_grad)), 4
    )
    down_weight_grad, up_weight_grad = (
        jnp.sum(terms.astype(jnp.float32), axis=0) for terms in (down_terms, up_terms)
    )

    hidden_low, branch_rows_one = lax.optimization_barrier((hidden_low, branch_rows_one))
    feed = row_share(contract_last(hidden_low, down_all))
    result = residual + feed + bias_down
    output = jnp.where(own_valid, result, 0.0).astype(jnp.bfloat16)

    attended_grad = jnp.dot(branch_rows_one, out_all, preferred_element_type=jnp.float32).astype(jnp.bfloat16)
    (head_grad,) = to_heads([attended_grad], [], heads_local, members, 5)
    head_query_grad, head_key_grad, head_value_grad = attend_back(
        head_queries, head_shared, head_grad, exact_mix, log_total, *plan, members, blocks_each
    )
    out_weight_part = contract_first(branch_rows_one, attended_low).astype(jnp.bfloat16)
    input_grad, sums_one, weight_grads, out_weight_grad, columns = finish_back(
        head_query_grad, head_key_grad, head_value_grad, projections, rows_one, residual_grad, hidden_in, gain_one,
        out_weight_part, heads_local, members, 7,
    )
    key_weight_grad, value_weight_grad, query_weight_grad = (
        weight_grads[:, k * head_width : (k + 1) * head_width] for k in range(3)
    )

    def column_sums(values):
        return jnp.sum(values.astype(jnp.float32), axis=0)

    def placed(values):
        whole = jnp.zeros((values.shape[0] * mp_count,), jnp.float32)
        return lax.dynamic_update_slice_in_dim(whole, values, mp_index * values.shape[0], 0)

    sums = (
        sums_one[0], sums_one[1], placed(columns[0, 2 * head_width :]), placed(columns[0, head_width : 2 * head_width]), sums_two[2],
        sums_two[0], sums_two[1], column_sums(branch_two), placed(column_sums(pre_grad)),
    )
    packed = jnp.concatenate([v.reshape(dp_count, -1, 128) for v in sums], axis=1)
    packed = jnp.pad(packed, ((0, 0), (0, -packed.shape[1] % 8), (0, 0)))
    summed = sum_vectors(packed, 8)
    vector_grads = [summed[k * each : (k + 1) * each].reshape(-1) for k in range(8)]
    up_bias_grad = summed[8 * each : 8 * each + up_each].reshape(-1)
    return (
        output,
        input_grad,
        vector_grads[0],
        vector_grads[1],
        query_weight_grad,
        vector_grads[2],
        key_weight_grad,
        value_weight_grad,
        vector_grads[3],
        out_weight_grad,
        vector_grads[4],
        vector_grads[5],
        vector_grads[6],
        up_weight_grad,
        up_bias_grad,
        down_weight_grad,
        vector_grads[7],
    )


def solution(mesh):
    return jax.shard_map(
        per_device,
        mesh=mesh,
        in_specs=(
            P(("dp", "mp"), None),
            P(("dp", "mp"), None),
            P("dp"),
            P("dp"),
            P("dp", "mp"),
            P("dp"),
            P("dp", "mp"),
            P("dp", "mp"),
            P("dp"),
            P("dp", "mp"),
            P("dp"),
            P("dp"),
            P("dp"),
            P("dp", "mp"),
            P("dp"),
            P("dp", "mp"),
            P("dp"),
            P(),
            P(),
            P(),
        ),
        out_specs=(
            P(("dp", "mp"), None),
            P(("dp", "mp"), None),
            P("dp"),
            P("dp"),
            P("dp", "mp"),
            P("dp"),
            P("dp", "mp"),
            P("dp", "mp"),
            P("dp"),
            P("dp", "mp"),
            P("dp"),
            P("dp"),
            P("dp"),
            P("dp", "mp"),
            P("dp"),
            P("dp", "mp"),
            P("dp"),
        ),
        check_vma=False,
    )
```

```python
import functools
import math

import jax
import jax.numpy as jnp
from jax import lax
from jax.experimental import pallas as pl
from jax.experimental.pallas import tpu as pltpu
from jax.sharding import PartitionSpec as P

HEAD_DIM = 128
BLOCK = 128
KEY_BLOCKS = 8
MESH = pl.DeviceIdType.MESH
ANY = pl.BlockSpec(memory_space=pl.ANY)
VMEM = pl.BlockSpec(memory_space=pltpu.VMEM)
SMEM = pl.BlockSpec(memory_space=pltpu.SMEM)
MIB = 1 << 20


big_negative = -1e30
norm_epsilon = 1e-05


def norm_back(upstream, normed, inverse, gain_row):
    scaled = upstream * gain_row
    mean_grad = jnp.mean(scaled, axis=-1, keepdims=True)
    second = jnp.mean(scaled * normed, axis=-1, keepdims=True)
    return inverse * (scaled - mean_grad - normed * second)


def contract_last(left, right):
    return lax.dot_general(
        left, right, (((1,), (1,)), ((), ())), preferred_element_type=jnp.float32
    )


def contract_first(left, right):
    return lax.dot_general(
        left, right, (((0,), (0,)), ((), ())), preferred_element_type=jnp.float32
    )


def whole_rows(local_part):
    return lax.all_gather(local_part, "mp", axis=0, tiled=True)


def row_share(term):
    term = term.astype(jnp.bfloat16)
    return lax.psum_scatter(term, "mp", scatter_dimension=0, tiled=True).astype(jnp.float32)


def greet(peers):
    barrier = pltpu.get_barrier_semaphore()
    for peer in peers:
        pl.semaphore_signal(barrier, inc=1, device_id=peer, device_id_type=MESH)
    pl.semaphore_wait(barrier, len(peers))


def remote(src, dst, send_sem, recv_sem, peer):
    return pltpu.make_async_remote_copy(
        src_ref=src, dst_ref=dst, send_sem=send_sem, recv_sem=recv_sem,
        device_id=peer, device_id_type=MESH,
    )


def head_place(heads, members):
    me = lax.axis_index("dp")
    return me, me // members, me % members, lax.axis_index("mp")


def lanes(head):
    return pl.ds(pl.multiple_of(head * HEAD_DIM, HEAD_DIM), HEAD_DIM)


def to_heads(owned, shared, heads, members, collective_id):
    rows = (owned + shared)[0].shape[0]
    n_owned, n_shared = len(owned), len(shared)
    count = n_owned + n_shared

    def kernel(*refs):
        ins, outs = refs[:count], refs[count : 2 * count]
        local_sem, send_sem, recv_sem, fwd_send, fwd_recv = refs[2 * count :]
        me, group, member, mp = head_place(heads, members)

        def dest(array, source):
            place = (source // members) if array < n_owned else source
            return outs[array].at[pl.ds(pl.multiple_of(place * rows, rows), rows)]

        head_peers = [((group ^ o) * members + member, mp) for o in range(1, heads)]
        pair_peers = [(group * members + (member ^ o), mp) for o in range(1, members)]
        greet(head_peers + pair_peers)
        order = list(range(n_owned, count)) + list(range(n_owned))
        sends, locals_, forwards = {}, [], []
        for a in order:
            for o in range(1, heads):
                copy = remote(ins[a].at[:, lanes(group ^ o)], dest(a, me), send_sem.at[a, o],
                              recv_sem.at[a, o], head_peers[o - 1])
                copy.start()
                sends[a, o] = copy
        for a in range(count):
            copy = pltpu.make_async_copy(ins[a].at[:, lanes(group)], dest(a, me), local_sem.at[a])
            copy.start()
            locals_.append(copy)
        for a in range(n_owned, count):
            for o in range(heads):
                source = (group ^ o) * members + member
                if o:
                    sends[a, o].wait_recv()
                for p in range(1, members):
                    piece = ins[a].at[:, lanes(group)] if o == 0 else dest(a, source)
                    copy = remote(piece, dest(a, source), fwd_send.at[a - n_owned, o, p],
                                  fwd_recv.at[a - n_owned, o, p], pair_peers[p - 1])
                    copy.start()
                    forwards.append(copy)
        for copy in locals_:
            copy.wait()
        for (a, o), copy in sends.items():
            copy.wait_send()
            if a < n_owned:
                copy.wait_recv()
        for copy in forwards:
            copy.wait()

    total = rows * lax.axis_size("dp")
    shapes = [jax.ShapeDtypeStruct((heads * rows, HEAD_DIM), a.dtype) for a in owned]
    shapes += [jax.ShapeDtypeStruct((total, HEAD_DIM), a.dtype) for a in shared]
    dma = pltpu.SemaphoreType.DMA
    return pl.pallas_call(
        kernel,
        out_shape=shapes,
        in_specs=[ANY] * count,
        out_specs=[ANY] * count,
        scratch_shapes=[
            dma((count,)), dma((count, heads)), dma((count, heads)),
            dma((max(n_shared, 1), heads, members)), dma((max(n_shared, 1), heads, members)),
        ],
        compiler_params=pltpu.CompilerParams(collective_id=collective_id, has_side_effects=True),
        cost_estimate=pl.CostEstimate(flops=0, bytes_accessed=100 * MIB, transcendentals=0),
    )(*owned, *shared)


def to_rows(owned, shared, heads, members, collective_id):
    rows = owned[0].shape[0] // heads
    n_owned, n_shared = len(owned), len(shared)
    count = n_owned + n_shared

    def kernel(*refs):
        ins, outs = refs[:count], refs[count : 2 * count]
        local_sem, send_sem, recv_sem, own_sem, part_send, part_recv = refs[2 * count : 2 * count + 6]
        me, group, member, mp = head_place(heads, members)
        head_peers = [((group ^ o) * members + member, mp) for o in range(1, heads)]
        pair_peers = [(group * members + (member ^ o), mp) for o in range(1, members)]
        greet(head_peers + pair_peers)
        if n_shared:
            own, parts, total = refs[2 * count + 6 :]
        copies, pending = [], {}

        def part(array, o, who):
            first = pl.multiple_of(((group ^ o) * members + who) * rows, rows)
            return ins[array].at[pl.ds(first, rows)]

        for s in range(n_shared):
            for o in range(heads):
                copy = pltpu.make_async_copy(part(n_owned + s, o, member), own.at[s, o], own_sem.at[s, o])
                copy.start()
                pending[s, o, 0] = copy
                for p in range(1, members):
                    copy = remote(part(n_owned + s, o, member ^ p), parts.at[s, o, p - 1],
                                  part_send.at[s, o, p], part_recv.at[s, o, p], pair_peers[p - 1])
                    copy.start()
                    pending[s, o, p] = copy
        for a in range(n_owned):
            for o in range(heads):
                piece = ins[a].at[pl.ds(pl.multiple_of((group ^ o) * rows, rows), rows)]
                place = outs[a].at[:, lanes(group)]
                if o:
                    copy = remote(piece, place, send_sem.at[a, o], recv_sem.at[a, o], head_peers[o - 1])
                else:
                    copy = pltpu.make_async_copy(piece, place, local_sem.at[a])
                copy.start()
                copies.append(copy)
        for o in list(range(1, heads)) + [0]:
            for s in range(n_shared):
                for p in range(members):
                    if p:
                        pending[s, o, p].wait_recv()
                    else:
                        pending[s, o, p].wait()
                value = own[s, o].astype(jnp.float32)
                for p in range(1, members):
                    value = value + parts[s, o, p - 1].astype(jnp.float32)
                total[s, o] = value.astype(total.dtype)
                a = n_owned + s
                place = outs[a].at[:, lanes(group)]
                if o:
                    copy = remote(total.at[s, o], place, send_sem.at[a, o], recv_sem.at[a, o], head_peers[o - 1])
                else:
                    copy = pltpu.make_async_copy(total.at[s, o], place, local_sem.at[a])
                copy.start()
                copies.append(copy)
        for s in range(n_shared):
            for o in range(heads):
                for p in range(1, members):
                    pending[s, o, p].wait_send()
        for copy in copies:
            copy.wait()

    dma = pltpu.SemaphoreType.DMA
    slots = max(n_shared, 1)
    scratch = [
        dma((count,)), dma((count, heads)), dma((count, heads)),
        dma((slots, heads)), dma((slots, heads, members)), dma((slots, heads, members)),
    ]
    if n_shared:
        kind = shared[0].dtype
        scratch += [
            pltpu.VMEM((n_shared, heads, rows, HEAD_DIM), kind),
            pltpu.VMEM((n_shared, heads, members - 1, rows, HEAD_DIM), kind),
            pltpu.VMEM((n_shared, heads, rows, HEAD_DIM), kind),
        ]
    return pl.pallas_call(
        kernel,
        out_shape=[jax.ShapeDtypeStruct((rows, heads * HEAD_DIM), a.dtype) for a in owned + shared],
        in_specs=[ANY] * count,
        out_specs=[ANY] * count,
        scratch_shapes=scratch,
        compiler_params=pltpu.CompilerParams(
            collective_id=collective_id, has_side_effects=True, vmem_limit_bytes=48 * MIB
        ),
        cost_estimate=pl.CostEstimate(flops=0, bytes_accessed=100 * MIB, transcendentals=0),
    )(*owned, *shared)


def sequence_of(place, lengths):
    first, length, running = jnp.int32(0), jnp.int32(0), jnp.int32(0)
    for s in range(lengths.shape[0]):
        inside = place >= running
        first = jnp.where(inside, running, first)
        length = jnp.where(inside, lengths[s], length)
        running = running + (lengths[s] + (BLOCK - 1)) // BLOCK
    return first, length - (place - first) * BLOCK


def list_queries(slot, index_list, place_list, members, blocks_each):
    member = lax.axis_index("dp") % members

    def visit(block, count):
        dealt = slot[block]
        owner = dealt // blocks_each

        @pl.when(owner % members == member)
        def _():
            index_list[count] = (owner // members) * blocks_each + dealt % blocks_each
            place_list[count] = block

        return count + (owner % members == member).astype(jnp.int32)

    lax.fori_loop(0, slot.shape[0], visit, jnp.int32(0))


def block_rows(block):
    return pl.ds(pl.multiple_of(block * BLOCK, BLOCK), BLOCK)


class QueryPair:
    def __init__(self, pair, lengths, index_list, place_list):
        self.index = [index_list[2 * pair + i] for i in range(2)]
        self.place = [place_list[2 * pair + i] for i in range(2)]
        found = [sequence_of(place, lengths) for place in self.place]
        self.start = found[0][0]
        lane = lax.broadcasted_iota(jnp.int32, (1, 2 * BLOCK), 1)
        right = lane >= BLOCK

        def lanes_of(left_value, right_value):
            return jnp.where(right, right_value, left_value)

        within = lane - lanes_of(0, BLOCK)
        base = self.start * BLOCK
        self.position = lanes_of(self.place[0], self.place[1]) * BLOCK + within - base
        self.lowest = lanes_of(found[0][0], found[1][0]) * BLOCK - base
        self.live = within < lanes_of(found[0][1], found[1][1])
        self.tiles = (self.place[1] - self.start) // KEY_BLOCKS + 1
        self.open_tiles = jnp.where(found[0][0] == found[1][0], (self.place[0] - self.start) // KEY_BLOCKS, 0)

    def row(self, tile):
        return pl.multiple_of((self.start + tile * KEY_BLOCKS) * BLOCK, BLOCK)

    def allowed(self, tile):
        width = KEY_BLOCKS * BLOCK
        key = lax.broadcasted_iota(jnp.int32, (width, 2 * BLOCK), 0)
        return (key <= self.position - tile * width) & (key >= self.lowest - tile * width)

    def load_t(self, ref):
        return jnp.concatenate([ref[block_rows(index)].T for index in self.index], axis=1)

    def load(self, ref):
        return jnp.concatenate([ref[block_rows(index)] for index in self.index], axis=0)

    def store_t(self, ref, value_t):
        for i, index in enumerate(self.index):
            ref[block_rows(index)] = value_t[:, i * BLOCK : (i + 1) * BLOCK].T.astype(ref.dtype)


def attend(queries, shared, lengths, order, slot, members, blocks_each):
    pairs, key_count = queries.shape[0] // (2 * BLOCK), shared.shape[1] // BLOCK
    width = KEY_BLOCKS * BLOCK
    padded = (key_count + KEY_BLOCKS - 1) * BLOCK
    scale = math.log2(math.e) / math.sqrt(HEAD_DIM)

    def kernel(lengths_ref, slot_ref, q_ref, shared_ref, out_ref, exact_ref, log_ref,
               index_list, place_list, keys, values_t):
        list_queries(slot_ref, index_list, place_list, members, blocks_each)

        @pl.loop(0, key_count)
        def _(block):
            source = block_rows(slot_ref[block])
            keys[block_rows(block)] = shared_ref[0, source]
            values_t[:, block_rows(block)] = shared_ref[1, source].T

        tail = pl.ds(key_count * BLOCK, padded - key_count * BLOCK)
        keys[tail] = jnp.zeros((padded - key_count * BLOCK, HEAD_DIM), keys.dtype)
        values_t[:, tail] = jnp.zeros((HEAD_DIM, padded - key_count * BLOCK), keys.dtype)

        @pl.loop(0, pairs)
        def _(index):
            pair = QueryPair(index, lengths_ref, index_list, place_list)
            query_t = pair.load_t(q_ref)

            def step(tile, carry, masked):
                top, total, mix = carry
                span = pl.ds(pair.row(tile), width)
                scores = jnp.dot(keys[span], query_t, preferred_element_type=jnp.float32)
                if masked:
                    scores = jnp.where(pair.allowed(tile), scores, big_negative)
                new_top = jnp.maximum(top, jnp.max(scores, axis=0, keepdims=True))
                weights = jnp.exp2((scores - new_top) * scale)
                fade = jnp.exp2((top - new_top) * scale)
                total = total * fade + jnp.sum(weights, axis=0, keepdims=True)
                mix = mix * fade + jnp.dot(
                    values_t[:, span], weights.astype(jnp.bfloat16), preferred_element_type=jnp.float32)
                return new_top, total, mix

            carry = (jnp.full((1, 2 * BLOCK), big_negative, jnp.float32), jnp.zeros((1, 2 * BLOCK), jnp.float32),
                     jnp.zeros((HEAD_DIM, 2 * BLOCK), jnp.float32))
            carry = lax.fori_loop(0, pair.open_tiles, lambda tile, c: step(tile, c, False), carry)
            top, total, mix = lax.fori_loop(pair.open_tiles, pair.tiles, lambda tile, c: step(tile, c, True), carry)
            mix = jnp.where(pair.live, mix / total, 0.0)
            exact_ref[index] = mix
            pair.store_t(out_ref, mix)
            log_ref[index] = jnp.where(pair.live, top * scale + jnp.log2(total), -big_negative)

    return pl.pallas_call(
        kernel,
        out_shape=[
            jax.ShapeDtypeStruct(queries.shape, jnp.bfloat16),
            jax.ShapeDtypeStruct((pairs, HEAD_DIM, 2 * BLOCK), jnp.float32),
            jax.ShapeDtypeStruct((pairs, 1, 2 * BLOCK), jnp.float32),
        ],
        in_specs=[SMEM] * 2 + [VMEM] * 2,
        out_specs=[VMEM] * 3,
        scratch_shapes=[
            pltpu.SMEM((2 * pairs,), jnp.int32), pltpu.SMEM((2 * pairs,), jnp.int32),
            pltpu.VMEM((padded, HEAD_DIM), jnp.bfloat16), pltpu.VMEM((HEAD_DIM, padded), jnp.bfloat16),
        ],
        compiler_params=pltpu.CompilerParams(vmem_limit_bytes=56 * MIB),
        cost_estimate=pl.CostEstimate(flops=8 << 30, bytes_accessed=50 * MIB, transcendentals=8 << 20),
    )(lengths, slot, queries, shared)


def attend_back(queries, shared, upstream, exact, logs, lengths, order, slot, members, blocks_each):
    pairs, key_count = queries.shape[0] // (2 * BLOCK), shared.shape[1] // BLOCK
    width = KEY_BLOCKS * BLOCK
    padded = (key_count + KEY_BLOCKS - 1) * BLOCK
    scale = math.log2(math.e) / math.sqrt(HEAD_DIM)
    plain_scale = 1.0 / math.sqrt(HEAD_DIM)

    def kernel(lengths_ref, slot_ref, q_ref, shared_ref, g_ref, exact_ref, log_ref, dq_ref, dk_ref, dv_ref,
               index_list, place_list, keys, keys_t, values, key_sum, value_sum):
        list_queries(slot_ref, index_list, place_list, members, blocks_each)

        @pl.loop(0, key_count)
        def _(block):
            source, to = block_rows(slot_ref[block]), block_rows(block)
            rows = shared_ref[0, source]
            keys[to] = rows
            keys_t[:, to] = rows.T
            values[to] = shared_ref[1, source]
            key_sum[to] = jnp.zeros((BLOCK, HEAD_DIM), jnp.float32)
            value_sum[to] = jnp.zeros((BLOCK, HEAD_DIM), jnp.float32)

        tail = pl.ds(key_count * BLOCK, padded - key_count * BLOCK)
        keys[tail] = jnp.zeros((padded - key_count * BLOCK, HEAD_DIM), keys.dtype)
        values[tail] = jnp.zeros((padded - key_count * BLOCK, HEAD_DIM), keys.dtype)
        keys_t[:, tail] = jnp.zeros((HEAD_DIM, padded - key_count * BLOCK), keys.dtype)
        key_sum[tail] = jnp.zeros((padded - key_count * BLOCK, HEAD_DIM), jnp.float32)
        value_sum[tail] = jnp.zeros((padded - key_count * BLOCK, HEAD_DIM), jnp.float32)

        @pl.loop(0, pairs)
        def _(index):
            pair = QueryPair(index, lengths_ref, index_list, place_list)
            query, grad = pair.load(q_ref), pair.load(g_ref)
            query_t, grad_t = pair.load_t(q_ref), pair.load_t(g_ref)
            delta = jnp.sum(grad_t.astype(jnp.float32) * exact_ref[index], axis=0, keepdims=True)
            log_total = log_ref[index]

            def step(tile, query_grad, masked):
                span = pl.ds(pair.row(tile), width)
                scores = jnp.dot(keys[span], query_t, preferred_element_type=jnp.float32)
                probability = jnp.exp2(scores * scale - log_total)
                if masked:
                    probability = jnp.where(pair.allowed(tile), probability, 0.0)
                prob_grad = jnp.dot(values[span], grad_t, preferred_element_type=jnp.float32)
                score_grad = (probability * (prob_grad - delta)).astype(jnp.bfloat16)
                value_sum[span] += jnp.dot(
                    probability.astype(jnp.bfloat16), grad, preferred_element_type=jnp.float32)
                key_sum[span] += jnp.dot(score_grad, query, preferred_element_type=jnp.float32)
                return query_grad + jnp.dot(keys_t[:, span], score_grad, preferred_element_type=jnp.float32)

            query_grad = jnp.zeros((HEAD_DIM, 2 * BLOCK), jnp.float32)
            query_grad = lax.fori_loop(0, pair.open_tiles, lambda tile, c: step(tile, c, False), query_grad)
            query_grad = lax.fori_loop(pair.open_tiles, pair.tiles, lambda tile, c: step(tile, c, True), query_grad)
            pair.store_t(dq_ref, query_grad * plain_scale)

        @pl.loop(0, key_count)
        def _(block):
            at, dealt = block_rows(block), block_rows(slot_ref[block])
            dk_ref[dealt] = (key_sum[at] * plain_scale).astype(dk_ref.dtype)
            dv_ref[dealt] = value_sum[at].astype(dv_ref.dtype)

    return pl.pallas_call(
        kernel,
        out_shape=[
            jax.ShapeDtypeStruct(queries.shape, jnp.bfloat16),
            jax.ShapeDtypeStruct(shared.shape[1:], jnp.bfloat16),
            jax.ShapeDtypeStruct(shared.shape[1:], jnp.bfloat16),
        ],
        in_specs=[SMEM] * 2 + [VMEM] * 5,
        out_specs=[VMEM] * 3,
        scratch_shapes=[
            pltpu.SMEM((2 * pairs,), jnp.int32), pltpu.SMEM((2 * pairs,), jnp.int32),
            pltpu.VMEM((padded, HEAD_DIM), jnp.bfloat16),
            pltpu.VMEM((HEAD_DIM, padded), jnp.bfloat16),
            pltpu.VMEM((padded, HEAD_DIM), jnp.bfloat16),
            pltpu.VMEM((padded, HEAD_DIM), jnp.float32),
            pltpu.VMEM((padded, HEAD_DIM), jnp.float32),
        ],
        compiler_params=pltpu.CompilerParams(vmem_limit_bytes=60 * MIB),
        cost_estimate=pl.CostEstimate(flops=20 << 30, bytes_accessed=100 * MIB, transcendentals=8 << 20),
    )(lengths, slot, queries, shared, upstream, exact, logs)


def line_neighbours(mp, count):
    return ((1, mp + 1 < count, jnp.minimum(mp + 1, count - 1)), (-1, mp >= 1, jnp.maximum(mp - 1, 0)))


def greet_all(fixed, dp, mp, count):
    barrier = pltpu.get_barrier_semaphore()
    for peer in fixed:
        pl.semaphore_signal(barrier, inc=1, device_id=peer, device_id_type=MESH)
    expected = jnp.int32(len(fixed))
    for _, there, place in line_neighbours(mp, count):

        @pl.when(there)
        def _():
            pl.semaphore_signal(barrier, inc=1, device_id=(dp, place), device_id_type=MESH)

        expected = expected + there.astype(jnp.int32)
    pl.semaphore_wait(barrier, expected)


class LineGather:
    def __init__(self, own, full, rows, pieces, send_sem, recv_sem, dp, mp, count):
        self.own, self.full, self.rows, self.pieces = own, full, rows, pieces
        self.send_sem, self.recv_sem, self.dp, self.mp, self.count = send_sem, recv_sem, dp, mp, count
        self.size = rows // pieces

    def place(self, block, piece):
        return self.full.at[pl.ds(pl.multiple_of(block * self.rows + piece * self.size, self.size), self.size)]

    def hop(self, way, step, piece):
        sign, there, neighbour = line_neighbours(self.mp, self.count)[way]
        origin = self.mp - sign * step
        exists = (origin >= 0) & (origin < self.count)
        origin = jnp.clip(origin, 0, self.count - 1)
        if step == 0:
            source = self.own.at[pl.ds(pl.multiple_of(piece * self.size, self.size), self.size)]
        else:
            source = self.place(origin, piece)
        def copy():
            return remote(source, self.place(origin, piece), self.send_sem.at[way, step, piece],
                          self.recv_sem.at[way, step, piece], (self.dp, neighbour))

        return exists, exists & there, copy

    def advance(self, step, piece, also=True):
        for way in range(2):
            if step:
                exists, _, _ = self.hop(way, step, piece)
                _, _, earlier = self.hop(way, step - 1, piece)

                @pl.when(exists & also)
                def _():
                    earlier().wait_recv()

            if step < self.count - 1:
                _, sends, copy = self.hop(way, step, piece)

                @pl.when(sends & also)
                def _():
                    copy().start()

    def finish(self):
        @pl.loop(0, self.pieces)
        def _(piece):
            for way in range(2):
                for step in range(self.count - 1):
                    _, sends, copy = self.hop(way, step, piece)

                    @pl.when(sends)
                    def _():
                        copy().wait_send()

    @staticmethod
    def semaphores(count, pieces):
        return [pltpu.SemaphoreType.DMA((2, count, pieces)), pltpu.SemaphoreType.DMA((2, count, pieces))]


class ShardGather:
    def __init__(self, shards, wholes, depth, cross_send, cross_recv, core_send, core_recv, own_sem, dp, mp, chips):
        self.shards, self.wholes, self.depth, self.own_sem = shards, wholes, depth, own_sem
        self.cross_send, self.cross_recv, self.core_send, self.core_recv = cross_send, cross_recv, core_send, core_recv
        self.dp, self.mp, self.chips = dp, mp, chips

    def place(self, array, owner):
        return self.wholes[array].at[pl.ds(pl.multiple_of(owner * self.depth, self.depth), self.depth)]

    def cross(self, array, o):
        return remote(self.shards[array], self.place(array, self.dp), self.cross_send.at[array, o],
                      self.cross_recv.at[array, o], (self.dp ^ (2 * o), self.mp))

    def core(self, array, o):
        owner = self.dp ^ (2 * o)
        source = self.place(array, owner) if o else self.shards[array]
        return remote(source, self.place(array, owner), self.core_send.at[array, o], self.core_recv.at[array, o],
                      (self.dp ^ 1, self.mp))

    def own(self, array):
        return pltpu.make_async_copy(self.shards[array], self.place(array, self.dp), self.own_sem.at[array])

    def begin(self):
        for array in range(len(self.shards)):
            for o in range(1, self.chips):
                self.cross(array, o).start()
        for array in range(len(self.shards)):
            self.own(array).start()
            self.core(array, 0).start()

    def spread(self, array):
        for o in range(1, self.chips):
            self.cross(array, o).wait_recv()
            self.core(array, o).start()

    def finish(self):
        for array in range(len(self.shards)):
            self.own(array).wait()
            for o in range(self.chips):
                self.core(array, o).wait()
                if o:
                    self.cross(array, o).wait_send()

    @staticmethod
    def semaphores(count, chips):
        return [pltpu.SemaphoreType.DMA((count, chips)) for _ in range(4)] + [pltpu.SemaphoreType.DMA((count,))]


class LineReduce:
    def __init__(self, part, flows, rows, pieces, send_sem, recv_sem, dp, mp, count):
        self.part, self.flows, self.rows, self.pieces = part, flows, rows, pieces
        self.send_sem, self.recv_sem, self.dp, self.mp, self.count = send_sem, recv_sem, dp, mp, count
        self.size = rows // pieces

    def span(self, block, piece):
        return pl.ds(pl.multiple_of(block * self.rows + piece * self.size, self.size), self.size)

    def hop(self, way, block, piece, first=False):
        neighbour = line_neighbours(self.mp, self.count)[way][2]
        span = self.span(block, piece)
        source = self.part.at[span] if first else self.flows.at[way, span]
        return remote(source, self.flows.at[way, span], self.send_sem.at[way, block, piece],
                      self.recv_sem.at[way, block, piece], (self.dp, neighbour))

    def roles(self, way, block):
        if way == 0:
            behind, ahead = self.mp >= 1, self.mp < block
        else:
            behind, ahead = self.mp < self.count - 1, self.mp > block
        return ahead & jnp.logical_not(behind), ahead & behind

    def targets(self):
        for index in range(self.count - 1):
            yield 0, self.count - 1 - index
            yield 1, index

    def begin(self, piece, also=True):
        for way, block in self.targets():
            begins, _ = self.roles(way, block)

            @pl.when(begins & also)
            def _():
                self.hop(way, block, piece, True).start()

    def advance(self, turn):
        for way, block in self.targets():
            _, hands_on = self.roles(way, block)
            passed = SKEW * (self.mp - 1 if way == 0 else self.count - 2 - self.mp)
            piece = jnp.clip(turn - passed, 0, self.pieces - 1)

            @pl.when(hands_on & (turn >= passed) & (turn - passed < self.pieces))
            def _():
                self.hop(way, block, piece).wait_recv()
                span = self.span(block, piece)
                value = self.flows[way, span].astype(jnp.float32) + self.part[span].astype(jnp.float32)
                self.flows[way, span] = value.astype(self.flows.dtype)
                self.hop(way, block, piece).start()

    def arrive(self, piece):
        for way in range(2):

            @pl.when(self.mp >= 1 if way == 0 else self.mp < self.count - 1)
            def _():
                self.hop(way, self.mp, piece).wait_recv()

    def total(self, piece, result):
        span = self.span(self.mp, piece)
        result[...] = self.part[span].astype(jnp.float32)
        for way in range(2):

            @pl.when(self.mp >= 1 if way == 0 else self.mp < self.count - 1)
            def _():
                result[...] += self.flows[way, span].astype(jnp.float32)

    def finish(self):
        @pl.loop(0, self.pieces)
        def _(piece):
            for way, block in self.targets():
                begins, hands_on = self.roles(way, block)

                @pl.when(begins)
                def _():
                    self.hop(way, block, piece, True).wait_send()

                @pl.when(hands_on)
                def _():
                    self.hop(way, block, piece).wait_send()

    @staticmethod
    def scratch(count, rows, width, pieces):
        return [pltpu.VMEM((2, count * rows, width), jnp.bfloat16),
                pltpu.SemaphoreType.DMA((2, count, pieces)), pltpu.SemaphoreType.DMA((2, count, pieces))]


AHEAD = 1
MAX_PIECES = 16
SKEW = 1


def pieces_of(rows):
    return min(MAX_PIECES, rows // 16)


def unit_rows(values):
    average = jnp.mean(values, axis=-1, keepdims=True)
    centred = values - average
    inverse = lax.rsqrt(jnp.mean(centred * centred, axis=-1, keepdims=True) + norm_epsilon)
    return centred * inverse, inverse


def project_first(
    hidden, output_grad, lengths, order, vectors, projections, out_weight, heads, members, collective_id
):
    rows, width = hidden.shape
    dp_count, mp_count = lax.axis_size("dp"), lax.axis_size("mp")
    chips, pieces = dp_count // 2, pieces_of(rows)
    group_rows, depth, columns = mp_count * rows, projections[0].shape[0], projections[0].shape[1]
    each = width // dp_count // 128
    tall = [v.shape[0] // 128 for v in vectors]
    slab = sum(tall) + -sum(tall) % 8
    halves, kinds = heads // 2, 3
    arrays = kinds + 2
    offsets = sorted({2 * o for o in range(1, chips)} | {o for o in range(1, members)} | {o * members for o in range(1, heads)})

    def kernel(lengths_ref, order_ref, hidden_ref, upstream_ref, *refs):
        given, refs = refs[: len(vectors)], refs[len(vectors) :]
        weight_refs, out_weight_ref = refs[:kinds], refs[kinds]
        normed, all_vectors, weights, all_out, shared, queries, branch, live = refs[kinds + 1 : kinds + 9]
        parts, refs = refs[-len(vectors) :], refs[: -len(vectors)]
        (vector_ref, upstream, load_sem, raw, stage, gains, biases, line_send, line_recv, row_sem, own_sem, cross_send, cross_recv, core_send, core_recv,
         head_local, head_send, head_recv, pair_send, pair_recv) = refs[kinds + 9 :]
        dp, mp = lax.axis_index("dp"), lax.axis_index("mp")
        loads = [pltpu.make_async_copy(given[k], parts[k], load_sem.at[k]) for k in range(len(vectors))]
        loads.append(pltpu.make_async_copy(upstream_ref, upstream, load_sem.at[len(vectors)]))
        for copy in loads:
            copy.start()
        vector_ref[...] = jnp.zeros_like(vector_ref)
        for copy in loads:
            copy.wait()
        first = 0
        for part, count in zip(parts, tall):
            for r in range(count):
                vector_ref[first + r] = part[r * 128 : (r + 1) * 128].astype(jnp.float32)
            first += count
        group, member = dp // members, dp % members
        partner = (dp ^ 1, mp)
        greet_all([(dp ^ o, mp) for o in offsets], dp, mp, mp_count)
        line = LineGather(hidden_ref, raw, rows, pieces, line_send, line_recv, dp, mp, mp_count)

        def source(array):
            return (list(weight_refs) + [out_weight_ref, vector_ref])[array]

        def place(array, owner):
            if array < kinds:
                return weights.at[pl.ds(pl.multiple_of(owner * depth, depth), depth), pl.ds(array * columns, columns)]
            if array == kinds:
                return all_out.at[pl.ds(pl.multiple_of(owner * depth, depth), depth)]
            return all_vectors.at[pl.ds(pl.multiple_of(owner * slab, slab), slab)]

        def cross(array, o):
            return remote(source(array), place(array, dp), cross_send.at[array, o], cross_recv.at[array, o],
                          (dp ^ (2 * o), mp))

        def core(array, o):
            owner = dp ^ (2 * o)
            return remote(place(array, owner) if o else source(array), place(array, owner),
                          core_send.at[array, o], core_recv.at[array, o], partner)

        def own(array):
            return pltpu.make_async_copy(source(array), place(array, dp), own_sem.at[array])

        def block_span(block):
            return pl.ds(pl.multiple_of(block * rows, rows), rows)

        first_to_last = [kinds + 1] + list(range(kinds + 1))
        for array in first_to_last:
            for o in range(1, chips):
                cross(array, o).start()
            if array == first_to_last[0]:

                @pl.loop(0, pieces)
                def _(piece):
                    line.advance(0, piece)

        for block in range(rows // BLOCK):
            found = order_ref[(dp * group_rows + mp * rows) // BLOCK + block]
            valid = sequence_of(found, lengths_ref)[1]
            span = slice(block * BLOCK, (block + 1) * BLOCK)
            live[span] = (lax.broadcasted_iota(jnp.int32, (BLOCK, 128), 0) < valid).astype(jnp.float32)
            keep = lax.broadcasted_iota(jnp.int32, (BLOCK, width), 0) < valid
            branch[span] = jnp.where(keep, upstream[span].astype(jnp.float32), 0.0).astype(branch.dtype)
        own_rows = pltpu.make_async_copy(hidden_ref, raw.at[block_span(mp)], row_sem)
        own_rows.start()
        for array in first_to_last:
            own(array).start()
            core(array, 0).start()

        def spread(array):
            for o in range(1, chips):
                cross(array, o).wait_recv()
                core(array, o).start()

        def settle(array):
            own(array).wait()
            for o in range(chips):
                core(array, o).wait_recv()

        def norm(block):
            chunk = 64

            @pl.loop(0, rows // chunk)
            def _(part):
                span = pl.ds(pl.multiple_of(block * rows + part * chunk, chunk), chunk)
                unit, _ = unit_rows(raw[span].astype(jnp.float32))
                normed[span] = (unit * gains[0:1] + gains[1:2]).astype(normed.dtype)

        def each_block(low, high, visit):
            @pl.loop(0, mp_count)
            def _(block):
                distance = jnp.abs(block - mp)

                @pl.when((distance >= low) & (distance <= high))
                def _():
                    visit(block)

        def rows_of(kind_ref, owner, block):
            return kind_ref.at[pl.ds(pl.multiple_of(owner * group_rows + block * rows, rows), rows)]

        def pass_on(kind, o, block, piece):
            giver = (group ^ o) * members + member
            return [remote(piece, rows_of(shared.at[kind], giver, block), pair_send.at[kind, o, block, p - 1],
                           pair_recv.at[kind, o, block, p - 1], (group * members + (member ^ p), mp))
                    for p in range(1, members)]

        def head_copy(kind, o, block, to_shared):
            target = group ^ o
            piece = stage.at[kind, block, target]
            landing = rows_of(shared.at[kind], dp, block) if to_shared else rows_of(queries, group, block)
            return remote(piece, landing, head_send.at[kind, o, block], head_recv.at[kind, o, block],
                          (target * members + member, mp))

        def local_copy(kind, block, to_shared):
            landing = rows_of(shared.at[kind], dp, block) if to_shared else rows_of(queries, group, block)
            return pltpu.make_async_copy(stage.at[kind, block, group], landing, head_local.at[kind, block])

        def project(tile, block):
            kind, half = tile // halves, tile % halves
            span = pl.ds(pl.multiple_of(half * 256, 256), 256)
            across = pl.ds(pl.multiple_of(kind * columns + half * 256, 256), 256)
            value = jnp.dot(normed[block_span(block)], weights[:, across], preferred_element_type=jnp.float32)
            value = (value + biases[pl.ds(kind, 1), span]).astype(stage.dtype)
            for h in range(2):
                head = 2 * half + h
                stage[kind, block, head] = value[:, h * HEAD_DIM : (h + 1) * HEAD_DIM]
            for h in range(2):
                o = (2 * half + h) ^ group
                for to_shared in (True, False):
                    chosen = (kind < 2) if to_shared else (kind == 2)

                    @pl.when(chosen & (o != 0))
                    def _():
                        head_copy(kind, o, block, to_shared).start()

                    @pl.when(chosen & (o == 0))
                    def _():
                        local_copy(kind, block, to_shared).start()
                        if to_shared:
                            for copy in pass_on(kind, 0, block, stage.at[kind, block, group]):
                                copy.start()

        def hand_on(block):
            @pl.loop(0, 2)
            def _(kind):
                for o in range(1, heads):
                    head_copy(kind, o, block, True).wait_recv()
                    giver = (group ^ o) * members + member
                    for copy in pass_on(kind, o, block, rows_of(shared.at[kind], giver, block)):
                        copy.start()

        last = mp_count - 1
        for step in range(1, last):

            @pl.loop(0, pieces)
            def _(piece):
                line.advance(step, piece)

            if step == 1:
                spread(kinds + 1)
                settle(kinds + 1)
                for owner in range(dp_count):
                    for r in range(each):
                        at = pl.ds((owner * each + r) * 128, 128)
                        for k in range(2):
                            gains[k : k + 1, at] = all_vectors[owner * slab + k * each + r : owner * slab + k * each + r + 1]
                biases[...] = jnp.zeros_like(biases)
                for head in range(heads):
                    feature = mp * heads + head
                    first = (feature // each) * slab + feature % each
                    for kind, k in ((1, 3), (2, 2)):
                        biases[kind : kind + 1, head * 128 : (head + 1) * 128] = all_vectors[pl.ds(first + k * each, 1)]
                own_rows.wait()
                each_block(0, 1, norm)
            else:
                each_block(step, step, norm)
        for array in range(kinds + 1):
            spread(array)
        for array in range(kinds):
            settle(array)
        tiles = kinds * halves

        @pl.loop(0, pieces)
        def _(piece):
            line.advance(last - 1 if last == 1 else last, piece)

            @pl.when(piece < tiles)
            def _():
                each_block(0, last - 1, lambda block: project(piece, block))

        each_block(last, last, norm)

        @pl.loop(0, tiles)
        def _(tile):
            each_block(last, last, lambda block: project(tile, block))

        each_block(0, last - 1, hand_on)
        each_block(last, last, hand_on)
        line.finish()
        settle(kinds)
        for array in first_to_last:
            for o in range(chips):
                core(array, o).wait_send()
                if o:
                    cross(array, o).wait_send()

        @pl.loop(0, mp_count)
        def _(block):
            for kind in range(kinds):
                to_shared = kind < 2
                local_copy(kind, block, to_shared).wait()
                for o in range(1, heads):
                    head_copy(kind, o, block, to_shared).wait_send()
                    if not to_shared:
                        head_copy(kind, o, block, to_shared).wait_recv()
                if to_shared:
                    for o in range(heads):
                        giver = (group ^ o) * members + member
                        for copy in pass_on(kind, o, block, rows_of(shared.at[kind], giver, block)):
                            copy.wait()

    dma = pltpu.SemaphoreType.DMA
    bf16, f32 = jnp.bfloat16, jnp.float32
    return pl.pallas_call(
        kernel,
        out_shape=[
            jax.ShapeDtypeStruct((group_rows, width), bf16),
            jax.ShapeDtypeStruct((dp_count * slab, 128), f32),
            jax.ShapeDtypeStruct((width, kinds * columns), bf16),
            jax.ShapeDtypeStruct((width, columns), bf16),
            jax.ShapeDtypeStruct((2, dp_count * group_rows, HEAD_DIM), bf16),
            jax.ShapeDtypeStruct((heads * group_rows, HEAD_DIM), bf16),
            jax.ShapeDtypeStruct((rows, width), bf16),
            jax.ShapeDtypeStruct((rows, 128), f32),
        ],
        in_specs=[SMEM, SMEM] + [ANY] * (len(vectors) + kinds + 3),
        out_specs=[VMEM, VMEM, VMEM, ANY, ANY, ANY, VMEM, VMEM],
        scratch_shapes=[
            pltpu.VMEM((slab, 128), f32),
            pltpu.VMEM((rows, width), bf16),
            dma((len(vectors) + 1,)),
            pltpu.VMEM((group_rows, width), bf16),
            pltpu.VMEM((kinds, mp_count, heads, rows, HEAD_DIM), bf16),
            pltpu.VMEM((8, width), f32),
            pltpu.VMEM((8, columns), f32),
        ]
        + LineGather.semaphores(mp_count, pieces)
        + [dma(()), dma((arrays,))]
        + [dma((arrays, chips)) for _ in range(4)]
        + [dma((kinds, mp_count)), dma((kinds, heads, mp_count)), dma((kinds, heads, mp_count))]
        + [dma((2, heads, mp_count, members)) for _ in range(2)]
        + [pltpu.VMEM(v.shape, v.dtype) for v in vectors],
        compiler_params=pltpu.CompilerParams(
            collective_id=collective_id, has_side_effects=True, vmem_limit_bytes=63 * MIB),
        cost_estimate=pl.CostEstimate(flops=8 << 30, bytes_accessed=250 * MIB, transcendentals=0),
    )(lengths, order, hidden, output_grad, *vectors, *projections, out_weight)


def reduce_norm_gather(part, hidden, out_bias, gain, shift, shards, collective_id):
    dp_count, mp_count = lax.axis_size("dp"), lax.axis_size("mp")
    chips, count = dp_count // 2, len(shards)
    rows, width = hidden.shape
    pieces = pieces_of(rows)
    size = rows // pieces

    turns = pieces + 2 * SKEW * (mp_count - 1)

    def kernel(part_ref, hidden_ref, bias_ref, gain_ref, shift_ref, *refs):
        shard_refs, (residual_ref, full_ref), whole_refs = refs[:count], refs[count : count + 2], refs[count + 2 : 2 * count + 2]
        total, normed, flows, red_send, red_recv, line_send, line_recv, own_sem, *weight_sems = refs[2 * count + 2 :]
        dp, mp = lax.axis_index("dp"), lax.axis_index("mp")
        greet_all([(dp ^ (2 * o), mp) for o in range(1, chips)] + [(dp ^ 1, mp)], dp, mp, mp_count)
        weights = ShardGather(shard_refs, whole_refs, shards[0].shape[0], *weight_sems, dp, mp, chips)
        weights.begin()
        reduce = LineReduce(part_ref, flows, rows, pieces, red_send, red_recv, dp, mp, mp_count)
        gather = LineGather(normed, full_ref, rows, pieces, line_send, line_recv, dp, mp, mp_count)
        for piece in range(AHEAD):
            reduce.begin(piece)

        @pl.loop(0, turns)
        def _(turn):
            for array in range(count):

                @pl.when(turn == turns - 1 - 6 * (count - 1 - array))
                def _():
                    weights.spread(array)

            reduce.begin(jnp.minimum(turn + AHEAD, pieces - 1), turn + AHEAD < pieces)
            reduce.advance(turn)
            done = turn - SKEW * (mp_count - 1)

            @pl.when((done >= 0) & (done < pieces))
            def _():
                reduce.arrive(done)
                reduce.total(done, total)
                span = pl.ds(pl.multiple_of(done * size, size), size)
                residual = hidden_ref[span].astype(jnp.float32) + total[...] + bias_ref[...]
                residual_ref[span] = residual
                unit, _ = unit_rows(residual)
                normed[span] = (unit * gain_ref[...] + shift_ref[...]).astype(normed.dtype)
                gather.advance(0, done)

            for step in range(1, mp_count):
                late = done - SKEW * step
                gather.advance(step, jnp.clip(late, 0, pieces - 1), (late >= 0) & (late < pieces))

        own = pltpu.make_async_copy(normed, full_ref.at[pl.ds(pl.multiple_of(mp * rows, rows), rows)], own_sem)
        own.start()
        reduce.finish()
        gather.finish()
        own.wait()
        weights.finish()

    return pl.pallas_call(
        kernel,
        out_shape=[
            jax.ShapeDtypeStruct((rows, width), jnp.float32),
            jax.ShapeDtypeStruct((mp_count * rows, width), jnp.bfloat16),
        ]
        + [jax.ShapeDtypeStruct((dp_count * a.shape[0], a.shape[1]), a.dtype) for a in shards],
        in_specs=[VMEM] * 5 + [ANY] * count,
        out_specs=[VMEM, ANY] + [ANY] * count,
        scratch_shapes=[pltpu.VMEM((size, width), jnp.float32), pltpu.VMEM((rows, width), jnp.bfloat16)]
        + LineReduce.scratch(mp_count, rows, width, pieces) + LineGather.semaphores(mp_count, pieces)
        + [pltpu.SemaphoreType.DMA(())] + ShardGather.semaphores(count, chips),
        compiler_params=pltpu.CompilerParams(
            collective_id=collective_id, has_side_effects=True, vmem_limit_bytes=63 * MIB),
        cost_estimate=pl.CostEstimate(flops=0, bytes_accessed=300 * MIB, transcendentals=0),
    )(part, hidden, out_bias, gain, shift, *shards)


def reduce_back_gather(part, residual, branch_two, gain, pairs, collective_id):
    dp_count, mp_count = lax.axis_size("dp"), lax.axis_size("mp")
    chips, count = dp_count // 2, len(pairs)
    rows, width = residual.shape
    pieces = pieces_of(rows)
    size, depth = rows // pieces, width // dp_count
    units = pairs[0][1].shape[1]
    turns = pieces + 2 * SKEW * (mp_count - 1)
    each = dp_count // 4
    busy = count * dp_count // each
    assert 1 + busy <= turns

    def kernel(part_ref, residual_ref, branch_ref, gain_ref, *refs):
        operands, refs = refs[: 2 * count], refs[2 * count :]
        (grad_ref, sums_ref, full_ref), terms, refs = refs[:3], refs[3 : 3 + count], refs[3 + count :]
        loaded, refs = refs[: 2 * count], refs[2 * count :]
        (total, low, kept, slices, from_partner, chip_sum, load_sem, keep_sem, pair_send, pair_recv, cross_send, cross_recv,
         flows, red_send, red_recv, line_send, line_recv, own_sem) = refs
        dp, mp = lax.axis_index("dp"), lax.axis_index("mp")
        partner = (dp ^ 1, mp)
        greet_all([(dp ^ (2 * o), mp) for o in range(1, chips)] + [partner], dp, mp, mp_count)
        reduce = LineReduce(part_ref, flows, rows, pieces, red_send, red_recv, dp, mp, mp_count)
        gather = LineGather(low, full_ref, rows, pieces, line_send, line_recv, dp, mp, mp_count)
        for piece in range(AHEAD):
            reduce.begin(piece)
        loads = [pltpu.make_async_copy(operands[k], loaded[k], load_sem.at[k]) for k in range(2 * count)]
        for copy in loads:
            copy.start()
        sums_ref[...] = jnp.zeros_like(sums_ref)

        def pair(mat, o):
            return remote(slices.at[o], from_partner.at[mat, o], pair_send.at[mat, o], pair_recv.at[mat, o], partner)

        def cross(mat, o, peer):
            return remote(chip_sum.at[mat, o - 1], terms[mat].at[o], cross_send.at[mat, o], cross_recv.at[mat, o],
                          (peer, mp))

        def weight_slice(mat, index):
            o = (index + 1) % chips
            mine = index >= chips
            owner = dp ^ (2 * o) ^ jnp.where(mine, 0, 1)
            left = loaded[2 * mat][:, pl.ds(pl.multiple_of(owner * depth, depth), depth)]
            value = contract_first(left, loaded[2 * mat + 1][...])

            @pl.when(jnp.logical_not(mine))
            def _():
                if mat:
                    pair(mat - 1, o).wait_send()
                slices[o] = value.astype(slices.dtype)
                pair(mat, o).start()

            @pl.when(mine)
            def _():
                pair(mat, o).wait_recv()
                both = (value + from_partner[mat, o].astype(jnp.float32)).astype(slices.dtype)

                @pl.when(o == 0)
                def _():
                    kept[mat] = both
                    pltpu.make_async_copy(kept.at[mat], terms[mat].at[0], keep_sem.at[mat]).start()

                @pl.when(o != 0)
                def _():
                    chip_sum[mat, o - 1] = both
                    cross(mat, o, owner).start()

        @pl.loop(0, turns)
        def _(turn):
            reduce.begin(jnp.minimum(turn + AHEAD, pieces - 1), turn + AHEAD < pieces)
            reduce.advance(turn)
            done = turn - SKEW * (mp_count - 1)

            @pl.when((done >= 0) & (done < pieces))
            def _():
                reduce.arrive(done)
                reduce.total(done, total)
                span = pl.ds(pl.multiple_of(done * size, size), size)
                unit, inverse = unit_rows(residual_ref[span])
                upstream = total[...]
                sums_ref[0:1] += jnp.sum(upstream * unit, axis=0, keepdims=True)
                sums_ref[1:2] += jnp.sum(upstream, axis=0, keepdims=True)
                grad = branch_ref[span].astype(jnp.float32) + norm_back(upstream, unit, inverse, gain_ref[...])
                grad_ref[span] = grad
                rounded = grad.astype(low.dtype)
                low[span] = rounded
                sums_ref[2:3] += jnp.sum(rounded.astype(jnp.float32), axis=0, keepdims=True)
                gather.advance(0, done)

            for step in range(1, mp_count):
                late = done - SKEW * step
                gather.advance(step, jnp.clip(late, 0, pieces - 1), (late >= 0) & (late < pieces))
            for mat in range(count):

                @pl.when(turn == 1 + mat * busy // count)
                def _():
                    for copy in loads[2 * mat : 2 * mat + 2]:
                        copy.wait()

                first = turn - 1 - mat * busy // count

                @pl.when((first >= 0) & (first < busy // count))
                def _():
                    for i in range(each):
                        weight_slice(mat, first * each + i)

        own = pltpu.make_async_copy(low, full_ref.at[pl.ds(pl.multiple_of(mp * rows, rows), rows)], own_sem)
        own.start()
        reduce.finish()
        gather.finish()
        own.wait()
        for mat in range(count):
            pltpu.make_async_copy(kept.at[mat], terms[mat].at[0], keep_sem.at[mat]).wait()
            for o in range(chips):
                if mat == count - 1:
                    pair(mat, o).wait_send()
                if o:
                    cross(mat, o, dp ^ (2 * o)).wait()

    bf16, f32 = jnp.bfloat16, jnp.float32
    dma = pltpu.SemaphoreType.DMA
    flat = [array for two in pairs for array in two]
    return pl.pallas_call(
        kernel,
        out_shape=[
            jax.ShapeDtypeStruct((rows, width), f32),
            jax.ShapeDtypeStruct((8, width), f32),
            jax.ShapeDtypeStruct((mp_count * rows, width), bf16),
        ]
        + [jax.ShapeDtypeStruct((chips, depth, units), bf16)] * count,
        in_specs=[VMEM] * 4 + [ANY] * (2 * count),
        out_specs=[VMEM, VMEM] + [ANY] * (1 + count),
        scratch_shapes=[pltpu.VMEM(a.shape, a.dtype) for a in flat]
        + [
            pltpu.VMEM((size, width), f32),
            pltpu.VMEM((rows, width), bf16),
            pltpu.VMEM((count, depth, units), bf16),
            pltpu.VMEM((chips, depth, units), bf16),
            pltpu.VMEM((count, chips, depth, units), bf16),
            pltpu.VMEM((count, chips - 1, depth, units), bf16),
            dma((2 * count,)), dma((count,)),
        ]
        + [dma((count, chips)) for _ in range(4)]
        + LineReduce.scratch(mp_count, rows, width, pieces) + LineGather.semaphores(mp_count, pieces)
        + [dma(())],
        compiler_params=pltpu.CompilerParams(
            collective_id=collective_id, has_side_effects=True, vmem_limit_bytes=63 * MIB),
        cost_estimate=pl.CostEstimate(flops=40 << 30, bytes_accessed=300 * MIB, transcendentals=0),
    )(part, residual, branch_two, gain, *flat)


QUARTERS = 4


def finish_back(query_grad, key_part, value_part, weights, normed, residual_grad, hidden, gain, out_part, vectors, heads, members,
                collective_id):
    rows, width = hidden.shape
    dp_count, mp_count = lax.axis_size("dp"), lax.axis_size("mp")
    chips, pieces = dp_count // 2, pieces_of(rows)
    size, depth, columns = rows // pieces, width // dp_count, heads * HEAD_DIM
    kinds, quarter = 3, rows // QUARTERS
    per_quarter = pieces // QUARTERS
    slice_rows = width // per_quarter
    turns = pieces + SKEW * (mp_count - 1)
    slices_each = max(dp_count // 8, 1)
    slice_turn = turns // 3
    group_rows = mp_count * rows
    slab, each = vectors.shape[1], width // dp_count // 128
    query_grad = query_grad.reshape(heads, mp_count, rows, HEAD_DIM)
    shared = [v.reshape(dp_count, mp_count, rows, HEAD_DIM) for v in (key_part, value_part)]

    def kernel(query_ref, key_ref, value_ref, weights_hbm, normed_hbm, residual_ref, hidden_ref, gain_ref, out_ref, vector_ref,
               grad_ref, weight_grad_ref, out_grad_ref, summed_ref,
               weights, normed, landed, own, parts, stage, part, total, flows, red_send, red_recv,
               slices, from_partner, chip_sum, from_chips, out_partner, out_sum, out_chips,
               load_sem, own_sem, part_send, part_recv, local_sem, head_send, head_recv,
               pair_send, pair_recv, cross_send, cross_recv,
               sums_ref, column_ref, packed, vector_parts, line_parts, vec_send, vec_recv, line_send, line_recv):
        dp, mp = lax.axis_index("dp"), lax.axis_index("mp")
        group, member = dp // members, dp % members
        partner = (dp ^ 1, mp)
        greet_all([(dp ^ o, mp) for o in range(1, dp_count)] + [(dp, mp ^ o) for o in range(1, mp_count)], dp, mp, mp_count)
        reduce = LineReduce(part, flows, rows, pieces, red_send, red_recv, dp, mp, mp_count)
        loads = [pltpu.make_async_copy(weights_hbm, weights, load_sem.at[0]),
                 pltpu.make_async_copy(normed_hbm, normed, load_sem.at[1])]
        shared_refs = (key_ref, value_ref)

        def rows_of(k):
            return pl.ds(k * quarter, quarter)

        def lane_span(kind, head):
            return pl.ds(pl.multiple_of(kind * columns + head * HEAD_DIM, HEAD_DIM), HEAD_DIM)

        def landing(kind, k, head):
            return landed.at[:, rows_of(k), lane_span(kind, head)]

        def own_copy(kind, o):
            return pltpu.make_async_copy(shared_refs[kind].at[(group ^ o) * members + member], own.at[kind, o],
                                         own_sem.at[kind, o])

        def part_copy(kind, o, p, k):
            return remote(shared_refs[kind].at[(group ^ o) * members + (member ^ p), :, rows_of(k)],
                          parts.at[kind, o, p - 1, :, rows_of(k)], part_send.at[kind, o, p - 1, k],
                          part_recv.at[kind, o, p - 1, k], (group * members + (member ^ p), mp))

        def head_copy(kind, o, k):
            source = query_ref.at[group ^ o, :, rows_of(k)] if kind == 2 else stage.at[kind, o, :, rows_of(k)]
            return remote(source, landing(kind, k, group), head_send.at[kind, o, k], head_recv.at[kind, o, k],
                          ((group ^ o) * members + member, mp))

        def local_copy(k):
            return pltpu.make_async_copy(query_ref.at[group, :, rows_of(k)], landing(2, k, group), local_sem.at[k])

        for k in range(QUARTERS):
            for kind in range(2):
                for o in range(heads):
                    for p in range(1, members):
                        part_copy(kind, o, p, k).start()
            if k == 0:
                for kind in range(2):
                    for o in range(heads):
                        own_copy(kind, o).start()
                for copy in loads:
                    copy.start()
            for o in range(1, heads):
                head_copy(2, o, k).start()
            local_copy(k).start()
        for k in range(QUARTERS):
            for kind in range(2):
                for o in list(range(1, heads)) + [0]:
                    if k == 0:
                        own_copy(kind, o).wait()
                    value = own[kind, o, :, k * quarter : (k + 1) * quarter].astype(jnp.float32)
                    for p in range(1, members):
                        part_copy(kind, o, p, k).wait_recv()
                        value = value + parts[kind, o, p - 1, :, k * quarter : (k + 1) * quarter].astype(jnp.float32)
                    if o:
                        stage[kind, o, :, k * quarter : (k + 1) * quarter] = value.astype(stage.dtype)
                        head_copy(kind, o, k).start()
                    else:
                        landed[:, k * quarter : (k + 1) * quarter, lane_span(kind, group)] = value.astype(landed.dtype)

        def arrived(k):
            for kind in range(kinds):
                for o in range(1, heads):
                    head_copy(kind, o, k).wait_recv()
            local_copy(k).wait()

        def project(k, first, count):
            span = pl.ds(pl.multiple_of(k * quarter, quarter), quarter)
            left = landed[:, span].reshape(mp_count * quarter, kinds * columns)
            features = pl.ds(pl.multiple_of(first, count), count)
            value = contract_last(left, weights[features]).astype(part.dtype)
            for block in range(mp_count):
                at = pl.ds(pl.multiple_of(block * rows + k * quarter, quarter), quarter)
                part[at, features] = value[block * quarter : (block + 1) * quarter]

        def slab(owner):
            return pl.ds(pl.multiple_of(owner * depth, depth), depth)

        def pair(o):
            return remote(slices.at[o], from_partner.at[o], pair_send.at[0, o], pair_recv.at[0, o], partner)

        def cross(o, peer):
            return remote(chip_sum.at[o], from_chips.at[o], cross_send.at[0, o], cross_recv.at[0, o], (peer, mp))

        def out_pair(o):
            return remote(out_ref.at[slab(dp ^ (2 * o) ^ 1)], out_partner.at[o], pair_send.at[1, o], pair_recv.at[1, o],
                          partner)

        def out_cross(o):
            return remote(out_sum.at[o], out_chips.at[o], cross_send.at[1, o], cross_recv.at[1, o], (dp ^ (2 * o), mp))

        def weight_slice(index):
            o = (index + 1) % chips
            mine = index >= chips
            owner = dp ^ (2 * o) ^ jnp.where(mine, 0, 1)
            rows_all = landed[...].reshape(group_rows, kinds * columns)
            value = contract_first(normed[:, slab(owner)], rows_all)

            @pl.when(jnp.logical_not(mine))
            def _():
                slices[o] = value.astype(slices.dtype)
                pair(o).start()

            @pl.when(mine)
            def _():
                pair(o).wait_recv()
                both = value + from_partner[o].astype(jnp.float32)

                @pl.when(o == 0)
                def _():
                    weight_grad_ref[...] = both

                @pl.when(o != 0)
                def _():
                    chip_sum[o] = both.astype(chip_sum.dtype)
                    cross(o, owner).start()

        for copy in loads:
            copy.wait()
        arrived(0)
        for part_index in range(per_quarter):
            project(0, part_index * slice_rows, slice_rows)
        for o in range(chips):
            out_pair(o).start()
        sums_ref[...] = jnp.zeros_like(sums_ref)

        @pl.loop(0, turns)
        def _(turn):
            @pl.when(turn < pieces)
            def _():
                reduce.begin(jnp.minimum(turn, pieces - 1))

            reduce.advance(turn)
            done = turn - SKEW * (mp_count - 1)

            @pl.when(done >= 0)
            def _():
                reduce.arrive(done)
                reduce.total(done, total)
                span = pl.ds(pl.multiple_of(done * size, size), size)
                unit, inverse = unit_rows(hidden_ref[span].astype(jnp.float32))
                upstream = total[...]
                sums_ref[0:1] += jnp.sum(upstream * unit, axis=0, keepdims=True)
                sums_ref[1:2] += jnp.sum(upstream, axis=0, keepdims=True)
                grad_ref[span] = residual_ref[span] + norm_back(upstream, unit, inverse, gain_ref[...])

            for k in range(1, QUARTERS):

                @pl.when(turn == (k - 1) * per_quarter)
                def _():
                    arrived(k)

            @pl.when(turn < (QUARTERS - 1) * per_quarter)
            def _():
                k, portion = turn // per_quarter + 1, turn % per_quarter
                project(k, portion * slice_rows, slice_rows)

            @pl.when(turn == slice_turn)
            def _():
                for o in list(range(1, chips)) + [0]:
                    out_pair(o).wait_recv()
                    value = out_ref[slab(dp ^ (2 * o))].astype(jnp.float32) + out_partner[o].astype(jnp.float32)
                    if o:
                        out_sum[o] = value.astype(out_sum.dtype)
                        out_cross(o).start()
                    else:
                        out_grad_ref[...] = value

            @pl.when(turn == late_turn - 1)
            def _():
                column_ref[0:1] = jnp.sum(
                    landed[...].reshape(group_rows, kinds * columns).astype(jnp.float32), axis=0, keepdims=True)

            @pl.when((turn >= late_turn) & (turn < late_turn + dp_count // slices_each))
            def _():
                for i in range(slices_each):
                    weight_slice((turn - late_turn) * slices_each + i)

        reduce.finish()
        packed[...] = vector_ref[...]
        for owner in range(dp_count):
            for r in range(each):
                at = slice((owner * each + r) * 128, (owner * each + r + 1) * 128)
                for k in range(2):
                    packed[owner, k * each + r : k * each + r + 1] = sums_ref[k : k + 1, at]
        for head in range(heads):
            feature = mp * heads + head
            for k, kind in ((2, 2), (3, 1)):
                at = slice(kind * columns + head * HEAD_DIM, kind * columns + (head + 1) * HEAD_DIM)
                packed[feature // each, pl.ds(k * each + feature % each, 1)] = column_ref[0:1, at]

        def vector_copy(o):
            return remote(packed.at[dp ^ o], vector_parts.at[o], vec_send.at[o], vec_recv.at[o], (dp ^ o, mp))

        def line_copy(o):
            return remote(line_parts.at[mp], line_parts.at[mp], line_send.at[o], line_recv.at[o], (dp, mp ^ o))

        for o in range(1, dp_count):
            vector_copy(o).start()
        value = packed[dp]
        for o in range(1, dp_count):
            vector_copy(o).wait_recv()
            value = value + vector_parts[o]
        line_parts[mp] = value
        for o in range(1, mp_count):
            line_copy(o).start()
        for o in range(chips):
            pair(o).wait_send()
            out_pair(o).wait_send()
            if o:
                cross(o, dp ^ (2 * o)).wait()
                weight_grad_ref[...] += from_chips[o].astype(jnp.float32)
                out_cross(o).wait()
                out_grad_ref[...] += out_chips[o].astype(jnp.float32)
        for k in range(QUARTERS):
            for o in range(heads):
                for kind in range(2):
                    for p in range(1, members):
                        part_copy(kind, o, p, k).wait_send()
                if o:
                    for kind in range(kinds):
                        head_copy(kind, o, k).wait_send()
        for o in range(1, mp_count):
            line_copy(o).wait()
        value = line_parts[0]
        for index in range(1, mp_count):
            value = value + line_parts[index]
        summed_ref[...] = value
        for o in range(1, dp_count):
            vector_copy(o).wait_send()

    late_turn = max(slice_turn, (QUARTERS - 2) * per_quarter + 1)
    assert late_turn + dp_count // slices_each <= turns
    dma = pltpu.SemaphoreType.DMA
    bf16, f32 = jnp.bfloat16, jnp.float32
    own_columns = out_part.shape[1]
    return pl.pallas_call(
        kernel,
        out_shape=[
            jax.ShapeDtypeStruct((rows, width), f32),
            jax.ShapeDtypeStruct((depth, kinds * columns), f32),
            jax.ShapeDtypeStruct((depth, own_columns), f32),
            jax.ShapeDtypeStruct((slab, 128), f32),
        ],
        in_specs=[ANY] * 5 + [VMEM] * 5,
        out_specs=[VMEM] * 4,
        scratch_shapes=[
            pltpu.VMEM((width, kinds * columns), bf16),
            pltpu.VMEM((group_rows, width), bf16),
            pltpu.VMEM((mp_count, rows, kinds * columns), bf16),
            pltpu.VMEM((2, heads, mp_count, rows, HEAD_DIM), bf16),
            pltpu.VMEM((2, heads, members - 1, mp_count, rows, HEAD_DIM), bf16),
            pltpu.VMEM((2, heads, mp_count, rows, HEAD_DIM), bf16),
            pltpu.VMEM((group_rows, width), bf16),
            pltpu.VMEM((size, width), f32),
        ]
        + LineReduce.scratch(mp_count, rows, width, pieces)
        + [pltpu.VMEM((chips, depth, kinds * columns), bf16) for _ in range(4)]
        + [pltpu.VMEM((chips, depth, own_columns), bf16) for _ in range(3)]
        + [dma((2,)), dma((2, heads))]
        + [dma((2, heads, members - 1, QUARTERS)) for _ in range(2)]
        + [dma((QUARTERS,)), dma((kinds, heads, QUARTERS)), dma((kinds, heads, QUARTERS))]
        + [dma((2, chips)) for _ in range(4)]
        + [pltpu.VMEM((8, width), f32), pltpu.VMEM((8, kinds * columns), f32)]
        + [pltpu.VMEM((count, slab, 128), f32) for count in (dp_count, dp_count, mp_count)]
        + [dma((dp_count,)), dma((dp_count,)), dma((mp_count,)), dma((mp_count,))],
        compiler_params=pltpu.CompilerParams(
            collective_id=collective_id, has_side_effects=True, vmem_limit_bytes=63 * MIB),
        cost_estimate=pl.CostEstimate(flops=20 << 30, bytes_accessed=300 * MIB, transcendentals=0),
    )(query_grad, *shared, weights, normed, residual_grad, hidden, gain, out_part, vectors)


UNITS = 512
CHUNK = 256


def feed_both_ways(rows_two, branch_rows, up_all, down_all, up_bias):
    rows, width = rows_two.shape
    units = up_all.shape[1]
    tile = min(UNITS, units)
    half_root = 1.0 / math.sqrt(2.0)
    density_scale = 1.0 / math.sqrt(2.0 * math.pi)

    def kernel(rows_ref, branch_ref, up_ref, down_ref, bias_ref, hidden_ref, grad_ref, column_ref, part_ref, total):
        step = pl.program_id(0)
        columns = jnp.zeros((1, tile), jnp.float32)
        up, down = up_ref[...], down_ref[...]
        for first in range(0, rows, CHUNK):
            span = slice(first, first + CHUNK)
            pre = jnp.dot(rows_ref[span], up, preferred_element_type=jnp.float32) + bias_ref[...]
            upstream = jnp.dot(branch_ref[span], down, preferred_element_type=jnp.float32)
            share = 0.5 + 0.5 * lax.erf(pre * half_root)
            hidden_ref[span] = (pre * share).astype(hidden_ref.dtype)
            slope = share + pre * (density_scale * jnp.exp(-0.5 * pre * pre))
            grad = (upstream * slope).astype(grad_ref.dtype)
            grad_ref[span] = grad
            columns = columns + jnp.sum(grad.astype(jnp.float32), axis=0, keepdims=True)
            back = contract_last(grad, up)

            @pl.when(step == 0)
            def _():
                total[span] = back

            @pl.when(step != 0)
            def _():
                total[span] += back

        column_ref[...] = columns

        @pl.when(step == units // tile - 1)
        def _():
            part_ref[...] = total[...].astype(part_ref.dtype)

    bf16 = jnp.bfloat16
    return pl.pallas_call(
        kernel,
        grid=(units // tile,),
        out_shape=[
            jax.ShapeDtypeStruct((rows, units), bf16),
            jax.ShapeDtypeStruct((rows, units), bf16),
            jax.ShapeDtypeStruct((1, units), jnp.float32),
            jax.ShapeDtypeStruct((rows, width), bf16),
        ],
        in_specs=[
            pl.BlockSpec((rows, width), lambda i: (0, 0)),
            pl.BlockSpec((rows, width), lambda i: (0, 0)),
            pl.BlockSpec((width, tile), lambda i: (0, i)),
            pl.BlockSpec((width, tile), lambda i: (0, i)),
            pl.BlockSpec((1, tile), lambda i: (0, i)),
        ],
        out_specs=[
            pl.BlockSpec((rows, tile), lambda i: (0, i)),
            pl.BlockSpec((rows, tile), lambda i: (0, i)),
            pl.BlockSpec((1, tile), lambda i: (0, i)),
            pl.BlockSpec((rows, width), lambda i: (0, 0)),
        ],
        scratch_shapes=[pltpu.VMEM((rows, width), jnp.float32)],
        compiler_params=pltpu.CompilerParams(vmem_limit_bytes=60 * MIB),
        cost_estimate=pl.CostEstimate(
            flops=6 * rows * width * units, bytes_accessed=40 * MIB, transcendentals=2 * rows * units),
    )(rows_two, branch_rows, up_all, down_all, up_bias)


def sum_terms(terms):
    return functools.reduce(jnp.add, [terms[k].astype(jnp.float32) for k in range(terms.shape[0])])


def per_device(
    hidden_in,
    output_grad,
    first_gain,
    first_shift,
    query_weight,
    query_bias,
    key_weight,
    value_weight,
    value_bias,
    out_weight,
    out_bias,
    second_gain,
    second_shift,
    up_weight,
    up_bias,
    down_weight,
    down_bias,
    seq_lengths,
    block_order,
    block_slot,
):
    local_rows, model_width = hidden_in.shape
    mp_count, dp_count = lax.axis_size("mp"), lax.axis_size("dp")
    mp_index, dp_index = lax.axis_index("mp"), lax.axis_index("dp")
    group_rows = local_rows * mp_count
    head_width = query_weight.shape[1]
    heads_local = head_width // HEAD_DIM
    hidden_width = up_weight.shape[1]
    members = dp_count // heads_local
    blocks_each = group_rows // BLOCK
    plan = (seq_lengths, block_order, block_slot)

    vectors = (first_gain, first_shift, query_bias, value_bias, out_bias, second_gain, second_shift, down_bias, up_bias)
    rows_one, vector_rows, projections, out_all, head_shared, head_queries, branch_two, live = project_first(
        hidden_in, output_grad, seq_lengths, block_order, vectors,
        (key_weight, value_weight, query_weight), out_weight, heads_local, members, 0,
    )
    own_valid = live[:, :1] > 0
    vector_rows = vector_rows.reshape(dp_count, -1, 128)
    each = model_width // dp_count // 128
    gain_one, _, _, _, bias_out, gain_two, shift_two, bias_down = (
        vector_rows[:, k * each : (k + 1) * each].reshape(1, model_width) for k in range(8)
    )
    up_each = up_bias.shape[0] // 128
    bias_up = vector_rows[:, 8 * each : 8 * each + up_each].reshape(1, up_bias.shape[0] * dp_count)

    branch_rows_two = whole_rows(branch_two)
    head_mix, exact_mix, log_total = attend(head_queries, head_shared, *plan, members, blocks_each)
    (attended_low,) = to_rows([head_mix], [], heads_local, members, 2)
    out_part = contract_last(attended_low, out_all).astype(jnp.bfloat16)
    residual, rows_two, up_all, down_all = reduce_norm_gather(
        out_part, hidden_in, bias_out, gain_two, shift_two, (up_weight, down_weight), 3
    )

    bias_hidden = lax.dynamic_slice_in_dim(bias_up, mp_index * hidden_width, hidden_width, 1)
    hidden_low, pre_grad, pre_columns, up_part = feed_both_ways(rows_two, branch_rows_two, up_all, down_all, bias_hidden)
    residual_grad, sums_two, branch_rows_one, down_terms, up_terms = reduce_back_gather(
        up_part, residual, branch_two, gain_two, ((branch_rows_two, hidden_low), (rows_two, pre_grad)), 4
    )
    down_weight_grad, up_weight_grad = (
        sum_terms(terms) for terms in (down_terms, up_terms)
    )

    hidden_low, branch_rows_one = lax.optimization_barrier((hidden_low, branch_rows_one))
    feed = row_share(contract_last(hidden_low, down_all))
    result = residual + feed + bias_down
    output = jnp.where(own_valid, result, 0.0).astype(jnp.bfloat16)

    attended_grad = jnp.dot(branch_rows_one, out_all, preferred_element_type=jnp.float32).astype(jnp.bfloat16)
    (head_grad,) = to_heads([attended_grad], [], heads_local, members, 5)
    head_query_grad, head_key_grad, head_value_grad = attend_back(
        head_queries, head_shared, head_grad, exact_mix, log_total, *plan, members, blocks_each
    )

    def column_sums(values):
        return jnp.sum(values.astype(jnp.float32), axis=0)

    def placed(values):
        whole = jnp.zeros((values.shape[0] * mp_count,), jnp.float32)
        return lax.dynamic_update_slice_in_dim(whole, values, mp_index * values.shape[0], 0)

    none = jnp.zeros((model_width,), jnp.float32)
    sums = (
        none, none, none, none, sums_two[2], sums_two[0], sums_two[1], column_sums(branch_two), placed(pre_columns[0]),
    )
    packed = jnp.concatenate([v.reshape(dp_count, -1, 128) for v in sums], axis=1)
    packed = jnp.pad(packed, ((0, 0), (0, -packed.shape[1] % 8), (0, 0)))
    out_weight_part = contract_first(branch_rows_one, attended_low).astype(jnp.bfloat16)
    input_grad, weight_grads, out_weight_grad, summed = finish_back(
        head_query_grad, head_key_grad, head_value_grad, projections, rows_one, residual_grad, hidden_in, gain_one,
        out_weight_part, packed, heads_local, members, 7,
    )
    key_weight_grad, value_weight_grad, query_weight_grad = (
        weight_grads[:, k * head_width : (k + 1) * head_width] for k in range(3)
    )
    vector_grads = [summed[k * each : (k + 1) * each].reshape(-1) for k in range(8)]
    up_bias_grad = summed[8 * each : 8 * each + up_each].reshape(-1)
    return (
        output,
        input_grad,
        vector_grads[0],
        vector_grads[1],
        query_weight_grad,
        vector_grads[2],
        key_weight_grad,
        value_weight_grad,
        vector_grads[3],
        out_weight_grad,
        vector_grads[4],
        vector_grads[5],
        vector_grads[6],
        up_weight_grad,
        up_bias_grad,
        down_weight_grad,
        vector_grads[7],
    )


def solution(mesh):
    return jax.shard_map(
        per_device,
        mesh=mesh,
        in_specs=(
            P(("dp", "mp"), None),
            P(("dp", "mp"), None),
            P("dp"),
            P("dp"),
            P("dp", "mp"),
            P("dp"),
            P("dp", "mp"),
            P("dp", "mp"),
            P("dp"),
            P("dp", "mp"),
            P("dp"),
            P("dp"),
            P("dp"),
            P("dp", "mp"),
            P("dp"),
            P("dp", "mp"),
            P("dp"),
            P(),
            P(),
            P(),
        ),
        out_specs=(
            P(("dp", "mp"), None),
            P(("dp", "mp"), None),
            P("dp"),
            P("dp"),
            P("dp", "mp"),
            P("dp"),
            P("dp", "mp"),
            P("dp", "mp"),
            P("dp"),
            P("dp", "mp"),
            P("dp"),
            P("dp"),
            P("dp"),
            P("dp", "mp"),
            P("dp"),
            P("dp", "mp"),
            P("dp"),
        ),
        check_vma=False,
    )
```

```python
import functools
import math

import jax
import jax.numpy as jnp
from jax import lax
from jax.experimental import pallas as pl
from jax.experimental.pallas import tpu as pltpu
from jax.sharding import PartitionSpec as P

HEAD_DIM = 128
BLOCK = 128
KEY_BLOCKS = 8
MESH = pl.DeviceIdType.MESH
ANY = pl.BlockSpec(memory_space=pl.ANY)
VMEM = pl.BlockSpec(memory_space=pltpu.VMEM)
SMEM = pl.BlockSpec(memory_space=pltpu.SMEM)
MIB = 1 << 20


big_negative = -1e30
norm_epsilon = 1e-05


def norm_back(upstream, normed, inverse, gain_row):
    scaled = upstream * gain_row
    mean_grad = jnp.mean(scaled, axis=-1, keepdims=True)
    second = jnp.mean(scaled * normed, axis=-1, keepdims=True)
    return inverse * (scaled - mean_grad - normed * second)


def contract_last(left, right):
    return lax.dot_general(
        left, right, (((1,), (1,)), ((), ())), preferred_element_type=jnp.float32
    )


def contract_first(left, right):
    return lax.dot_general(
        left, right, (((0,), (0,)), ((), ())), preferred_element_type=jnp.float32
    )


def whole_rows(local_part):
    return lax.all_gather(local_part, "mp", axis=0, tiled=True)


def row_share(term):
    term = term.astype(jnp.bfloat16)
    return lax.psum_scatter(term, "mp", scatter_dimension=0, tiled=True).astype(jnp.float32)


def greet(peers):
    barrier = pltpu.get_barrier_semaphore()
    for peer in peers:
        pl.semaphore_signal(barrier, inc=1, device_id=peer, device_id_type=MESH)
    pl.semaphore_wait(barrier, len(peers))


def remote(src, dst, send_sem, recv_sem, peer):
    return pltpu.make_async_remote_copy(
        src_ref=src, dst_ref=dst, send_sem=send_sem, recv_sem=recv_sem,
        device_id=peer, device_id_type=MESH,
    )


def head_place(heads, members):
    me = lax.axis_index("dp")
    return me, me // members, me % members, lax.axis_index("mp")


def lanes(head):
    return pl.ds(pl.multiple_of(head * HEAD_DIM, HEAD_DIM), HEAD_DIM)


def sequence_of(place, lengths):
    first, length, running = jnp.int32(0), jnp.int32(0), jnp.int32(0)
    for s in range(lengths.shape[0]):
        inside = place >= running
        first = jnp.where(inside, running, first)
        length = jnp.where(inside, lengths[s], length)
        running = running + (lengths[s] + (BLOCK - 1)) // BLOCK
    return first, length - (place - first) * BLOCK


def list_queries(slot, index_list, place_list, members, blocks_each):
    member = lax.axis_index("dp") % members

    def visit(block, count):
        dealt = slot[block]
        owner = dealt // blocks_each

        @pl.when(owner % members == member)
        def _():
            index_list[count] = (owner // members) * blocks_each + dealt % blocks_each
            place_list[count] = block

        return count + (owner % members == member).astype(jnp.int32)

    lax.fori_loop(0, slot.shape[0], visit, jnp.int32(0))


def block_rows(block):
    return pl.ds(pl.multiple_of(block * BLOCK, BLOCK), BLOCK)


class QueryPair:
    def __init__(self, pair, lengths, index_list, place_list):
        self.index = [index_list[2 * pair + i] for i in range(2)]
        self.place = [place_list[2 * pair + i] for i in range(2)]
        found = [sequence_of(place, lengths) for place in self.place]
        self.start = found[0][0]
        lane = lax.broadcasted_iota(jnp.int32, (1, 2 * BLOCK), 1)
        right = lane >= BLOCK

        def lanes_of(left_value, right_value):
            return jnp.where(right, right_value, left_value)

        within = lane - lanes_of(0, BLOCK)
        base = self.start * BLOCK
        self.position = lanes_of(self.place[0], self.place[1]) * BLOCK + within - base
        self.lowest = lanes_of(found[0][0], found[1][0]) * BLOCK - base
        self.live = within < lanes_of(found[0][1], found[1][1])
        self.tiles = (self.place[1] - self.start) // KEY_BLOCKS + 1
        self.open_tiles = jnp.where(found[0][0] == found[1][0], (self.place[0] - self.start) // KEY_BLOCKS, 0)

    def row(self, tile):
        return pl.multiple_of((self.start + tile * KEY_BLOCKS) * BLOCK, BLOCK)

    def allowed(self, tile):
        width = KEY_BLOCKS * BLOCK
        key = lax.broadcasted_iota(jnp.int32, (width, 2 * BLOCK), 0)
        return (key <= self.position - tile * width) & (key >= self.lowest - tile * width)

    def load_t(self, ref):
        return jnp.concatenate([ref[block_rows(index)].T for index in self.index], axis=1)

    def load(self, ref):
        return jnp.concatenate([ref[block_rows(index)] for index in self.index], axis=0)

    def store_t(self, ref, value_t):
        for i, index in enumerate(self.index):
            ref[block_rows(index)] = value_t[:, i * BLOCK : (i + 1) * BLOCK].T.astype(ref.dtype)


def attend(queries, shared, lengths, order, slot, members, blocks_each):
    pairs, key_count = queries.shape[0] // (2 * BLOCK), shared.shape[1] // BLOCK
    width = KEY_BLOCKS * BLOCK
    padded = (key_count + KEY_BLOCKS - 1) * BLOCK
    scale = math.log2(math.e) / math.sqrt(HEAD_DIM)

    def kernel(lengths_ref, slot_ref, q_ref, shared_ref, out_ref, exact_ref, log_ref,
               index_list, place_list, keys, values_t):
        list_queries(slot_ref, index_list, place_list, members, blocks_each)

        @pl.loop(0, key_count)
        def _(block):
            source = block_rows(slot_ref[block])
            keys[block_rows(block)] = shared_ref[0, source]
            values_t[:, block_rows(block)] = shared_ref[1, source].T

        tail = pl.ds(key_count * BLOCK, padded - key_count * BLOCK)
        keys[tail] = jnp.zeros((padded - key_count * BLOCK, HEAD_DIM), keys.dtype)
        values_t[:, tail] = jnp.zeros((HEAD_DIM, padded - key_count * BLOCK), keys.dtype)

        @pl.loop(0, pairs)
        def _(index):
            pair = QueryPair(index, lengths_ref, index_list, place_list)
            query_t = pair.load_t(q_ref)

            def step(tile, carry, masked):
                top, total, mix = carry
                span = pl.ds(pair.row(tile), width)
                scores = jnp.dot(keys[span], query_t, preferred_element_type=jnp.float32)
                if masked:
                    scores = jnp.where(pair.allowed(tile), scores, big_negative)
                new_top = jnp.maximum(top, jnp.max(scores, axis=0, keepdims=True))
                weights = jnp.exp2((scores - new_top) * scale)
                fade = jnp.exp2((top - new_top) * scale)
                total = total * fade + jnp.sum(weights, axis=0, keepdims=True)
                mix = mix * fade + jnp.dot(
                    values_t[:, span], weights.astype(jnp.bfloat16), preferred_element_type=jnp.float32)
                return new_top, total, mix

            carry = (jnp.full((1, 2 * BLOCK), big_negative, jnp.float32), jnp.zeros((1, 2 * BLOCK), jnp.float32),
                     jnp.zeros((HEAD_DIM, 2 * BLOCK), jnp.float32))
            carry = lax.fori_loop(0, pair.open_tiles, lambda tile, c: step(tile, c, False), carry)
            top, total, mix = lax.fori_loop(pair.open_tiles, pair.tiles, lambda tile, c: step(tile, c, True), carry)
            mix = jnp.where(pair.live, mix / total, 0.0)
            exact_ref[index] = mix
            pair.store_t(out_ref, mix)
            log_ref[index] = jnp.where(pair.live, top * scale + jnp.log2(total), -big_negative)

    return pl.pallas_call(
        kernel,
        out_shape=[
            jax.ShapeDtypeStruct(queries.shape, jnp.bfloat16),
            jax.ShapeDtypeStruct((pairs, HEAD_DIM, 2 * BLOCK), jnp.float32),
            jax.ShapeDtypeStruct((pairs, 1, 2 * BLOCK), jnp.float32),
        ],
        in_specs=[SMEM] * 2 + [VMEM] * 2,
        out_specs=[VMEM] * 3,
        scratch_shapes=[
            pltpu.SMEM((2 * pairs,), jnp.int32), pltpu.SMEM((2 * pairs,), jnp.int32),
            pltpu.VMEM((padded, HEAD_DIM), jnp.bfloat16), pltpu.VMEM((HEAD_DIM, padded), jnp.bfloat16),
        ],
        compiler_params=pltpu.CompilerParams(vmem_limit_bytes=56 * MIB),
        cost_estimate=pl.CostEstimate(flops=8 << 30, bytes_accessed=50 * MIB, transcendentals=8 << 20),
    )(lengths, slot, queries, shared)


def attend_back(queries, shared, upstream, exact, logs, lengths, order, slot, members, blocks_each):
    pairs, key_count = queries.shape[0] // (2 * BLOCK), shared.shape[1] // BLOCK
    width = KEY_BLOCKS * BLOCK
    padded = (key_count + KEY_BLOCKS - 1) * BLOCK
    scale = math.log2(math.e) / math.sqrt(HEAD_DIM)
    plain_scale = 1.0 / math.sqrt(HEAD_DIM)

    def kernel(lengths_ref, slot_ref, q_ref, shared_ref, g_ref, exact_ref, log_ref, dq_ref, dk_ref, dv_ref,
               index_list, place_list, keys, keys_t, values, key_sum, value_sum):
        list_queries(slot_ref, index_list, place_list, members, blocks_each)

        @pl.loop(0, key_count)
        def _(block):
            source, to = block_rows(slot_ref[block]), block_rows(block)
            rows = shared_ref[0, source]
            keys[to] = rows
            keys_t[:, to] = rows.T
            values[to] = shared_ref[1, source]
            key_sum[to] = jnp.zeros((BLOCK, HEAD_DIM), jnp.float32)
            value_sum[to] = jnp.zeros((BLOCK, HEAD_DIM), jnp.float32)

        tail = pl.ds(key_count * BLOCK, padded - key_count * BLOCK)
        keys[tail] = jnp.zeros((padded - key_count * BLOCK, HEAD_DIM), keys.dtype)
        values[tail] = jnp.zeros((padded - key_count * BLOCK, HEAD_DIM), keys.dtype)
        keys_t[:, tail] = jnp.zeros((HEAD_DIM, padded - key_count * BLOCK), keys.dtype)
        key_sum[tail] = jnp.zeros((padded - key_count * BLOCK, HEAD_DIM), jnp.float32)
        value_sum[tail] = jnp.zeros((padded - key_count * BLOCK, HEAD_DIM), jnp.float32)

        @pl.loop(0, pairs)
        def _(index):
            pair = QueryPair(index, lengths_ref, index_list, place_list)
            query, grad = pair.load(q_ref), pair.load(g_ref)
            query_t, grad_t = pair.load_t(q_ref), pair.load_t(g_ref)
            delta = jnp.sum(grad_t.astype(jnp.float32) * exact_ref[index], axis=0, keepdims=True)
            log_total = log_ref[index]

            def step(tile, query_grad, masked):
                span = pl.ds(pair.row(tile), width)
                scores = jnp.dot(keys[span], query_t, preferred_element_type=jnp.float32)
                probability = jnp.exp2(scores * scale - log_total)
                if masked:
                    probability = jnp.where(pair.allowed(tile), probability, 0.0)
                prob_grad = jnp.dot(values[span], grad_t, preferred_element_type=jnp.float32)
                score_grad = (probability * (prob_grad - delta)).astype(jnp.bfloat16)
                value_sum[span] += jnp.dot(
                    probability.astype(jnp.bfloat16), grad, preferred_element_type=jnp.float32)
                key_sum[span] += jnp.dot(score_grad, query, preferred_element_type=jnp.float32)
                return query_grad + jnp.dot(keys_t[:, span], score_grad, preferred_element_type=jnp.float32)

            query_grad = jnp.zeros((HEAD_DIM, 2 * BLOCK), jnp.float32)
            query_grad = lax.fori_loop(0, pair.open_tiles, lambda tile, c: step(tile, c, False), query_grad)
            query_grad = lax.fori_loop(pair.open_tiles, pair.tiles, lambda tile, c: step(tile, c, True), query_grad)
            pair.store_t(dq_ref, query_grad * plain_scale)

        @pl.loop(0, key_count)
        def _(block):
            at, dealt = block_rows(block), block_rows(slot_ref[block])
            dk_ref[dealt] = (key_sum[at] * plain_scale).astype(dk_ref.dtype)
            dv_ref[dealt] = value_sum[at].astype(dv_ref.dtype)

    return pl.pallas_call(
        kernel,
        out_shape=[
            jax.ShapeDtypeStruct(queries.shape, jnp.bfloat16),
            jax.ShapeDtypeStruct(shared.shape[1:], jnp.bfloat16),
            jax.ShapeDtypeStruct(shared.shape[1:], jnp.bfloat16),
        ],
        in_specs=[SMEM] * 2 + [VMEM] * 5,
        out_specs=[VMEM] * 3,
        scratch_shapes=[
            pltpu.SMEM((2 * pairs,), jnp.int32), pltpu.SMEM((2 * pairs,), jnp.int32),
            pltpu.VMEM((padded, HEAD_DIM), jnp.bfloat16),
            pltpu.VMEM((HEAD_DIM, padded), jnp.bfloat16),
            pltpu.VMEM((padded, HEAD_DIM), jnp.bfloat16),
            pltpu.VMEM((padded, HEAD_DIM), jnp.float32),
            pltpu.VMEM((padded, HEAD_DIM), jnp.float32),
        ],
        compiler_params=pltpu.CompilerParams(vmem_limit_bytes=60 * MIB),
        cost_estimate=pl.CostEstimate(flops=20 << 30, bytes_accessed=100 * MIB, transcendentals=8 << 20),
    )(lengths, slot, queries, shared, upstream, exact, logs)


def line_neighbours(mp, count):
    return ((1, mp + 1 < count, jnp.minimum(mp + 1, count - 1)), (-1, mp >= 1, jnp.maximum(mp - 1, 0)))


def greet_all(fixed, dp, mp, count):
    barrier = pltpu.get_barrier_semaphore()
    for peer in fixed:
        pl.semaphore_signal(barrier, inc=1, device_id=peer, device_id_type=MESH)
    expected = jnp.int32(len(fixed))
    for _, there, place in line_neighbours(mp, count):

        @pl.when(there)
        def _():
            pl.semaphore_signal(barrier, inc=1, device_id=(dp, place), device_id_type=MESH)

        expected = expected + there.astype(jnp.int32)
    pl.semaphore_wait(barrier, expected)


class LineGather:
    def __init__(self, own, full, rows, pieces, send_sem, recv_sem, dp, mp, count):
        self.own, self.full, self.rows, self.pieces = own, full, rows, pieces
        self.send_sem, self.recv_sem, self.dp, self.mp, self.count = send_sem, recv_sem, dp, mp, count
        self.size = rows // pieces

    def place(self, block, piece):
        return self.full.at[pl.ds(pl.multiple_of(block * self.rows + piece * self.size, self.size), self.size)]

    def hop(self, way, step, piece):
        sign, there, neighbour = line_neighbours(self.mp, self.count)[way]
        origin = self.mp - sign * step
        exists = (origin >= 0) & (origin < self.count)
        origin = jnp.clip(origin, 0, self.count - 1)
        if step == 0:
            source = self.own.at[pl.ds(pl.multiple_of(piece * self.size, self.size), self.size)]
        else:
            source = self.place(origin, piece)
        def copy():
            return remote(source, self.place(origin, piece), self.send_sem.at[way, step, piece],
                          self.recv_sem.at[way, step, piece], (self.dp, neighbour))

        return exists, exists & there, copy

    def advance(self, step, piece, also=True, ways=(0, 1)):
        for way in ways:
            if step:
                exists, _, _ = self.hop(way, step, piece)
                _, _, earlier = self.hop(way, step - 1, piece)

                @pl.when(exists & also)
                def _():
                    earlier().wait_recv()

            if step < self.count - 1:
                _, sends, copy = self.hop(way, step, piece)

                @pl.when(sends & also)
                def _():
                    copy().start()

    def finish(self):
        @pl.loop(0, self.pieces)
        def _(piece):
            for way in range(2):
                for step in range(self.count - 1):
                    _, sends, copy = self.hop(way, step, piece)

                    @pl.when(sends)
                    def _():
                        copy().wait_send()

    @staticmethod
    def semaphores(count, pieces):
        return [pltpu.SemaphoreType.DMA((2, count, pieces)), pltpu.SemaphoreType.DMA((2, count, pieces))]


class ShardGather:
    def __init__(self, shards, wholes, depth, cross_send, cross_recv, core_send, core_recv, own_sem, dp, mp, chips):
        self.shards, self.wholes, self.depth, self.own_sem = shards, wholes, depth, own_sem
        self.cross_send, self.cross_recv, self.core_send, self.core_recv = cross_send, cross_recv, core_send, core_recv
        self.dp, self.mp, self.chips = dp, mp, chips

    def place(self, array, owner):
        return self.wholes[array].at[pl.ds(pl.multiple_of(owner * self.depth, self.depth), self.depth)]

    def cross(self, array, o):
        return remote(self.shards[array], self.place(array, self.dp), self.cross_send.at[array, o],
                      self.cross_recv.at[array, o], (self.dp ^ (2 * o), self.mp))

    def core(self, array, o):
        owner = self.dp ^ (2 * o)
        source = self.place(array, owner) if o else self.shards[array]
        return remote(source, self.place(array, owner), self.core_send.at[array, o], self.core_recv.at[array, o],
                      (self.dp ^ 1, self.mp))

    def own(self, array):
        return pltpu.make_async_copy(self.shards[array], self.place(array, self.dp), self.own_sem.at[array])

    def begin(self):
        for array in range(len(self.shards)):
            for o in range(1, self.chips):
                self.cross(array, o).start()
        for array in range(len(self.shards)):
            self.own(array).start()
            self.core(array, 0).start()

    def spread(self, array):
        for o in range(1, self.chips):
            self.cross(array, o).wait_recv()
            self.core(array, o).start()

    def finish(self):
        for array in range(len(self.shards)):
            self.own(array).wait()
            for o in range(self.chips):
                self.core(array, o).wait()
                if o:
                    self.cross(array, o).wait_send()

    @staticmethod
    def semaphores(count, chips):
        return [pltpu.SemaphoreType.DMA((count, chips)) for _ in range(4)] + [pltpu.SemaphoreType.DMA((count,))]


class LineReduce:
    def __init__(self, part, flows, rows, pieces, send_sem, recv_sem, dp, mp, count):
        self.part, self.flows, self.rows, self.pieces = part, flows, rows, pieces
        self.send_sem, self.recv_sem, self.dp, self.mp, self.count = send_sem, recv_sem, dp, mp, count
        self.size = rows // pieces

    def span(self, block, piece):
        return pl.ds(pl.multiple_of(block * self.rows + piece * self.size, self.size), self.size)

    def hop(self, way, block, piece, first=False):
        neighbour = line_neighbours(self.mp, self.count)[way][2]
        span = self.span(block, piece)
        source = self.part.at[span] if first else self.flows.at[way, span]
        return remote(source, self.flows.at[way, span], self.send_sem.at[way, block, piece],
                      self.recv_sem.at[way, block, piece], (self.dp, neighbour))

    def roles(self, way, block):
        if way == 0:
            behind, ahead = self.mp >= 1, self.mp < block
        else:
            behind, ahead = self.mp < self.count - 1, self.mp > block
        return ahead & jnp.logical_not(behind), ahead & behind

    def targets(self):
        for index in range(self.count - 1):
            yield 0, self.count - 1 - index
            yield 1, index

    def begin(self, piece, also=True):
        for way, block in self.targets():
            begins, _ = self.roles(way, block)

            @pl.when(begins & also)
            def _():
                self.hop(way, block, piece, True).start()

    def advance(self, turn):
        for way, block in self.targets():
            _, hands_on = self.roles(way, block)
            passed = SKEW * (self.mp - 1 if way == 0 else self.count - 2 - self.mp)
            piece = jnp.clip(turn - passed, 0, self.pieces - 1)

            @pl.when(hands_on & (turn >= passed) & (turn - passed < self.pieces))
            def _():
                self.hop(way, block, piece).wait_recv()
                span = self.span(block, piece)
                value = self.flows[way, span].astype(jnp.float32) + self.part[span].astype(jnp.float32)
                self.flows[way, span] = value.astype(self.flows.dtype)
                self.hop(way, block, piece).start()

    def arrive(self, piece):
        for way in range(2):

            @pl.when(self.mp >= 1 if way == 0 else self.mp < self.count - 1)
            def _():
                self.hop(way, self.mp, piece).wait_recv()

    def total(self, piece, result):
        span = self.span(self.mp, piece)
        result[...] = self.part[span].astype(jnp.float32)
        for way in range(2):

            @pl.when(self.mp >= 1 if way == 0 else self.mp < self.count - 1)
            def _():
                result[...] += self.flows[way, span].astype(jnp.float32)

    def finish(self):
        @pl.loop(0, self.pieces)
        def _(piece):
            for way, block in self.targets():
                begins, hands_on = self.roles(way, block)

                @pl.when(begins)
                def _():
                    self.hop(way, block, piece, True).wait_send()

                @pl.when(hands_on)
                def _():
                    self.hop(way, block, piece).wait_send()

    @staticmethod
    def scratch(count, rows, width, pieces):
        return [pltpu.VMEM((2, count * rows, width), jnp.bfloat16),
                pltpu.SemaphoreType.DMA((2, count, pieces)), pltpu.SemaphoreType.DMA((2, count, pieces))]


AHEAD = 1
QUARTERS = 4
MAX_PIECES = 16
SKEW = 1


def pieces_of(rows):
    return min(MAX_PIECES, rows // 16)


def unit_rows(values):
    average = jnp.mean(values, axis=-1, keepdims=True)
    centred = values - average
    inverse = lax.rsqrt(jnp.mean(centred * centred, axis=-1, keepdims=True) + norm_epsilon)
    return centred * inverse, inverse


def project_first(
    hidden, output_grad, lengths, order, vectors, projections, out_weight, heads, members, collective_id
):
    rows, width = hidden.shape
    dp_count, mp_count = lax.axis_size("dp"), lax.axis_size("mp")
    chips, pieces, half = dp_count // 2, pieces_of(rows), rows // 2
    half_pieces = pieces_of(half)
    group_rows, depth, columns = mp_count * rows, projections[0].shape[0], projections[0].shape[1]
    each = width // dp_count // 128
    tall = [v.shape[0] // 128 for v in vectors]
    slab = sum(tall) + -sum(tall) % 8
    halves, kinds = heads // 2, 3
    arrays = kinds + 2
    offsets = sorted({2 * o for o in range(1, chips)} | {o for o in range(1, members)} | {o * members for o in range(1, heads)})

    def kernel(lengths_ref, order_ref, hidden_ref, upstream_ref, *refs):
        given, refs = refs[: len(vectors)], refs[len(vectors) :]
        weight_refs, out_weight_ref = refs[:kinds], refs[kinds]
        normed, all_vectors, weights, all_out, shared, queries, branch, live, half_rows = refs[kinds + 1 : kinds + 10]
        parts, refs = refs[-len(vectors) :], refs[: -len(vectors)]
        (vector_ref, upstream, load_sem, raw, stage, gains, biases, line_send, line_recv, row_sem, own_sem, cross_send, cross_recv, core_send, core_recv,
         head_local, head_send, head_recv, pair_send, pair_recv, half_send, half_recv, half_sem) = refs[kinds + 10 :]
        dp, mp = lax.axis_index("dp"), lax.axis_index("mp")
        loads = [pltpu.make_async_copy(given[k], parts[k], load_sem.at[k]) for k in range(len(vectors))]
        loads.append(pltpu.make_async_copy(upstream_ref, upstream, load_sem.at[len(vectors)]))
        for copy in loads:
            copy.start()
        vector_ref[...] = jnp.zeros_like(vector_ref)
        for copy in loads:
            copy.wait()
        first = 0
        for part, count in zip(parts, tall):
            for r in range(count):
                vector_ref[first + r] = part[r * 128 : (r + 1) * 128].astype(jnp.float32)
            first += count
        group, member = dp // members, dp % members
        partner = (dp ^ 1, mp)
        greet_all([(dp ^ o, mp) for o in offsets], dp, mp, mp_count)
        line = LineGather(hidden_ref, raw, rows, pieces, line_send, line_recv, dp, mp, mp_count)

        behind = LineGather(branch, half_rows, half, half_pieces, half_send, half_recv, dp, mp, mp_count)

        def follow(step):
            for way, steps in ((0, mp), (1, mp_count - 1 - mp)):

                @pl.loop(0, half_pieces)
                def _(piece):
                    behind.advance(0, piece, steps == step, (way,))

        between = (mp > 0) & (mp < mp_count - 1)

        def hand_half(step, also=True):
            @pl.loop(0, half_pieces)
            def _(piece):
                behind.advance(step, piece, also)

        def source(array):
            return (list(weight_refs) + [out_weight_ref, vector_ref])[array]

        def place(array, owner):
            if array < kinds:
                return weights.at[pl.ds(pl.multiple_of(owner * depth, depth), depth), pl.ds(array * columns, columns)]
            if array == kinds:
                return all_out.at[pl.ds(pl.multiple_of(owner * depth, depth), depth)]
            return all_vectors.at[pl.ds(pl.multiple_of(owner * slab, slab), slab)]

        def cross(array, o):
            return remote(source(array), place(array, dp), cross_send.at[array, o], cross_recv.at[array, o],
                          (dp ^ (2 * o), mp))

        def core(array, o):
            owner = dp ^ (2 * o)
            return remote(place(array, owner) if o else source(array), place(array, owner),
                          core_send.at[array, o], core_recv.at[array, o], partner)

        def own(array):
            return pltpu.make_async_copy(source(array), place(array, dp), own_sem.at[array])

        def block_span(block):
            return pl.ds(pl.multiple_of(block * rows, rows), rows)

        first_to_last = [kinds + 1] + list(range(kinds + 1))
        for array in first_to_last:
            for o in range(1, chips):
                cross(array, o).start()
            if array == first_to_last[0]:

                @pl.loop(0, pieces)
                def _(piece):
                    line.advance(0, piece)

        for block in range(rows // BLOCK):
            found = order_ref[(dp * group_rows + mp * rows) // BLOCK + block]
            valid = sequence_of(found, lengths_ref)[1]
            span = slice(block * BLOCK, (block + 1) * BLOCK)
            live[span] = (lax.broadcasted_iota(jnp.int32, (BLOCK, 128), 0) < valid).astype(jnp.float32)
            keep = lax.broadcasted_iota(jnp.int32, (BLOCK, width), 0) < valid
            branch[span] = jnp.where(keep, upstream[span].astype(jnp.float32), 0.0).astype(branch.dtype)
        own_half = pltpu.make_async_copy(
            branch.at[pl.ds(0, half)], half_rows.at[pl.ds(pl.multiple_of(mp * half, half), half)], half_sem)
        own_half.start()
        follow(0)
        own_rows = pltpu.make_async_copy(hidden_ref, raw.at[block_span(mp)], row_sem)
        own_rows.start()
        for array in first_to_last:
            own(array).start()
            core(array, 0).start()

        def spread(array):
            for o in range(1, chips):
                cross(array, o).wait_recv()
                core(array, o).start()

        def settle(array):
            own(array).wait()
            for o in range(chips):
                core(array, o).wait_recv()

        def norm(block):
            chunk = 64

            @pl.loop(0, rows // chunk)
            def _(part):
                span = pl.ds(pl.multiple_of(block * rows + part * chunk, chunk), chunk)
                unit, _ = unit_rows(raw[span].astype(jnp.float32))
                normed[span] = (unit * gains[0:1] + gains[1:2]).astype(normed.dtype)

        def each_block(low, high, visit):
            @pl.loop(0, mp_count)
            def _(block):
                distance = jnp.abs(block - mp)

                @pl.when((distance >= low) & (distance <= high))
                def _():
                    visit(block)

        def rows_of(kind_ref, owner, block):
            return kind_ref.at[pl.ds(pl.multiple_of(owner * group_rows + block * rows, rows), rows)]

        def pass_on(kind, o, block, piece):
            giver = (group ^ o) * members + member
            return [remote(piece, rows_of(shared.at[kind], giver, block), pair_send.at[kind, o, block, p - 1],
                           pair_recv.at[kind, o, block, p - 1], (group * members + (member ^ p), mp))
                    for p in range(1, members)]

        def head_copy(kind, o, block, to_shared):
            target = group ^ o
            piece = stage.at[kind, block, target]
            landing = rows_of(shared.at[kind], dp, block) if to_shared else rows_of(queries, group, block)
            return remote(piece, landing, head_send.at[kind, o, block], head_recv.at[kind, o, block],
                          (target * members + member, mp))

        def local_copy(kind, block, to_shared):
            landing = rows_of(shared.at[kind], dp, block) if to_shared else rows_of(queries, group, block)
            return pltpu.make_async_copy(stage.at[kind, block, group], landing, head_local.at[kind, block])

        def project(tile, block):
            kind, half = tile // halves, tile % halves
            span = pl.ds(pl.multiple_of(half * 256, 256), 256)
            across = pl.ds(pl.multiple_of(kind * columns + half * 256, 256), 256)
            value = jnp.dot(normed[block_span(block)], weights[:, across], preferred_element_type=jnp.float32)
            value = (value + biases[pl.ds(kind, 1), span]).astype(stage.dtype)
            for h in range(2):
                head = 2 * half + h
                stage[kind, block, head] = value[:, h * HEAD_DIM : (h + 1) * HEAD_DIM]
            for h in range(2):
                o = (2 * half + h) ^ group
                for to_shared in (True, False):
                    chosen = (kind < 2) if to_shared else (kind == 2)

                    @pl.when(chosen & (o != 0))
                    def _():
                        head_copy(kind, o, block, to_shared).start()

                    @pl.when(chosen & (o == 0))
                    def _():
                        local_copy(kind, block, to_shared).start()
                        if to_shared:
                            for copy in pass_on(kind, 0, block, stage.at[kind, block, group]):
                                copy.start()

        def hand_on(block):
            @pl.loop(0, 2)
            def _(kind):
                for o in range(1, heads):
                    head_copy(kind, o, block, True).wait_recv()
                    giver = (group ^ o) * members + member
                    for copy in pass_on(kind, o, block, rows_of(shared.at[kind], giver, block)):
                        copy.start()

        last = mp_count - 1
        for step in range(1, last):

            @pl.loop(0, pieces)
            def _(piece):
                line.advance(step, piece)

            follow(step)
            if step == 1:
                spread(kinds + 1)
                settle(kinds + 1)
                for owner in range(dp_count):
                    for r in range(each):
                        at = pl.ds((owner * each + r) * 128, 128)
                        for k in range(2):
                            gains[k : k + 1, at] = all_vectors[owner * slab + k * each + r : owner * slab + k * each + r + 1]
                biases[...] = jnp.zeros_like(biases)
                for head in range(heads):
                    feature = mp * heads + head
                    first = (feature // each) * slab + feature % each
                    for kind, k in ((1, 3), (2, 2)):
                        biases[kind : kind + 1, head * 128 : (head + 1) * 128] = all_vectors[pl.ds(first + k * each, 1)]
                own_rows.wait()
                each_block(0, 1, norm)
            else:
                each_block(step, step, norm)
        for array in range(kinds + 1):
            spread(array)
        for array in range(kinds):
            settle(array)
        tiles = kinds * halves

        @pl.loop(0, pieces)
        def _(piece):
            line.advance(last - 1 if last == 1 else last, piece)

            @pl.when(piece >= pieces - half_pieces)
            def _():
                behind.advance(1, piece - (pieces - half_pieces), between)

            @pl.when(piece < tiles)
            def _():
                each_block(0, last - 1, lambda block: project(piece, block))

        for step in range(2, last):
            hand_half(step, between)
        each_block(last, last, norm)

        @pl.loop(0, tiles)
        def _(tile):
            each_block(last, last, lambda block: project(tile, block))

        each_block(0, last - 1, hand_on)
        each_block(last, last, hand_on)
        for step in range(1, last):
            hand_half(step, jnp.logical_not(between))
        hand_half(last)
        line.finish()
        behind.finish()
        own_half.wait()
        settle(kinds)
        for array in first_to_last:
            for o in range(chips):
                core(array, o).wait_send()
                if o:
                    cross(array, o).wait_send()

        @pl.loop(0, mp_count)
        def _(block):
            for kind in range(kinds):
                to_shared = kind < 2
                local_copy(kind, block, to_shared).wait()
                for o in range(1, heads):
                    head_copy(kind, o, block, to_shared).wait_send()
                    if not to_shared:
                        head_copy(kind, o, block, to_shared).wait_recv()
                if to_shared:
                    for o in range(heads):
                        giver = (group ^ o) * members + member
                        for copy in pass_on(kind, o, block, rows_of(shared.at[kind], giver, block)):
                            copy.wait()

    dma = pltpu.SemaphoreType.DMA
    bf16, f32 = jnp.bfloat16, jnp.float32
    return pl.pallas_call(
        kernel,
        out_shape=[
            jax.ShapeDtypeStruct((group_rows, width), bf16),
            jax.ShapeDtypeStruct((dp_count * slab, 128), f32),
            jax.ShapeDtypeStruct((width, kinds * columns), bf16),
            jax.ShapeDtypeStruct((width, columns), bf16),
            jax.ShapeDtypeStruct((2, dp_count * group_rows, HEAD_DIM), bf16),
            jax.ShapeDtypeStruct((heads * group_rows, HEAD_DIM), bf16),
            jax.ShapeDtypeStruct((rows, width), bf16),
            jax.ShapeDtypeStruct((rows, 128), f32),
            jax.ShapeDtypeStruct((mp_count * half, width), bf16),
        ],
        in_specs=[SMEM, SMEM] + [ANY] * (len(vectors) + kinds + 3),
        out_specs=[VMEM, VMEM, VMEM, ANY, ANY, ANY, VMEM, VMEM, ANY],
        scratch_shapes=[
            pltpu.VMEM((slab, 128), f32),
            pltpu.VMEM((rows, width), bf16),
            dma((len(vectors) + 1,)),
            pltpu.VMEM((group_rows, width), bf16),
            pltpu.VMEM((kinds, mp_count, heads, rows, HEAD_DIM), bf16),
            pltpu.VMEM((8, width), f32),
            pltpu.VMEM((8, columns), f32),
        ]
        + LineGather.semaphores(mp_count, pieces)
        + [dma(()), dma((arrays,))]
        + [dma((arrays, chips)) for _ in range(4)]
        + [dma((kinds, mp_count)), dma((kinds, heads, mp_count)), dma((kinds, heads, mp_count))]
        + [dma((2, heads, mp_count, members)) for _ in range(2)]
        + LineGather.semaphores(mp_count, half_pieces) + [dma(())]
        + [pltpu.VMEM(v.shape, v.dtype) for v in vectors],
        compiler_params=pltpu.CompilerParams(
            collective_id=collective_id, has_side_effects=True, vmem_limit_bytes=63 * MIB),
        cost_estimate=pl.CostEstimate(flops=8 << 30, bytes_accessed=250 * MIB, transcendentals=0),
    )(lengths, order, hidden, output_grad, *vectors, *projections, out_weight)


def mix_norm_gather(mixed, out_weight, hidden, out_bias, gain, shift, shards, heads, members, collective_id):
    dp_count, mp_count = lax.axis_size("dp"), lax.axis_size("mp")
    chips, count = dp_count // 2, len(shards)
    rows, width = hidden.shape
    pieces = pieces_of(rows)
    size, columns, group_rows = rows // pieces, heads * HEAD_DIM, mp_count * rows
    quarter, per_quarter = rows // QUARTERS, pieces // QUARTERS
    slice_rows = width // per_quarter
    offsets = sorted({2 * o for o in range(1, chips)} | {1} | {o * members for o in range(1, heads)})
    mixed = mixed.reshape(heads, mp_count, rows, HEAD_DIM)
    turns = pieces + 2 * SKEW * (mp_count - 1)

    def kernel(mixed_ref, out_hbm, hidden_ref, bias_ref, gain_ref, shift_ref, *refs):
        shard_refs, (residual_ref, landed, full_ref), refs = refs[:count], refs[count : count + 3], refs[count + 3 :]
        whole_refs, refs = refs[:count], refs[count:]
        (part, out_rows, load_sem, local_sem, head_send, head_recv,
         total, normed, flows, red_send, red_recv, line_send, line_recv, own_sem, *weight_sems) = refs
        dp, mp = lax.axis_index("dp"), lax.axis_index("mp")
        group, member = dp // members, dp % members
        greet_all([(dp ^ o, mp) for o in offsets], dp, mp, mp_count)

        def landing(k, head):
            return landed.at[:, pl.ds(k * quarter, quarter), lanes(head)]

        def head_copy(o, k):
            return remote(mixed_ref.at[group ^ o, :, pl.ds(k * quarter, quarter)], landing(k, group),
                          head_send.at[o, k], head_recv.at[o, k], ((group ^ o) * members + member, mp))

        def local_copy(k):
            return pltpu.make_async_copy(mixed_ref.at[group, :, pl.ds(k * quarter, quarter)], landing(k, group),
                                         local_sem.at[k])

        def arrived(k):
            for o in range(1, heads):
                head_copy(o, k).wait_recv()
            local_copy(k).wait()

        def project(k, first, count):
            span = pl.ds(pl.multiple_of(k * quarter, quarter), quarter)
            left = landed[:, span].reshape(mp_count * quarter, columns)
            features = pl.ds(pl.multiple_of(first, count), count)
            value = contract_last(left, out_rows[features]).astype(part.dtype)
            for block in range(mp_count):
                at = pl.ds(pl.multiple_of(block * rows + k * quarter, quarter), quarter)
                part[at, features] = value[block * quarter : (block + 1) * quarter]

        load = pltpu.make_async_copy(out_hbm, out_rows, load_sem)
        load.start()
        for k in range(QUARTERS):
            for o in range(1, heads):
                head_copy(o, k).start()
            local_copy(k).start()
        weights = ShardGather(shard_refs, whole_refs, shards[0].shape[0], *weight_sems, dp, mp, chips)
        weights.begin()
        reduce = LineReduce(part, flows, rows, pieces, red_send, red_recv, dp, mp, mp_count)
        gather = LineGather(normed, full_ref, rows, pieces, line_send, line_recv, dp, mp, mp_count)
        load.wait()
        arrived(0)
        for portion in range(per_quarter):
            project(0, portion * slice_rows, slice_rows)
        for piece in range(AHEAD):
            reduce.begin(piece)

        @pl.loop(0, turns)
        def _(turn):
            for array in range(count):

                @pl.when(turn == turns - 1 - 6 * (count - 1 - array))
                def _():
                    weights.spread(array)

            for k in range(1, QUARTERS):

                @pl.when(turn == (k - 1) * per_quarter)
                def _():
                    arrived(k)

            @pl.when(turn < (QUARTERS - 1) * per_quarter)
            def _():
                project(turn // per_quarter + 1, (turn % per_quarter) * slice_rows, slice_rows)

            reduce.begin(jnp.minimum(turn + AHEAD, pieces - 1), turn + AHEAD < pieces)
            reduce.advance(turn)
            done = turn - SKEW * (mp_count - 1)

            @pl.when((done >= 0) & (done < pieces))
            def _():
                reduce.arrive(done)
                reduce.total(done, total)
                span = pl.ds(pl.multiple_of(done * size, size), size)
                residual = hidden_ref[span].astype(jnp.float32) + total[...] + bias_ref[...]
                residual_ref[span] = residual
                unit, _ = unit_rows(residual)
                normed[span] = (unit * gain_ref[...] + shift_ref[...]).astype(normed.dtype)
                gather.advance(0, done)

            for step in range(1, mp_count):
                late = done - SKEW * step
                gather.advance(step, jnp.clip(late, 0, pieces - 1), (late >= 0) & (late < pieces))

        own = pltpu.make_async_copy(normed, full_ref.at[pl.ds(pl.multiple_of(mp * rows, rows), rows)], own_sem)
        own.start()
        reduce.finish()
        gather.finish()
        own.wait()
        weights.finish()
        for k in range(QUARTERS):
            for o in range(1, heads):
                head_copy(o, k).wait_send()

    dma = pltpu.SemaphoreType.DMA
    return pl.pallas_call(
        kernel,
        out_shape=[
            jax.ShapeDtypeStruct((rows, width), jnp.float32),
            jax.ShapeDtypeStruct((mp_count, rows, columns), jnp.bfloat16),
            jax.ShapeDtypeStruct((group_rows, width), jnp.bfloat16),
        ]
        + [jax.ShapeDtypeStruct((dp_count * a.shape[0], a.shape[1]), a.dtype) for a in shards],
        in_specs=[ANY] * 2 + [VMEM] * 4 + [ANY] * count,
        out_specs=[VMEM, VMEM, ANY] + [ANY] * count,
        scratch_shapes=[
            pltpu.VMEM((group_rows, width), jnp.bfloat16), pltpu.VMEM((width, columns), jnp.bfloat16),
            dma(()), dma((QUARTERS,)), dma((heads, QUARTERS)), dma((heads, QUARTERS)),
        ]
        + [pltpu.VMEM((size, width), jnp.float32), pltpu.VMEM((rows, width), jnp.bfloat16)]
        + LineReduce.scratch(mp_count, rows, width, pieces) + LineGather.semaphores(mp_count, pieces)
        + [pltpu.SemaphoreType.DMA(())] + ShardGather.semaphores(count, chips),
        compiler_params=pltpu.CompilerParams(
            collective_id=collective_id, has_side_effects=True, vmem_limit_bytes=63 * MIB),
        cost_estimate=pl.CostEstimate(flops=0, bytes_accessed=300 * MIB, transcendentals=0),
    )(mixed, out_weight, hidden, out_bias, gain, shift, *shards)


def reduce_back_gather(
    part, residual, branch_two, gain, halves, pairs, down_weight, out_weight, heads, members, collective_id
):
    dp_count, mp_count = lax.axis_size("dp"), lax.axis_size("mp")
    chips, count = dp_count // 2, len(pairs)
    rows, width = residual.shape
    half = rows // 2
    pieces = pieces_of(rows)
    size, depth = rows // pieces, width // dp_count
    units = pairs[0][1].shape[1]
    turns = pieces + 2 * SKEW * (mp_count - 1)
    each = dp_count // 4
    busy = count * dp_count // each
    feed_slices = 8
    feed_rows = width // feed_slices
    assert 1 + busy + feed_slices <= turns
    quarter, per_quarter, columns = rows // QUARTERS, pieces // QUARTERS, heads * HEAD_DIM
    group_rows = mp_count * rows
    offsets = sorted({2 * o for o in range(1, chips)} | {1} | {o * members for o in range(1, heads)})

    def kernel(part_ref, residual_ref, branch_ref, gain_ref, *refs):
        operands, down_ref, out_hbm, refs = refs[: 2 * count + 1], refs[2 * count + 1], refs[2 * count + 2], refs[2 * count + 3 :]
        (grad_ref, sums_ref, full_ref, feed_ref, heads_ref), terms, refs = refs[:5], refs[5 : 5 + count], refs[5 + count :]
        loaded, refs = refs[: 2 * count], refs[2 * count :]
        (credit, down_rows, down_sem, fed, fed_sem, out_rows, out_sem, gathered, gathered_sem, stage,
         stage_sem, head_send, head_recv, half_sem, total, low, kept, slices, from_partner, chip_sum, load_sem, keep_sem, pair_send, pair_recv, cross_send, cross_recv,
         flows, red_send, red_recv, line_send, line_recv, own_sem) = refs
        dp, mp = lax.axis_index("dp"), lax.axis_index("mp")
        partner = (dp ^ 1, mp)
        group, member = dp // members, dp % members
        greet_all([(dp ^ o, mp) for o in offsets], dp, mp, mp_count)
        reduce = LineReduce(part_ref, flows, rows, pieces, red_send, red_recv, dp, mp, mp_count)
        gather = LineGather(low, full_ref, rows, pieces, line_send, line_recv, dp, mp, mp_count)
        for piece in range(AHEAD):
            reduce.begin(piece)
        loads = [[] for _ in range(count)]
        for h in range(2):
            for b in range(mp_count):
                to = pl.ds(b * rows + h * half, half)
                loads[0].append(pltpu.make_async_copy(
                    operands[h].at[pl.ds(b * half, half)], loaded[0].at[to], half_sem.at[h, b]))
        for index in range(1, 2 * count):
            loads[index // 2].append(pltpu.make_async_copy(operands[index + 1], loaded[index], load_sem.at[index]))
        for copy in loads[0] + loads[1]:
            copy.start()
        sums_ref[...] = jnp.zeros_like(sums_ref)

        def pair(mat, o):
            return remote(slices.at[o], from_partner.at[o], pair_send.at[mat, o], pair_recv.at[mat, o], partner)

        def cross(mat, o, peer):
            return remote(chip_sum.at[mat, o - 1], terms[mat].at[o], cross_send.at[mat, o], cross_recv.at[mat, o],
                          (peer, mp))

        def weight_slice(mat, index):
            o = (index + 1) % chips
            mine = index >= chips
            owner = dp ^ (2 * o) ^ jnp.where(mine, 0, 1)
            left = loaded[2 * mat][:, pl.ds(pl.multiple_of(owner * depth, depth), depth)]
            value = contract_first(left, loaded[2 * mat + 1][...])

            @pl.when(jnp.logical_not(mine))
            def _():
                if mat:
                    pair(mat - 1, o).wait_send()
                    pl.semaphore_wait(credit, 1)
                slices[o] = value.astype(slices.dtype)
                pair(mat, o).start()

            @pl.when(mine)
            def _():
                pair(mat, o).wait_recv()
                both = (value + from_partner[o].astype(jnp.float32)).astype(slices.dtype)
                if mat < count - 1:
                    pl.semaphore_signal(credit, inc=1, device_id=partner, device_id_type=MESH)

                @pl.when(o == 0)
                def _():
                    kept[mat] = both
                    pltpu.make_async_copy(kept.at[mat], terms[mat].at[0], keep_sem.at[mat]).start()

                @pl.when(o != 0)
                def _():
                    chip_sum[mat, o - 1] = both
                    cross(mat, o, owner).start()

        def down_load(index):
            at = pl.ds(pl.multiple_of(index * feed_rows, feed_rows), feed_rows)
            return pltpu.make_async_copy(down_ref.at[at], down_rows.at[index % 2], down_sem.at[index % 2])

        def feed_store(index):
            at = pl.ds(pl.multiple_of(index * feed_rows, feed_rows), feed_rows)
            return pltpu.make_async_copy(fed.at[index % 2], feed_ref.at[:, at], fed_sem.at[index % 2])

        def feed_slice(index):
            down_load(index).wait()

            @pl.when(index + 1 < feed_slices)
            def _():
                down_load(index + 1).start()

            @pl.when(index >= 2)
            def _():
                feed_store(index - 2).wait()

            fed[index % 2] = contract_last(loaded[1][...], down_rows[index % 2]).astype(fed.dtype)
            feed_store(index).start()

        def rows_load(k, block, own):
            source = low.at[pl.ds(k * quarter, quarter)] if own else full_ref.at[
                pl.ds(pl.multiple_of(block * rows + k * quarter, quarter), quarter)]
            return pltpu.make_async_copy(source, gathered.at[block], gathered_sem.at[block])

        def head_copy(o, k):
            span = pl.ds(k * quarter, quarter)
            return remote(stage.at[:, span, lanes(group ^ o)], heads_ref.at[group, :, span], head_send.at[o, k],
                          head_recv.at[o, k], ((group ^ o) * members + member, mp))

        def local_copy(k):
            span = pl.ds(k * quarter, quarter)
            return pltpu.make_async_copy(stage.at[:, span, lanes(group)], heads_ref.at[group, :, span], stage_sem.at[k])

        def to_heads(k):
            for block in range(mp_count):
                for own in (True, False):

                    @pl.when((mp == block) if own else (mp != block))
                    def _():
                        rows_load(k, block, own).start()

            for block in range(mp_count):
                for own in (True, False):

                    @pl.when((mp == block) if own else (mp != block))
                    def _():
                        rows_load(k, block, own).wait()

            value = jnp.dot(gathered[...].reshape(mp_count * quarter, width), out_rows[...],
                            preferred_element_type=jnp.float32)
            stage[:, k * quarter : (k + 1) * quarter] = value.reshape(mp_count, quarter, columns).astype(stage.dtype)
            for o in range(1, heads):
                head_copy(o, k).start()
            local_copy(k).start()

        out_load = pltpu.make_async_copy(out_hbm, out_rows, out_sem)
        out_load.start()
        down_load(0).start()

        @pl.loop(0, turns)
        def _(turn):
            reduce.begin(jnp.minimum(turn + AHEAD, pieces - 1), turn + AHEAD < pieces)
            reduce.advance(turn)
            done = turn - SKEW * (mp_count - 1)

            @pl.when((done >= 0) & (done < pieces))
            def _():
                reduce.arrive(done)
                reduce.total(done, total)
                span = pl.ds(pl.multiple_of(done * size, size), size)
                unit, inverse = unit_rows(residual_ref[span])
                upstream = total[...]
                sums_ref[0:1] += jnp.sum(upstream * unit, axis=0, keepdims=True)
                sums_ref[1:2] += jnp.sum(upstream, axis=0, keepdims=True)
                grad = branch_ref[span].astype(jnp.float32) + norm_back(upstream, unit, inverse, gain_ref[...])
                grad_ref[span] = grad
                rounded = grad.astype(low.dtype)
                low[span] = rounded
                sums_ref[2:3] += jnp.sum(rounded.astype(jnp.float32), axis=0, keepdims=True)
                gather.advance(0, done)

            for step in range(1, mp_count):
                late = done - SKEW * step
                gather.advance(step, jnp.clip(late, 0, pieces - 1), (late >= 0) & (late < pieces))
            for mat in range(count):

                @pl.when(turn == 1 + mat * busy // count)
                def _():
                    for copy in loads[mat]:
                        copy.wait()

                first = turn - 1 - mat * busy // count

                @pl.when((first >= 0) & (first < busy // count))
                def _():
                    for i in range(each):
                        weight_slice(mat, first * each + i)

            @pl.when((turn >= 1 + busy) & (turn < 1 + busy + feed_slices))
            def _():
                feed_slice(turn - 1 - busy)

            for k in range(QUARTERS):

                @pl.when(turn == (k + 1) * per_quarter - 1 + 2 * SKEW * (mp_count - 1))
                def _():
                    if k == 0:
                        out_load.wait()
                    to_heads(k)

        own = pltpu.make_async_copy(low, full_ref.at[pl.ds(pl.multiple_of(mp * rows, rows), rows)], own_sem)
        own.start()
        reduce.finish()
        gather.finish()
        own.wait()
        for index in range(feed_slices - 2, feed_slices):
            feed_store(index).wait()
        for k in range(QUARTERS):
            local_copy(k).wait()
            for o in range(1, heads):
                head_copy(o, k).wait()
        for mat in range(count):
            pltpu.make_async_copy(kept.at[mat], terms[mat].at[0], keep_sem.at[mat]).wait()
            for o in range(chips):
                if mat == count - 1:
                    pair(mat, o).wait_send()
                if o:
                    cross(mat, o, dp ^ (2 * o)).wait()

    bf16, f32 = jnp.bfloat16, jnp.float32
    dma = pltpu.SemaphoreType.DMA
    flat = [array for two in pairs for array in two][1:]
    return pl.pallas_call(
        kernel,
        out_shape=[
            jax.ShapeDtypeStruct((rows, width), f32),
            jax.ShapeDtypeStruct((8, width), f32),
            jax.ShapeDtypeStruct((group_rows, width), bf16),
            jax.ShapeDtypeStruct((group_rows, width), bf16),
            jax.ShapeDtypeStruct((heads, mp_count, rows, HEAD_DIM), bf16),
        ]
        + [jax.ShapeDtypeStruct((chips, depth, units), bf16)] * count,
        in_specs=[VMEM] * 4 + [ANY] * (2 * count + 3),
        out_specs=[VMEM, VMEM] + [ANY] * (3 + count),
        scratch_shapes=[pltpu.VMEM((mp_count * rows, width), bf16)] + [pltpu.VMEM(a.shape, a.dtype) for a in flat]
        + [
            pltpu.SemaphoreType.REGULAR,
            pltpu.VMEM((2, feed_rows, units), bf16), dma((2,)),
            pltpu.VMEM((2, group_rows, feed_rows), bf16), dma((2,)),
            pltpu.VMEM((width, columns), bf16), dma(()),
            pltpu.VMEM((mp_count, quarter, width), bf16), dma((mp_count,)),
            pltpu.VMEM((mp_count, rows, columns), bf16), dma((QUARTERS,)),
            dma((heads, QUARTERS)), dma((heads, QUARTERS)),
            dma((2, mp_count)),
            pltpu.VMEM((size, width), f32),
            pltpu.VMEM((rows, width), bf16),
            pltpu.VMEM((count, depth, units), bf16),
            pltpu.VMEM((chips, depth, units), bf16),
            pltpu.VMEM((chips, depth, units), bf16),
            pltpu.VMEM((count, chips - 1, depth, units), bf16),
            dma((2 * count,)), dma((count,)),
        ]
        + [dma((count, chips)) for _ in range(4)]
        + LineReduce.scratch(mp_count, rows, width, pieces) + LineGather.semaphores(mp_count, pieces)
        + [dma(())],
        compiler_params=pltpu.CompilerParams(
            collective_id=collective_id, has_side_effects=True, vmem_limit_bytes=63 * MIB),
        cost_estimate=pl.CostEstimate(flops=40 << 30, bytes_accessed=300 * MIB, transcendentals=0),
    )(part, residual, branch_two, gain, *halves, *flat, down_weight, out_weight)


def finish_back(query_grad, key_part, value_part, weights, normed, residual_grad, hidden, gain, out_part, vectors, heads, members,
                collective_id):
    rows, width = hidden.shape
    dp_count, mp_count = lax.axis_size("dp"), lax.axis_size("mp")
    chips, pieces = dp_count // 2, pieces_of(rows)
    size, depth, columns = rows // pieces, width // dp_count, heads * HEAD_DIM
    kinds, quarter = 3, rows // QUARTERS
    per_quarter = pieces // QUARTERS
    slice_rows = width // per_quarter
    turns = pieces + SKEW * (mp_count - 1)
    slices_each = max(dp_count // 8, 1)
    slice_turn = turns // 3
    group_rows = mp_count * rows
    slab, each = vectors.shape[1], width // dp_count // 128
    query_grad = query_grad.reshape(heads, mp_count, rows, HEAD_DIM)
    shared = [v.reshape(dp_count, mp_count, rows, HEAD_DIM) for v in (key_part, value_part)]

    def kernel(query_ref, key_ref, value_ref, weights_hbm, normed_hbm, residual_ref, hidden_ref, gain_ref, out_ref, vector_ref,
               grad_ref, weight_grad_ref, out_grad_ref, summed_ref,
               weights, normed, landed, own, parts, stage, part, total, flows, red_send, red_recv,
               slices, from_partner, chip_sum, from_chips, out_partner, out_sum, out_chips,
               load_sem, own_sem, part_send, part_recv, local_sem, head_send, head_recv,
               pair_send, pair_recv, cross_send, cross_recv,
               sums_ref, column_ref, packed, vector_parts, line_parts, vec_send, vec_recv, line_send, line_recv):
        dp, mp = lax.axis_index("dp"), lax.axis_index("mp")
        group, member = dp // members, dp % members
        partner = (dp ^ 1, mp)
        greet_all([(dp ^ o, mp) for o in range(1, dp_count)] + [(dp, mp ^ o) for o in range(1, mp_count)], dp, mp, mp_count)
        reduce = LineReduce(part, flows, rows, pieces, red_send, red_recv, dp, mp, mp_count)
        loads = [pltpu.make_async_copy(weights_hbm, weights, load_sem.at[0]),
                 pltpu.make_async_copy(normed_hbm, normed, load_sem.at[1])]
        shared_refs = (key_ref, value_ref)

        def rows_of(k):
            return pl.ds(k * quarter, quarter)

        def lane_span(kind, head):
            return pl.ds(pl.multiple_of(kind * columns + head * HEAD_DIM, HEAD_DIM), HEAD_DIM)

        def landing(kind, k, head):
            return landed.at[:, rows_of(k), lane_span(kind, head)]

        def own_copy(kind, o):
            return pltpu.make_async_copy(shared_refs[kind].at[(group ^ o) * members + member], own.at[kind, o],
                                         own_sem.at[kind, o])

        def part_copy(kind, o, p, k):
            return remote(shared_refs[kind].at[(group ^ o) * members + (member ^ p), :, rows_of(k)],
                          parts.at[kind, o, p - 1, :, rows_of(k)], part_send.at[kind, o, p - 1, k],
                          part_recv.at[kind, o, p - 1, k], (group * members + (member ^ p), mp))

        def head_copy(kind, o, k):
            source = query_ref.at[group ^ o, :, rows_of(k)] if kind == 2 else stage.at[kind, o, :, rows_of(k)]
            return remote(source, landing(kind, k, group), head_send.at[kind, o, k], head_recv.at[kind, o, k],
                          ((group ^ o) * members + member, mp))

        def local_copy(k):
            return pltpu.make_async_copy(query_ref.at[group, :, rows_of(k)], landing(2, k, group), local_sem.at[k])

        for k in range(QUARTERS):
            for kind in range(2):
                for o in range(heads):
                    for p in range(1, members):
                        part_copy(kind, o, p, k).start()
            if k == 0:
                for kind in range(2):
                    for o in range(heads):
                        own_copy(kind, o).start()
                for copy in loads:
                    copy.start()
            for o in range(1, heads):
                head_copy(2, o, k).start()
            local_copy(k).start()
        for k in range(QUARTERS):
            for kind in range(2):
                for o in list(range(1, heads)) + [0]:
                    if k == 0:
                        own_copy(kind, o).wait()
                    value = own[kind, o, :, k * quarter : (k + 1) * quarter].astype(jnp.float32)
                    for p in range(1, members):
                        part_copy(kind, o, p, k).wait_recv()
                        value = value + parts[kind, o, p - 1, :, k * quarter : (k + 1) * quarter].astype(jnp.float32)
                    if o:
                        stage[kind, o, :, k * quarter : (k + 1) * quarter] = value.astype(stage.dtype)
                        head_copy(kind, o, k).start()
                    else:
                        landed[:, k * quarter : (k + 1) * quarter, lane_span(kind, group)] = value.astype(landed.dtype)

        def arrived(k):
            for kind in range(kinds):
                for o in range(1, heads):
                    head_copy(kind, o, k).wait_recv()
            local_copy(k).wait()

        def project(k, first, count):
            span = pl.ds(pl.multiple_of(k * quarter, quarter), quarter)
            left = landed[:, span].reshape(mp_count * quarter, kinds * columns)
            features = pl.ds(pl.multiple_of(first, count), count)
            value = contract_last(left, weights[features]).astype(part.dtype)
            for block in range(mp_count):
                at = pl.ds(pl.multiple_of(block * rows + k * quarter, quarter), quarter)
                part[at, features] = value[block * quarter : (block + 1) * quarter]

        def slab(owner):
            return pl.ds(pl.multiple_of(owner * depth, depth), depth)

        def pair(o):
            return remote(slices.at[o], from_partner.at[o], pair_send.at[0, o], pair_recv.at[0, o], partner)

        def cross(o, peer):
            return remote(chip_sum.at[o], from_chips.at[o], cross_send.at[0, o], cross_recv.at[0, o], (peer, mp))

        def out_pair(o):
            return remote(out_ref.at[slab(dp ^ (2 * o) ^ 1)], out_partner.at[o], pair_send.at[1, o], pair_recv.at[1, o],
                          partner)

        def out_cross(o):
            return remote(out_sum.at[o], out_chips.at[o], cross_send.at[1, o], cross_recv.at[1, o], (dp ^ (2 * o), mp))

        def weight_slice(index):
            o = (index + 1) % chips
            mine = index >= chips
            owner = dp ^ (2 * o) ^ jnp.where(mine, 0, 1)
            rows_all = landed[...].reshape(group_rows, kinds * columns)
            value = contract_first(normed[:, slab(owner)], rows_all)

            @pl.when(jnp.logical_not(mine))
            def _():
                slices[o] = value.astype(slices.dtype)
                pair(o).start()

            @pl.when(mine)
            def _():
                pair(o).wait_recv()
                both = value + from_partner[o].astype(jnp.float32)

                @pl.when(o == 0)
                def _():
                    weight_grad_ref[...] = both

                @pl.when(o != 0)
                def _():
                    chip_sum[o] = both.astype(chip_sum.dtype)
                    cross(o, owner).start()

        for copy in loads:
            copy.wait()
        arrived(0)
        for part_index in range(per_quarter):
            project(0, part_index * slice_rows, slice_rows)
        for o in range(chips):
            out_pair(o).start()
        sums_ref[...] = jnp.zeros_like(sums_ref)

        @pl.loop(0, turns)
        def _(turn):
            @pl.when(turn < pieces)
            def _():
                reduce.begin(jnp.minimum(turn, pieces - 1))

            reduce.advance(turn)
            done = turn - SKEW * (mp_count - 1)

            @pl.when(done >= 0)
            def _():
                reduce.arrive(done)
                reduce.total(done, total)
                span = pl.ds(pl.multiple_of(done * size, size), size)
                unit, inverse = unit_rows(hidden_ref[span].astype(jnp.float32))
                upstream = total[...]
                sums_ref[0:1] += jnp.sum(upstream * unit, axis=0, keepdims=True)
                sums_ref[1:2] += jnp.sum(upstream, axis=0, keepdims=True)
                grad_ref[span] = residual_ref[span] + norm_back(upstream, unit, inverse, gain_ref[...])

            for k in range(1, QUARTERS):

                @pl.when(turn == (k - 1) * per_quarter)
                def _():
                    arrived(k)

            @pl.when(turn < (QUARTERS - 1) * per_quarter)
            def _():
                k, portion = turn // per_quarter + 1, turn % per_quarter
                project(k, portion * slice_rows, slice_rows)

            @pl.when(turn == slice_turn)
            def _():
                for o in list(range(1, chips)) + [0]:
                    out_pair(o).wait_recv()
                    value = out_ref[slab(dp ^ (2 * o))].astype(jnp.float32) + out_partner[o].astype(jnp.float32)
                    if o:
                        out_sum[o] = value.astype(out_sum.dtype)
                        out_cross(o).start()
                    else:
                        out_grad_ref[...] = value

            @pl.when(turn == late_turn - 1)
            def _():
                column_ref[0:1] = jnp.sum(
                    landed[...].reshape(group_rows, kinds * columns).astype(jnp.float32), axis=0, keepdims=True)

            @pl.when((turn >= late_turn) & (turn < late_turn + dp_count // slices_each))
            def _():
                for i in range(slices_each):
                    weight_slice((turn - late_turn) * slices_each + i)

        reduce.finish()
        packed[...] = vector_ref[...]
        for owner in range(dp_count):
            for r in range(each):
                at = slice((owner * each + r) * 128, (owner * each + r + 1) * 128)
                for k in range(2):
                    packed[owner, k * each + r : k * each + r + 1] = sums_ref[k : k + 1, at]
        for head in range(heads):
            feature = mp * heads + head
            for k, kind in ((2, 2), (3, 1)):
                at = slice(kind * columns + head * HEAD_DIM, kind * columns + (head + 1) * HEAD_DIM)
                packed[feature // each, pl.ds(k * each + feature % each, 1)] = column_ref[0:1, at]

        def vector_copy(o):
            return remote(packed.at[dp ^ o], vector_parts.at[o], vec_send.at[o], vec_recv.at[o], (dp ^ o, mp))

        def line_copy(o):
            return remote(line_parts.at[mp], line_parts.at[mp], line_send.at[o], line_recv.at[o], (dp, mp ^ o))

        for o in range(1, dp_count):
            vector_copy(o).start()
        value = packed[dp]
        for o in range(1, dp_count):
            vector_copy(o).wait_recv()
            value = value + vector_parts[o]
        line_parts[mp] = value
        for o in range(1, mp_count):
            line_copy(o).start()
        for o in range(chips):
            pair(o).wait_send()
            out_pair(o).wait_send()
            if o:
                cross(o, dp ^ (2 * o)).wait()
                weight_grad_ref[...] += from_chips[o].astype(jnp.float32)
                out_cross(o).wait()
                out_grad_ref[...] += out_chips[o].astype(jnp.float32)
        for k in range(QUARTERS):
            for o in range(heads):
                for kind in range(2):
                    for p in range(1, members):
                        part_copy(kind, o, p, k).wait_send()
                if o:
                    for kind in range(kinds):
                        head_copy(kind, o, k).wait_send()
        for o in range(1, mp_count):
            line_copy(o).wait()
        value = line_parts[0]
        for index in range(1, mp_count):
            value = value + line_parts[index]
        summed_ref[...] = value
        for o in range(1, dp_count):
            vector_copy(o).wait_send()

    late_turn = max(slice_turn, (QUARTERS - 2) * per_quarter + 1)
    assert late_turn + dp_count // slices_each <= turns
    dma = pltpu.SemaphoreType.DMA
    bf16, f32 = jnp.bfloat16, jnp.float32
    own_columns = out_part.shape[1]
    return pl.pallas_call(
        kernel,
        out_shape=[
            jax.ShapeDtypeStruct((rows, width), f32),
            jax.ShapeDtypeStruct((depth, kinds * columns), f32),
            jax.ShapeDtypeStruct((depth, own_columns), f32),
            jax.ShapeDtypeStruct((slab, 128), f32),
        ],
        in_specs=[ANY] * 5 + [VMEM] * 5,
        out_specs=[VMEM] * 4,
        scratch_shapes=[
            pltpu.VMEM((width, kinds * columns), bf16),
            pltpu.VMEM((group_rows, width), bf16),
            pltpu.VMEM((mp_count, rows, kinds * columns), bf16),
            pltpu.VMEM((2, heads, mp_count, rows, HEAD_DIM), bf16),
            pltpu.VMEM((2, heads, members - 1, mp_count, rows, HEAD_DIM), bf16),
            pltpu.VMEM((2, heads, mp_count, rows, HEAD_DIM), bf16),
            pltpu.VMEM((group_rows, width), bf16),
            pltpu.VMEM((size, width), f32),
        ]
        + LineReduce.scratch(mp_count, rows, width, pieces)
        + [pltpu.VMEM((chips, depth, kinds * columns), bf16) for _ in range(4)]
        + [pltpu.VMEM((chips, depth, own_columns), bf16) for _ in range(3)]
        + [dma((2,)), dma((2, heads))]
        + [dma((2, heads, members - 1, QUARTERS)) for _ in range(2)]
        + [dma((QUARTERS,)), dma((kinds, heads, QUARTERS)), dma((kinds, heads, QUARTERS))]
        + [dma((2, chips)) for _ in range(4)]
        + [pltpu.VMEM((8, width), f32), pltpu.VMEM((8, kinds * columns), f32)]
        + [pltpu.VMEM((count, slab, 128), f32) for count in (dp_count, dp_count, mp_count)]
        + [dma((dp_count,)), dma((dp_count,)), dma((mp_count,)), dma((mp_count,))],
        compiler_params=pltpu.CompilerParams(
            collective_id=collective_id, has_side_effects=True, vmem_limit_bytes=63 * MIB),
        cost_estimate=pl.CostEstimate(flops=20 << 30, bytes_accessed=300 * MIB, transcendentals=0),
    )(query_grad, *shared, weights, normed, residual_grad, hidden, gain, out_part, vectors)


UNITS = 512
CHUNK = 256


def feed_both_ways(rows_two, branch_halves, block, up_all, down_all, up_bias):
    rows, width = rows_two.shape
    units = up_all.shape[1]
    tile = min(UNITS, units)
    half = block // 2
    half_root = 1.0 / math.sqrt(2.0)
    density_scale = 1.0 / math.sqrt(2.0 * math.pi)

    def kernel(rows_ref, first_ref, second_ref, up_ref, down_ref, bias_ref, hidden_ref, grad_ref, column_ref, part_ref, total):
        step = pl.program_id(0)
        columns = jnp.zeros((1, tile), jnp.float32)
        up, down = up_ref[...], down_ref[...]
        for first in range(0, rows, CHUNK):
            span = slice(first, first + CHUNK)
            pre = jnp.dot(rows_ref[span], up, preferred_element_type=jnp.float32) + bias_ref[...]
            upstream = jnp.concatenate([
                jnp.dot(ref[b * half : (b + 1) * half], down, preferred_element_type=jnp.float32)
                for b in range(first // block, (first + CHUNK) // block) for ref in (first_ref, second_ref)
            ], axis=0)
            share = 0.5 + 0.5 * lax.erf(pre * half_root)
            hidden_ref[span] = (pre * share).astype(hidden_ref.dtype)
            slope = share + pre * (density_scale * jnp.exp(-0.5 * pre * pre))
            grad = (upstream * slope).astype(grad_ref.dtype)
            grad_ref[span] = grad
            columns = columns + jnp.sum(grad.astype(jnp.float32), axis=0, keepdims=True)
            back = contract_last(grad, up)

            @pl.when(step == 0)
            def _():
                total[span] = back

            @pl.when(step != 0)
            def _():
                total[span] += back

        column_ref[...] = columns

        @pl.when(step == units // tile - 1)
        def _():
            part_ref[...] = total[...].astype(part_ref.dtype)

    bf16 = jnp.bfloat16
    return pl.pallas_call(
        kernel,
        grid=(units // tile,),
        out_shape=[
            jax.ShapeDtypeStruct((rows, units), bf16),
            jax.ShapeDtypeStruct((rows, units), bf16),
            jax.ShapeDtypeStruct((1, units), jnp.float32),
            jax.ShapeDtypeStruct((rows, width), bf16),
        ],
        in_specs=[
            pl.BlockSpec((rows, width), lambda i: (0, 0)),
            pl.BlockSpec((rows // 2, width), lambda i: (0, 0)),
            pl.BlockSpec((rows // 2, width), lambda i: (0, 0)),
            pl.BlockSpec((width, tile), lambda i: (0, i)),
            pl.BlockSpec((width, tile), lambda i: (0, i)),
            pl.BlockSpec((1, tile), lambda i: (0, i)),
        ],
        out_specs=[
            pl.BlockSpec((rows, tile), lambda i: (0, i)),
            pl.BlockSpec((rows, tile), lambda i: (0, i)),
            pl.BlockSpec((1, tile), lambda i: (0, i)),
            pl.BlockSpec((rows, width), lambda i: (0, 0)),
        ],
        scratch_shapes=[pltpu.VMEM((rows, width), jnp.float32)],
        compiler_params=pltpu.CompilerParams(vmem_limit_bytes=60 * MIB),
        cost_estimate=pl.CostEstimate(
            flops=6 * rows * width * units, bytes_accessed=40 * MIB, transcendentals=2 * rows * units),
    )(rows_two, *branch_halves, up_all, down_all, up_bias)


def sum_terms(terms):
    return functools.reduce(jnp.add, [terms[k].astype(jnp.float32) for k in range(terms.shape[0])])


def per_device(
    hidden_in,
    output_grad,
    first_gain,
    first_shift,
    query_weight,
    query_bias,
    key_weight,
    value_weight,
    value_bias,
    out_weight,
    out_bias,
    second_gain,
    second_shift,
    up_weight,
    up_bias,
    down_weight,
    down_bias,
    seq_lengths,
    block_order,
    block_slot,
):
    local_rows, model_width = hidden_in.shape
    mp_count, dp_count = lax.axis_size("mp"), lax.axis_size("dp")
    mp_index, dp_index = lax.axis_index("mp"), lax.axis_index("dp")
    group_rows = local_rows * mp_count
    head_width = query_weight.shape[1]
    heads_local = head_width // HEAD_DIM
    hidden_width = up_weight.shape[1]
    members = dp_count // heads_local
    blocks_each = group_rows // BLOCK
    plan = (seq_lengths, block_order, block_slot)

    vectors = (first_gain, first_shift, query_bias, value_bias, out_bias, second_gain, second_shift, down_bias, up_bias)
    rows_one, vector_rows, projections, out_all, head_shared, head_queries, branch_two, live, branch_first = project_first(
        hidden_in, output_grad, seq_lengths, block_order, vectors,
        (key_weight, value_weight, query_weight), out_weight, heads_local, members, 0,
    )
    own_valid = live[:, :1] > 0
    vector_rows = vector_rows.reshape(dp_count, -1, 128)
    each = model_width // dp_count // 128
    gain_one, _, _, _, bias_out, gain_two, shift_two, bias_down = (
        vector_rows[:, k * each : (k + 1) * each].reshape(1, model_width) for k in range(8)
    )
    up_each = up_bias.shape[0] // 128
    bias_up = vector_rows[:, 8 * each : 8 * each + up_each].reshape(1, up_bias.shape[0] * dp_count)

    half = local_rows // 2
    branch_second = whole_rows(branch_two[half:])
    head_mix, exact_mix, log_total = attend(head_queries, head_shared, *plan, members, blocks_each)
    residual, attended_low, rows_two, up_all, down_all = mix_norm_gather(
        head_mix, out_all, hidden_in, bias_out, gain_two, shift_two, (up_weight, down_weight), heads_local, members, 3
    )
    attended_low = attended_low.reshape(group_rows, head_width)

    bias_hidden = lax.dynamic_slice_in_dim(bias_up, mp_index * hidden_width, hidden_width, 1)
    hidden_low, pre_grad, pre_columns, up_part = feed_both_ways(
        rows_two, (branch_first, branch_second), local_rows, up_all, down_all, bias_hidden
    )
    residual_grad, sums_two, branch_rows_one, feed_part, head_grad, down_terms, up_terms = reduce_back_gather(
        up_part, residual, branch_two, gain_two, (branch_first, branch_second),
        ((None, hidden_low), (rows_two, pre_grad)), down_all, out_all, heads_local, members, 4,
    )
    down_weight_grad, up_weight_grad = (
        sum_terms(terms) for terms in (down_terms, up_terms)
    )

    feed = row_share(feed_part)
    result = residual + feed + bias_down
    output = jnp.where(own_valid, result, 0.0).astype(jnp.bfloat16)

    head_grad = head_grad.reshape(heads_local * group_rows, HEAD_DIM)
    head_query_grad, head_key_grad, head_value_grad = attend_back(
        head_queries, head_shared, head_grad, exact_mix, log_total, *plan, members, blocks_each
    )

    def column_sums(values):
        return jnp.sum(values.astype(jnp.float32), axis=0)

    def placed(values):
        whole = jnp.zeros((values.shape[0] * mp_count,), jnp.float32)
        return lax.dynamic_update_slice_in_dim(whole, values, mp_index * values.shape[0], 0)

    none = jnp.zeros((model_width,), jnp.float32)
    sums = (
        none, none, none, none, sums_two[2], sums_two[0], sums_two[1], column_sums(branch_two), placed(pre_columns[0]),
    )
    packed = jnp.concatenate([v.reshape(dp_count, -1, 128) for v in sums], axis=1)
    packed = jnp.pad(packed, ((0, 0), (0, -packed.shape[1] % 8), (0, 0)))
    out_weight_part = contract_first(branch_rows_one, attended_low).astype(jnp.bfloat16)
    input_grad, weight_grads, out_weight_grad, summed = finish_back(
        head_query_grad, head_key_grad, head_value_grad, projections, rows_one, residual_grad, hidden_in, gain_one,
        out_weight_part, packed, heads_local, members, 7,
    )
    key_weight_grad, value_weight_grad, query_weight_grad = (
        weight_grads[:, k * head_width : (k + 1) * head_width] for k in range(3)
    )
    vector_grads = [summed[k * each : (k + 1) * each].reshape(-1) for k in range(8)]
    up_bias_grad = summed[8 * each : 8 * each + up_each].reshape(-1)
    return (
        output,
        input_grad,
        vector_grads[0],
        vector_grads[1],
        query_weight_grad,
        vector_grads[2],
        key_weight_grad,
        value_weight_grad,
        vector_grads[3],
        out_weight_grad,
        vector_grads[4],
        vector_grads[5],
        vector_grads[6],
        up_weight_grad,
        up_bias_grad,
        down_weight_grad,
        vector_grads[7],
    )


def solution(mesh):
    return jax.shard_map(
        per_device,
        mesh=mesh,
        in_specs=(
            P(("dp", "mp"), None),
            P(("dp", "mp"), None),
            P("dp"),
            P("dp"),
            P("dp", "mp"),
            P("dp"),
            P("dp", "mp"),
            P("dp", "mp"),
            P("dp"),
            P("dp", "mp"),
            P("dp"),
            P("dp"),
            P("dp"),
            P("dp", "mp"),
            P("dp"),
            P("dp", "mp"),
            P("dp"),
            P(),
            P(),
            P(),
        ),
        out_specs=(
            P(("dp", "mp"), None),
            P(("dp", "mp"), None),
            P("dp"),
            P("dp"),
            P("dp", "mp"),
            P("dp"),
            P("dp", "mp"),
            P("dp", "mp"),
            P("dp"),
            P("dp", "mp"),
            P("dp"),
            P("dp"),
            P("dp"),
            P("dp", "mp"),
            P("dp"),
            P("dp", "mp"),
            P("dp"),
        ),
        check_vma=False,
    )
```

```python
import functools
import math

import jax
import jax.numpy as jnp
from jax import lax
from jax.experimental import pallas as pl
from jax.experimental.pallas import tpu as pltpu
from jax.sharding import PartitionSpec as P

HEAD_DIM = 128
BLOCK = 128
KEY_BLOCKS = 8
MESH = pl.DeviceIdType.MESH
ANY = pl.BlockSpec(memory_space=pl.ANY)
VMEM = pl.BlockSpec(memory_space=pltpu.VMEM)
SMEM = pl.BlockSpec(memory_space=pltpu.SMEM)
MIB = 1 << 20


big_negative = -1e30
norm_epsilon = 1e-05


def norm_back(upstream, normed, inverse, gain_row):
    scaled = upstream * gain_row
    mean_grad = jnp.mean(scaled, axis=-1, keepdims=True)
    second = jnp.mean(scaled * normed, axis=-1, keepdims=True)
    return inverse * (scaled - mean_grad - normed * second)


def contract_last(left, right):
    return lax.dot_general(
        left, right, (((1,), (1,)), ((), ())), preferred_element_type=jnp.float32
    )


def contract_first(left, right):
    return lax.dot_general(
        left, right, (((0,), (0,)), ((), ())), preferred_element_type=jnp.float32
    )


def whole_rows(local_part):
    return lax.all_gather(local_part, "mp", axis=0, tiled=True)


def row_share(term):
    term = term.astype(jnp.bfloat16)
    return lax.psum_scatter(term, "mp", scatter_dimension=0, tiled=True).astype(jnp.float32)


def greet(peers):
    barrier = pltpu.get_barrier_semaphore()
    for peer in peers:
        pl.semaphore_signal(barrier, inc=1, device_id=peer, device_id_type=MESH)
    pl.semaphore_wait(barrier, len(peers))


def remote(src, dst, send_sem, recv_sem, peer):
    return pltpu.make_async_remote_copy(
        src_ref=src, dst_ref=dst, send_sem=send_sem, recv_sem=recv_sem,
        device_id=peer, device_id_type=MESH,
    )


def head_place(heads, members):
    me = lax.axis_index("dp")
    return me, me // members, me % members, lax.axis_index("mp")


def lanes(head):
    return pl.ds(pl.multiple_of(head * HEAD_DIM, HEAD_DIM), HEAD_DIM)


def sequence_of(place, lengths):
    first, length, running = jnp.int32(0), jnp.int32(0), jnp.int32(0)
    for s in range(lengths.shape[0]):
        inside = place >= running
        first = jnp.where(inside, running, first)
        length = jnp.where(inside, lengths[s], length)
        running = running + (lengths[s] + (BLOCK - 1)) // BLOCK
    return first, length - (place - first) * BLOCK


def list_queries(slot, index_list, place_list, members, blocks_each):
    member = lax.axis_index("dp") % members

    def visit(block, count):
        dealt = slot[block]
        owner = dealt // blocks_each

        @pl.when(owner % members == member)
        def _():
            index_list[count] = (owner // members) * blocks_each + dealt % blocks_each
            place_list[count] = block

        return count + (owner % members == member).astype(jnp.int32)

    lax.fori_loop(0, slot.shape[0], visit, jnp.int32(0))


def block_rows(block):
    return pl.ds(pl.multiple_of(block * BLOCK, BLOCK), BLOCK)


class QueryPair:
    def __init__(self, pair, lengths, index_list, place_list):
        self.index = [index_list[2 * pair + i] for i in range(2)]
        self.place = [place_list[2 * pair + i] for i in range(2)]
        found = [sequence_of(place, lengths) for place in self.place]
        self.start = found[0][0]
        lane = lax.broadcasted_iota(jnp.int32, (1, 2 * BLOCK), 1)
        right = lane >= BLOCK

        def lanes_of(left_value, right_value):
            return jnp.where(right, right_value, left_value)

        within = lane - lanes_of(0, BLOCK)
        base = self.start * BLOCK
        self.position = lanes_of(self.place[0], self.place[1]) * BLOCK + within - base
        self.lowest = lanes_of(found[0][0], found[1][0]) * BLOCK - base
        self.live = within < lanes_of(found[0][1], found[1][1])
        self.tiles = (self.place[1] - self.start) // KEY_BLOCKS + 1
        self.open_tiles = jnp.where(found[0][0] == found[1][0], (self.place[0] - self.start) // KEY_BLOCKS, 0)

    def row(self, tile):
        return pl.multiple_of((self.start + tile * KEY_BLOCKS) * BLOCK, BLOCK)

    def allowed(self, tile):
        width = KEY_BLOCKS * BLOCK
        key = lax.broadcasted_iota(jnp.int32, (width, 2 * BLOCK), 0)
        return (key <= self.position - tile * width) & (key >= self.lowest - tile * width)

    def load_t(self, ref):
        return jnp.concatenate([ref[block_rows(index)].T for index in self.index], axis=1)

    def load(self, ref):
        return jnp.concatenate([ref[block_rows(index)] for index in self.index], axis=0)

    def store_t(self, ref, value_t):
        for i, index in enumerate(self.index):
            ref[block_rows(index)] = value_t[:, i * BLOCK : (i + 1) * BLOCK].T.astype(ref.dtype)


def attend(queries, shared, lengths, order, slot, members, blocks_each):
    pairs, key_count = queries.shape[0] // (2 * BLOCK), shared.shape[1] // BLOCK
    width = KEY_BLOCKS * BLOCK
    padded = (key_count + KEY_BLOCKS - 1) * BLOCK
    scale = math.log2(math.e) / math.sqrt(HEAD_DIM)

    def kernel(lengths_ref, slot_ref, q_ref, shared_ref, out_ref, exact_ref, log_ref,
               index_list, place_list, keys, values_t):
        list_queries(slot_ref, index_list, place_list, members, blocks_each)

        @pl.loop(0, key_count)
        def _(block):
            source = block_rows(slot_ref[block])
            keys[block_rows(block)] = shared_ref[0, source]
            values_t[:, block_rows(block)] = shared_ref[1, source].T

        tail = pl.ds(key_count * BLOCK, padded - key_count * BLOCK)
        keys[tail] = jnp.zeros((padded - key_count * BLOCK, HEAD_DIM), keys.dtype)
        values_t[:, tail] = jnp.zeros((HEAD_DIM, padded - key_count * BLOCK), keys.dtype)

        @pl.loop(0, pairs)
        def _(index):
            pair = QueryPair(index, lengths_ref, index_list, place_list)
            query_t = pair.load_t(q_ref)

            def step(tile, carry, masked):
                top, total, mix = carry
                span = pl.ds(pair.row(tile), width)
                scores = jnp.dot(keys[span], query_t, preferred_element_type=jnp.float32)
                if masked:
                    scores = jnp.where(pair.allowed(tile), scores, big_negative)
                new_top = jnp.maximum(top, jnp.max(scores, axis=0, keepdims=True))
                weights = jnp.exp2((scores - new_top) * scale)
                fade = jnp.exp2((top - new_top) * scale)
                total = total * fade + jnp.sum(weights, axis=0, keepdims=True)
                mix = mix * fade + jnp.dot(
                    values_t[:, span], weights.astype(jnp.bfloat16), preferred_element_type=jnp.float32)
                return new_top, total, mix

            carry = (jnp.full((1, 2 * BLOCK), big_negative, jnp.float32), jnp.zeros((1, 2 * BLOCK), jnp.float32),
                     jnp.zeros((HEAD_DIM, 2 * BLOCK), jnp.float32))
            carry = lax.fori_loop(0, pair.open_tiles, lambda tile, c: step(tile, c, False), carry)
            top, total, mix = lax.fori_loop(pair.open_tiles, pair.tiles, lambda tile, c: step(tile, c, True), carry)
            mix = jnp.where(pair.live, mix / total, 0.0)
            exact_ref[index] = mix
            pair.store_t(out_ref, mix)
            log_ref[index] = jnp.where(pair.live, top * scale + jnp.log2(total), -big_negative)

    return pl.pallas_call(
        kernel,
        out_shape=[
            jax.ShapeDtypeStruct(queries.shape, jnp.bfloat16),
            jax.ShapeDtypeStruct((pairs, HEAD_DIM, 2 * BLOCK), jnp.float32),
            jax.ShapeDtypeStruct((pairs, 1, 2 * BLOCK), jnp.float32),
        ],
        in_specs=[SMEM] * 2 + [VMEM] * 2,
        out_specs=[VMEM] * 3,
        scratch_shapes=[
            pltpu.SMEM((2 * pairs,), jnp.int32), pltpu.SMEM((2 * pairs,), jnp.int32),
            pltpu.VMEM((padded, HEAD_DIM), jnp.bfloat16), pltpu.VMEM((HEAD_DIM, padded), jnp.bfloat16),
        ],
        compiler_params=pltpu.CompilerParams(vmem_limit_bytes=56 * MIB),
        cost_estimate=pl.CostEstimate(flops=8 << 30, bytes_accessed=50 * MIB, transcendentals=8 << 20),
    )(lengths, slot, queries, shared)


def attend_back(queries, shared, upstream, exact, logs, lengths, order, slot, members, blocks_each):
    pairs, key_count = queries.shape[0] // (2 * BLOCK), shared.shape[1] // BLOCK
    width = KEY_BLOCKS * BLOCK
    padded = (key_count + KEY_BLOCKS - 1) * BLOCK
    scale = math.log2(math.e) / math.sqrt(HEAD_DIM)
    plain_scale = 1.0 / math.sqrt(HEAD_DIM)

    def kernel(lengths_ref, slot_ref, q_ref, shared_ref, g_ref, exact_ref, log_ref, dq_ref, dk_ref, dv_ref,
               index_list, place_list, keys, keys_t, values, key_sum, value_sum):
        list_queries(slot_ref, index_list, place_list, members, blocks_each)

        @pl.loop(0, key_count)
        def _(block):
            source, to = block_rows(slot_ref[block]), block_rows(block)
            rows = shared_ref[0, source]
            keys[to] = rows
            keys_t[:, to] = rows.T
            values[to] = shared_ref[1, source]
            key_sum[to] = jnp.zeros((BLOCK, HEAD_DIM), jnp.float32)
            value_sum[to] = jnp.zeros((BLOCK, HEAD_DIM), jnp.float32)

        tail = pl.ds(key_count * BLOCK, padded - key_count * BLOCK)
        keys[tail] = jnp.zeros((padded - key_count * BLOCK, HEAD_DIM), keys.dtype)
        values[tail] = jnp.zeros((padded - key_count * BLOCK, HEAD_DIM), keys.dtype)
        keys_t[:, tail] = jnp.zeros((HEAD_DIM, padded - key_count * BLOCK), keys.dtype)
        key_sum[tail] = jnp.zeros((padded - key_count * BLOCK, HEAD_DIM), jnp.float32)
        value_sum[tail] = jnp.zeros((padded - key_count * BLOCK, HEAD_DIM), jnp.float32)

        @pl.loop(0, pairs)
        def _(index):
            pair = QueryPair(index, lengths_ref, index_list, place_list)
            query, grad = pair.load(q_ref), pair.load(g_ref)
            query_t, grad_t = pair.load_t(q_ref), pair.load_t(g_ref)
            delta = jnp.sum(grad_t.astype(jnp.float32) * exact_ref[index], axis=0, keepdims=True)
            log_total = log_ref[index]

            def step(tile, query_grad, masked):
                span = pl.ds(pair.row(tile), width)
                scores = jnp.dot(keys[span], query_t, preferred_element_type=jnp.float32)
                probability = jnp.exp2(scores * scale - log_total)
                if masked:
                    probability = jnp.where(pair.allowed(tile), probability, 0.0)
                prob_grad = jnp.dot(values[span], grad_t, preferred_element_type=jnp.float32)
                score_grad = (probability * (prob_grad - delta)).astype(jnp.bfloat16)
                value_sum[span] += jnp.dot(
                    probability.astype(jnp.bfloat16), grad, preferred_element_type=jnp.float32)
                key_sum[span] += jnp.dot(score_grad, query, preferred_element_type=jnp.float32)
                return query_grad + jnp.dot(keys_t[:, span], score_grad, preferred_element_type=jnp.float32)

            query_grad = jnp.zeros((HEAD_DIM, 2 * BLOCK), jnp.float32)
            query_grad = lax.fori_loop(0, pair.open_tiles, lambda tile, c: step(tile, c, False), query_grad)
            query_grad = lax.fori_loop(pair.open_tiles, pair.tiles, lambda tile, c: step(tile, c, True), query_grad)
            pair.store_t(dq_ref, query_grad * plain_scale)

        @pl.loop(0, key_count)
        def _(block):
            at, dealt = block_rows(block), block_rows(slot_ref[block])
            dk_ref[dealt] = (key_sum[at] * plain_scale).astype(dk_ref.dtype)
            dv_ref[dealt] = value_sum[at].astype(dv_ref.dtype)

    return pl.pallas_call(
        kernel,
        out_shape=[
            jax.ShapeDtypeStruct(queries.shape, jnp.bfloat16),
            jax.ShapeDtypeStruct(shared.shape[1:], jnp.bfloat16),
            jax.ShapeDtypeStruct(shared.shape[1:], jnp.bfloat16),
        ],
        in_specs=[SMEM] * 2 + [VMEM] * 5,
        out_specs=[VMEM] * 3,
        scratch_shapes=[
            pltpu.SMEM((2 * pairs,), jnp.int32), pltpu.SMEM((2 * pairs,), jnp.int32),
            pltpu.VMEM((padded, HEAD_DIM), jnp.bfloat16),
            pltpu.VMEM((HEAD_DIM, padded), jnp.bfloat16),
            pltpu.VMEM((padded, HEAD_DIM), jnp.bfloat16),
            pltpu.VMEM((padded, HEAD_DIM), jnp.float32),
            pltpu.VMEM((padded, HEAD_DIM), jnp.float32),
        ],
        compiler_params=pltpu.CompilerParams(vmem_limit_bytes=60 * MIB),
        cost_estimate=pl.CostEstimate(flops=20 << 30, bytes_accessed=100 * MIB, transcendentals=8 << 20),
    )(lengths, slot, queries, shared, upstream, exact, logs)


def line_neighbours(mp, count):
    return ((1, mp + 1 < count, jnp.minimum(mp + 1, count - 1)), (-1, mp >= 1, jnp.maximum(mp - 1, 0)))


def greet_all(fixed, dp, mp, count):
    barrier = pltpu.get_barrier_semaphore()
    for peer in fixed:
        pl.semaphore_signal(barrier, inc=1, device_id=peer, device_id_type=MESH)
    expected = jnp.int32(len(fixed))
    for _, there, place in line_neighbours(mp, count):

        @pl.when(there)
        def _():
            pl.semaphore_signal(barrier, inc=1, device_id=(dp, place), device_id_type=MESH)

        expected = expected + there.astype(jnp.int32)
    pl.semaphore_wait(barrier, expected)


class LineGather:
    def __init__(self, own, full, rows, pieces, send_sem, recv_sem, dp, mp, count):
        self.own, self.full, self.rows, self.pieces = own, full, rows, pieces
        self.send_sem, self.recv_sem, self.dp, self.mp, self.count = send_sem, recv_sem, dp, mp, count
        self.size = rows // pieces

    def place(self, block, piece):
        return self.full.at[pl.ds(pl.multiple_of(block * self.rows + piece * self.size, self.size), self.size)]

    def hop(self, way, step, piece):
        sign, there, neighbour = line_neighbours(self.mp, self.count)[way]
        origin = self.mp - sign * step
        exists = (origin >= 0) & (origin < self.count)
        origin = jnp.clip(origin, 0, self.count - 1)
        if step == 0:
            source = self.own.at[pl.ds(pl.multiple_of(piece * self.size, self.size), self.size)]
        else:
            source = self.place(origin, piece)
        def copy():
            return remote(source, self.place(origin, piece), self.send_sem.at[way, step, piece],
                          self.recv_sem.at[way, step, piece], (self.dp, neighbour))

        return exists, exists & there, copy

    def advance(self, step, piece, also=True, ways=(0, 1)):
        for way in ways:
            if step:
                exists, _, _ = self.hop(way, step, piece)
                _, _, earlier = self.hop(way, step - 1, piece)

                @pl.when(exists & also)
                def _():
                    earlier().wait_recv()

            if step < self.count - 1:
                _, sends, copy = self.hop(way, step, piece)

                @pl.when(sends & also)
                def _():
                    copy().start()

    def finish(self):
        @pl.loop(0, self.pieces)
        def _(piece):
            for way in range(2):
                for step in range(self.count - 1):
                    _, sends, copy = self.hop(way, step, piece)

                    @pl.when(sends)
                    def _():
                        copy().wait_send()

    @staticmethod
    def semaphores(count, pieces):
        return [pltpu.SemaphoreType.DMA((2, count, pieces)), pltpu.SemaphoreType.DMA((2, count, pieces))]


class ShardGather:
    def __init__(self, shards, wholes, depth, cross_send, cross_recv, core_send, core_recv, own_sem, dp, mp, chips):
        self.shards, self.wholes, self.depth, self.own_sem = shards, wholes, depth, own_sem
        self.cross_send, self.cross_recv, self.core_send, self.core_recv = cross_send, cross_recv, core_send, core_recv
        self.dp, self.mp, self.chips = dp, mp, chips

    def place(self, array, owner):
        return self.wholes[array].at[pl.ds(pl.multiple_of(owner * self.depth, self.depth), self.depth)]

    def cross(self, array, o):
        return remote(self.shards[array], self.place(array, self.dp), self.cross_send.at[array, o],
                      self.cross_recv.at[array, o], (self.dp ^ (2 * o), self.mp))

    def core(self, array, o):
        owner = self.dp ^ (2 * o)
        source = self.place(array, owner) if o else self.shards[array]
        return remote(source, self.place(array, owner), self.core_send.at[array, o], self.core_recv.at[array, o],
                      (self.dp ^ 1, self.mp))

    def own(self, array):
        return pltpu.make_async_copy(self.shards[array], self.place(array, self.dp), self.own_sem.at[array])

    def begin(self):
        for array in range(len(self.shards)):
            for o in range(1, self.chips):
                self.cross(array, o).start()
        for array in range(len(self.shards)):
            self.own(array).start()
            self.core(array, 0).start()

    def spread(self, array):
        for o in range(1, self.chips):
            self.cross(array, o).wait_recv()
            self.core(array, o).start()

    def finish(self):
        for array in range(len(self.shards)):
            self.own(array).wait()
            for o in range(self.chips):
                self.core(array, o).wait()
                if o:
                    self.cross(array, o).wait_send()

    @staticmethod
    def semaphores(count, chips):
        return [pltpu.SemaphoreType.DMA((count, chips)) for _ in range(4)] + [pltpu.SemaphoreType.DMA((count,))]


class LineReduce:
    def __init__(self, part, flows, rows, pieces, send_sem, recv_sem, dp, mp, count):
        self.part, self.flows, self.rows, self.pieces = part, flows, rows, pieces
        self.send_sem, self.recv_sem, self.dp, self.mp, self.count = send_sem, recv_sem, dp, mp, count
        self.size = rows // pieces

    def span(self, block, piece):
        return pl.ds(pl.multiple_of(block * self.rows + piece * self.size, self.size), self.size)

    def hop(self, way, block, piece, first=False):
        neighbour = line_neighbours(self.mp, self.count)[way][2]
        span = self.span(block, piece)
        source = self.part.at[span] if first else self.flows.at[way, span]
        return remote(source, self.flows.at[way, span], self.send_sem.at[way, block, piece],
                      self.recv_sem.at[way, block, piece], (self.dp, neighbour))

    def roles(self, way, block):
        if way == 0:
            behind, ahead = self.mp >= 1, self.mp < block
        else:
            behind, ahead = self.mp < self.count - 1, self.mp > block
        return ahead & jnp.logical_not(behind), ahead & behind

    def targets(self):
        for index in range(self.count - 1):
            yield 0, self.count - 1 - index
            yield 1, index

    def begin(self, piece, also=True):
        for way, block in self.targets():
            begins, _ = self.roles(way, block)

            @pl.when(begins & also)
            def _():
                self.hop(way, block, piece, True).start()

    def advance(self, turn):
        for way, block in self.targets():
            _, hands_on = self.roles(way, block)
            passed = SKEW * (self.mp - 1 if way == 0 else self.count - 2 - self.mp)
            piece = jnp.clip(turn - passed, 0, self.pieces - 1)

            @pl.when(hands_on & (turn >= passed) & (turn - passed < self.pieces))
            def _():
                self.hop(way, block, piece).wait_recv()
                span = self.span(block, piece)
                value = self.flows[way, span].astype(jnp.float32) + self.part[span].astype(jnp.float32)
                self.flows[way, span] = value.astype(self.flows.dtype)
                self.hop(way, block, piece).start()

    def arrive(self, piece):
        for way in range(2):

            @pl.when(self.mp >= 1 if way == 0 else self.mp < self.count - 1)
            def _():
                self.hop(way, self.mp, piece).wait_recv()

    def total(self, piece, result):
        span = self.span(self.mp, piece)
        result[...] = self.part[span].astype(jnp.float32)
        for way in range(2):

            @pl.when(self.mp >= 1 if way == 0 else self.mp < self.count - 1)
            def _():
                result[...] += self.flows[way, span].astype(jnp.float32)

    def finish(self):
        @pl.loop(0, self.pieces)
        def _(piece):
            for way, block in self.targets():
                begins, hands_on = self.roles(way, block)

                @pl.when(begins)
                def _():
                    self.hop(way, block, piece, True).wait_send()

                @pl.when(hands_on)
                def _():
                    self.hop(way, block, piece).wait_send()

    @staticmethod
    def scratch(count, rows, width, pieces):
        return [pltpu.VMEM((2, count * rows, width), jnp.bfloat16),
                pltpu.SemaphoreType.DMA((2, count, pieces)), pltpu.SemaphoreType.DMA((2, count, pieces))]


AHEAD = 1
QUARTERS = 4
MAX_PIECES = 16
SKEW = 1


def pieces_of(rows):
    return min(MAX_PIECES, rows // 16)


def unit_rows(values):
    average = jnp.mean(values, axis=-1, keepdims=True)
    centred = values - average
    inverse = lax.rsqrt(jnp.mean(centred * centred, axis=-1, keepdims=True) + norm_epsilon)
    return centred * inverse, inverse


def project_first(
    hidden, output_grad, lengths, order, vectors, projections, out_weight, heads, members, collective_id
):
    rows, width = hidden.shape
    dp_count, mp_count = lax.axis_size("dp"), lax.axis_size("mp")
    chips, pieces, half = dp_count // 2, pieces_of(rows), rows // 2
    half_pieces = pieces_of(half)
    group_rows, depth, columns = mp_count * rows, projections[0].shape[0], projections[0].shape[1]
    each = width // dp_count // 128
    tall = [v.shape[0] // 128 for v in vectors]
    slab = sum(tall) + -sum(tall) % 8
    halves, kinds = heads // 2, 3
    arrays = kinds + 2
    offsets = sorted({2 * o for o in range(1, chips)} | {o for o in range(1, members)} | {o * members for o in range(1, heads)})

    def kernel(lengths_ref, order_ref, hidden_ref, upstream_ref, *refs):
        given, refs = refs[: len(vectors)], refs[len(vectors) :]
        weight_refs, out_weight_ref = refs[:kinds], refs[kinds]
        (normed_out, all_vectors, weights_out, all_out, shared, queries, branch, rest, live,
         half_rows) = refs[kinds + 1 : kinds + 11]
        parts, refs = refs[-len(vectors) :], refs[: -len(vectors)]
        (vector_ref, upstream, load_sem, raw, stage, gains, biases, line_send, line_recv, row_sem, own_sem, cross_send, cross_recv, core_send, core_recv,
         head_local, head_send, head_recv, pair_send, pair_recv, half_send, half_recv, half_sem,
         normed, weights, out_sem) = refs[kinds + 11 :]
        dp, mp = lax.axis_index("dp"), lax.axis_index("mp")
        loads = [pltpu.make_async_copy(given[k], parts[k], load_sem.at[k]) for k in range(len(vectors))]
        loads.append(pltpu.make_async_copy(upstream_ref, upstream, load_sem.at[len(vectors)]))
        for copy in loads:
            copy.start()
        vector_ref[...] = jnp.zeros_like(vector_ref)
        for copy in loads:
            copy.wait()
        first = 0
        for part, count in zip(parts, tall):
            for r in range(count):
                vector_ref[first + r] = part[r * 128 : (r + 1) * 128].astype(jnp.float32)
            first += count
        group, member = dp // members, dp % members
        partner = (dp ^ 1, mp)
        greet_all([(dp ^ o, mp) for o in offsets], dp, mp, mp_count)
        line = LineGather(hidden_ref, raw, rows, pieces, line_send, line_recv, dp, mp, mp_count)

        behind = LineGather(branch, half_rows, half, half_pieces, half_send, half_recv, dp, mp, mp_count)

        def follow(step):
            for way, steps in ((0, mp), (1, mp_count - 1 - mp)):

                @pl.loop(0, half_pieces)
                def _(piece):
                    behind.advance(0, piece, steps == step, (way,))

        between = (mp > 0) & (mp < mp_count - 1)

        def hand_half(step, also=True):
            @pl.loop(0, half_pieces)
            def _(piece):
                behind.advance(step, piece, also)

        def source(array):
            return (list(weight_refs) + [out_weight_ref, vector_ref])[array]

        def place(array, owner):
            if array < kinds:
                return weights.at[pl.ds(pl.multiple_of(owner * depth, depth), depth), pl.ds(array * columns, columns)]
            if array == kinds:
                return all_out.at[pl.ds(pl.multiple_of(owner * depth, depth), depth)]
            return all_vectors.at[pl.ds(pl.multiple_of(owner * slab, slab), slab)]

        def cross(array, o):
            return remote(source(array), place(array, dp), cross_send.at[array, o], cross_recv.at[array, o],
                          (dp ^ (2 * o), mp))

        def core(array, o):
            owner = dp ^ (2 * o)
            return remote(place(array, owner) if o else source(array), place(array, owner),
                          core_send.at[array, o], core_recv.at[array, o], partner)

        def own(array):
            return pltpu.make_async_copy(source(array), place(array, dp), own_sem.at[array])

        def block_span(block):
            return pl.ds(pl.multiple_of(block * rows, rows), rows)

        first_to_last = [kinds + 1] + list(range(kinds + 1))
        for array in first_to_last:
            for o in range(1, chips):
                cross(array, o).start()
            if array == first_to_last[0]:

                @pl.loop(0, pieces)
                def _(piece):
                    line.advance(0, piece)

        for block in range(rows // BLOCK):
            found = order_ref[(dp * group_rows + mp * rows) // BLOCK + block]
            valid = sequence_of(found, lengths_ref)[1]
            span = slice(block * BLOCK, (block + 1) * BLOCK)
            live[span] = (lax.broadcasted_iota(jnp.int32, (BLOCK, 128), 0) < valid).astype(jnp.float32)
            keep = lax.broadcasted_iota(jnp.int32, (BLOCK, width), 0) < valid
            branch[span] = jnp.where(keep, upstream[span].astype(jnp.float32), 0.0).astype(branch.dtype)
        rest[...] = branch[half:]
        own_half = pltpu.make_async_copy(
            branch.at[pl.ds(0, half)], half_rows.at[pl.ds(pl.multiple_of(mp * half, half), half)], half_sem)
        own_half.start()
        follow(0)
        own_rows = pltpu.make_async_copy(hidden_ref, raw.at[block_span(mp)], row_sem)
        own_rows.start()
        for array in first_to_last:
            own(array).start()
            core(array, 0).start()

        def spread(array):
            for o in range(1, chips):
                cross(array, o).wait_recv()
                core(array, o).start()

        def settle(array):
            own(array).wait()
            for o in range(chips):
                core(array, o).wait_recv()

        def norm(block):
            chunk = 64

            @pl.loop(0, rows // chunk)
            def _(part):
                span = pl.ds(pl.multiple_of(block * rows + part * chunk, chunk), chunk)
                unit, _ = unit_rows(raw[span].astype(jnp.float32))
                normed[span] = (unit * gains[0:1] + gains[1:2]).astype(normed.dtype)

            normed_copy(block).start()

        def normed_copy(block):
            return pltpu.make_async_copy(
                normed.at[block_span(block)], normed_out.at[block_span(block)], out_sem.at[block])

        weights_copy = pltpu.make_async_copy(weights, weights_out, out_sem.at[mp_count])

        def each_block(low, high, visit):
            @pl.loop(0, mp_count)
            def _(block):
                distance = jnp.abs(block - mp)

                @pl.when((distance >= low) & (distance <= high))
                def _():
                    visit(block)

        def rows_of(kind_ref, owner, block):
            return kind_ref.at[pl.ds(pl.multiple_of(owner * group_rows + block * rows, rows), rows)]

        def pass_on(kind, o, block, piece):
            giver = (group ^ o) * members + member
            return [remote(piece, rows_of(shared.at[kind], giver, block), pair_send.at[kind, o, block, p - 1],
                           pair_recv.at[kind, o, block, p - 1], (group * members + (member ^ p), mp))
                    for p in range(1, members)]

        def head_copy(kind, o, block, to_shared):
            target = group ^ o
            piece = stage.at[kind, block, target]
            landing = rows_of(shared.at[kind], dp, block) if to_shared else rows_of(queries, group, block)
            return remote(piece, landing, head_send.at[kind, o, block], head_recv.at[kind, o, block],
                          (target * members + member, mp))

        def local_copy(kind, block, to_shared):
            landing = rows_of(shared.at[kind], dp, block) if to_shared else rows_of(queries, group, block)
            return pltpu.make_async_copy(stage.at[kind, block, group], landing, head_local.at[kind, block])

        def project(tile, block):
            kind, half = tile // halves, tile % halves
            span = pl.ds(pl.multiple_of(half * 256, 256), 256)
            across = pl.ds(pl.multiple_of(kind * columns + half * 256, 256), 256)
            value = jnp.dot(normed[block_span(block)], weights[:, across], preferred_element_type=jnp.float32)
            value = (value + biases[pl.ds(kind, 1), span]).astype(stage.dtype)
            for h in range(2):
                head = 2 * half + h
                stage[kind, block, head] = value[:, h * HEAD_DIM : (h + 1) * HEAD_DIM]
            for h in range(2):
                o = (2 * half + h) ^ group
                for to_shared in (True, False):
                    chosen = (kind < 2) if to_shared else (kind == 2)

                    @pl.when(chosen & (o != 0))
                    def _():
                        head_copy(kind, o, block, to_shared).start()

                    @pl.when(chosen & (o == 0))
                    def _():
                        local_copy(kind, block, to_shared).start()
                        if to_shared:
                            for copy in pass_on(kind, 0, block, stage.at[kind, block, group]):
                                copy.start()

        def hand_on(block):
            @pl.loop(0, 2)
            def _(kind):
                for o in range(1, heads):
                    head_copy(kind, o, block, True).wait_recv()
                    giver = (group ^ o) * members + member
                    for copy in pass_on(kind, o, block, rows_of(shared.at[kind], giver, block)):
                        copy.start()

        last = mp_count - 1
        for step in range(1, last):

            @pl.loop(0, pieces)
            def _(piece):
                line.advance(step, piece)

            follow(step)
            if step == 1:
                spread(kinds + 1)
                settle(kinds + 1)
                for owner in range(dp_count):
                    for r in range(each):
                        at = pl.ds((owner * each + r) * 128, 128)
                        for k in range(2):
                            gains[k : k + 1, at] = all_vectors[owner * slab + k * each + r : owner * slab + k * each + r + 1]
                biases[...] = jnp.zeros_like(biases)
                for head in range(heads):
                    feature = mp * heads + head
                    first = (feature // each) * slab + feature % each
                    for kind, k in ((1, 3), (2, 2)):
                        biases[kind : kind + 1, head * 128 : (head + 1) * 128] = all_vectors[pl.ds(first + k * each, 1)]
                own_rows.wait()
                each_block(0, 1, norm)
            else:
                each_block(step, step, norm)
        for array in range(kinds + 1):
            spread(array)
        for array in range(kinds):
            settle(array)
        weights_copy.start()
        tiles = kinds * halves

        @pl.loop(0, pieces)
        def _(piece):
            line.advance(last - 1 if last == 1 else last, piece)

            @pl.when(piece >= pieces - half_pieces)
            def _():
                behind.advance(1, piece - (pieces - half_pieces), between)

            @pl.when(piece < tiles)
            def _():
                each_block(0, last - 1, lambda block: project(piece, block))

        for step in range(2, last):
            hand_half(step, between)
        each_block(last, last, norm)

        @pl.loop(0, tiles)
        def _(tile):
            each_block(last, last, lambda block: project(tile, block))

        each_block(0, last - 1, hand_on)
        each_block(last, last, hand_on)
        for step in range(1, last):
            hand_half(step, jnp.logical_not(between))
        hand_half(last)
        line.finish()
        weights_copy.wait()
        for block in range(mp_count):
            normed_copy(block).wait()
        behind.finish()
        own_half.wait()
        settle(kinds)
        for array in first_to_last:
            for o in range(chips):
                core(array, o).wait_send()
                if o:
                    cross(array, o).wait_send()

        @pl.loop(0, mp_count)
        def _(block):
            for kind in range(kinds):
                to_shared = kind < 2
                local_copy(kind, block, to_shared).wait()
                for o in range(1, heads):
                    head_copy(kind, o, block, to_shared).wait_send()
                    if not to_shared:
                        head_copy(kind, o, block, to_shared).wait_recv()
                if to_shared:
                    for o in range(heads):
                        giver = (group ^ o) * members + member
                        for copy in pass_on(kind, o, block, rows_of(shared.at[kind], giver, block)):
                            copy.wait()

    dma = pltpu.SemaphoreType.DMA
    bf16, f32 = jnp.bfloat16, jnp.float32
    return pl.pallas_call(
        kernel,
        out_shape=[
            jax.ShapeDtypeStruct((group_rows, width), bf16),
            jax.ShapeDtypeStruct((dp_count * slab, 128), f32),
            jax.ShapeDtypeStruct((width, kinds * columns), bf16),
            jax.ShapeDtypeStruct((width, columns), bf16),
            jax.ShapeDtypeStruct((2, dp_count * group_rows, HEAD_DIM), bf16),
            jax.ShapeDtypeStruct((heads * group_rows, HEAD_DIM), bf16),
            jax.ShapeDtypeStruct((rows, width), bf16),
            jax.ShapeDtypeStruct((rows - half, width), bf16),
            jax.ShapeDtypeStruct((rows, 128), f32),
            jax.ShapeDtypeStruct((mp_count * half, width), bf16),
        ],
        in_specs=[SMEM, SMEM] + [ANY] * (len(vectors) + kinds + 3),
        out_specs=[ANY, VMEM, ANY, ANY, ANY, ANY, VMEM, VMEM, VMEM, ANY],
        scratch_shapes=[
            pltpu.VMEM((slab, 128), f32),
            pltpu.VMEM((rows, width), bf16),
            dma((len(vectors) + 1,)),
            pltpu.VMEM((group_rows, width), bf16),
            pltpu.VMEM((kinds, mp_count, heads, rows, HEAD_DIM), bf16),
            pltpu.VMEM((8, width), f32),
            pltpu.VMEM((8, columns), f32),
        ]
        + LineGather.semaphores(mp_count, pieces)
        + [dma(()), dma((arrays,))]
        + [dma((arrays, chips)) for _ in range(4)]
        + [dma((kinds, mp_count)), dma((kinds, heads, mp_count)), dma((kinds, heads, mp_count))]
        + [dma((2, heads, mp_count, members)) for _ in range(2)]
        + LineGather.semaphores(mp_count, half_pieces) + [dma(())]
        + [pltpu.VMEM((group_rows, width), bf16), pltpu.VMEM((width, kinds * columns), bf16), dma((mp_count + 1,))]
        + [pltpu.VMEM(v.shape, v.dtype) for v in vectors],
        compiler_params=pltpu.CompilerParams(
            collective_id=collective_id, has_side_effects=True, vmem_limit_bytes=63 * MIB),
        cost_estimate=pl.CostEstimate(flops=8 << 30, bytes_accessed=250 * MIB, transcendentals=0),
    )(lengths, order, hidden, output_grad, *vectors, *projections, out_weight)


def mix_norm_gather(mixed, out_weight, hidden, out_bias, gain, shift, shards, heads, members, collective_id):
    dp_count, mp_count = lax.axis_size("dp"), lax.axis_size("mp")
    chips, count = dp_count // 2, len(shards)
    rows, width = hidden.shape
    pieces = pieces_of(rows)
    size, columns, group_rows = rows // pieces, heads * HEAD_DIM, mp_count * rows
    quarter, per_quarter = rows // QUARTERS, pieces // QUARTERS
    slice_rows = width // per_quarter
    offsets = sorted({2 * o for o in range(1, chips)} | {1} | {o * members for o in range(1, heads)})
    mixed = mixed.reshape(heads, mp_count, rows, HEAD_DIM)
    turns = pieces + 2 * SKEW * (mp_count - 1)

    def kernel(mixed_ref, out_hbm, hidden_ref, bias_ref, gain_ref, shift_ref, *refs):
        shard_refs, (residual_ref, landed, full_ref), refs = refs[:count], refs[count : count + 3], refs[count + 3 :]
        whole_refs, refs = refs[:count], refs[count:]
        (part, out_rows, load_sem, local_sem, head_send, head_recv,
         total, normed, flows, red_send, red_recv, line_send, line_recv, own_sem, *weight_sems) = refs
        dp, mp = lax.axis_index("dp"), lax.axis_index("mp")
        group, member = dp // members, dp % members
        greet_all([(dp ^ o, mp) for o in offsets], dp, mp, mp_count)

        def landing(k, head):
            return landed.at[:, pl.ds(k * quarter, quarter), lanes(head)]

        def head_copy(o, k):
            return remote(mixed_ref.at[group ^ o, :, pl.ds(k * quarter, quarter)], landing(k, group),
                          head_send.at[o, k], head_recv.at[o, k], ((group ^ o) * members + member, mp))

        def local_copy(k):
            return pltpu.make_async_copy(mixed_ref.at[group, :, pl.ds(k * quarter, quarter)], landing(k, group),
                                         local_sem.at[k])

        def arrived(k):
            for o in range(1, heads):
                head_copy(o, k).wait_recv()
            local_copy(k).wait()

        def project(k, first, count):
            span = pl.ds(pl.multiple_of(k * quarter, quarter), quarter)
            left = landed[:, span].reshape(mp_count * quarter, columns)
            features = pl.ds(pl.multiple_of(first, count), count)
            value = contract_last(left, out_rows[features]).astype(part.dtype)
            for block in range(mp_count):
                at = pl.ds(pl.multiple_of(block * rows + k * quarter, quarter), quarter)
                part[at, features] = value[block * quarter : (block + 1) * quarter]

        load = pltpu.make_async_copy(out_hbm, out_rows, load_sem)
        load.start()
        for k in range(QUARTERS):
            for o in range(1, heads):
                head_copy(o, k).start()
            local_copy(k).start()
        weights = ShardGather(shard_refs, whole_refs, shards[0].shape[0], *weight_sems, dp, mp, chips)
        weights.begin()
        reduce = LineReduce(part, flows, rows, pieces, red_send, red_recv, dp, mp, mp_count)
        gather = LineGather(normed, full_ref, rows, pieces, line_send, line_recv, dp, mp, mp_count)
        load.wait()
        arrived(0)
        for portion in range(per_quarter):
            project(0, portion * slice_rows, slice_rows)
        for piece in range(AHEAD):
            reduce.begin(piece)

        @pl.loop(0, turns)
        def _(turn):
            for array in range(count):

                @pl.when(turn == turns - 1 - 6 * (count - 1 - array))
                def _():
                    weights.spread(array)

            for k in range(1, QUARTERS):

                @pl.when(turn == (k - 1) * per_quarter)
                def _():
                    arrived(k)

            @pl.when(turn < (QUARTERS - 1) * per_quarter)
            def _():
                project(turn // per_quarter + 1, (turn % per_quarter) * slice_rows, slice_rows)

            reduce.begin(jnp.minimum(turn + AHEAD, pieces - 1), turn + AHEAD < pieces)
            reduce.advance(turn)
            done = turn - SKEW * (mp_count - 1)

            @pl.when((done >= 0) & (done < pieces))
            def _():
                reduce.arrive(done)
                reduce.total(done, total)
                span = pl.ds(pl.multiple_of(done * size, size), size)
                residual = hidden_ref[span].astype(jnp.float32) + total[...] + bias_ref[...]
                residual_ref[span] = residual
                unit, _ = unit_rows(residual)
                normed[span] = (unit * gain_ref[...] + shift_ref[...]).astype(normed.dtype)
                gather.advance(0, done)

            for step in range(1, mp_count):
                late = done - SKEW * step
                gather.advance(step, jnp.clip(late, 0, pieces - 1), (late >= 0) & (late < pieces))

        own = pltpu.make_async_copy(normed, full_ref.at[pl.ds(pl.multiple_of(mp * rows, rows), rows)], own_sem)
        own.start()
        reduce.finish()
        gather.finish()
        own.wait()
        weights.finish()
        for k in range(QUARTERS):
            for o in range(1, heads):
                head_copy(o, k).wait_send()

    dma = pltpu.SemaphoreType.DMA
    return pl.pallas_call(
        kernel,
        out_shape=[
            jax.ShapeDtypeStruct((rows, width), jnp.float32),
            jax.ShapeDtypeStruct((mp_count, rows, columns), jnp.bfloat16),
            jax.ShapeDtypeStruct((group_rows, width), jnp.bfloat16),
        ]
        + [jax.ShapeDtypeStruct((dp_count * a.shape[0], a.shape[1]), a.dtype) for a in shards],
        in_specs=[ANY] * 2 + [VMEM] * 4 + [ANY] * count,
        out_specs=[VMEM, VMEM, ANY] + [ANY] * count,
        scratch_shapes=[
            pltpu.VMEM((group_rows, width), jnp.bfloat16), pltpu.VMEM((width, columns), jnp.bfloat16),
            dma(()), dma((QUARTERS,)), dma((heads, QUARTERS)), dma((heads, QUARTERS)),
        ]
        + [pltpu.VMEM((size, width), jnp.float32), pltpu.VMEM((rows, width), jnp.bfloat16)]
        + LineReduce.scratch(mp_count, rows, width, pieces) + LineGather.semaphores(mp_count, pieces)
        + [pltpu.SemaphoreType.DMA(())] + ShardGather.semaphores(count, chips),
        compiler_params=pltpu.CompilerParams(
            collective_id=collective_id, has_side_effects=True, vmem_limit_bytes=63 * MIB),
        cost_estimate=pl.CostEstimate(flops=0, bytes_accessed=300 * MIB, transcendentals=0),
    )(mixed, out_weight, hidden, out_bias, gain, shift, *shards)


def reduce_back_gather(
    part, residual, branch_two, gain, halves, pairs, down_weight, out_weight, heads, members, collective_id
):
    dp_count, mp_count = lax.axis_size("dp"), lax.axis_size("mp")
    chips, count = dp_count // 2, len(pairs)
    rows, width = residual.shape
    half = rows // 2
    pieces = pieces_of(rows)
    size, depth = rows // pieces, width // dp_count
    units = pairs[0][1].shape[1]
    turns = pieces + 2 * SKEW * (mp_count - 1)
    each = dp_count // 4
    busy = count * dp_count // each
    feed_slices = 8
    feed_rows = width // feed_slices
    assert 1 + busy + feed_slices <= turns
    quarter, per_quarter, columns = rows // QUARTERS, pieces // QUARTERS, heads * HEAD_DIM
    group_rows = mp_count * rows
    offsets = sorted({2 * o for o in range(1, chips)} | {1} | {o * members for o in range(1, heads)})

    def kernel(part_ref, residual_ref, branch_ref, gain_ref, *refs):
        operands, down_ref, out_hbm, refs = refs[: 2 * count + 1], refs[2 * count + 1], refs[2 * count + 2], refs[2 * count + 3 :]
        (grad_ref, sums_ref, full_ref, feed_ref, heads_ref), terms, refs = refs[:5], refs[5 : 5 + count], refs[5 + count :]
        loaded, refs = refs[: 2 * count], refs[2 * count :]
        (credit, down_rows, down_sem, fed, fed_sem, out_rows, out_sem, gathered, gathered_sem, stage,
         stage_sem, head_send, head_recv, half_sem, total, low, kept, slices, from_partner, chip_sum, load_sem, keep_sem, pair_send, pair_recv, cross_send, cross_recv,
         flows, red_send, red_recv, line_send, line_recv, own_sem) = refs
        dp, mp = lax.axis_index("dp"), lax.axis_index("mp")
        partner = (dp ^ 1, mp)
        group, member = dp // members, dp % members
        greet_all([(dp ^ o, mp) for o in offsets], dp, mp, mp_count)
        reduce = LineReduce(part_ref, flows, rows, pieces, red_send, red_recv, dp, mp, mp_count)
        gather = LineGather(low, full_ref, rows, pieces, line_send, line_recv, dp, mp, mp_count)
        for piece in range(AHEAD):
            reduce.begin(piece)
        loads = [[] for _ in range(count)]
        for h in range(2):
            for b in range(mp_count):
                to = pl.ds(b * rows + h * half, half)
                loads[0].append(pltpu.make_async_copy(
                    operands[h].at[pl.ds(b * half, half)], loaded[0].at[to], half_sem.at[h, b]))
        for index in range(1, 2 * count):
            loads[index // 2].append(pltpu.make_async_copy(operands[index + 1], loaded[index], load_sem.at[index]))
        for copy in loads[0] + loads[1]:
            copy.start()
        sums_ref[...] = jnp.zeros_like(sums_ref)

        def pair(mat, o):
            return remote(slices.at[o], from_partner.at[o], pair_send.at[mat, o], pair_recv.at[mat, o], partner)

        def cross(mat, o, peer):
            return remote(chip_sum.at[mat, o - 1], terms[mat].at[o], cross_send.at[mat, o], cross_recv.at[mat, o],
                          (peer, mp))

        def weight_slice(mat, index):
            o = (index + 1) % chips
            mine = index >= chips
            owner = dp ^ (2 * o) ^ jnp.where(mine, 0, 1)
            left = loaded[2 * mat][:, pl.ds(pl.multiple_of(owner * depth, depth), depth)]
            value = contract_first(left, loaded[2 * mat + 1][...])

            @pl.when(jnp.logical_not(mine))
            def _():
                if mat:
                    pair(mat - 1, o).wait_send()
                    pl.semaphore_wait(credit, 1)
                slices[o] = value.astype(slices.dtype)
                pair(mat, o).start()

            @pl.when(mine)
            def _():
                pair(mat, o).wait_recv()
                both = (value + from_partner[o].astype(jnp.float32)).astype(slices.dtype)
                if mat < count - 1:
                    pl.semaphore_signal(credit, inc=1, device_id=partner, device_id_type=MESH)

                @pl.when(o == 0)
                def _():
                    kept[mat] = both
                    pltpu.make_async_copy(kept.at[mat], terms[mat].at[0], keep_sem.at[mat]).start()

                @pl.when(o != 0)
                def _():
                    chip_sum[mat, o - 1] = both
                    cross(mat, o, owner).start()

        def down_load(index):
            at = pl.ds(pl.multiple_of(index * feed_rows, feed_rows), feed_rows)
            return pltpu.make_async_copy(down_ref.at[at], down_rows.at[index % 2], down_sem.at[index % 2])

        def feed_store(index):
            at = pl.ds(pl.multiple_of(index * feed_rows, feed_rows), feed_rows)
            return pltpu.make_async_copy(fed.at[index % 2], feed_ref.at[:, at], fed_sem.at[index % 2])

        def feed_slice(index):
            down_load(index).wait()

            @pl.when(index + 1 < feed_slices)
            def _():
                down_load(index + 1).start()

            @pl.when(index >= 2)
            def _():
                feed_store(index - 2).wait()

            fed[index % 2] = contract_last(loaded[1][...], down_rows[index % 2]).astype(fed.dtype)
            feed_store(index).start()

        def rows_load(k, block, own):
            source = low.at[pl.ds(k * quarter, quarter)] if own else full_ref.at[
                pl.ds(pl.multiple_of(block * rows + k * quarter, quarter), quarter)]
            return pltpu.make_async_copy(source, gathered.at[block], gathered_sem.at[block])

        def head_copy(o, k):
            span = pl.ds(k * quarter, quarter)
            return remote(stage.at[:, span, lanes(group ^ o)], heads_ref.at[group, :, span], head_send.at[o, k],
                          head_recv.at[o, k], ((group ^ o) * members + member, mp))

        def local_copy(k):
            span = pl.ds(k * quarter, quarter)
            return pltpu.make_async_copy(stage.at[:, span, lanes(group)], heads_ref.at[group, :, span], stage_sem.at[k])

        def to_heads(k):
            for block in range(mp_count):
                for own in (True, False):

                    @pl.when((mp == block) if own else (mp != block))
                    def _():
                        rows_load(k, block, own).start()

            for block in range(mp_count):
                for own in (True, False):

                    @pl.when((mp == block) if own else (mp != block))
                    def _():
                        rows_load(k, block, own).wait()

            value = jnp.dot(gathered[...].reshape(mp_count * quarter, width), out_rows[...],
                            preferred_element_type=jnp.float32)
            stage[:, k * quarter : (k + 1) * quarter] = value.reshape(mp_count, quarter, columns).astype(stage.dtype)
            for o in range(1, heads):
                head_copy(o, k).start()
            local_copy(k).start()

        out_load = pltpu.make_async_copy(out_hbm, out_rows, out_sem)
        out_load.start()
        down_load(0).start()

        @pl.loop(0, turns)
        def _(turn):
            reduce.begin(jnp.minimum(turn + AHEAD, pieces - 1), turn + AHEAD < pieces)
            reduce.advance(turn)
            done = turn - SKEW * (mp_count - 1)

            @pl.when((done >= 0) & (done < pieces))
            def _():
                reduce.arrive(done)
                reduce.total(done, total)
                span = pl.ds(pl.multiple_of(done * size, size), size)
                unit, inverse = unit_rows(residual_ref[span])
                upstream = total[...]
                sums_ref[0:1] += jnp.sum(upstream * unit, axis=0, keepdims=True)
                sums_ref[1:2] += jnp.sum(upstream, axis=0, keepdims=True)
                grad = branch_ref[span].astype(jnp.float32) + norm_back(upstream, unit, inverse, gain_ref[...])
                grad_ref[span] = grad
                rounded = grad.astype(low.dtype)
                low[span] = rounded
                sums_ref[2:3] += jnp.sum(rounded.astype(jnp.float32), axis=0, keepdims=True)
                gather.advance(0, done)

            for step in range(1, mp_count):
                late = done - SKEW * step
                gather.advance(step, jnp.clip(late, 0, pieces - 1), (late >= 0) & (late < pieces))
            for mat in range(count):

                @pl.when(turn == 1 + mat * busy // count)
                def _():
                    for copy in loads[mat]:
                        copy.wait()

                first = turn - 1 - mat * busy // count

                @pl.when((first >= 0) & (first < busy // count))
                def _():
                    for i in range(each):
                        weight_slice(mat, first * each + i)

            @pl.when((turn >= 1 + busy) & (turn < 1 + busy + feed_slices))
            def _():
                feed_slice(turn - 1 - busy)

            for k in range(QUARTERS):

                @pl.when(turn == (k + 1) * per_quarter - 1 + 2 * SKEW * (mp_count - 1))
                def _():
                    if k == 0:
                        out_load.wait()
                    to_heads(k)

        own = pltpu.make_async_copy(low, full_ref.at[pl.ds(pl.multiple_of(mp * rows, rows), rows)], own_sem)
        own.start()
        reduce.finish()
        gather.finish()
        own.wait()
        for index in range(feed_slices - 2, feed_slices):
            feed_store(index).wait()
        for k in range(QUARTERS):
            local_copy(k).wait()
            for o in range(1, heads):
                head_copy(o, k).wait()
        for mat in range(count):
            pltpu.make_async_copy(kept.at[mat], terms[mat].at[0], keep_sem.at[mat]).wait()
            for o in range(chips):
                if mat == count - 1:
                    pair(mat, o).wait_send()
                if o:
                    cross(mat, o, dp ^ (2 * o)).wait()

    bf16, f32 = jnp.bfloat16, jnp.float32
    dma = pltpu.SemaphoreType.DMA
    flat = [array for two in pairs for array in two][1:]
    return pl.pallas_call(
        kernel,
        out_shape=[
            jax.ShapeDtypeStruct((rows, width), f32),
            jax.ShapeDtypeStruct((8, width), f32),
            jax.ShapeDtypeStruct((group_rows, width), bf16),
            jax.ShapeDtypeStruct((group_rows, width), bf16),
            jax.ShapeDtypeStruct((heads, mp_count, rows, HEAD_DIM), bf16),
        ]
        + [jax.ShapeDtypeStruct((chips, depth, units), bf16)] * count,
        in_specs=[VMEM] * 4 + [ANY] * (2 * count + 3),
        out_specs=[VMEM, VMEM] + [ANY] * (3 + count),
        scratch_shapes=[pltpu.VMEM((mp_count * rows, width), bf16)] + [pltpu.VMEM(a.shape, a.dtype) for a in flat]
        + [
            pltpu.SemaphoreType.REGULAR,
            pltpu.VMEM((2, feed_rows, units), bf16), dma((2,)),
            pltpu.VMEM((2, group_rows, feed_rows), bf16), dma((2,)),
            pltpu.VMEM((width, columns), bf16), dma(()),
            pltpu.VMEM((mp_count, quarter, width), bf16), dma((mp_count,)),
            pltpu.VMEM((mp_count, rows, columns), bf16), dma((QUARTERS,)),
            dma((heads, QUARTERS)), dma((heads, QUARTERS)),
            dma((2, mp_count)),
            pltpu.VMEM((size, width), f32),
            pltpu.VMEM((rows, width), bf16),
            pltpu.VMEM((count, depth, units), bf16),
            pltpu.VMEM((chips, depth, units), bf16),
            pltpu.VMEM((chips, depth, units), bf16),
            pltpu.VMEM((count, chips - 1, depth, units), bf16),
            dma((2 * count,)), dma((count,)),
        ]
        + [dma((count, chips)) for _ in range(4)]
        + LineReduce.scratch(mp_count, rows, width, pieces) + LineGather.semaphores(mp_count, pieces)
        + [dma(())],
        compiler_params=pltpu.CompilerParams(
            collective_id=collective_id, has_side_effects=True, vmem_limit_bytes=63 * MIB),
        cost_estimate=pl.CostEstimate(flops=40 << 30, bytes_accessed=300 * MIB, transcendentals=0),
    )(part, residual, branch_two, gain, *halves, *flat, down_weight, out_weight)


def finish_back(query_grad, key_part, value_part, weights, normed, residual_grad, hidden, gain, out_part, vectors, heads, members,
                collective_id):
    rows, width = hidden.shape
    dp_count, mp_count = lax.axis_size("dp"), lax.axis_size("mp")
    chips, pieces = dp_count // 2, pieces_of(rows)
    size, depth, columns = rows // pieces, width // dp_count, heads * HEAD_DIM
    kinds, quarter = 3, rows // QUARTERS
    per_quarter = pieces // QUARTERS
    slice_rows = width // per_quarter
    turns = pieces + SKEW * (mp_count - 1)
    slices_each = max(dp_count // 4, 1)
    group_rows = mp_count * rows
    slab, each = vectors.shape[1], width // dp_count // 128
    query_grad = query_grad.reshape(heads, mp_count, rows, HEAD_DIM)
    shared = [v.reshape(dp_count, mp_count, rows, HEAD_DIM) for v in (key_part, value_part)]

    def kernel(query_ref, key_ref, value_ref, weights_hbm, normed_hbm, residual_ref, hidden_ref, gain_ref, out_ref, vector_ref,
               grad_ref, weight_grad_ref, out_grad_ref, summed_ref,
               weights, normed, landed, own, parts, stage, part, total, flows, red_send, red_recv,
               slices, from_partner, chip_sum, from_chips, out_partner, out_sum, out_chips,
               load_sem, own_sem, part_send, part_recv, local_sem, head_send, head_recv,
               pair_send, pair_recv, cross_send, cross_recv,
               sums_ref, column_ref, packed, vector_parts, line_parts, vec_send, vec_recv, line_send, line_recv):
        dp, mp = lax.axis_index("dp"), lax.axis_index("mp")
        group, member = dp // members, dp % members
        partner = (dp ^ 1, mp)
        greet_all([(dp ^ o, mp) for o in range(1, dp_count)] + [(dp, mp ^ o) for o in range(1, mp_count)], dp, mp, mp_count)
        reduce = LineReduce(part, flows, rows, pieces, red_send, red_recv, dp, mp, mp_count)
        loads = [pltpu.make_async_copy(weights_hbm, weights, load_sem.at[0]),
                 pltpu.make_async_copy(normed_hbm, normed, load_sem.at[1])]
        shared_refs = (key_ref, value_ref)

        def rows_of(k):
            return pl.ds(k * quarter, quarter)

        def lane_span(kind, head):
            return pl.ds(pl.multiple_of(kind * columns + head * HEAD_DIM, HEAD_DIM), HEAD_DIM)

        def landing(kind, k, head):
            return landed.at[:, rows_of(k), lane_span(kind, head)]

        def own_copy(kind, o):
            return pltpu.make_async_copy(shared_refs[kind].at[(group ^ o) * members + member], own.at[kind, o],
                                         own_sem.at[kind, o])

        def part_copy(kind, o, p, k):
            return remote(shared_refs[kind].at[(group ^ o) * members + (member ^ p), :, rows_of(k)],
                          parts.at[kind, o, p - 1, :, rows_of(k)], part_send.at[kind, o, p - 1, k],
                          part_recv.at[kind, o, p - 1, k], (group * members + (member ^ p), mp))

        def head_copy(kind, o, k):
            source = query_ref.at[group ^ o, :, rows_of(k)] if kind == 2 else stage.at[kind, o, :, rows_of(k)]
            return remote(source, landing(kind, k, group), head_send.at[kind, o, k], head_recv.at[kind, o, k],
                          ((group ^ o) * members + member, mp))

        def local_copy(k):
            return pltpu.make_async_copy(query_ref.at[group, :, rows_of(k)], landing(2, k, group), local_sem.at[k])

        for k in range(QUARTERS):
            for kind in range(2):
                for o in range(heads):
                    for p in range(1, members):
                        part_copy(kind, o, p, k).start()
            if k == 0:
                for kind in range(2):
                    for o in range(heads):
                        own_copy(kind, o).start()
                for copy in loads:
                    copy.start()
            for o in range(1, heads):
                head_copy(2, o, k).start()
            local_copy(k).start()
        for k in range(QUARTERS):
            for kind in range(2):
                for o in list(range(1, heads)) + [0]:
                    if k == 0:
                        own_copy(kind, o).wait()
                    value = own[kind, o, :, k * quarter : (k + 1) * quarter].astype(jnp.float32)
                    for p in range(1, members):
                        part_copy(kind, o, p, k).wait_recv()
                        value = value + parts[kind, o, p - 1, :, k * quarter : (k + 1) * quarter].astype(jnp.float32)
                    if o:
                        stage[kind, o, :, k * quarter : (k + 1) * quarter] = value.astype(stage.dtype)
                        head_copy(kind, o, k).start()
                    else:
                        landed[:, k * quarter : (k + 1) * quarter, lane_span(kind, group)] = value.astype(landed.dtype)

        def arrived(k):
            for kind in range(kinds):
                for o in range(1, heads):
                    head_copy(kind, o, k).wait_recv()
            local_copy(k).wait()

        def project(k, first, count):
            span = pl.ds(pl.multiple_of(k * quarter, quarter), quarter)
            left = landed[:, span].reshape(mp_count * quarter, kinds * columns)
            features = pl.ds(pl.multiple_of(first, count), count)
            value = contract_last(left, weights[features]).astype(part.dtype)
            for block in range(mp_count):
                at = pl.ds(pl.multiple_of(block * rows + k * quarter, quarter), quarter)
                part[at, features] = value[block * quarter : (block + 1) * quarter]

        def slab(owner):
            return pl.ds(pl.multiple_of(owner * depth, depth), depth)

        def pair(o):
            return remote(slices.at[o], from_partner.at[o], pair_send.at[0, o], pair_recv.at[0, o], partner)

        def cross(o, peer):
            return remote(chip_sum.at[o], from_chips.at[o], cross_send.at[0, o], cross_recv.at[0, o], (peer, mp))

        def out_pair(o):
            return remote(out_ref.at[slab(dp ^ (2 * o) ^ 1)], out_partner.at[o], pair_send.at[1, o], pair_recv.at[1, o],
                          partner)

        def out_cross(o):
            return remote(out_sum.at[o], out_chips.at[o], cross_send.at[1, o], cross_recv.at[1, o], (dp ^ (2 * o), mp))

        def weight_slice(index):
            o = (index + 1) % chips
            mine = index >= chips
            owner = dp ^ (2 * o) ^ jnp.where(mine, 0, 1)
            rows_all = landed[...].reshape(group_rows, kinds * columns)
            value = contract_first(normed[:, slab(owner)], rows_all)

            @pl.when(jnp.logical_not(mine))
            def _():
                slices[o] = value.astype(slices.dtype)
                pair(o).start()

            @pl.when(mine)
            def _():
                pair(o).wait_recv()
                both = value + from_partner[o].astype(jnp.float32)

                @pl.when(o == 0)
                def _():
                    weight_grad_ref[...] = both

                @pl.when(o != 0)
                def _():
                    chip_sum[o] = both.astype(chip_sum.dtype)
                    cross(o, owner).start()

        for copy in loads:
            copy.wait()
        arrived(0)
        for part_index in range(per_quarter):
            project(0, part_index * slice_rows, slice_rows)
        for piece in range(AHEAD):
            reduce.begin(piece)
        for o in range(chips):
            out_pair(o).start()
        sums_ref[...] = jnp.zeros_like(sums_ref)

        @pl.loop(0, turns)
        def _(turn):
            for k in range(1, QUARTERS):

                @pl.when(turn == min(2, per_quarter) * (k - 1))
                def _():
                    arrived(k)

            @pl.when(turn < (QUARTERS - 1) * per_quarter)
            def _():
                k, portion = turn // per_quarter + 1, turn % per_quarter
                project(k, portion * slice_rows, slice_rows)

            reduce.begin(jnp.minimum(turn + AHEAD, pieces - 1), turn + AHEAD < pieces)
            reduce.advance(turn)
            done = turn - SKEW * (mp_count - 1)

            @pl.when(done >= 0)
            def _():
                reduce.arrive(done)
                reduce.total(done, total)
                span = pl.ds(pl.multiple_of(done * size, size), size)
                unit, inverse = unit_rows(hidden_ref[span].astype(jnp.float32))
                upstream = total[...]
                sums_ref[0:1] += jnp.sum(upstream * unit, axis=0, keepdims=True)
                sums_ref[1:2] += jnp.sum(upstream, axis=0, keepdims=True)
                grad_ref[span] = residual_ref[span] + norm_back(upstream, unit, inverse, gain_ref[...])

            @pl.when(turn == late_turn - 1)
            def _():
                for o in list(range(1, chips)) + [0]:
                    out_pair(o).wait_recv()
                    value = out_ref[slab(dp ^ (2 * o))].astype(jnp.float32) + out_partner[o].astype(jnp.float32)
                    if o:
                        out_sum[o] = value.astype(out_sum.dtype)
                        out_cross(o).start()
                    else:
                        out_grad_ref[...] = value

            @pl.when(turn == late_turn - 1)
            def _():
                column_ref[0:1] = jnp.sum(
                    landed[...].reshape(group_rows, kinds * columns).astype(jnp.float32), axis=0, keepdims=True)

            @pl.when((turn >= late_turn) & (turn < late_turn + dp_count // slices_each))
            def _():
                for i in range(slices_each):
                    weight_slice((turn - late_turn) * slices_each + i)

        reduce.finish()
        packed[...] = vector_ref[...]
        for owner in range(dp_count):
            for r in range(each):
                at = slice((owner * each + r) * 128, (owner * each + r + 1) * 128)
                for k in range(2):
                    packed[owner, k * each + r : k * each + r + 1] = sums_ref[k : k + 1, at]
        for head in range(heads):
            feature = mp * heads + head
            for k, kind in ((2, 2), (3, 1)):
                at = slice(kind * columns + head * HEAD_DIM, kind * columns + (head + 1) * HEAD_DIM)
                packed[feature // each, pl.ds(k * each + feature % each, 1)] = column_ref[0:1, at]

        def vector_copy(o):
            return remote(packed.at[dp ^ o], vector_parts.at[o], vec_send.at[o], vec_recv.at[o], (dp ^ o, mp))

        def line_copy(o):
            return remote(line_parts.at[mp], line_parts.at[mp], line_send.at[o], line_recv.at[o], (dp, mp ^ o))

        for o in range(1, dp_count):
            vector_copy(o).start()
        value = packed[dp]
        for o in range(1, dp_count):
            vector_copy(o).wait_recv()
            value = value + vector_parts[o]
        line_parts[mp] = value
        for o in range(1, mp_count):
            line_copy(o).start()
        for o in range(chips):
            pair(o).wait_send()
            out_pair(o).wait_send()
            if o:
                cross(o, dp ^ (2 * o)).wait()
                weight_grad_ref[...] += from_chips[o].astype(jnp.float32)
                out_cross(o).wait()
                out_grad_ref[...] += out_chips[o].astype(jnp.float32)
        for k in range(QUARTERS):
            for o in range(heads):
                for kind in range(2):
                    for p in range(1, members):
                        part_copy(kind, o, p, k).wait_send()
                if o:
                    for kind in range(kinds):
                        head_copy(kind, o, k).wait_send()
        for o in range(1, mp_count):
            line_copy(o).wait()
        value = line_parts[0]
        for index in range(1, mp_count):
            value = value + line_parts[index]
        summed_ref[...] = value
        for o in range(1, dp_count):
            vector_copy(o).wait_send()

    late_turn = min(2, per_quarter) * (QUARTERS - 2) + 1
    assert late_turn + dp_count // slices_each <= turns
    dma = pltpu.SemaphoreType.DMA
    bf16, f32 = jnp.bfloat16, jnp.float32
    own_columns = out_part.shape[1]
    return pl.pallas_call(
        kernel,
        out_shape=[
            jax.ShapeDtypeStruct((rows, width), f32),
            jax.ShapeDtypeStruct((depth, kinds * columns), f32),
            jax.ShapeDtypeStruct((depth, own_columns), f32),
            jax.ShapeDtypeStruct((slab, 128), f32),
        ],
        in_specs=[ANY] * 5 + [VMEM] * 5,
        out_specs=[VMEM] * 4,
        scratch_shapes=[
            pltpu.VMEM((width, kinds * columns), bf16),
            pltpu.VMEM((group_rows, width), bf16),
            pltpu.VMEM((mp_count, rows, kinds * columns), bf16),
            pltpu.VMEM((2, heads, mp_count, rows, HEAD_DIM), bf16),
            pltpu.VMEM((2, heads, members - 1, mp_count, rows, HEAD_DIM), bf16),
            pltpu.VMEM((2, heads, mp_count, rows, HEAD_DIM), bf16),
            pltpu.VMEM((group_rows, width), bf16),
            pltpu.VMEM((size, width), f32),
        ]
        + LineReduce.scratch(mp_count, rows, width, pieces)
        + [pltpu.VMEM((chips, depth, kinds * columns), bf16) for _ in range(4)]
        + [pltpu.VMEM((chips, depth, own_columns), bf16) for _ in range(3)]
        + [dma((2,)), dma((2, heads))]
        + [dma((2, heads, members - 1, QUARTERS)) for _ in range(2)]
        + [dma((QUARTERS,)), dma((kinds, heads, QUARTERS)), dma((kinds, heads, QUARTERS))]
        + [dma((2, chips)) for _ in range(4)]
        + [pltpu.VMEM((8, width), f32), pltpu.VMEM((8, kinds * columns), f32)]
        + [pltpu.VMEM((count, slab, 128), f32) for count in (dp_count, dp_count, mp_count)]
        + [dma((dp_count,)), dma((dp_count,)), dma((mp_count,)), dma((mp_count,))],
        compiler_params=pltpu.CompilerParams(
            collective_id=collective_id, has_side_effects=True, vmem_limit_bytes=63 * MIB),
        cost_estimate=pl.CostEstimate(flops=20 << 30, bytes_accessed=300 * MIB, transcendentals=0),
    )(query_grad, *shared, weights, normed, residual_grad, hidden, gain, out_part, vectors)


UNITS = 512
CHUNK = 256


def feed_both_ways(rows_two, branch_halves, block, up_all, down_all, up_bias):
    rows, width = rows_two.shape
    units = up_all.shape[1]
    tile = min(UNITS, units)
    half = block // 2
    half_root = 1.0 / math.sqrt(2.0)
    density_scale = 1.0 / math.sqrt(2.0 * math.pi)

    def kernel(rows_ref, first_ref, second_ref, up_ref, down_ref, bias_ref, hidden_ref, grad_ref, column_ref, part_ref, total):
        step = pl.program_id(0)
        columns = jnp.zeros((1, tile), jnp.float32)
        up, down = up_ref[...], down_ref[...]
        for first in range(0, rows, CHUNK):
            span = slice(first, first + CHUNK)
            pre = jnp.dot(rows_ref[span], up, preferred_element_type=jnp.float32) + bias_ref[...]
            upstream = jnp.concatenate([
                jnp.dot(ref[b * half : (b + 1) * half], down, preferred_element_type=jnp.float32)
                for b in range(first // block, (first + CHUNK) // block) for ref in (first_ref, second_ref)
            ], axis=0)
            share = 0.5 + 0.5 * lax.erf(pre * half_root)
            hidden_ref[span] = (pre * share).astype(hidden_ref.dtype)
            slope = share + pre * (density_scale * jnp.exp(-0.5 * pre * pre))
            grad = (upstream * slope).astype(grad_ref.dtype)
            grad_ref[span] = grad
            columns = columns + jnp.sum(grad.astype(jnp.float32), axis=0, keepdims=True)
            back = contract_last(grad, up)

            @pl.when(step == 0)
            def _():
                total[span] = back

            @pl.when(step != 0)
            def _():
                total[span] += back

        column_ref[...] = columns

        @pl.when(step == units // tile - 1)
        def _():
            part_ref[...] = total[...].astype(part_ref.dtype)

    bf16 = jnp.bfloat16
    return pl.pallas_call(
        kernel,
        grid=(units // tile,),
        out_shape=[
            jax.ShapeDtypeStruct((rows, units), bf16),
            jax.ShapeDtypeStruct((rows, units), bf16),
            jax.ShapeDtypeStruct((1, units), jnp.float32),
            jax.ShapeDtypeStruct((rows, width), bf16),
        ],
        in_specs=[
            pl.BlockSpec((rows, width), lambda i: (0, 0)),
            pl.BlockSpec((rows // 2, width), lambda i: (0, 0)),
            pl.BlockSpec((rows // 2, width), lambda i: (0, 0)),
            pl.BlockSpec((width, tile), lambda i: (0, i)),
            pl.BlockSpec((width, tile), lambda i: (0, i)),
            pl.BlockSpec((1, tile), lambda i: (0, i)),
        ],
        out_specs=[
            pl.BlockSpec((rows, tile), lambda i: (0, i)),
            pl.BlockSpec((rows, tile), lambda i: (0, i)),
            pl.BlockSpec((1, tile), lambda i: (0, i)),
            pl.BlockSpec((rows, width), lambda i: (0, 0)),
        ],
        scratch_shapes=[pltpu.VMEM((rows, width), jnp.float32)],
        compiler_params=pltpu.CompilerParams(vmem_limit_bytes=60 * MIB),
        cost_estimate=pl.CostEstimate(
            flops=6 * rows * width * units, bytes_accessed=40 * MIB, transcendentals=2 * rows * units),
    )(rows_two, *branch_halves, up_all, down_all, up_bias)


def sum_terms(terms):
    return functools.reduce(jnp.add, [terms[k].astype(jnp.float32) for k in range(terms.shape[0])])


def per_device(
    hidden_in,
    output_grad,
    first_gain,
    first_shift,
    query_weight,
    query_bias,
    key_weight,
    value_weight,
    value_bias,
    out_weight,
    out_bias,
    second_gain,
    second_shift,
    up_weight,
    up_bias,
    down_weight,
    down_bias,
    seq_lengths,
    block_order,
    block_slot,
):
    local_rows, model_width = hidden_in.shape
    mp_count, dp_count = lax.axis_size("mp"), lax.axis_size("dp")
    mp_index, dp_index = lax.axis_index("mp"), lax.axis_index("dp")
    group_rows = local_rows * mp_count
    head_width = query_weight.shape[1]
    heads_local = head_width // HEAD_DIM
    hidden_width = up_weight.shape[1]
    members = dp_count // heads_local
    blocks_each = group_rows // BLOCK
    plan = (seq_lengths, block_order, block_slot)

    vectors = (first_gain, first_shift, query_bias, value_bias, out_bias, second_gain, second_shift, down_bias, up_bias)
    rows_one, vector_rows, projections, out_all, head_shared, head_queries, branch_two, branch_rest, live, branch_first = project_first(
        hidden_in, output_grad, seq_lengths, block_order, vectors,
        (key_weight, value_weight, query_weight), out_weight, heads_local, members, 0,
    )
    own_valid = live[:, :1] > 0
    vector_rows = vector_rows.reshape(dp_count, -1, 128)
    each = model_width // dp_count // 128
    gain_one, _, _, _, bias_out, gain_two, shift_two, bias_down = (
        vector_rows[:, k * each : (k + 1) * each].reshape(1, model_width) for k in range(8)
    )
    up_each = up_bias.shape[0] // 128
    bias_up = vector_rows[:, 8 * each : 8 * each + up_each].reshape(1, up_bias.shape[0] * dp_count)

    branch_second = whole_rows(branch_rest)
    head_mix, exact_mix, log_total = attend(head_queries, head_shared, *plan, members, blocks_each)
    residual, attended_low, rows_two, up_all, down_all = mix_norm_gather(
        head_mix, out_all, hidden_in, bias_out, gain_two, shift_two, (up_weight, down_weight), heads_local, members, 3
    )
    attended_low = attended_low.reshape(group_rows, head_width)

    bias_hidden = lax.dynamic_slice_in_dim(bias_up, mp_index * hidden_width, hidden_width, 1)
    hidden_low, pre_grad, pre_columns, up_part = feed_both_ways(
        rows_two, (branch_first, branch_second), local_rows, up_all, down_all, bias_hidden
    )
    residual_grad, sums_two, branch_rows_one, feed_part, head_grad, down_terms, up_terms = reduce_back_gather(
        up_part, residual, branch_two, gain_two, (branch_first, branch_second),
        ((None, hidden_low), (rows_two, pre_grad)), down_all, out_all, heads_local, members, 4,
    )
    down_weight_grad, up_weight_grad = (
        sum_terms(terms) for terms in (down_terms, up_terms)
    )
    residual_grad, down_weight_grad, up_weight_grad = lax.optimization_barrier(
        (residual_grad, down_weight_grad, up_weight_grad)
    )

    feed = row_share(feed_part)
    result = residual + feed + bias_down
    output = jnp.where(own_valid, result, 0.0).astype(jnp.bfloat16)

    head_grad = head_grad.reshape(heads_local * group_rows, HEAD_DIM)
    head_query_grad, head_key_grad, head_value_grad = attend_back(
        head_queries, head_shared, head_grad, exact_mix, log_total, *plan, members, blocks_each
    )

    def column_sums(values):
        return jnp.sum(values.astype(jnp.float32), axis=0)

    def placed(values):
        whole = jnp.zeros((values.shape[0] * mp_count,), jnp.float32)
        return lax.dynamic_update_slice_in_dim(whole, values, mp_index * values.shape[0], 0)

    none = jnp.zeros((model_width,), jnp.float32)
    sums = (
        none, none, none, none, sums_two[2], sums_two[0], sums_two[1], column_sums(branch_two), placed(pre_columns[0]),
    )
    packed = jnp.concatenate([v.reshape(dp_count, -1, 128) for v in sums], axis=1)
    packed = jnp.pad(packed, ((0, 0), (0, -packed.shape[1] % 8), (0, 0)))
    out_weight_part = contract_first(branch_rows_one, attended_low).astype(jnp.bfloat16)
    input_grad, weight_grads, out_weight_grad, summed = finish_back(
        head_query_grad, head_key_grad, head_value_grad, projections, rows_one, residual_grad, hidden_in, gain_one,
        out_weight_part, packed, heads_local, members, 7,
    )
    key_weight_grad, value_weight_grad, query_weight_grad = (
        weight_grads[:, k * head_width : (k + 1) * head_width] for k in range(3)
    )
    vector_grads = [summed[k * each : (k + 1) * each].reshape(-1) for k in range(8)]
    up_bias_grad = summed[8 * each : 8 * each + up_each].reshape(-1)
    return (
        output,
        input_grad,
        vector_grads[0],
        vector_grads[1],
        query_weight_grad,
        vector_grads[2],
        key_weight_grad,
        value_weight_grad,
        vector_grads[3],
        out_weight_grad,
        vector_grads[4],
        vector_grads[5],
        vector_grads[6],
        up_weight_grad,
        up_bias_grad,
        down_weight_grad,
        vector_grads[7],
    )


def solution(mesh):
    return jax.shard_map(
        per_device,
        mesh=mesh,
        in_specs=(
            P(("dp", "mp"), None),
            P(("dp", "mp"), None),
            P("dp"),
            P("dp"),
            P("dp", "mp"),
            P("dp"),
            P("dp", "mp"),
            P("dp", "mp"),
            P("dp"),
            P("dp", "mp"),
            P("dp"),
            P("dp"),
            P("dp"),
            P("dp", "mp"),
            P("dp"),
            P("dp", "mp"),
            P("dp"),
            P(),
            P(),
            P(),
        ),
        out_specs=(
            P(("dp", "mp"), None),
            P(("dp", "mp"), None),
            P("dp"),
            P("dp"),
            P("dp", "mp"),
            P("dp"),
            P("dp", "mp"),
            P("dp", "mp"),
            P("dp"),
            P("dp", "mp"),
            P("dp"),
            P("dp"),
            P("dp"),
            P("dp", "mp"),
            P("dp"),
            P("dp", "mp"),
            P("dp"),
        ),
        check_vma=False,
    )
```

```python
import functools
import math

import jax
import jax.numpy as jnp
from jax import lax
from jax.experimental import pallas as pl
from jax.experimental.pallas import tpu as pltpu
from jax.sharding import PartitionSpec as P

HEAD_DIM = 128
BLOCK = 128
KEY_BLOCKS = 8
MESH = pl.DeviceIdType.MESH
ANY = pl.BlockSpec(memory_space=pl.ANY)
VMEM = pl.BlockSpec(memory_space=pltpu.VMEM)
SMEM = pl.BlockSpec(memory_space=pltpu.SMEM)
MIB = 1 << 20


big_negative = -1e30
norm_epsilon = 1e-05


def norm_back(upstream, normed, inverse, gain_row):
    scaled = upstream * gain_row
    mean_grad = jnp.mean(scaled, axis=-1, keepdims=True)
    second = jnp.mean(scaled * normed, axis=-1, keepdims=True)
    return inverse * (scaled - mean_grad - normed * second)


def contract_last(left, right):
    return lax.dot_general(
        left, right, (((1,), (1,)), ((), ())), preferred_element_type=jnp.float32
    )


def contract_first(left, right):
    return lax.dot_general(
        left, right, (((0,), (0,)), ((), ())), preferred_element_type=jnp.float32
    )


def whole_rows(local_part):
    return lax.all_gather(local_part, "mp", axis=0, tiled=True)


def row_share(term):
    term = term.astype(jnp.bfloat16)
    return lax.psum_scatter(term, "mp", scatter_dimension=0, tiled=True).astype(jnp.float32)


def greet(peers):
    barrier = pltpu.get_barrier_semaphore()
    for peer in peers:
        pl.semaphore_signal(barrier, inc=1, device_id=peer, device_id_type=MESH)
    pl.semaphore_wait(barrier, len(peers))


def remote(src, dst, send_sem, recv_sem, peer):
    return pltpu.make_async_remote_copy(
        src_ref=src, dst_ref=dst, send_sem=send_sem, recv_sem=recv_sem,
        device_id=peer, device_id_type=MESH,
    )


def head_place(heads, members):
    me = lax.axis_index("dp")
    return me, me // members, me % members, lax.axis_index("mp")


def lanes(head):
    return pl.ds(pl.multiple_of(head * HEAD_DIM, HEAD_DIM), HEAD_DIM)


def sequence_of(place, lengths):
    first, length, running = jnp.int32(0), jnp.int32(0), jnp.int32(0)
    for s in range(lengths.shape[0]):
        inside = place >= running
        first = jnp.where(inside, running, first)
        length = jnp.where(inside, lengths[s], length)
        running = running + (lengths[s] + (BLOCK - 1)) // BLOCK
    return first, length - (place - first) * BLOCK


def list_queries(slot, index_list, place_list, members, blocks_each):
    member = lax.axis_index("dp") % members

    def visit(block, count):
        dealt = slot[block]
        owner = dealt // blocks_each

        @pl.when(owner % members == member)
        def _():
            index_list[count] = (owner // members) * blocks_each + dealt % blocks_each
            place_list[count] = block

        return count + (owner % members == member).astype(jnp.int32)

    lax.fori_loop(0, slot.shape[0], visit, jnp.int32(0))


def block_rows(block):
    return pl.ds(pl.multiple_of(block * BLOCK, BLOCK), BLOCK)


class QueryPair:
    def __init__(self, pair, lengths, index_list, place_list):
        self.index = [index_list[2 * pair + i] for i in range(2)]
        self.place = [place_list[2 * pair + i] for i in range(2)]
        found = [sequence_of(place, lengths) for place in self.place]
        self.start = found[0][0]
        lane = lax.broadcasted_iota(jnp.int32, (1, 2 * BLOCK), 1)
        right = lane >= BLOCK

        def lanes_of(left_value, right_value):
            return jnp.where(right, right_value, left_value)

        within = lane - lanes_of(0, BLOCK)
        base = self.start * BLOCK
        self.position = lanes_of(self.place[0], self.place[1]) * BLOCK + within - base
        self.lowest = lanes_of(found[0][0], found[1][0]) * BLOCK - base
        self.live = within < lanes_of(found[0][1], found[1][1])
        self.tiles = (self.place[1] - self.start) // KEY_BLOCKS + 1
        self.open_tiles = jnp.where(found[0][0] == found[1][0], (self.place[0] - self.start) // KEY_BLOCKS, 0)

    def row(self, tile):
        return pl.multiple_of((self.start + tile * KEY_BLOCKS) * BLOCK, BLOCK)

    def allowed(self, tile):
        width = KEY_BLOCKS * BLOCK
        key = lax.broadcasted_iota(jnp.int32, (width, 2 * BLOCK), 0)
        return (key <= self.position - tile * width) & (key >= self.lowest - tile * width)

    def load_t(self, ref):
        return jnp.concatenate([ref[block_rows(index)].T for index in self.index], axis=1)

    def load(self, ref):
        return jnp.concatenate([ref[block_rows(index)] for index in self.index], axis=0)

    def store_t(self, ref, value_t):
        for i, index in enumerate(self.index):
            ref[block_rows(index)] = value_t[:, i * BLOCK : (i + 1) * BLOCK].T.astype(ref.dtype)


def attend(queries, shared, lengths, order, slot, members, blocks_each):
    pairs, key_count = queries.shape[0] // (2 * BLOCK), shared.shape[1] // BLOCK
    width = KEY_BLOCKS * BLOCK
    padded = (key_count + KEY_BLOCKS - 1) * BLOCK
    scale = math.log2(math.e) / math.sqrt(HEAD_DIM)

    def kernel(lengths_ref, slot_ref, q_ref, shared_ref, out_ref, exact_ref, log_ref,
               index_list, place_list, keys, values_t):
        list_queries(slot_ref, index_list, place_list, members, blocks_each)

        @pl.loop(0, key_count)
        def _(block):
            source = block_rows(slot_ref[block])
            keys[block_rows(block)] = shared_ref[0, source]
            values_t[:, block_rows(block)] = shared_ref[1, source].T

        tail = pl.ds(key_count * BLOCK, padded - key_count * BLOCK)
        keys[tail] = jnp.zeros((padded - key_count * BLOCK, HEAD_DIM), keys.dtype)
        values_t[:, tail] = jnp.zeros((HEAD_DIM, padded - key_count * BLOCK), keys.dtype)

        @pl.loop(0, pairs)
        def _(index):
            pair = QueryPair(index, lengths_ref, index_list, place_list)
            query_t = pair.load_t(q_ref)

            def step(tile, carry, masked):
                top, total, mix = carry
                span = pl.ds(pair.row(tile), width)
                scores = jnp.dot(keys[span], query_t, preferred_element_type=jnp.float32)
                if masked:
                    scores = jnp.where(pair.allowed(tile), scores, big_negative)
                new_top = jnp.maximum(top, jnp.max(scores, axis=0, keepdims=True))
                weights = jnp.exp2((scores - new_top) * scale)
                fade = jnp.exp2((top - new_top) * scale)
                total = total * fade + jnp.sum(weights, axis=0, keepdims=True)
                mix = mix * fade + jnp.dot(
                    values_t[:, span], weights.astype(jnp.bfloat16), preferred_element_type=jnp.float32)
                return new_top, total, mix

            carry = (jnp.full((1, 2 * BLOCK), big_negative, jnp.float32), jnp.zeros((1, 2 * BLOCK), jnp.float32),
                     jnp.zeros((HEAD_DIM, 2 * BLOCK), jnp.float32))
            carry = lax.fori_loop(0, pair.open_tiles, lambda tile, c: step(tile, c, False), carry)
            top, total, mix = lax.fori_loop(pair.open_tiles, pair.tiles, lambda tile, c: step(tile, c, True), carry)
            mix = jnp.where(pair.live, mix / total, 0.0)
            exact_ref[index] = mix
            pair.store_t(out_ref, mix)
            log_ref[index] = jnp.where(pair.live, top * scale + jnp.log2(total), -big_negative)

    return pl.pallas_call(
        kernel,
        out_shape=[
            jax.ShapeDtypeStruct(queries.shape, jnp.bfloat16),
            jax.ShapeDtypeStruct((pairs, HEAD_DIM, 2 * BLOCK), jnp.float32),
            jax.ShapeDtypeStruct((pairs, 1, 2 * BLOCK), jnp.float32),
        ],
        in_specs=[SMEM] * 2 + [VMEM] * 2,
        out_specs=[VMEM] * 3,
        scratch_shapes=[
            pltpu.SMEM((2 * pairs,), jnp.int32), pltpu.SMEM((2 * pairs,), jnp.int32),
            pltpu.VMEM((padded, HEAD_DIM), jnp.bfloat16), pltpu.VMEM((HEAD_DIM, padded), jnp.bfloat16),
        ],
        compiler_params=pltpu.CompilerParams(vmem_limit_bytes=56 * MIB),
        cost_estimate=pl.CostEstimate(flops=8 << 30, bytes_accessed=50 * MIB, transcendentals=8 << 20),
    )(lengths, slot, queries, shared)


def attend_back(queries, shared, upstream, exact, logs, lengths, order, slot, members, blocks_each):
    pairs, key_count = queries.shape[0] // (2 * BLOCK), shared.shape[1] // BLOCK
    width = KEY_BLOCKS * BLOCK
    padded = (key_count + KEY_BLOCKS - 1) * BLOCK
    scale = math.log2(math.e) / math.sqrt(HEAD_DIM)
    plain_scale = 1.0 / math.sqrt(HEAD_DIM)

    def kernel(lengths_ref, slot_ref, q_ref, shared_ref, g_ref, exact_ref, log_ref, dq_ref, dk_ref, dv_ref,
               index_list, place_list, keys, keys_t, values, key_sum, value_sum):
        list_queries(slot_ref, index_list, place_list, members, blocks_each)

        @pl.loop(0, key_count)
        def _(block):
            source, to = block_rows(slot_ref[block]), block_rows(block)
            rows = shared_ref[0, source]
            keys[to] = rows
            keys_t[:, to] = rows.T
            values[to] = shared_ref[1, source]
            key_sum[to] = jnp.zeros((BLOCK, HEAD_DIM), jnp.float32)
            value_sum[to] = jnp.zeros((BLOCK, HEAD_DIM), jnp.float32)

        tail = pl.ds(key_count * BLOCK, padded - key_count * BLOCK)
        keys[tail] = jnp.zeros((padded - key_count * BLOCK, HEAD_DIM), keys.dtype)
        values[tail] = jnp.zeros((padded - key_count * BLOCK, HEAD_DIM), keys.dtype)
        keys_t[:, tail] = jnp.zeros((HEAD_DIM, padded - key_count * BLOCK), keys.dtype)
        key_sum[tail] = jnp.zeros((padded - key_count * BLOCK, HEAD_DIM), jnp.float32)
        value_sum[tail] = jnp.zeros((padded - key_count * BLOCK, HEAD_DIM), jnp.float32)

        @pl.loop(0, pairs)
        def _(index):
            pair = QueryPair(index, lengths_ref, index_list, place_list)
            query, grad = pair.load(q_ref), pair.load(g_ref)
            query_t, grad_t = pair.load_t(q_ref), pair.load_t(g_ref)
            delta = jnp.sum(grad_t.astype(jnp.float32) * exact_ref[index], axis=0, keepdims=True)
            log_total = log_ref[index]

            def step(tile, query_grad, masked):
                span = pl.ds(pair.row(tile), width)
                scores = jnp.dot(keys[span], query_t, preferred_element_type=jnp.float32)
                probability = jnp.exp2(scores * scale - log_total)
                if masked:
                    probability = jnp.where(pair.allowed(tile), probability, 0.0)
                prob_grad = jnp.dot(values[span], grad_t, preferred_element_type=jnp.float32)
                score_grad = (probability * (prob_grad - delta)).astype(jnp.bfloat16)
                value_sum[span] += jnp.dot(
                    probability.astype(jnp.bfloat16), grad, preferred_element_type=jnp.float32)
                key_sum[span] += jnp.dot(score_grad, query, preferred_element_type=jnp.float32)
                return query_grad + jnp.dot(keys_t[:, span], score_grad, preferred_element_type=jnp.float32)

            query_grad = jnp.zeros((HEAD_DIM, 2 * BLOCK), jnp.float32)
            query_grad = lax.fori_loop(0, pair.open_tiles, lambda tile, c: step(tile, c, False), query_grad)
            query_grad = lax.fori_loop(pair.open_tiles, pair.tiles, lambda tile, c: step(tile, c, True), query_grad)
            pair.store_t(dq_ref, query_grad * plain_scale)

        @pl.loop(0, key_count)
        def _(block):
            at, dealt = block_rows(block), block_rows(slot_ref[block])
            dk_ref[dealt] = (key_sum[at] * plain_scale).astype(dk_ref.dtype)
            dv_ref[dealt] = value_sum[at].astype(dv_ref.dtype)

    return pl.pallas_call(
        kernel,
        out_shape=[
            jax.ShapeDtypeStruct(queries.shape, jnp.bfloat16),
            jax.ShapeDtypeStruct(shared.shape[1:], jnp.bfloat16),
            jax.ShapeDtypeStruct(shared.shape[1:], jnp.bfloat16),
        ],
        in_specs=[SMEM] * 2 + [VMEM] * 5,
        out_specs=[VMEM] * 3,
        scratch_shapes=[
            pltpu.SMEM((2 * pairs,), jnp.int32), pltpu.SMEM((2 * pairs,), jnp.int32),
            pltpu.VMEM((padded, HEAD_DIM), jnp.bfloat16),
            pltpu.VMEM((HEAD_DIM, padded), jnp.bfloat16),
            pltpu.VMEM((padded, HEAD_DIM), jnp.bfloat16),
            pltpu.VMEM((padded, HEAD_DIM), jnp.float32),
            pltpu.VMEM((padded, HEAD_DIM), jnp.float32),
        ],
        compiler_params=pltpu.CompilerParams(vmem_limit_bytes=60 * MIB),
        cost_estimate=pl.CostEstimate(flops=20 << 30, bytes_accessed=100 * MIB, transcendentals=8 << 20),
    )(lengths, slot, queries, shared, upstream, exact, logs)


def line_neighbours(mp, count):
    return ((1, mp + 1 < count, jnp.minimum(mp + 1, count - 1)), (-1, mp >= 1, jnp.maximum(mp - 1, 0)))


def greet_all(fixed, dp, mp, count):
    barrier = pltpu.get_barrier_semaphore()
    for peer in fixed:
        pl.semaphore_signal(barrier, inc=1, device_id=peer, device_id_type=MESH)
    expected = jnp.int32(len(fixed))
    for _, there, place in line_neighbours(mp, count):

        @pl.when(there)
        def _():
            pl.semaphore_signal(barrier, inc=1, device_id=(dp, place), device_id_type=MESH)

        expected = expected + there.astype(jnp.int32)
    pl.semaphore_wait(barrier, expected)


class LineGather:
    def __init__(self, own, full, rows, pieces, send_sem, recv_sem, dp, mp, count):
        self.own, self.full, self.rows, self.pieces = own, full, rows, pieces
        self.send_sem, self.recv_sem, self.dp, self.mp, self.count = send_sem, recv_sem, dp, mp, count
        self.size = rows // pieces

    def place(self, block, piece):
        return self.full.at[pl.ds(pl.multiple_of(block * self.rows + piece * self.size, self.size), self.size)]

    def hop(self, way, step, piece):
        sign, there, neighbour = line_neighbours(self.mp, self.count)[way]
        origin = self.mp - sign * step
        exists = (origin >= 0) & (origin < self.count)
        origin = jnp.clip(origin, 0, self.count - 1)
        if step == 0:
            source = self.own.at[pl.ds(pl.multiple_of(piece * self.size, self.size), self.size)]
        else:
            source = self.place(origin, piece)
        def copy():
            return remote(source, self.place(origin, piece), self.send_sem.at[way, step, piece],
                          self.recv_sem.at[way, step, piece], (self.dp, neighbour))

        return exists, exists & there, copy

    def advance(self, step, piece, also=True, ways=(0, 1)):
        for way in ways:
            if step:
                exists, _, _ = self.hop(way, step, piece)
                _, _, earlier = self.hop(way, step - 1, piece)

                @pl.when(exists & also)
                def _():
                    earlier().wait_recv()

            if step < self.count - 1:
                _, sends, copy = self.hop(way, step, piece)

                @pl.when(sends & also)
                def _():
                    copy().start()

    def finish(self):
        @pl.loop(0, self.pieces)
        def _(piece):
            for way in range(2):
                for step in range(self.count - 1):
                    _, sends, copy = self.hop(way, step, piece)

                    @pl.when(sends)
                    def _():
                        copy().wait_send()

    @staticmethod
    def semaphores(count, pieces):
        return [pltpu.SemaphoreType.DMA((2, count, pieces)), pltpu.SemaphoreType.DMA((2, count, pieces))]


class ShardGather:
    def __init__(self, shards, wholes, depth, cross_send, cross_recv, core_send, core_recv, own_sem, dp, mp, chips):
        self.shards, self.wholes, self.depth, self.own_sem = shards, wholes, depth, own_sem
        self.cross_send, self.cross_recv, self.core_send, self.core_recv = cross_send, cross_recv, core_send, core_recv
        self.dp, self.mp, self.chips = dp, mp, chips

    def place(self, array, owner):
        return self.wholes[array].at[pl.ds(pl.multiple_of(owner * self.depth, self.depth), self.depth)]

    def cross(self, array, o):
        return remote(self.shards[array], self.place(array, self.dp), self.cross_send.at[array, o],
                      self.cross_recv.at[array, o], (self.dp ^ (2 * o), self.mp))

    def core(self, array, o):
        owner = self.dp ^ (2 * o)
        source = self.place(array, owner) if o else self.shards[array]
        return remote(source, self.place(array, owner), self.core_send.at[array, o], self.core_recv.at[array, o],
                      (self.dp ^ 1, self.mp))

    def own(self, array):
        return pltpu.make_async_copy(self.shards[array], self.place(array, self.dp), self.own_sem.at[array])

    def begin(self):
        for array in range(len(self.shards)):
            for o in range(1, self.chips):
                self.cross(array, o).start()
        for array in range(len(self.shards)):
            self.own(array).start()
            self.core(array, 0).start()

    def spread(self, array):
        for o in range(1, self.chips):
            self.cross(array, o).wait_recv()
            self.core(array, o).start()

    def finish(self):
        for array in range(len(self.shards)):
            self.own(array).wait()
            for o in range(self.chips):
                self.core(array, o).wait()
                if o:
                    self.cross(array, o).wait_send()

    @staticmethod
    def semaphores(count, chips):
        return [pltpu.SemaphoreType.DMA((count, chips)) for _ in range(4)] + [pltpu.SemaphoreType.DMA((count,))]


class LineReduce:
    def __init__(self, part, flows, rows, pieces, send_sem, recv_sem, dp, mp, count):
        self.part, self.flows, self.rows, self.pieces = part, flows, rows, pieces
        self.send_sem, self.recv_sem, self.dp, self.mp, self.count = send_sem, recv_sem, dp, mp, count
        self.size = rows // pieces

    def span(self, block, piece):
        return pl.ds(pl.multiple_of(block * self.rows + piece * self.size, self.size), self.size)

    def hop(self, way, block, piece, first=False):
        neighbour = line_neighbours(self.mp, self.count)[way][2]
        span = self.span(block, piece)
        source = self.part.at[span] if first else self.flows.at[way, span]
        return remote(source, self.flows.at[way, span], self.send_sem.at[way, block, piece],
                      self.recv_sem.at[way, block, piece], (self.dp, neighbour))

    def roles(self, way, block):
        if way == 0:
            behind, ahead = self.mp >= 1, self.mp < block
        else:
            behind, ahead = self.mp < self.count - 1, self.mp > block
        return ahead & jnp.logical_not(behind), ahead & behind

    def targets(self):
        for index in range(self.count - 1):
            yield 0, self.count - 1 - index
            yield 1, index

    def begin(self, piece, also=True):
        for way, block in self.targets():
            begins, _ = self.roles(way, block)

            @pl.when(begins & also)
            def _():
                self.hop(way, block, piece, True).start()

    def advance(self, turn):
        for way, block in self.targets():
            _, hands_on = self.roles(way, block)
            passed = SKEW * (self.mp - 1 if way == 0 else self.count - 2 - self.mp)
            piece = jnp.clip(turn - passed, 0, self.pieces - 1)

            @pl.when(hands_on & (turn >= passed) & (turn - passed < self.pieces))
            def _():
                self.hop(way, block, piece).wait_recv()
                span = self.span(block, piece)
                value = self.flows[way, span].astype(jnp.float32) + self.part[span].astype(jnp.float32)
                self.flows[way, span] = value.astype(self.flows.dtype)
                self.hop(way, block, piece).start()

    def arrive(self, piece):
        for way in range(2):

            @pl.when(self.mp >= 1 if way == 0 else self.mp < self.count - 1)
            def _():
                self.hop(way, self.mp, piece).wait_recv()

    def total(self, piece, result):
        span = self.span(self.mp, piece)
        result[...] = self.part[span].astype(jnp.float32)
        for way in range(2):

            @pl.when(self.mp >= 1 if way == 0 else self.mp < self.count - 1)
            def _():
                result[...] += self.flows[way, span].astype(jnp.float32)

    def finish(self):
        @pl.loop(0, self.pieces)
        def _(piece):
            for way, block in self.targets():
                begins, hands_on = self.roles(way, block)

                @pl.when(begins)
                def _():
                    self.hop(way, block, piece, True).wait_send()

                @pl.when(hands_on)
                def _():
                    self.hop(way, block, piece).wait_send()

    @staticmethod
    def scratch(count, rows, width, pieces):
        return [pltpu.VMEM((2, count * rows, width), jnp.bfloat16),
                pltpu.SemaphoreType.DMA((2, count, pieces)), pltpu.SemaphoreType.DMA((2, count, pieces))]


AHEAD = 1
QUARTERS = 4
MAX_PIECES = 16
SKEW = 1


def pieces_of(rows):
    return min(MAX_PIECES, rows // 16)


def unit_rows(values):
    average = jnp.mean(values, axis=-1, keepdims=True)
    centred = values - average
    inverse = lax.rsqrt(jnp.mean(centred * centred, axis=-1, keepdims=True) + norm_epsilon)
    return centred * inverse, inverse


def project_first(
    hidden, output_grad, lengths, order, vectors, projections, out_weight, heads, members, collective_id
):
    rows, width = hidden.shape
    dp_count, mp_count = lax.axis_size("dp"), lax.axis_size("mp")
    chips, pieces, half = dp_count // 2, pieces_of(rows), rows // 2
    half_pieces = pieces_of(half)
    group_rows, depth, columns = mp_count * rows, projections[0].shape[0], projections[0].shape[1]
    each = width // dp_count // 128
    tall = [v.shape[0] // 128 for v in vectors]
    slab = sum(tall) + -sum(tall) % 8
    halves, kinds = heads // 2, 3
    arrays = kinds + 2
    offsets = sorted({2 * o for o in range(1, chips)} | {o for o in range(1, members)} | {o * members for o in range(1, heads)})

    def kernel(lengths_ref, order_ref, hidden_ref, upstream_ref, *refs):
        given, refs = refs[: len(vectors)], refs[len(vectors) :]
        weight_refs, out_weight_ref = refs[:kinds], refs[kinds]
        (normed_out, all_vectors, weights_out, all_out, shared, queries, branch, rest, live,
         half_rows) = refs[kinds + 1 : kinds + 11]
        parts, refs = refs[-len(vectors) :], refs[: -len(vectors)]
        (vector_ref, upstream, load_sem, raw, stage, gains, biases, line_send, line_recv, row_sem, own_sem, cross_send, cross_recv, core_send, core_recv,
         head_local, head_send, head_recv, pair_send, pair_recv, half_send, half_recv, half_sem,
         normed, weights, out_sem) = refs[kinds + 11 :]
        dp, mp = lax.axis_index("dp"), lax.axis_index("mp")
        loads = [pltpu.make_async_copy(given[k], parts[k], load_sem.at[k]) for k in range(len(vectors))]
        loads.append(pltpu.make_async_copy(upstream_ref, upstream, load_sem.at[len(vectors)]))
        for copy in loads:
            copy.start()
        vector_ref[...] = jnp.zeros_like(vector_ref)
        for copy in loads:
            copy.wait()
        first = 0
        for part, count in zip(parts, tall):
            for r in range(count):
                vector_ref[first + r] = part[r * 128 : (r + 1) * 128].astype(jnp.float32)
            first += count
        group, member = dp // members, dp % members
        partner = (dp ^ 1, mp)
        greet_all([(dp ^ o, mp) for o in offsets], dp, mp, mp_count)
        line = LineGather(hidden_ref, raw, rows, pieces, line_send, line_recv, dp, mp, mp_count)

        behind = LineGather(branch, half_rows, half, half_pieces, half_send, half_recv, dp, mp, mp_count)

        def follow(step):
            for way, steps in ((0, mp), (1, mp_count - 1 - mp)):

                @pl.loop(0, half_pieces)
                def _(piece):
                    behind.advance(0, piece, steps == step, (way,))

        between = (mp > 0) & (mp < mp_count - 1)

        def hand_half(step, also=True):
            @pl.loop(0, half_pieces)
            def _(piece):
                behind.advance(step, piece, also)

        def source(array):
            return (list(weight_refs) + [out_weight_ref, vector_ref])[array]

        def place(array, owner):
            if array < kinds:
                return weights.at[pl.ds(pl.multiple_of(owner * depth, depth), depth), pl.ds(array * columns, columns)]
            if array == kinds:
                return all_out.at[pl.ds(pl.multiple_of(owner * depth, depth), depth)]
            return all_vectors.at[pl.ds(pl.multiple_of(owner * slab, slab), slab)]

        def cross(array, o):
            return remote(source(array), place(array, dp), cross_send.at[array, o], cross_recv.at[array, o],
                          (dp ^ (2 * o), mp))

        def core(array, o):
            owner = dp ^ (2 * o)
            return remote(place(array, owner) if o else source(array), place(array, owner),
                          core_send.at[array, o], core_recv.at[array, o], partner)

        def own(array):
            return pltpu.make_async_copy(source(array), place(array, dp), own_sem.at[array])

        def block_span(block):
            return pl.ds(pl.multiple_of(block * rows, rows), rows)

        first_to_last = [kinds + 1] + list(range(kinds + 1))
        for array in first_to_last:
            for o in range(1, chips):
                cross(array, o).start()
            if array == first_to_last[0]:

                @pl.loop(0, pieces)
                def _(piece):
                    line.advance(0, piece)

        for block in range(rows // BLOCK):
            found = order_ref[(dp * group_rows + mp * rows) // BLOCK + block]
            valid = sequence_of(found, lengths_ref)[1]
            span = slice(block * BLOCK, (block + 1) * BLOCK)
            live[span] = (lax.broadcasted_iota(jnp.int32, (BLOCK, 128), 0) < valid).astype(jnp.float32)
            keep = lax.broadcasted_iota(jnp.int32, (BLOCK, width), 0) < valid
            branch[span] = jnp.where(keep, upstream[span].astype(jnp.float32), 0.0).astype(branch.dtype)
        rest[...] = branch[half:]
        own_half = pltpu.make_async_copy(
            branch.at[pl.ds(0, half)], half_rows.at[pl.ds(pl.multiple_of(mp * half, half), half)], half_sem)
        own_half.start()
        follow(0)
        own_rows = pltpu.make_async_copy(hidden_ref, raw.at[block_span(mp)], row_sem)
        own_rows.start()
        for array in first_to_last:
            own(array).start()
            core(array, 0).start()

        def spread(array):
            for o in range(1, chips):
                cross(array, o).wait_recv()
                core(array, o).start()

        def settle(array):
            own(array).wait()
            for o in range(chips):
                core(array, o).wait_recv()

        def norm(block):
            chunk = 64

            @pl.loop(0, rows // chunk)
            def _(part):
                span = pl.ds(pl.multiple_of(block * rows + part * chunk, chunk), chunk)
                unit, _ = unit_rows(raw[span].astype(jnp.float32))
                normed[span] = (unit * gains[0:1] + gains[1:2]).astype(normed.dtype)

            normed_copy(block).start()

        def normed_copy(block):
            return pltpu.make_async_copy(
                normed.at[block_span(block)], normed_out.at[block_span(block)], out_sem.at[block])

        weights_copy = pltpu.make_async_copy(weights, weights_out, out_sem.at[mp_count])

        def each_block(low, high, visit):
            @pl.loop(0, mp_count)
            def _(block):
                distance = jnp.abs(block - mp)

                @pl.when((distance >= low) & (distance <= high))
                def _():
                    visit(block)

        def rows_of(kind_ref, owner, block):
            return kind_ref.at[pl.ds(pl.multiple_of(owner * group_rows + block * rows, rows), rows)]

        def pass_on(kind, o, block, piece):
            giver = (group ^ o) * members + member
            return [remote(piece, rows_of(shared.at[kind], giver, block), pair_send.at[kind, o, block, p - 1],
                           pair_recv.at[kind, o, block, p - 1], (group * members + (member ^ p), mp))
                    for p in range(1, members)]

        def head_copy(kind, o, block, to_shared):
            target = group ^ o
            piece = stage.at[kind, block, target]
            landing = rows_of(shared.at[kind], dp, block) if to_shared else rows_of(queries, group, block)
            return remote(piece, landing, head_send.at[kind, o, block], head_recv.at[kind, o, block],
                          (target * members + member, mp))

        def local_copy(kind, block, to_shared):
            landing = rows_of(shared.at[kind], dp, block) if to_shared else rows_of(queries, group, block)
            return pltpu.make_async_copy(stage.at[kind, block, group], landing, head_local.at[kind, block])

        def project(tile, block):
            kind, half = tile // halves, tile % halves
            span = pl.ds(pl.multiple_of(half * 256, 256), 256)
            across = pl.ds(pl.multiple_of(kind * columns + half * 256, 256), 256)
            value = jnp.dot(normed[block_span(block)], weights[:, across], preferred_element_type=jnp.float32)
            value = (value + biases[pl.ds(kind, 1), span]).astype(stage.dtype)
            for h in range(2):
                head = 2 * half + h
                stage[kind, block, head] = value[:, h * HEAD_DIM : (h + 1) * HEAD_DIM]
            for h in range(2):
                o = (2 * half + h) ^ group
                for to_shared in (True, False):
                    chosen = (kind < 2) if to_shared else (kind == 2)

                    @pl.when(chosen & (o != 0))
                    def _():
                        head_copy(kind, o, block, to_shared).start()

                    @pl.when(chosen & (o == 0))
                    def _():
                        local_copy(kind, block, to_shared).start()
                        if to_shared:
                            for copy in pass_on(kind, 0, block, stage.at[kind, block, group]):
                                copy.start()

        def hand_on(block):
            @pl.loop(0, 2)
            def _(kind):
                for o in range(1, heads):
                    head_copy(kind, o, block, True).wait_recv()
                    giver = (group ^ o) * members + member
                    for copy in pass_on(kind, o, block, rows_of(shared.at[kind], giver, block)):
                        copy.start()

        last = mp_count - 1
        for step in range(1, last):

            @pl.loop(0, pieces)
            def _(piece):
                line.advance(step, piece)

            follow(step)
            if step == 1:
                spread(kinds + 1)
                settle(kinds + 1)
                for owner in range(dp_count):
                    for r in range(each):
                        at = pl.ds((owner * each + r) * 128, 128)
                        for k in range(2):
                            gains[k : k + 1, at] = all_vectors[owner * slab + k * each + r : owner * slab + k * each + r + 1]
                biases[...] = jnp.zeros_like(biases)
                for head in range(heads):
                    feature = mp * heads + head
                    first = (feature // each) * slab + feature % each
                    for kind, k in ((1, 3), (2, 2)):
                        biases[kind : kind + 1, head * 128 : (head + 1) * 128] = all_vectors[pl.ds(first + k * each, 1)]
                own_rows.wait()
                each_block(0, 1, norm)
            else:
                each_block(step, step, norm)
        for array in range(kinds + 1):
            spread(array)
        for array in range(kinds):
            settle(array)
        weights_copy.start()
        tiles = kinds * halves

        @pl.loop(0, pieces)
        def _(piece):
            line.advance(last - 1 if last == 1 else last, piece)

            @pl.when(piece >= pieces - half_pieces)
            def _():
                behind.advance(1, piece - (pieces - half_pieces), between)

            @pl.when(piece < tiles)
            def _():
                each_block(0, last - 1, lambda block: project(piece, block))

        for step in range(2, last):
            hand_half(step, between)
        each_block(last, last, norm)

        @pl.loop(0, tiles)
        def _(tile):
            each_block(last, last, lambda block: project(tile, block))

        each_block(0, last - 1, hand_on)
        each_block(last, last, hand_on)
        for step in range(1, last):
            hand_half(step, jnp.logical_not(between))
        hand_half(last)
        line.finish()
        weights_copy.wait()
        for block in range(mp_count):
            normed_copy(block).wait()
        behind.finish()
        own_half.wait()
        settle(kinds)
        for array in first_to_last:
            for o in range(chips):
                core(array, o).wait_send()
                if o:
                    cross(array, o).wait_send()

        @pl.loop(0, mp_count)
        def _(block):
            for kind in range(kinds):
                to_shared = kind < 2
                local_copy(kind, block, to_shared).wait()
                for o in range(1, heads):
                    head_copy(kind, o, block, to_shared).wait_send()
                    if not to_shared:
                        head_copy(kind, o, block, to_shared).wait_recv()
                if to_shared:
                    for o in range(heads):
                        giver = (group ^ o) * members + member
                        for copy in pass_on(kind, o, block, rows_of(shared.at[kind], giver, block)):
                            copy.wait()

    dma = pltpu.SemaphoreType.DMA
    bf16, f32 = jnp.bfloat16, jnp.float32
    return pl.pallas_call(
        kernel,
        out_shape=[
            jax.ShapeDtypeStruct((group_rows, width), bf16),
            jax.ShapeDtypeStruct((dp_count * slab, 128), f32),
            jax.ShapeDtypeStruct((width, kinds * columns), bf16),
            jax.ShapeDtypeStruct((width, columns), bf16),
            jax.ShapeDtypeStruct((2, dp_count * group_rows, HEAD_DIM), bf16),
            jax.ShapeDtypeStruct((heads * group_rows, HEAD_DIM), bf16),
            jax.ShapeDtypeStruct((rows, width), bf16),
            jax.ShapeDtypeStruct((rows - half, width), bf16),
            jax.ShapeDtypeStruct((rows, 128), f32),
            jax.ShapeDtypeStruct((mp_count * half, width), bf16),
        ],
        in_specs=[SMEM, SMEM] + [ANY] * (len(vectors) + kinds + 3),
        out_specs=[ANY, VMEM, ANY, ANY, ANY, ANY, VMEM, VMEM, VMEM, ANY],
        scratch_shapes=[
            pltpu.VMEM((slab, 128), f32),
            pltpu.VMEM((rows, width), bf16),
            dma((len(vectors) + 1,)),
            pltpu.VMEM((group_rows, width), bf16),
            pltpu.VMEM((kinds, mp_count, heads, rows, HEAD_DIM), bf16),
            pltpu.VMEM((8, width), f32),
            pltpu.VMEM((8, columns), f32),
        ]
        + LineGather.semaphores(mp_count, pieces)
        + [dma(()), dma((arrays,))]
        + [dma((arrays, chips)) for _ in range(4)]
        + [dma((kinds, mp_count)), dma((kinds, heads, mp_count)), dma((kinds, heads, mp_count))]
        + [dma((2, heads, mp_count, members)) for _ in range(2)]
        + LineGather.semaphores(mp_count, half_pieces) + [dma(())]
        + [pltpu.VMEM((group_rows, width), bf16), pltpu.VMEM((width, kinds * columns), bf16), dma((mp_count + 1,))]
        + [pltpu.VMEM(v.shape, v.dtype) for v in vectors],
        compiler_params=pltpu.CompilerParams(
            collective_id=collective_id, has_side_effects=True, vmem_limit_bytes=63 * MIB),
        cost_estimate=pl.CostEstimate(flops=8 << 30, bytes_accessed=250 * MIB, transcendentals=0),
    )(lengths, order, hidden, output_grad, *vectors, *projections, out_weight)


def mix_norm_gather(mixed, out_weight, hidden, out_bias, gain, shift, shards, heads, members, collective_id):
    dp_count, mp_count = lax.axis_size("dp"), lax.axis_size("mp")
    chips, count = dp_count // 2, len(shards)
    rows, width = hidden.shape
    pieces = pieces_of(rows)
    size, columns, group_rows = rows // pieces, heads * HEAD_DIM, mp_count * rows
    quarter, per_quarter = rows // QUARTERS, pieces // QUARTERS
    slice_rows = width // per_quarter
    offsets = sorted({2 * o for o in range(1, chips)} | {1} | {o * members for o in range(1, heads)})
    mixed = mixed.reshape(heads, mp_count, rows, HEAD_DIM)
    turns = pieces + 2 * SKEW * (mp_count - 1)

    def kernel(mixed_ref, out_hbm, hidden_ref, bias_ref, gain_ref, shift_ref, *refs):
        shard_refs, (residual_ref, landed, full_ref), refs = refs[:count], refs[count : count + 3], refs[count + 3 :]
        whole_refs, refs = refs[:count], refs[count:]
        (part, out_rows, load_sem, local_sem, head_send, head_recv,
         total, normed, flows, red_send, red_recv, line_send, line_recv, own_sem, *weight_sems) = refs
        dp, mp = lax.axis_index("dp"), lax.axis_index("mp")
        group, member = dp // members, dp % members
        greet_all([(dp ^ o, mp) for o in offsets], dp, mp, mp_count)

        def landing(k, head):
            return landed.at[:, pl.ds(k * quarter, quarter), lanes(head)]

        def head_copy(o, k):
            return remote(mixed_ref.at[group ^ o, :, pl.ds(k * quarter, quarter)], landing(k, group),
                          head_send.at[o, k], head_recv.at[o, k], ((group ^ o) * members + member, mp))

        def local_copy(k):
            return pltpu.make_async_copy(mixed_ref.at[group, :, pl.ds(k * quarter, quarter)], landing(k, group),
                                         local_sem.at[k])

        def arrived(k):
            for o in range(1, heads):
                head_copy(o, k).wait_recv()
            local_copy(k).wait()

        def project(k, first, count):
            span = pl.ds(pl.multiple_of(k * quarter, quarter), quarter)
            left = landed[:, span].reshape(mp_count * quarter, columns)
            features = pl.ds(pl.multiple_of(first, count), count)
            value = contract_last(left, out_rows[features]).astype(part.dtype)
            for block in range(mp_count):
                at = pl.ds(pl.multiple_of(block * rows + k * quarter, quarter), quarter)
                part[at, features] = value[block * quarter : (block + 1) * quarter]

        load = pltpu.make_async_copy(out_hbm, out_rows, load_sem)
        load.start()
        for k in range(QUARTERS):
            for o in range(1, heads):
                head_copy(o, k).start()
            local_copy(k).start()
        weights = ShardGather(shard_refs, whole_refs, shards[0].shape[0], *weight_sems, dp, mp, chips)
        weights.begin()
        reduce = LineReduce(part, flows, rows, pieces, red_send, red_recv, dp, mp, mp_count)
        gather = LineGather(normed, full_ref, rows, pieces, line_send, line_recv, dp, mp, mp_count)
        load.wait()
        arrived(0)
        for portion in range(per_quarter):
            project(0, portion * slice_rows, slice_rows)
        for piece in range(AHEAD):
            reduce.begin(piece)

        @pl.loop(0, turns)
        def _(turn):
            for array in range(count):

                @pl.when(turn == turns - 1 - 6 * (count - 1 - array))
                def _():
                    weights.spread(array)

            for k in range(1, QUARTERS):

                @pl.when(turn == (k - 1) * per_quarter)
                def _():
                    arrived(k)

            @pl.when(turn < (QUARTERS - 1) * per_quarter)
            def _():
                project(turn // per_quarter + 1, (turn % per_quarter) * slice_rows, slice_rows)

            reduce.begin(jnp.minimum(turn + AHEAD, pieces - 1), turn + AHEAD < pieces)
            reduce.advance(turn)
            done = turn - SKEW * (mp_count - 1)

            @pl.when((done >= 0) & (done < pieces))
            def _():
                reduce.arrive(done)
                reduce.total(done, total)
                span = pl.ds(pl.multiple_of(done * size, size), size)
                residual = hidden_ref[span].astype(jnp.float32) + total[...] + bias_ref[...]
                residual_ref[span] = residual
                unit, _ = unit_rows(residual)
                normed[span] = (unit * gain_ref[...] + shift_ref[...]).astype(normed.dtype)
                gather.advance(0, done)

            for step in range(1, mp_count):
                late = done - SKEW * step
                gather.advance(step, jnp.clip(late, 0, pieces - 1), (late >= 0) & (late < pieces))

        own = pltpu.make_async_copy(normed, full_ref.at[pl.ds(pl.multiple_of(mp * rows, rows), rows)], own_sem)
        own.start()
        reduce.finish()
        gather.finish()
        own.wait()
        weights.finish()
        for k in range(QUARTERS):
            for o in range(1, heads):
                head_copy(o, k).wait_send()

    dma = pltpu.SemaphoreType.DMA
    return pl.pallas_call(
        kernel,
        out_shape=[
            jax.ShapeDtypeStruct((rows, width), jnp.float32),
            jax.ShapeDtypeStruct((mp_count, rows, columns), jnp.bfloat16),
            jax.ShapeDtypeStruct((group_rows, width), jnp.bfloat16),
        ]
        + [jax.ShapeDtypeStruct((dp_count * a.shape[0], a.shape[1]), a.dtype) for a in shards],
        in_specs=[ANY] * 2 + [VMEM] * 4 + [ANY] * count,
        out_specs=[VMEM, VMEM, ANY] + [ANY] * count,
        scratch_shapes=[
            pltpu.VMEM((group_rows, width), jnp.bfloat16), pltpu.VMEM((width, columns), jnp.bfloat16),
            dma(()), dma((QUARTERS,)), dma((heads, QUARTERS)), dma((heads, QUARTERS)),
        ]
        + [pltpu.VMEM((size, width), jnp.float32), pltpu.VMEM((rows, width), jnp.bfloat16)]
        + LineReduce.scratch(mp_count, rows, width, pieces) + LineGather.semaphores(mp_count, pieces)
        + [pltpu.SemaphoreType.DMA(())] + ShardGather.semaphores(count, chips),
        compiler_params=pltpu.CompilerParams(
            collective_id=collective_id, has_side_effects=True, vmem_limit_bytes=63 * MIB),
        cost_estimate=pl.CostEstimate(flops=0, bytes_accessed=300 * MIB, transcendentals=0),
    )(mixed, out_weight, hidden, out_bias, gain, shift, *shards)


def reduce_back_gather(
    part, residual, branch_two, gain, halves, pairs, down_weight, out_weight, heads, members, collective_id
):
    dp_count, mp_count = lax.axis_size("dp"), lax.axis_size("mp")
    chips, count = dp_count // 2, len(pairs)
    rows, width = residual.shape
    half = rows // 2
    pieces = pieces_of(rows)
    size, depth = rows // pieces, width // dp_count
    units = pairs[0][1].shape[1]
    turns = pieces + 2 * SKEW * (mp_count - 1)
    each = dp_count // 4
    busy = count * dp_count // each
    feed_slices = 8
    feed_rows = width // feed_slices
    assert 1 + busy + feed_slices <= turns
    quarter, per_quarter, columns = rows // QUARTERS, pieces // QUARTERS, heads * HEAD_DIM
    group_rows = mp_count * rows
    offsets = sorted({2 * o for o in range(1, chips)} | {1} | {o * members for o in range(1, heads)})

    def kernel(part_ref, residual_ref, branch_ref, gain_ref, *refs):
        operands, down_ref, out_hbm, refs = refs[: 2 * count + 1], refs[2 * count + 1], refs[2 * count + 2], refs[2 * count + 3 :]
        (grad_ref, sums_ref, full_ref, feed_ref, heads_ref), terms, refs = refs[:5], refs[5 : 5 + count], refs[5 + count :]
        loaded, refs = refs[: 2 * count], refs[2 * count :]
        (credit, down_rows, down_sem, fed, fed_sem, out_rows, out_sem, gathered, gathered_sem, stage,
         stage_sem, head_send, head_recv, half_sem, total, low, kept, slices, from_partner, chip_sum, load_sem, keep_sem, pair_send, pair_recv, cross_send, cross_recv,
         flows, red_send, red_recv, line_send, line_recv, own_sem) = refs
        dp, mp = lax.axis_index("dp"), lax.axis_index("mp")
        partner = (dp ^ 1, mp)
        group, member = dp // members, dp % members
        greet_all([(dp ^ o, mp) for o in offsets], dp, mp, mp_count)
        reduce = LineReduce(part_ref, flows, rows, pieces, red_send, red_recv, dp, mp, mp_count)
        gather = LineGather(low, full_ref, rows, pieces, line_send, line_recv, dp, mp, mp_count)
        for piece in range(AHEAD):
            reduce.begin(piece)
        loads = [[] for _ in range(count)]
        for h in range(2):
            for b in range(mp_count):
                to = pl.ds(b * rows + h * half, half)
                loads[0].append(pltpu.make_async_copy(
                    operands[h].at[pl.ds(b * half, half)], loaded[0].at[to], half_sem.at[h, b]))
        for index in range(1, 2 * count):
            loads[index // 2].append(pltpu.make_async_copy(operands[index + 1], loaded[index], load_sem.at[index]))
        for copy in loads[0] + loads[1]:
            copy.start()
        sums_ref[...] = jnp.zeros_like(sums_ref)

        def pair(mat, o):
            return remote(slices.at[o], from_partner.at[o], pair_send.at[mat, o], pair_recv.at[mat, o], partner)

        def cross(mat, o, peer):
            return remote(chip_sum.at[mat, o - 1], terms[mat].at[o], cross_send.at[mat, o], cross_recv.at[mat, o],
                          (peer, mp))

        def weight_slice(mat, index):
            o = (index + 1) % chips
            mine = index >= chips
            owner = dp ^ (2 * o) ^ jnp.where(mine, 0, 1)
            left = loaded[2 * mat][:, pl.ds(pl.multiple_of(owner * depth, depth), depth)]
            value = contract_first(left, loaded[2 * mat + 1][...])

            @pl.when(jnp.logical_not(mine))
            def _():
                if mat:
                    pair(mat - 1, o).wait_send()
                    pl.semaphore_wait(credit, 1)
                slices[o] = value.astype(slices.dtype)
                pair(mat, o).start()

            @pl.when(mine)
            def _():
                pair(mat, o).wait_recv()
                both = (value + from_partner[o].astype(jnp.float32)).astype(slices.dtype)
                if mat < count - 1:
                    pl.semaphore_signal(credit, inc=1, device_id=partner, device_id_type=MESH)

                @pl.when(o == 0)
                def _():
                    kept[mat] = both
                    pltpu.make_async_copy(kept.at[mat], terms[mat].at[0], keep_sem.at[mat]).start()

                @pl.when(o != 0)
                def _():
                    chip_sum[mat, o - 1] = both
                    cross(mat, o, owner).start()

        def down_load(index):
            at = pl.ds(pl.multiple_of(index * feed_rows, feed_rows), feed_rows)
            return pltpu.make_async_copy(down_ref.at[at], down_rows.at[index % 2], down_sem.at[index % 2])

        def feed_store(index):
            at = pl.ds(pl.multiple_of(index * feed_rows, feed_rows), feed_rows)
            return pltpu.make_async_copy(fed.at[index % 2], feed_ref.at[:, at], fed_sem.at[index % 2])

        def feed_slice(index):
            down_load(index).wait()

            @pl.when(index + 1 < feed_slices)
            def _():
                down_load(index + 1).start()

            @pl.when(index >= 2)
            def _():
                feed_store(index - 2).wait()

            fed[index % 2] = contract_last(loaded[1][...], down_rows[index % 2]).astype(fed.dtype)
            feed_store(index).start()

        def rows_load(k, block, own):
            source = low.at[pl.ds(k * quarter, quarter)] if own else full_ref.at[
                pl.ds(pl.multiple_of(block * rows + k * quarter, quarter), quarter)]
            return pltpu.make_async_copy(source, gathered.at[block], gathered_sem.at[block])

        def head_copy(o, k):
            span = pl.ds(k * quarter, quarter)
            return remote(stage.at[:, span, lanes(group ^ o)], heads_ref.at[group, :, span], head_send.at[o, k],
                          head_recv.at[o, k], ((group ^ o) * members + member, mp))

        def local_copy(k):
            span = pl.ds(k * quarter, quarter)
            return pltpu.make_async_copy(stage.at[:, span, lanes(group)], heads_ref.at[group, :, span], stage_sem.at[k])

        def to_heads(k):
            for block in range(mp_count):
                for own in (True, False):

                    @pl.when((mp == block) if own else (mp != block))
                    def _():
                        rows_load(k, block, own).start()

            for block in range(mp_count):
                for own in (True, False):

                    @pl.when((mp == block) if own else (mp != block))
                    def _():
                        rows_load(k, block, own).wait()

            value = jnp.dot(gathered[...].reshape(mp_count * quarter, width), out_rows[...],
                            preferred_element_type=jnp.float32)
            stage[:, k * quarter : (k + 1) * quarter] = value.reshape(mp_count, quarter, columns).astype(stage.dtype)
            for o in range(1, heads):
                head_copy(o, k).start()
            local_copy(k).start()

        out_load = pltpu.make_async_copy(out_hbm, out_rows, out_sem)
        out_load.start()
        down_load(0).start()

        @pl.loop(0, turns)
        def _(turn):
            reduce.begin(jnp.minimum(turn + AHEAD, pieces - 1), turn + AHEAD < pieces)
            reduce.advance(turn)
            done = turn - SKEW * (mp_count - 1)

            @pl.when((done >= 0) & (done < pieces))
            def _():
                reduce.arrive(done)
                reduce.total(done, total)
                span = pl.ds(pl.multiple_of(done * size, size), size)
                unit, inverse = unit_rows(residual_ref[span])
                upstream = total[...]
                sums_ref[0:1] += jnp.sum(upstream * unit, axis=0, keepdims=True)
                sums_ref[1:2] += jnp.sum(upstream, axis=0, keepdims=True)
                grad = branch_ref[span].astype(jnp.float32) + norm_back(upstream, unit, inverse, gain_ref[...])
                grad_ref[span] = grad
                rounded = grad.astype(low.dtype)
                low[span] = rounded
                sums_ref[2:3] += jnp.sum(rounded.astype(jnp.float32), axis=0, keepdims=True)
                gather.advance(0, done)

            for step in range(1, mp_count):
                late = done - SKEW * step
                gather.advance(step, jnp.clip(late, 0, pieces - 1), (late >= 0) & (late < pieces))
            for mat in range(count):

                @pl.when(turn == 1 + mat * busy // count)
                def _():
                    for copy in loads[mat]:
                        copy.wait()

                first = turn - 1 - mat * busy // count

                @pl.when((first >= 0) & (first < busy // count))
                def _():
                    for i in range(each):
                        weight_slice(mat, first * each + i)

            @pl.when((turn >= 1 + busy) & (turn < 1 + busy + feed_slices))
            def _():
                feed_slice(turn - 1 - busy)

            for k in range(QUARTERS):

                @pl.when(turn == (k + 1) * per_quarter - 1 + 2 * SKEW * (mp_count - 1))
                def _():
                    if k == 0:
                        out_load.wait()
                    to_heads(k)

        own = pltpu.make_async_copy(low, full_ref.at[pl.ds(pl.multiple_of(mp * rows, rows), rows)], own_sem)
        own.start()
        reduce.finish()
        gather.finish()
        own.wait()
        for index in range(feed_slices - 2, feed_slices):
            feed_store(index).wait()
        for k in range(QUARTERS):
            local_copy(k).wait()
            for o in range(1, heads):
                head_copy(o, k).wait()
        for mat in range(count):
            pltpu.make_async_copy(kept.at[mat], terms[mat].at[0], keep_sem.at[mat]).wait()
            for o in range(chips):
                if mat == count - 1:
                    pair(mat, o).wait_send()
                if o:
                    cross(mat, o, dp ^ (2 * o)).wait()

    bf16, f32 = jnp.bfloat16, jnp.float32
    dma = pltpu.SemaphoreType.DMA
    flat = [array for two in pairs for array in two][1:]
    return pl.pallas_call(
        kernel,
        out_shape=[
            jax.ShapeDtypeStruct((rows, width), f32),
            jax.ShapeDtypeStruct((8, width), f32),
            jax.ShapeDtypeStruct((group_rows, width), bf16),
            jax.ShapeDtypeStruct((group_rows, width), bf16),
            jax.ShapeDtypeStruct((heads, mp_count, rows, HEAD_DIM), bf16),
        ]
        + [jax.ShapeDtypeStruct((chips, depth, units), bf16)] * count,
        in_specs=[VMEM] * 4 + [ANY] * (2 * count + 3),
        out_specs=[VMEM, VMEM] + [ANY] * (3 + count),
        scratch_shapes=[pltpu.VMEM((mp_count * rows, width), bf16)] + [pltpu.VMEM(a.shape, a.dtype) for a in flat]
        + [
            pltpu.SemaphoreType.REGULAR,
            pltpu.VMEM((2, feed_rows, units), bf16), dma((2,)),
            pltpu.VMEM((2, group_rows, feed_rows), bf16), dma((2,)),
            pltpu.VMEM((width, columns), bf16), dma(()),
            pltpu.VMEM((mp_count, quarter, width), bf16), dma((mp_count,)),
            pltpu.VMEM((mp_count, rows, columns), bf16), dma((QUARTERS,)),
            dma((heads, QUARTERS)), dma((heads, QUARTERS)),
            dma((2, mp_count)),
            pltpu.VMEM((size, width), f32),
            pltpu.VMEM((rows, width), bf16),
            pltpu.VMEM((count, depth, units), bf16),
            pltpu.VMEM((chips, depth, units), bf16),
            pltpu.VMEM((chips, depth, units), bf16),
            pltpu.VMEM((count, chips - 1, depth, units), bf16),
            dma((2 * count,)), dma((count,)),
        ]
        + [dma((count, chips)) for _ in range(4)]
        + LineReduce.scratch(mp_count, rows, width, pieces) + LineGather.semaphores(mp_count, pieces)
        + [dma(())],
        compiler_params=pltpu.CompilerParams(
            collective_id=collective_id, has_side_effects=True, vmem_limit_bytes=63 * MIB),
        cost_estimate=pl.CostEstimate(flops=40 << 30, bytes_accessed=300 * MIB, transcendentals=0),
    )(part, residual, branch_two, gain, *halves, *flat, down_weight, out_weight)


def finish_back(query_grad, key_part, value_part, weights, normed, residual_grad, hidden, gain, out_part, vectors, heads, members,
                collective_id):
    rows, width = hidden.shape
    dp_count, mp_count = lax.axis_size("dp"), lax.axis_size("mp")
    chips, pieces = dp_count // 2, pieces_of(rows)
    size, depth, columns = rows // pieces, width // dp_count, heads * HEAD_DIM
    kinds, quarter = 3, rows // QUARTERS
    per_quarter = pieces // QUARTERS
    slice_rows = width // per_quarter
    turns = pieces + SKEW * (mp_count - 1)
    slices_each = max(dp_count // 4, 1)
    group_rows = mp_count * rows
    slab, each = vectors.shape[1], width // dp_count // 128
    query_grad = query_grad.reshape(heads, mp_count, rows, HEAD_DIM)
    shared = [v.reshape(dp_count, mp_count, rows, HEAD_DIM) for v in (key_part, value_part)]

    def kernel(query_ref, key_ref, value_ref, weights_hbm, normed_hbm, residual_ref, hidden_ref, gain_ref, out_ref, vector_ref,
               grad_ref, weight_grad_ref, out_grad_ref, summed_ref,
               weights, normed, landed, own, parts, stage, part, total, flows, red_send, red_recv,
               slices, from_partner, chip_sum, from_chips, out_partner, out_sum, out_chips,
               load_sem, own_sem, part_send, part_recv, local_sem, head_send, head_recv,
               pair_send, pair_recv, cross_send, cross_recv,
               sums_ref, column_ref, packed, vector_parts, line_parts, vec_send, vec_recv, line_send, line_recv):
        dp, mp = lax.axis_index("dp"), lax.axis_index("mp")
        group, member = dp // members, dp % members
        partner = (dp ^ 1, mp)
        greet_all([(dp ^ o, mp) for o in range(1, dp_count)] + [(dp, mp ^ o) for o in range(1, mp_count)], dp, mp, mp_count)
        reduce = LineReduce(part, flows, rows, pieces, red_send, red_recv, dp, mp, mp_count)
        loads = [pltpu.make_async_copy(weights_hbm, weights, load_sem.at[0]),
                 pltpu.make_async_copy(normed_hbm, normed, load_sem.at[1])]
        shared_refs = (key_ref, value_ref)

        def rows_of(k):
            return pl.ds(k * quarter, quarter)

        def lane_span(kind, head):
            return pl.ds(pl.multiple_of(kind * columns + head * HEAD_DIM, HEAD_DIM), HEAD_DIM)

        def landing(kind, k, head):
            return landed.at[:, rows_of(k), lane_span(kind, head)]

        def own_copy(kind, o):
            return pltpu.make_async_copy(shared_refs[kind].at[(group ^ o) * members + member], own.at[kind, o],
                                         own_sem.at[kind, o])

        def part_copy(kind, o, p, k):
            return remote(shared_refs[kind].at[(group ^ o) * members + (member ^ p), :, rows_of(k)],
                          parts.at[kind, o, p - 1, :, rows_of(k)], part_send.at[kind, o, p - 1, k],
                          part_recv.at[kind, o, p - 1, k], (group * members + (member ^ p), mp))

        def head_copy(kind, o, k):
            source = query_ref.at[group ^ o, :, rows_of(k)] if kind == 2 else stage.at[kind, o, :, rows_of(k)]
            return remote(source, landing(kind, k, group), head_send.at[kind, o, k], head_recv.at[kind, o, k],
                          ((group ^ o) * members + member, mp))

        def local_copy(k):
            return pltpu.make_async_copy(query_ref.at[group, :, rows_of(k)], landing(2, k, group), local_sem.at[k])

        for k in range(QUARTERS):
            for kind in range(2):
                for o in range(heads):
                    for p in range(1, members):
                        part_copy(kind, o, p, k).start()
            if k == 0:
                for kind in range(2):
                    for o in range(heads):
                        own_copy(kind, o).start()
                for copy in loads:
                    copy.start()
            for o in range(1, heads):
                head_copy(2, o, k).start()
            local_copy(k).start()
        for k in range(QUARTERS):
            for kind in range(2):
                for o in list(range(1, heads)) + [0]:
                    if k == 0:
                        own_copy(kind, o).wait()
                    value = own[kind, o, :, k * quarter : (k + 1) * quarter].astype(jnp.float32)
                    for p in range(1, members):
                        part_copy(kind, o, p, k).wait_recv()
                        value = value + parts[kind, o, p - 1, :, k * quarter : (k + 1) * quarter].astype(jnp.float32)
                    if o:
                        stage[kind, o, :, k * quarter : (k + 1) * quarter] = value.astype(stage.dtype)
                        head_copy(kind, o, k).start()
                    else:
                        landed[:, k * quarter : (k + 1) * quarter, lane_span(kind, group)] = value.astype(landed.dtype)

        def arrived(k):
            for kind in range(kinds):
                for o in range(1, heads):
                    head_copy(kind, o, k).wait_recv()
            local_copy(k).wait()

        def project(k, first, count):
            span = pl.ds(pl.multiple_of(k * quarter, quarter), quarter)
            left = landed[:, span].reshape(mp_count * quarter, kinds * columns)
            features = pl.ds(pl.multiple_of(first, count), count)
            value = contract_last(left, weights[features]).astype(part.dtype)
            for block in range(mp_count):
                at = pl.ds(pl.multiple_of(block * rows + k * quarter, quarter), quarter)
                part[at, features] = value[block * quarter : (block + 1) * quarter]

        def slab(owner):
            return pl.ds(pl.multiple_of(owner * depth, depth), depth)

        def pair(o):
            return remote(slices.at[o], from_partner.at[o], pair_send.at[0, o], pair_recv.at[0, o], partner)

        def cross(o, peer):
            return remote(chip_sum.at[o], from_chips.at[o], cross_send.at[0, o], cross_recv.at[0, o], (peer, mp))

        def out_pair(o):
            return remote(out_ref.at[slab(dp ^ (2 * o) ^ 1)], out_partner.at[o], pair_send.at[1, o], pair_recv.at[1, o],
                          partner)

        def out_cross(o):
            return remote(out_sum.at[o], out_chips.at[o], cross_send.at[1, o], cross_recv.at[1, o], (dp ^ (2 * o), mp))

        def weight_slice(index):
            o = (index + 1) % chips
            mine = index >= chips
            owner = dp ^ (2 * o) ^ jnp.where(mine, 0, 1)
            rows_all = landed[...].reshape(group_rows, kinds * columns)
            value = contract_first(normed[:, slab(owner)], rows_all)

            @pl.when(jnp.logical_not(mine))
            def _():
                slices[o] = value.astype(slices.dtype)
                pair(o).start()

            @pl.when(mine)
            def _():
                pair(o).wait_recv()
                both = value + from_partner[o].astype(jnp.float32)

                @pl.when(o == 0)
                def _():
                    weight_grad_ref[...] = both

                @pl.when(o != 0)
                def _():
                    chip_sum[o] = both.astype(chip_sum.dtype)
                    cross(o, owner).start()

        for copy in loads:
            copy.wait()
        arrived(0)
        for part_index in range(per_quarter):
            project(0, part_index * slice_rows, slice_rows)
        for piece in range(AHEAD):
            reduce.begin(piece)
        for o in range(chips):
            out_pair(o).start()
        sums_ref[...] = jnp.zeros_like(sums_ref)

        @pl.loop(0, turns)
        def _(turn):
            for k in range(1, QUARTERS):

                @pl.when(turn == min(2, per_quarter) * (k - 1))
                def _():
                    arrived(k)

            @pl.when(turn < (QUARTERS - 1) * per_quarter)
            def _():
                k, portion = turn // per_quarter + 1, turn % per_quarter
                project(k, portion * slice_rows, slice_rows)

            reduce.begin(jnp.minimum(turn + AHEAD, pieces - 1), turn + AHEAD < pieces)
            reduce.advance(turn)
            done = turn - SKEW * (mp_count - 1)

            @pl.when(done >= 0)
            def _():
                reduce.arrive(done)
                reduce.total(done, total)
                span = pl.ds(pl.multiple_of(done * size, size), size)
                unit, inverse = unit_rows(hidden_ref[span].astype(jnp.float32))
                upstream = total[...]
                sums_ref[0:1] += jnp.sum(upstream * unit, axis=0, keepdims=True)
                sums_ref[1:2] += jnp.sum(upstream, axis=0, keepdims=True)
                grad_ref[span] = residual_ref[span] + norm_back(upstream, unit, inverse, gain_ref[...])

            @pl.when(turn == late_turn - 1)
            def _():
                for o in list(range(1, chips)) + [0]:
                    out_pair(o).wait_recv()
                    value = out_ref[slab(dp ^ (2 * o))].astype(jnp.float32) + out_partner[o].astype(jnp.float32)
                    if o:
                        out_sum[o] = value.astype(out_sum.dtype)
                        out_cross(o).start()
                    else:
                        out_grad_ref[...] = value

            @pl.when(turn == late_turn - 1)
            def _():
                column_ref[0:1] = jnp.sum(
                    landed[...].reshape(group_rows, kinds * columns).astype(jnp.float32), axis=0, keepdims=True)

            @pl.when((turn >= late_turn) & (turn < late_turn + dp_count // slices_each))
            def _():
                for i in range(slices_each):
                    weight_slice((turn - late_turn) * slices_each + i)

        reduce.finish()
        packed[...] = vector_ref[...]
        for owner in range(dp_count):
            for r in range(each):
                at = slice((owner * each + r) * 128, (owner * each + r + 1) * 128)
                for k in range(2):
                    packed[owner, k * each + r : k * each + r + 1] = sums_ref[k : k + 1, at]
        for head in range(heads):
            feature = mp * heads + head
            for k, kind in ((2, 2), (3, 1)):
                at = slice(kind * columns + head * HEAD_DIM, kind * columns + (head + 1) * HEAD_DIM)
                packed[feature // each, pl.ds(k * each + feature % each, 1)] = column_ref[0:1, at]

        def vector_copy(o):
            return remote(packed.at[dp ^ o], vector_parts.at[o], vec_send.at[o], vec_recv.at[o], (dp ^ o, mp))

        def line_copy(o):
            return remote(line_parts.at[mp], line_parts.at[mp], line_send.at[o], line_recv.at[o], (dp, mp ^ o))

        for o in range(1, dp_count):
            vector_copy(o).start()
        value = packed[dp]
        for o in range(1, dp_count):
            vector_copy(o).wait_recv()
            value = value + vector_parts[o]
        line_parts[mp] = value
        for o in range(1, mp_count):
            line_copy(o).start()
        for o in range(chips):
            pair(o).wait_send()
            out_pair(o).wait_send()
            if o:
                cross(o, dp ^ (2 * o)).wait()
                weight_grad_ref[...] += from_chips[o].astype(jnp.float32)
                out_cross(o).wait()
                out_grad_ref[...] += out_chips[o].astype(jnp.float32)
        for k in range(QUARTERS):
            for o in range(heads):
                for kind in range(2):
                    for p in range(1, members):
                        part_copy(kind, o, p, k).wait_send()
                if o:
                    for kind in range(kinds):
                        head_copy(kind, o, k).wait_send()
        for o in range(1, mp_count):
            line_copy(o).wait()
        value = line_parts[0]
        for index in range(1, mp_count):
            value = value + line_parts[index]
        summed_ref[...] = value
        for o in range(1, dp_count):
            vector_copy(o).wait_send()

    late_turn = min(2, per_quarter) * (QUARTERS - 2) + 1
    assert late_turn + dp_count // slices_each <= turns
    dma = pltpu.SemaphoreType.DMA
    bf16, f32 = jnp.bfloat16, jnp.float32
    own_columns = out_part.shape[1]
    return pl.pallas_call(
        kernel,
        out_shape=[
            jax.ShapeDtypeStruct((rows, width), f32),
            jax.ShapeDtypeStruct((depth, kinds * columns), f32),
            jax.ShapeDtypeStruct((depth, own_columns), f32),
            jax.ShapeDtypeStruct((slab, 128), f32),
        ],
        in_specs=[ANY] * 5 + [VMEM] * 5,
        out_specs=[VMEM] * 4,
        scratch_shapes=[
            pltpu.VMEM((width, kinds * columns), bf16),
            pltpu.VMEM((group_rows, width), bf16),
            pltpu.VMEM((mp_count, rows, kinds * columns), bf16),
            pltpu.VMEM((2, heads, mp_count, rows, HEAD_DIM), bf16),
            pltpu.VMEM((2, heads, members - 1, mp_count, rows, HEAD_DIM), bf16),
            pltpu.VMEM((2, heads, mp_count, rows, HEAD_DIM), bf16),
            pltpu.VMEM((group_rows, width), bf16),
            pltpu.VMEM((size, width), f32),
        ]
        + LineReduce.scratch(mp_count, rows, width, pieces)
        + [pltpu.VMEM((chips, depth, kinds * columns), bf16) for _ in range(4)]
        + [pltpu.VMEM((chips, depth, own_columns), bf16) for _ in range(3)]
        + [dma((2,)), dma((2, heads))]
        + [dma((2, heads, members - 1, QUARTERS)) for _ in range(2)]
        + [dma((QUARTERS,)), dma((kinds, heads, QUARTERS)), dma((kinds, heads, QUARTERS))]
        + [dma((2, chips)) for _ in range(4)]
        + [pltpu.VMEM((8, width), f32), pltpu.VMEM((8, kinds * columns), f32)]
        + [pltpu.VMEM((count, slab, 128), f32) for count in (dp_count, dp_count, mp_count)]
        + [dma((dp_count,)), dma((dp_count,)), dma((mp_count,)), dma((mp_count,))],
        compiler_params=pltpu.CompilerParams(
            collective_id=collective_id, has_side_effects=True, vmem_limit_bytes=63 * MIB),
        cost_estimate=pl.CostEstimate(flops=20 << 30, bytes_accessed=300 * MIB, transcendentals=0),
    )(query_grad, *shared, weights, normed, residual_grad, hidden, gain, out_part, vectors)


UNITS = 512
CHUNK = 1024


def feed_both_ways(rows_two, branch_halves, block, up_all, down_all, up_bias):
    rows, width = rows_two.shape
    units = up_all.shape[1]
    tile = min(UNITS, units)
    half = block // 2
    half_root = 1.0 / math.sqrt(2.0)
    density_scale = 1.0 / math.sqrt(2.0 * math.pi)

    def kernel(rows_ref, first_ref, second_ref, up_ref, down_ref, bias_ref, hidden_ref, grad_ref, column_ref, part_ref, total):
        step = pl.program_id(0)
        columns = jnp.zeros((1, tile), jnp.float32)
        up, down = up_ref[...], down_ref[...]
        for first in range(0, rows, CHUNK):
            span = slice(first, first + CHUNK)
            pre = jnp.dot(rows_ref[span], up, preferred_element_type=jnp.float32) + bias_ref[...]
            upstream = jnp.concatenate([
                jnp.dot(ref[b * half : (b + 1) * half], down, preferred_element_type=jnp.float32)
                for b in range(first // block, (first + CHUNK) // block) for ref in (first_ref, second_ref)
            ], axis=0)
            share = 0.5 + 0.5 * lax.erf(pre * half_root)
            hidden_ref[span] = (pre * share).astype(hidden_ref.dtype)
            slope = share + pre * (density_scale * jnp.exp(-0.5 * pre * pre))
            grad = (upstream * slope).astype(grad_ref.dtype)
            grad_ref[span] = grad
            columns = columns + jnp.sum(grad.astype(jnp.float32), axis=0, keepdims=True)
            back = contract_last(grad, up)

            @pl.when(step == 0)
            def _():
                total[span] = back

            @pl.when(step != 0)
            def _():
                total[span] += back

        column_ref[...] = columns

        @pl.when(step == units // tile - 1)
        def _():
            part_ref[...] = total[...].astype(part_ref.dtype)

    bf16 = jnp.bfloat16
    return pl.pallas_call(
        kernel,
        grid=(units // tile,),
        out_shape=[
            jax.ShapeDtypeStruct((rows, units), bf16),
            jax.ShapeDtypeStruct((rows, units), bf16),
            jax.ShapeDtypeStruct((1, units), jnp.float32),
            jax.ShapeDtypeStruct((rows, width), bf16),
        ],
        in_specs=[
            pl.BlockSpec((rows, width), lambda i: (0, 0)),
            pl.BlockSpec((rows // 2, width), lambda i: (0, 0)),
            pl.BlockSpec((rows // 2, width), lambda i: (0, 0)),
            pl.BlockSpec((width, tile), lambda i: (0, i)),
            pl.BlockSpec((width, tile), lambda i: (0, i)),
            pl.BlockSpec((1, tile), lambda i: (0, i)),
        ],
        out_specs=[
            pl.BlockSpec((rows, tile), lambda i: (0, i)),
            pl.BlockSpec((rows, tile), lambda i: (0, i)),
            pl.BlockSpec((1, tile), lambda i: (0, i)),
            pl.BlockSpec((rows, width), lambda i: (0, 0)),
        ],
        scratch_shapes=[pltpu.VMEM((rows, width), jnp.float32)],
        compiler_params=pltpu.CompilerParams(vmem_limit_bytes=60 * MIB),
        cost_estimate=pl.CostEstimate(
            flops=6 * rows * width * units, bytes_accessed=40 * MIB, transcendentals=2 * rows * units),
    )(rows_two, *branch_halves, up_all, down_all, up_bias)


def sum_terms(terms):
    return functools.reduce(jnp.add, [terms[k].astype(jnp.float32) for k in range(terms.shape[0])])


def per_device(
    hidden_in,
    output_grad,
    first_gain,
    first_shift,
    query_weight,
    query_bias,
    key_weight,
    value_weight,
    value_bias,
    out_weight,
    out_bias,
    second_gain,
    second_shift,
    up_weight,
    up_bias,
    down_weight,
    down_bias,
    seq_lengths,
    block_order,
    block_slot,
):
    local_rows, model_width = hidden_in.shape
    mp_count, dp_count = lax.axis_size("mp"), lax.axis_size("dp")
    mp_index, dp_index = lax.axis_index("mp"), lax.axis_index("dp")
    group_rows = local_rows * mp_count
    head_width = query_weight.shape[1]
    heads_local = head_width // HEAD_DIM
    hidden_width = up_weight.shape[1]
    members = dp_count // heads_local
    blocks_each = group_rows // BLOCK
    plan = (seq_lengths, block_order, block_slot)

    vectors = (first_gain, first_shift, query_bias, value_bias, out_bias, second_gain, second_shift, down_bias, up_bias)
    rows_one, vector_rows, projections, out_all, head_shared, head_queries, branch_two, branch_rest, live, branch_first = project_first(
        hidden_in, output_grad, seq_lengths, block_order, vectors,
        (key_weight, value_weight, query_weight), out_weight, heads_local, members, 0,
    )
    own_valid = live[:, :1] > 0
    vector_rows = vector_rows.reshape(dp_count, -1, 128)
    each = model_width // dp_count // 128
    gain_one, _, _, _, bias_out, gain_two, shift_two, bias_down = (
        vector_rows[:, k * each : (k + 1) * each].reshape(1, model_width) for k in range(8)
    )
    up_each = up_bias.shape[0] // 128
    bias_up = vector_rows[:, 8 * each : 8 * each + up_each].reshape(1, up_bias.shape[0] * dp_count)

    branch_second = whole_rows(branch_rest)
    head_mix, exact_mix, log_total = attend(head_queries, head_shared, *plan, members, blocks_each)
    residual, attended_low, rows_two, up_all, down_all = mix_norm_gather(
        head_mix, out_all, hidden_in, bias_out, gain_two, shift_two, (up_weight, down_weight), heads_local, members, 3
    )
    attended_low = attended_low.reshape(group_rows, head_width)

    bias_hidden = lax.dynamic_slice_in_dim(bias_up, mp_index * hidden_width, hidden_width, 1)
    hidden_low, pre_grad, pre_columns, up_part = feed_both_ways(
        rows_two, (branch_first, branch_second), local_rows, up_all, down_all, bias_hidden
    )
    residual_grad, sums_two, branch_rows_one, feed_part, head_grad, down_terms, up_terms = reduce_back_gather(
        up_part, residual, branch_two, gain_two, (branch_first, branch_second),
        ((None, hidden_low), (rows_two, pre_grad)), down_all, out_all, heads_local, members, 4,
    )
    down_weight_grad, up_weight_grad = (
        sum_terms(terms) for terms in (down_terms, up_terms)
    )
    residual_grad, down_weight_grad, up_weight_grad = lax.optimization_barrier(
        (residual_grad, down_weight_grad, up_weight_grad)
    )

    feed = row_share(feed_part)
    result = residual + feed + bias_down
    output = jnp.where(own_valid, result, 0.0).astype(jnp.bfloat16)

    head_grad = head_grad.reshape(heads_local * group_rows, HEAD_DIM)
    head_query_grad, head_key_grad, head_value_grad = attend_back(
        head_queries, head_shared, head_grad, exact_mix, log_total, *plan, members, blocks_each
    )

    def column_sums(values):
        return jnp.sum(values.astype(jnp.float32), axis=0)

    def placed(values):
        whole = jnp.zeros((values.shape[0] * mp_count,), jnp.float32)
        return lax.dynamic_update_slice_in_dim(whole, values, mp_index * values.shape[0], 0)

    none = jnp.zeros((model_width,), jnp.float32)
    sums = (
        none, none, none, none, sums_two[2], sums_two[0], sums_two[1], column_sums(branch_two), placed(pre_columns[0]),
    )
    packed = jnp.concatenate([v.reshape(dp_count, -1, 128) for v in sums], axis=1)
    packed = jnp.pad(packed, ((0, 0), (0, -packed.shape[1] % 8), (0, 0)))
    out_weight_part = contract_first(branch_rows_one, attended_low).astype(jnp.bfloat16)
    input_grad, weight_grads, out_weight_grad, summed = finish_back(
        head_query_grad, head_key_grad, head_value_grad, projections, rows_one, residual_grad, hidden_in, gain_one,
        out_weight_part, packed, heads_local, members, 7,
    )
    key_weight_grad, value_weight_grad, query_weight_grad = (
        weight_grads[:, k * head_width : (k + 1) * head_width] for k in range(3)
    )
    vector_grads = [summed[k * each : (k + 1) * each].reshape(-1) for k in range(8)]
    up_bias_grad = summed[8 * each : 8 * each + up_each].reshape(-1)
    return (
        output,
        input_grad,
        vector_grads[0],
        vector_grads[1],
        query_weight_grad,
        vector_grads[2],
        key_weight_grad,
        value_weight_grad,
        vector_grads[3],
        out_weight_grad,
        vector_grads[4],
        vector_grads[5],
        vector_grads[6],
        up_weight_grad,
        up_bias_grad,
        down_weight_grad,
        vector_grads[7],
    )


def solution(mesh):
    return jax.shard_map(
        per_device,
        mesh=mesh,
        in_specs=(
            P(("dp", "mp"), None),
            P(("dp", "mp"), None),
            P("dp"),
            P("dp"),
            P("dp", "mp"),
            P("dp"),
            P("dp", "mp"),
            P("dp", "mp"),
            P("dp"),
            P("dp", "mp"),
            P("dp"),
            P("dp"),
            P("dp"),
            P("dp", "mp"),
            P("dp"),
            P("dp", "mp"),
            P("dp"),
            P(),
            P(),
            P(),
        ),
        out_specs=(
            P(("dp", "mp"), None),
            P(("dp", "mp"), None),
            P("dp"),
            P("dp"),
            P("dp", "mp"),
            P("dp"),
            P("dp", "mp"),
            P("dp", "mp"),
            P("dp"),
            P("dp", "mp"),
            P("dp"),
            P("dp"),
            P("dp"),
            P("dp", "mp"),
            P("dp"),
            P("dp", "mp"),
            P("dp"),
        ),
        check_vma=False,
    )
```

```python
import functools
import math

import jax
import jax.numpy as jnp
from jax import lax
from jax.experimental import pallas as pl
from jax.experimental.pallas import tpu as pltpu
from jax.sharding import PartitionSpec as P

HEAD_DIM = 128
BLOCK = 128
KEY_BLOCKS = 8
MESH = pl.DeviceIdType.MESH
ANY = pl.BlockSpec(memory_space=pl.ANY)
VMEM = pl.BlockSpec(memory_space=pltpu.VMEM)
SMEM = pl.BlockSpec(memory_space=pltpu.SMEM)
MIB = 1 << 20


big_negative = -1e30
norm_epsilon = 1e-05


def norm_back(upstream, normed, inverse, gain_row):
    scaled = upstream * gain_row
    mean_grad = jnp.mean(scaled, axis=-1, keepdims=True)
    second = jnp.mean(scaled * normed, axis=-1, keepdims=True)
    return inverse * (scaled - mean_grad - normed * second)


def contract_last(left, right):
    return lax.dot_general(
        left, right, (((1,), (1,)), ((), ())), preferred_element_type=jnp.float32
    )


def contract_first(left, right):
    return lax.dot_general(
        left, right, (((0,), (0,)), ((), ())), preferred_element_type=jnp.float32
    )


def whole_rows(local_part):
    return lax.all_gather(local_part, "mp", axis=0, tiled=True)


def row_share(term):
    term = term.astype(jnp.bfloat16)
    return lax.psum_scatter(term, "mp", scatter_dimension=0, tiled=True).astype(jnp.float32)


def greet(peers):
    barrier = pltpu.get_barrier_semaphore()
    for peer in peers:
        pl.semaphore_signal(barrier, inc=1, device_id=peer, device_id_type=MESH)
    pl.semaphore_wait(barrier, len(peers))


def remote(src, dst, send_sem, recv_sem, peer):
    return pltpu.make_async_remote_copy(
        src_ref=src, dst_ref=dst, send_sem=send_sem, recv_sem=recv_sem,
        device_id=peer, device_id_type=MESH,
    )


def head_place(heads, members):
    me = lax.axis_index("dp")
    return me, me // members, me % members, lax.axis_index("mp")


def lanes(head):
    return pl.ds(pl.multiple_of(head * HEAD_DIM, HEAD_DIM), HEAD_DIM)


def sequence_of(place, lengths):
    first, length, running = jnp.int32(0), jnp.int32(0), jnp.int32(0)
    for s in range(lengths.shape[0]):
        inside = place >= running
        first = jnp.where(inside, running, first)
        length = jnp.where(inside, lengths[s], length)
        running = running + (lengths[s] + (BLOCK - 1)) // BLOCK
    return first, length - (place - first) * BLOCK


def list_queries(slot, index_list, place_list, members, blocks_each):
    member = lax.axis_index("dp") % members

    def visit(block, count):
        dealt = slot[block]
        owner = dealt // blocks_each

        @pl.when(owner % members == member)
        def _():
            index_list[count] = (owner // members) * blocks_each + dealt % blocks_each
            place_list[count] = block

        return count + (owner % members == member).astype(jnp.int32)

    lax.fori_loop(0, slot.shape[0], visit, jnp.int32(0))


def block_rows(block):
    return pl.ds(pl.multiple_of(block * BLOCK, BLOCK), BLOCK)


class QueryPair:
    def __init__(self, pair, lengths, index_list, place_list):
        self.index = [index_list[2 * pair + i] for i in range(2)]
        self.place = [place_list[2 * pair + i] for i in range(2)]
        found = [sequence_of(place, lengths) for place in self.place]
        self.start = found[0][0]
        lane = lax.broadcasted_iota(jnp.int32, (1, 2 * BLOCK), 1)
        right = lane >= BLOCK

        def lanes_of(left_value, right_value):
            return jnp.where(right, right_value, left_value)

        within = lane - lanes_of(0, BLOCK)
        base = self.start * BLOCK
        self.position = lanes_of(self.place[0], self.place[1]) * BLOCK + within - base
        self.lowest = lanes_of(found[0][0], found[1][0]) * BLOCK - base
        self.live = within < lanes_of(found[0][1], found[1][1])
        self.tiles = (self.place[1] - self.start) // KEY_BLOCKS + 1
        self.open_tiles = jnp.where(found[0][0] == found[1][0], (self.place[0] - self.start) // KEY_BLOCKS, 0)

    def row(self, tile):
        return pl.multiple_of((self.start + tile * KEY_BLOCKS) * BLOCK, BLOCK)

    def allowed(self, tile):
        width = KEY_BLOCKS * BLOCK
        key = lax.broadcasted_iota(jnp.int32, (width, 2 * BLOCK), 0)
        return (key <= self.position - tile * width) & (key >= self.lowest - tile * width)

    def load_t(self, ref):
        return jnp.concatenate([ref[block_rows(index)].T for index in self.index], axis=1)

    def load(self, ref):
        return jnp.concatenate([ref[block_rows(index)] for index in self.index], axis=0)

    def store_t(self, ref, value_t):
        for i, index in enumerate(self.index):
            ref[block_rows(index)] = value_t[:, i * BLOCK : (i + 1) * BLOCK].T.astype(ref.dtype)


def attend(queries, shared, lengths, order, slot, members, blocks_each):
    pairs, key_count = queries.shape[0] // (2 * BLOCK), shared.shape[1] // BLOCK
    width = KEY_BLOCKS * BLOCK
    padded = (key_count + KEY_BLOCKS - 1) * BLOCK
    scale = math.log2(math.e) / math.sqrt(HEAD_DIM)

    def kernel(lengths_ref, slot_ref, q_ref, shared_ref, out_ref, exact_ref, log_ref,
               index_list, place_list, keys, values_t):
        list_queries(slot_ref, index_list, place_list, members, blocks_each)

        @pl.loop(0, key_count)
        def _(block):
            source = block_rows(slot_ref[block])
            keys[block_rows(block)] = shared_ref[0, source]
            values_t[:, block_rows(block)] = shared_ref[1, source].T

        tail = pl.ds(key_count * BLOCK, padded - key_count * BLOCK)
        keys[tail] = jnp.zeros((padded - key_count * BLOCK, HEAD_DIM), keys.dtype)
        values_t[:, tail] = jnp.zeros((HEAD_DIM, padded - key_count * BLOCK), keys.dtype)

        @pl.loop(0, pairs)
        def _(index):
            pair = QueryPair(index, lengths_ref, index_list, place_list)
            query_t = pair.load_t(q_ref)

            def step(tile, carry, masked):
                top, total, mix = carry
                span = pl.ds(pair.row(tile), width)
                scores = jnp.dot(keys[span], query_t, preferred_element_type=jnp.float32)
                if masked:
                    scores = jnp.where(pair.allowed(tile), scores, big_negative)
                new_top = jnp.maximum(top, jnp.max(scores, axis=0, keepdims=True))
                weights = jnp.exp2((scores - new_top) * scale)
                fade = jnp.exp2((top - new_top) * scale)
                total = total * fade + jnp.sum(weights, axis=0, keepdims=True)
                mix = mix * fade + jnp.dot(
                    values_t[:, span], weights.astype(jnp.bfloat16), preferred_element_type=jnp.float32)
                return new_top, total, mix

            carry = (jnp.full((1, 2 * BLOCK), big_negative, jnp.float32), jnp.zeros((1, 2 * BLOCK), jnp.float32),
                     jnp.zeros((HEAD_DIM, 2 * BLOCK), jnp.float32))
            carry = lax.fori_loop(0, pair.open_tiles, lambda tile, c: step(tile, c, False), carry)
            top, total, mix = lax.fori_loop(pair.open_tiles, pair.tiles, lambda tile, c: step(tile, c, True), carry)
            mix = jnp.where(pair.live, mix / total, 0.0)
            exact_ref[index] = mix
            pair.store_t(out_ref, mix)
            log_ref[index] = jnp.where(pair.live, top * scale + jnp.log2(total), -big_negative)

    return pl.pallas_call(
        kernel,
        out_shape=[
            jax.ShapeDtypeStruct(queries.shape, jnp.bfloat16),
            jax.ShapeDtypeStruct((pairs, HEAD_DIM, 2 * BLOCK), jnp.float32),
            jax.ShapeDtypeStruct((pairs, 1, 2 * BLOCK), jnp.float32),
        ],
        in_specs=[SMEM] * 2 + [VMEM] * 2,
        out_specs=[VMEM] * 3,
        scratch_shapes=[
            pltpu.SMEM((2 * pairs,), jnp.int32), pltpu.SMEM((2 * pairs,), jnp.int32),
            pltpu.VMEM((padded, HEAD_DIM), jnp.bfloat16), pltpu.VMEM((HEAD_DIM, padded), jnp.bfloat16),
        ],
        compiler_params=pltpu.CompilerParams(vmem_limit_bytes=56 * MIB),
        cost_estimate=pl.CostEstimate(flops=8 << 30, bytes_accessed=50 * MIB, transcendentals=8 << 20),
    )(lengths, slot, queries, shared)


def attend_back(queries, shared, upstream, exact, logs, lengths, order, slot, members, blocks_each):
    pairs, key_count = queries.shape[0] // (2 * BLOCK), shared.shape[1] // BLOCK
    width = KEY_BLOCKS * BLOCK
    padded = (key_count + KEY_BLOCKS - 1) * BLOCK
    scale = math.log2(math.e) / math.sqrt(HEAD_DIM)
    plain_scale = 1.0 / math.sqrt(HEAD_DIM)

    def kernel(lengths_ref, slot_ref, q_ref, shared_ref, g_ref, exact_ref, log_ref, dq_ref, dk_ref, dv_ref,
               index_list, place_list, keys, keys_t, values, key_sum, value_sum):
        list_queries(slot_ref, index_list, place_list, members, blocks_each)

        @pl.loop(0, key_count)
        def _(block):
            source, to = block_rows(slot_ref[block]), block_rows(block)
            rows = shared_ref[0, source]
            keys[to] = rows
            keys_t[:, to] = rows.T
            values[to] = shared_ref[1, source]
            key_sum[to] = jnp.zeros((BLOCK, HEAD_DIM), jnp.float32)
            value_sum[to] = jnp.zeros((BLOCK, HEAD_DIM), jnp.float32)

        tail = pl.ds(key_count * BLOCK, padded - key_count * BLOCK)
        keys[tail] = jnp.zeros((padded - key_count * BLOCK, HEAD_DIM), keys.dtype)
        values[tail] = jnp.zeros((padded - key_count * BLOCK, HEAD_DIM), keys.dtype)
        keys_t[:, tail] = jnp.zeros((HEAD_DIM, padded - key_count * BLOCK), keys.dtype)
        key_sum[tail] = jnp.zeros((padded - key_count * BLOCK, HEAD_DIM), jnp.float32)
        value_sum[tail] = jnp.zeros((padded - key_count * BLOCK, HEAD_DIM), jnp.float32)

        @pl.loop(0, pairs)
        def _(index):
            pair = QueryPair(index, lengths_ref, index_list, place_list)
            query, grad = pair.load(q_ref), pair.load(g_ref)
            query_t, grad_t = pair.load_t(q_ref), pair.load_t(g_ref)
            delta = jnp.sum(grad_t.astype(jnp.float32) * exact_ref[index], axis=0, keepdims=True)
            log_total = log_ref[index]

            def step(tile, query_grad, masked):
                span = pl.ds(pair.row(tile), width)
                scores = jnp.dot(keys[span], query_t, preferred_element_type=jnp.float32)
                probability = jnp.exp2(scores * scale - log_total)
                if masked:
                    probability = jnp.where(pair.allowed(tile), probability, 0.0)
                prob_grad = jnp.dot(values[span], grad_t, preferred_element_type=jnp.float32)
                score_grad = (probability * (prob_grad - delta)).astype(jnp.bfloat16)
                value_sum[span] += jnp.dot(
                    probability.astype(jnp.bfloat16), grad, preferred_element_type=jnp.float32)
                key_sum[span] += jnp.dot(score_grad, query, preferred_element_type=jnp.float32)
                return query_grad + jnp.dot(keys_t[:, span], score_grad, preferred_element_type=jnp.float32)

            query_grad = jnp.zeros((HEAD_DIM, 2 * BLOCK), jnp.float32)
            query_grad = lax.fori_loop(0, pair.open_tiles, lambda tile, c: step(tile, c, False), query_grad)
            query_grad = lax.fori_loop(pair.open_tiles, pair.tiles, lambda tile, c: step(tile, c, True), query_grad)
            pair.store_t(dq_ref, query_grad * plain_scale)

        @pl.loop(0, key_count)
        def _(block):
            at, dealt = block_rows(block), block_rows(slot_ref[block])
            dk_ref[dealt] = (key_sum[at] * plain_scale).astype(dk_ref.dtype)
            dv_ref[dealt] = value_sum[at].astype(dv_ref.dtype)

    return pl.pallas_call(
        kernel,
        out_shape=[
            jax.ShapeDtypeStruct(queries.shape, jnp.bfloat16),
            jax.ShapeDtypeStruct(shared.shape[1:], jnp.bfloat16),
            jax.ShapeDtypeStruct(shared.shape[1:], jnp.bfloat16),
        ],
        in_specs=[SMEM] * 2 + [VMEM] * 5,
        out_specs=[VMEM] * 3,
        scratch_shapes=[
            pltpu.SMEM((2 * pairs,), jnp.int32), pltpu.SMEM((2 * pairs,), jnp.int32),
            pltpu.VMEM((padded, HEAD_DIM), jnp.bfloat16),
            pltpu.VMEM((HEAD_DIM, padded), jnp.bfloat16),
            pltpu.VMEM((padded, HEAD_DIM), jnp.bfloat16),
            pltpu.VMEM((padded, HEAD_DIM), jnp.float32),
            pltpu.VMEM((padded, HEAD_DIM), jnp.float32),
        ],
        compiler_params=pltpu.CompilerParams(vmem_limit_bytes=60 * MIB),
        cost_estimate=pl.CostEstimate(flops=20 << 30, bytes_accessed=100 * MIB, transcendentals=8 << 20),
    )(lengths, slot, queries, shared, upstream, exact, logs)


def line_neighbours(mp, count):
    return ((1, mp + 1 < count, jnp.minimum(mp + 1, count - 1)), (-1, mp >= 1, jnp.maximum(mp - 1, 0)))


def greet_all(fixed, dp, mp, count):
    barrier = pltpu.get_barrier_semaphore()
    for peer in fixed:
        pl.semaphore_signal(barrier, inc=1, device_id=peer, device_id_type=MESH)
    expected = jnp.int32(len(fixed))
    for _, there, place in line_neighbours(mp, count):

        @pl.when(there)
        def _():
            pl.semaphore_signal(barrier, inc=1, device_id=(dp, place), device_id_type=MESH)

        expected = expected + there.astype(jnp.int32)
    pl.semaphore_wait(barrier, expected)


class LineGather:
    def __init__(self, own, full, rows, pieces, send_sem, recv_sem, dp, mp, count):
        self.own, self.full, self.rows, self.pieces = own, full, rows, pieces
        self.send_sem, self.recv_sem, self.dp, self.mp, self.count = send_sem, recv_sem, dp, mp, count
        self.size = rows // pieces

    def place(self, block, piece):
        return self.full.at[pl.ds(pl.multiple_of(block * self.rows + piece * self.size, self.size), self.size)]

    def hop(self, way, step, piece):
        sign, there, neighbour = line_neighbours(self.mp, self.count)[way]
        origin = self.mp - sign * step
        exists = (origin >= 0) & (origin < self.count)
        origin = jnp.clip(origin, 0, self.count - 1)
        if step == 0:
            source = self.own.at[pl.ds(pl.multiple_of(piece * self.size, self.size), self.size)]
        else:
            source = self.place(origin, piece)
        def copy():
            return remote(source, self.place(origin, piece), self.send_sem.at[way, step, piece],
                          self.recv_sem.at[way, step, piece], (self.dp, neighbour))

        return exists, exists & there, copy

    def advance(self, step, piece, also=True, ways=(0, 1)):
        for way in ways:
            if step:
                exists, _, _ = self.hop(way, step, piece)
                _, _, earlier = self.hop(way, step - 1, piece)

                @pl.when(exists & also)
                def _():
                    earlier().wait_recv()

            if step < self.count - 1:
                _, sends, copy = self.hop(way, step, piece)

                @pl.when(sends & also)
                def _():
                    copy().start()

    def finish(self):
        @pl.loop(0, self.pieces)
        def _(piece):
            for way in range(2):
                for step in range(self.count - 1):
                    _, sends, copy = self.hop(way, step, piece)

                    @pl.when(sends)
                    def _():
                        copy().wait_send()

    @staticmethod
    def semaphores(count, pieces):
        return [pltpu.SemaphoreType.DMA((2, count, pieces)), pltpu.SemaphoreType.DMA((2, count, pieces))]


class ShardGather:
    def __init__(self, shards, wholes, depth, cross_send, cross_recv, core_send, core_recv, own_sem, dp, mp, chips):
        self.shards, self.wholes, self.depth, self.own_sem = shards, wholes, depth, own_sem
        self.cross_send, self.cross_recv, self.core_send, self.core_recv = cross_send, cross_recv, core_send, core_recv
        self.dp, self.mp, self.chips = dp, mp, chips

    def place(self, array, owner):
        return self.wholes[array].at[pl.ds(pl.multiple_of(owner * self.depth, self.depth), self.depth)]

    def cross(self, array, o):
        return remote(self.shards[array], self.place(array, self.dp), self.cross_send.at[array, o],
                      self.cross_recv.at[array, o], (self.dp ^ (2 * o), self.mp))

    def core(self, array, o):
        owner = self.dp ^ (2 * o)
        source = self.place(array, owner) if o else self.shards[array]
        return remote(source, self.place(array, owner), self.core_send.at[array, o], self.core_recv.at[array, o],
                      (self.dp ^ 1, self.mp))

    def own(self, array):
        return pltpu.make_async_copy(self.shards[array], self.place(array, self.dp), self.own_sem.at[array])

    def begin(self):
        for array in range(len(self.shards)):
            for o in range(1, self.chips):
                self.cross(array, o).start()
        for array in range(len(self.shards)):
            self.own(array).start()
            self.core(array, 0).start()

    def spread(self, array):
        for o in range(1, self.chips):
            self.cross(array, o).wait_recv()
            self.core(array, o).start()

    def finish(self):
        for array in range(len(self.shards)):
            self.own(array).wait()
            for o in range(self.chips):
                self.core(array, o).wait()
                if o:
                    self.cross(array, o).wait_send()

    @staticmethod
    def semaphores(count, chips):
        return [pltpu.SemaphoreType.DMA((count, chips)) for _ in range(4)] + [pltpu.SemaphoreType.DMA((count,))]


class LineReduce:
    def __init__(self, part, flows, rows, pieces, send_sem, recv_sem, dp, mp, count):
        self.part, self.flows, self.rows, self.pieces = part, flows, rows, pieces
        self.send_sem, self.recv_sem, self.dp, self.mp, self.count = send_sem, recv_sem, dp, mp, count
        self.size = rows // pieces

    def span(self, block, piece):
        return pl.ds(pl.multiple_of(block * self.rows + piece * self.size, self.size), self.size)

    def hop(self, way, block, piece, first=False):
        neighbour = line_neighbours(self.mp, self.count)[way][2]
        span = self.span(block, piece)
        source = self.part.at[span] if first else self.flows.at[way, span]
        return remote(source, self.flows.at[way, span], self.send_sem.at[way, block, piece],
                      self.recv_sem.at[way, block, piece], (self.dp, neighbour))

    def roles(self, way, block):
        if way == 0:
            behind, ahead = self.mp >= 1, self.mp < block
        else:
            behind, ahead = self.mp < self.count - 1, self.mp > block
        return ahead & jnp.logical_not(behind), ahead & behind

    def targets(self):
        for index in range(self.count - 1):
            yield 0, self.count - 1 - index
            yield 1, index

    def begin(self, piece, also=True):
        for way, block in self.targets():
            begins, _ = self.roles(way, block)

            @pl.when(begins & also)
            def _():
                self.hop(way, block, piece, True).start()

    def advance(self, turn):
        for way, block in self.targets():
            _, hands_on = self.roles(way, block)
            passed = SKEW * (self.mp - 1 if way == 0 else self.count - 2 - self.mp)
            piece = jnp.clip(turn - passed, 0, self.pieces - 1)

            @pl.when(hands_on & (turn >= passed) & (turn - passed < self.pieces))
            def _():
                self.hop(way, block, piece).wait_recv()
                span = self.span(block, piece)
                value = self.flows[way, span].astype(jnp.float32) + self.part[span].astype(jnp.float32)
                self.flows[way, span] = value.astype(self.flows.dtype)
                self.hop(way, block, piece).start()

    def arrive(self, piece):
        for way in range(2):

            @pl.when(self.mp >= 1 if way == 0 else self.mp < self.count - 1)
            def _():
                self.hop(way, self.mp, piece).wait_recv()

    def total(self, piece, result):
        span = self.span(self.mp, piece)
        result[...] = self.part[span].astype(jnp.float32)
        for way in range(2):

            @pl.when(self.mp >= 1 if way == 0 else self.mp < self.count - 1)
            def _():
                result[...] += self.flows[way, span].astype(jnp.float32)

    def finish(self):
        @pl.loop(0, self.pieces)
        def _(piece):
            for way, block in self.targets():
                begins, hands_on = self.roles(way, block)

                @pl.when(begins)
                def _():
                    self.hop(way, block, piece, True).wait_send()

                @pl.when(hands_on)
                def _():
                    self.hop(way, block, piece).wait_send()

    @staticmethod
    def scratch(count, rows, width, pieces):
        return [pltpu.VMEM((2, count * rows, width), jnp.bfloat16),
                pltpu.SemaphoreType.DMA((2, count, pieces)), pltpu.SemaphoreType.DMA((2, count, pieces))]


AHEAD = 1
QUARTERS = 4
MAX_PIECES = 16
SKEW = 1


def pieces_of(rows):
    return min(MAX_PIECES, rows // 16)


def unit_rows(values):
    average = jnp.mean(values, axis=-1, keepdims=True)
    centred = values - average
    inverse = lax.rsqrt(jnp.mean(centred * centred, axis=-1, keepdims=True) + norm_epsilon)
    return centred * inverse, inverse


def project_first(
    hidden, output_grad, lengths, order, vectors, projections, out_weight, heads, members, collective_id
):
    rows, width = hidden.shape
    dp_count, mp_count = lax.axis_size("dp"), lax.axis_size("mp")
    chips, pieces, half = dp_count // 2, pieces_of(rows), rows // 2
    half_pieces = pieces_of(half)
    group_rows, depth, columns = mp_count * rows, projections[0].shape[0], projections[0].shape[1]
    each = width // dp_count // 128
    tall = [v.shape[0] // 128 for v in vectors]
    slab = sum(tall) + -sum(tall) % 8
    halves, kinds = heads // 2, 3
    arrays = kinds + 2
    offsets = sorted({2 * o for o in range(1, chips)} | {o for o in range(1, members)} | {o * members for o in range(1, heads)})

    def kernel(lengths_ref, order_ref, hidden_ref, upstream_ref, *refs):
        given, refs = refs[: len(vectors)], refs[len(vectors) :]
        weight_refs, out_weight_ref = refs[:kinds], refs[kinds]
        (normed_out, all_vectors, weights_out, all_out, shared, queries, branch, rest, live,
         half_rows) = refs[kinds + 1 : kinds + 11]
        parts, refs = refs[-len(vectors) :], refs[: -len(vectors)]
        (vector_ref, upstream, load_sem, raw, stage, gains, biases, line_send, line_recv, row_sem, own_sem, cross_send, cross_recv, core_send, core_recv,
         head_local, head_send, head_recv, pair_send, pair_recv, half_send, half_recv, half_sem,
         normed, weights, out_sem) = refs[kinds + 11 :]
        dp, mp = lax.axis_index("dp"), lax.axis_index("mp")
        loads = [pltpu.make_async_copy(given[k], parts[k], load_sem.at[k]) for k in range(len(vectors))]
        loads.append(pltpu.make_async_copy(upstream_ref, upstream, load_sem.at[len(vectors)]))
        for copy in loads:
            copy.start()
        vector_ref[...] = jnp.zeros_like(vector_ref)
        for copy in loads:
            copy.wait()
        first = 0
        for part, count in zip(parts, tall):
            for r in range(count):
                vector_ref[first + r] = part[r * 128 : (r + 1) * 128].astype(jnp.float32)
            first += count
        group, member = dp // members, dp % members
        partner = (dp ^ 1, mp)
        greet_all([(dp ^ o, mp) for o in offsets], dp, mp, mp_count)
        line = LineGather(hidden_ref, raw, rows, pieces, line_send, line_recv, dp, mp, mp_count)

        behind = LineGather(branch, half_rows, half, half_pieces, half_send, half_recv, dp, mp, mp_count)

        def follow(step):
            for way, steps in ((0, mp), (1, mp_count - 1 - mp)):

                @pl.loop(0, half_pieces)
                def _(piece):
                    behind.advance(0, piece, steps == step, (way,))

        between = (mp > 0) & (mp < mp_count - 1)

        def hand_half(step, also=True):
            @pl.loop(0, half_pieces)
            def _(piece):
                behind.advance(step, piece, also)

        def source(array):
            return (list(weight_refs) + [out_weight_ref, vector_ref])[array]

        def place(array, owner):
            if array < kinds:
                return weights.at[pl.ds(pl.multiple_of(owner * depth, depth), depth), pl.ds(array * columns, columns)]
            if array == kinds:
                return all_out.at[pl.ds(pl.multiple_of(owner * depth, depth), depth)]
            return all_vectors.at[pl.ds(pl.multiple_of(owner * slab, slab), slab)]

        def cross(array, o):
            return remote(source(array), place(array, dp), cross_send.at[array, o], cross_recv.at[array, o],
                          (dp ^ (2 * o), mp))

        def core(array, o):
            owner = dp ^ (2 * o)
            return remote(place(array, owner) if o else source(array), place(array, owner),
                          core_send.at[array, o], core_recv.at[array, o], partner)

        def own(array):
            return pltpu.make_async_copy(source(array), place(array, dp), own_sem.at[array])

        def block_span(block):
            return pl.ds(pl.multiple_of(block * rows, rows), rows)

        first_to_last = [kinds + 1] + list(range(kinds + 1))
        for array in first_to_last:
            for o in range(1, chips):
                cross(array, o).start()
            if array == first_to_last[0]:

                @pl.loop(0, pieces)
                def _(piece):
                    line.advance(0, piece)

        for block in range(rows // BLOCK):
            found = order_ref[(dp * group_rows + mp * rows) // BLOCK + block]
            valid = sequence_of(found, lengths_ref)[1]
            span = slice(block * BLOCK, (block + 1) * BLOCK)
            live[span] = (lax.broadcasted_iota(jnp.int32, (BLOCK, 128), 0) < valid).astype(jnp.float32)
            keep = lax.broadcasted_iota(jnp.int32, (BLOCK, width), 0) < valid
            branch[span] = jnp.where(keep, upstream[span].astype(jnp.float32), 0.0).astype(branch.dtype)
        rest[...] = branch[half:]
        own_half = pltpu.make_async_copy(
            branch.at[pl.ds(0, half)], half_rows.at[pl.ds(pl.multiple_of(mp * half, half), half)], half_sem)
        own_half.start()
        follow(0)
        own_rows = pltpu.make_async_copy(hidden_ref, raw.at[block_span(mp)], row_sem)
        own_rows.start()
        for array in first_to_last:
            own(array).start()
            core(array, 0).start()

        def spread(array):
            for o in range(1, chips):
                cross(array, o).wait_recv()
                core(array, o).start()

        def settle(array):
            own(array).wait()
            for o in range(chips):
                core(array, o).wait_recv()

        def norm(block):
            chunk = 64

            @pl.loop(0, rows // chunk)
            def _(part):
                span = pl.ds(pl.multiple_of(block * rows + part * chunk, chunk), chunk)
                unit, _ = unit_rows(raw[span].astype(jnp.float32))
                normed[span] = (unit * gains[0:1] + gains[1:2]).astype(normed.dtype)

            normed_copy(block).start()

        def normed_copy(block):
            return pltpu.make_async_copy(
                normed.at[block_span(block)], normed_out.at[block_span(block)], out_sem.at[block])

        weights_copy = pltpu.make_async_copy(weights, weights_out, out_sem.at[mp_count])

        def each_block(low, high, visit):
            @pl.loop(0, mp_count)
            def _(block):
                distance = jnp.abs(block - mp)

                @pl.when((distance >= low) & (distance <= high))
                def _():
                    visit(block)

        def rows_of(kind_ref, owner, block):
            return kind_ref.at[pl.ds(pl.multiple_of(owner * group_rows + block * rows, rows), rows)]

        def pass_on(kind, o, block, piece):
            giver = (group ^ o) * members + member
            return [remote(piece, rows_of(shared.at[kind], giver, block), pair_send.at[kind, o, block, p - 1],
                           pair_recv.at[kind, o, block, p - 1], (group * members + (member ^ p), mp))
                    for p in range(1, members)]

        def head_copy(kind, o, block, to_shared):
            target = group ^ o
            piece = stage.at[kind, block, target]
            landing = rows_of(shared.at[kind], dp, block) if to_shared else rows_of(queries, group, block)
            return remote(piece, landing, head_send.at[kind, o, block], head_recv.at[kind, o, block],
                          (target * members + member, mp))

        def local_copy(kind, block, to_shared):
            landing = rows_of(shared.at[kind], dp, block) if to_shared else rows_of(queries, group, block)
            return pltpu.make_async_copy(stage.at[kind, block, group], landing, head_local.at[kind, block])

        def project(tile, block):
            kind, half = tile // halves, tile % halves
            span = pl.ds(pl.multiple_of(half * 256, 256), 256)
            across = pl.ds(pl.multiple_of(kind * columns + half * 256, 256), 256)
            value = jnp.dot(normed[block_span(block)], weights[:, across], preferred_element_type=jnp.float32)
            value = (value + biases[pl.ds(kind, 1), span]).astype(stage.dtype)
            for h in range(2):
                head = 2 * half + h
                stage[kind, block, head] = value[:, h * HEAD_DIM : (h + 1) * HEAD_DIM]
            for h in range(2):
                o = (2 * half + h) ^ group
                for to_shared in (True, False):
                    chosen = (kind < 2) if to_shared else (kind == 2)

                    @pl.when(chosen & (o != 0))
                    def _():
                        head_copy(kind, o, block, to_shared).start()

                    @pl.when(chosen & (o == 0))
                    def _():
                        local_copy(kind, block, to_shared).start()
                        if to_shared:
                            for copy in pass_on(kind, 0, block, stage.at[kind, block, group]):
                                copy.start()

        def hand_on(block):
            @pl.loop(0, 2)
            def _(kind):
                for o in range(1, heads):
                    head_copy(kind, o, block, True).wait_recv()
                    giver = (group ^ o) * members + member
                    for copy in pass_on(kind, o, block, rows_of(shared.at[kind], giver, block)):
                        copy.start()

        last = mp_count - 1
        for step in range(1, last):

            @pl.loop(0, pieces)
            def _(piece):
                line.advance(step, piece)

            follow(step)
            if step == 1:
                spread(kinds + 1)
                settle(kinds + 1)
                for owner in range(dp_count):
                    for r in range(each):
                        at = pl.ds((owner * each + r) * 128, 128)
                        for k in range(2):
                            gains[k : k + 1, at] = all_vectors[owner * slab + k * each + r : owner * slab + k * each + r + 1]
                biases[...] = jnp.zeros_like(biases)
                for head in range(heads):
                    feature = mp * heads + head
                    first = (feature // each) * slab + feature % each
                    for kind, k in ((1, 3), (2, 2)):
                        biases[kind : kind + 1, head * 128 : (head + 1) * 128] = all_vectors[pl.ds(first + k * each, 1)]
                own_rows.wait()
                each_block(0, 1, norm)
            else:
                each_block(step, step, norm)
        for array in range(kinds + 1):
            spread(array)
        for array in range(kinds):
            settle(array)
        weights_copy.start()
        tiles = kinds * halves

        @pl.loop(0, pieces)
        def _(piece):
            line.advance(last - 1 if last == 1 else last, piece)

            @pl.when(piece >= pieces - half_pieces)
            def _():
                behind.advance(1, piece - (pieces - half_pieces), between)

            @pl.when(piece < tiles)
            def _():
                each_block(0, last - 1, lambda block: project(piece, block))

        for step in range(2, last):
            hand_half(step, between)
        each_block(last, last, norm)

        @pl.loop(0, tiles)
        def _(tile):
            each_block(last, last, lambda block: project(tile, block))

        each_block(0, last - 1, hand_on)
        each_block(last, last, hand_on)
        for step in range(1, last):
            hand_half(step, jnp.logical_not(between))
        hand_half(last)
        line.finish()
        weights_copy.wait()
        for block in range(mp_count):
            normed_copy(block).wait()
        behind.finish()
        own_half.wait()
        settle(kinds)
        for array in first_to_last:
            for o in range(chips):
                core(array, o).wait_send()
                if o:
                    cross(array, o).wait_send()

        @pl.loop(0, mp_count)
        def _(block):
            for kind in range(kinds):
                to_shared = kind < 2
                local_copy(kind, block, to_shared).wait()
                for o in range(1, heads):
                    head_copy(kind, o, block, to_shared).wait_send()
                    if not to_shared:
                        head_copy(kind, o, block, to_shared).wait_recv()
                if to_shared:
                    for o in range(heads):
                        giver = (group ^ o) * members + member
                        for copy in pass_on(kind, o, block, rows_of(shared.at[kind], giver, block)):
                            copy.wait()

    dma = pltpu.SemaphoreType.DMA
    bf16, f32 = jnp.bfloat16, jnp.float32
    return pl.pallas_call(
        kernel,
        out_shape=[
            jax.ShapeDtypeStruct((group_rows, width), bf16),
            jax.ShapeDtypeStruct((dp_count * slab, 128), f32),
            jax.ShapeDtypeStruct((width, kinds * columns), bf16),
            jax.ShapeDtypeStruct((width, columns), bf16),
            jax.ShapeDtypeStruct((2, dp_count * group_rows, HEAD_DIM), bf16),
            jax.ShapeDtypeStruct((heads * group_rows, HEAD_DIM), bf16),
            jax.ShapeDtypeStruct((rows, width), bf16),
            jax.ShapeDtypeStruct((rows - half, width), bf16),
            jax.ShapeDtypeStruct((rows, 128), f32),
            jax.ShapeDtypeStruct((mp_count * half, width), bf16),
        ],
        in_specs=[SMEM, SMEM] + [ANY] * (len(vectors) + kinds + 3),
        out_specs=[ANY, VMEM, ANY, ANY, ANY, ANY, VMEM, VMEM, VMEM, ANY],
        scratch_shapes=[
            pltpu.VMEM((slab, 128), f32),
            pltpu.VMEM((rows, width), bf16),
            dma((len(vectors) + 1,)),
            pltpu.VMEM((group_rows, width), bf16),
            pltpu.VMEM((kinds, mp_count, heads, rows, HEAD_DIM), bf16),
            pltpu.VMEM((8, width), f32),
            pltpu.VMEM((8, columns), f32),
        ]
        + LineGather.semaphores(mp_count, pieces)
        + [dma(()), dma((arrays,))]
        + [dma((arrays, chips)) for _ in range(4)]
        + [dma((kinds, mp_count)), dma((kinds, heads, mp_count)), dma((kinds, heads, mp_count))]
        + [dma((2, heads, mp_count, members)) for _ in range(2)]
        + LineGather.semaphores(mp_count, half_pieces) + [dma(())]
        + [pltpu.VMEM((group_rows, width), bf16), pltpu.VMEM((width, kinds * columns), bf16), dma((mp_count + 1,))]
        + [pltpu.VMEM(v.shape, v.dtype) for v in vectors],
        compiler_params=pltpu.CompilerParams(
            collective_id=collective_id, has_side_effects=True, vmem_limit_bytes=63 * MIB),
        cost_estimate=pl.CostEstimate(flops=8 << 30, bytes_accessed=250 * MIB, transcendentals=0),
    )(lengths, order, hidden, output_grad, *vectors, *projections, out_weight)


def mix_norm_gather(mixed, out_weight, hidden, out_bias, gain, shift, shards, heads, members, collective_id):
    dp_count, mp_count = lax.axis_size("dp"), lax.axis_size("mp")
    chips, count = dp_count // 2, len(shards)
    rows, width = hidden.shape
    pieces = pieces_of(rows)
    size, columns, group_rows = rows // pieces, heads * HEAD_DIM, mp_count * rows
    quarter, per_quarter = rows // QUARTERS, pieces // QUARTERS
    slice_rows = width // per_quarter
    offsets = sorted({2 * o for o in range(1, chips)} | {1} | {o * members for o in range(1, heads)})
    mixed = mixed.reshape(heads, mp_count, rows, HEAD_DIM)
    turns = pieces + 2 * SKEW * (mp_count - 1)

    def kernel(mixed_ref, out_hbm, hidden_ref, bias_ref, gain_ref, shift_ref, *refs):
        shard_refs, (residual_ref, landed, full_ref), refs = refs[:count], refs[count : count + 3], refs[count + 3 :]
        whole_refs, refs = refs[:count], refs[count:]
        (part, out_rows, load_sem, local_sem, head_send, head_recv,
         total, normed, flows, red_send, red_recv, line_send, line_recv, own_sem, *weight_sems) = refs
        dp, mp = lax.axis_index("dp"), lax.axis_index("mp")
        group, member = dp // members, dp % members
        greet_all([(dp ^ o, mp) for o in offsets], dp, mp, mp_count)

        def landing(k, head):
            return landed.at[:, pl.ds(k * quarter, quarter), lanes(head)]

        def head_copy(o, k):
            return remote(mixed_ref.at[group ^ o, :, pl.ds(k * quarter, quarter)], landing(k, group),
                          head_send.at[o, k], head_recv.at[o, k], ((group ^ o) * members + member, mp))

        def local_copy(k):
            return pltpu.make_async_copy(mixed_ref.at[group, :, pl.ds(k * quarter, quarter)], landing(k, group),
                                         local_sem.at[k])

        def arrived(k):
            for o in range(1, heads):
                head_copy(o, k).wait_recv()
            local_copy(k).wait()

        def project(k, first, count):
            span = pl.ds(pl.multiple_of(k * quarter, quarter), quarter)
            left = landed[:, span].reshape(mp_count * quarter, columns)
            features = pl.ds(pl.multiple_of(first, count), count)
            value = contract_last(left, out_rows[features]).astype(part.dtype)
            for block in range(mp_count):
                at = pl.ds(pl.multiple_of(block * rows + k * quarter, quarter), quarter)
                part[at, features] = value[block * quarter : (block + 1) * quarter]

        load = pltpu.make_async_copy(out_hbm, out_rows, load_sem)
        load.start()
        for k in range(QUARTERS):
            for o in range(1, heads):
                head_copy(o, k).start()
            local_copy(k).start()
        weights = ShardGather(shard_refs, whole_refs, shards[0].shape[0], *weight_sems, dp, mp, chips)
        weights.begin()
        reduce = LineReduce(part, flows, rows, pieces, red_send, red_recv, dp, mp, mp_count)
        gather = LineGather(normed, full_ref, rows, pieces, line_send, line_recv, dp, mp, mp_count)
        load.wait()
        arrived(0)
        for portion in range(per_quarter):
            project(0, portion * slice_rows, slice_rows)
        for piece in range(AHEAD):
            reduce.begin(piece)

        @pl.loop(0, turns)
        def _(turn):
            for array in range(count):

                @pl.when(turn == turns - 3 - 6 * (count - 1 - array))
                def _():
                    weights.spread(array)

            for k in range(1, QUARTERS):

                @pl.when(turn == (k - 1) * per_quarter)
                def _():
                    arrived(k)

            @pl.when(turn < (QUARTERS - 1) * per_quarter)
            def _():
                project(turn // per_quarter + 1, (turn % per_quarter) * slice_rows, slice_rows)

            reduce.begin(jnp.minimum(turn + AHEAD, pieces - 1), turn + AHEAD < pieces)
            reduce.advance(turn)
            done = turn - SKEW * (mp_count - 1)

            @pl.when((done >= 0) & (done < pieces))
            def _():
                reduce.arrive(done)
                reduce.total(done, total)
                span = pl.ds(pl.multiple_of(done * size, size), size)
                residual = hidden_ref[span].astype(jnp.float32) + total[...] + bias_ref[...]
                residual_ref[span] = residual
                unit, _ = unit_rows(residual)
                normed[span] = (unit * gain_ref[...] + shift_ref[...]).astype(normed.dtype)
                gather.advance(0, done)

            for step in range(1, mp_count):
                late = done - SKEW * step
                gather.advance(step, jnp.clip(late, 0, pieces - 1), (late >= 0) & (late < pieces))

        own = pltpu.make_async_copy(normed, full_ref.at[pl.ds(pl.multiple_of(mp * rows, rows), rows)], own_sem)
        own.start()
        reduce.finish()
        gather.finish()
        own.wait()
        weights.finish()
        for k in range(QUARTERS):
            for o in range(1, heads):
                head_copy(o, k).wait_send()

    dma = pltpu.SemaphoreType.DMA
    return pl.pallas_call(
        kernel,
        out_shape=[
            jax.ShapeDtypeStruct((rows, width), jnp.float32),
            jax.ShapeDtypeStruct((mp_count, rows, columns), jnp.bfloat16),
            jax.ShapeDtypeStruct((group_rows, width), jnp.bfloat16),
        ]
        + [jax.ShapeDtypeStruct((dp_count * a.shape[0], a.shape[1]), a.dtype) for a in shards],
        in_specs=[ANY] * 2 + [VMEM] * 4 + [ANY] * count,
        out_specs=[VMEM, VMEM, ANY] + [ANY] * count,
        scratch_shapes=[
            pltpu.VMEM((group_rows, width), jnp.bfloat16), pltpu.VMEM((width, columns), jnp.bfloat16),
            dma(()), dma((QUARTERS,)), dma((heads, QUARTERS)), dma((heads, QUARTERS)),
        ]
        + [pltpu.VMEM((size, width), jnp.float32), pltpu.VMEM((rows, width), jnp.bfloat16)]
        + LineReduce.scratch(mp_count, rows, width, pieces) + LineGather.semaphores(mp_count, pieces)
        + [pltpu.SemaphoreType.DMA(())] + ShardGather.semaphores(count, chips),
        compiler_params=pltpu.CompilerParams(
            collective_id=collective_id, has_side_effects=True, vmem_limit_bytes=63 * MIB),
        cost_estimate=pl.CostEstimate(flops=0, bytes_accessed=300 * MIB, transcendentals=0),
    )(mixed, out_weight, hidden, out_bias, gain, shift, *shards)


def reduce_back_gather(
    part, residual, branch_two, gain, halves, pairs, down_weight, out_weight, heads, members, collective_id
):
    dp_count, mp_count = lax.axis_size("dp"), lax.axis_size("mp")
    chips, count = dp_count // 2, len(pairs)
    rows, width = residual.shape
    half = rows // 2
    pieces = pieces_of(rows)
    size, depth = rows // pieces, width // dp_count
    units = pairs[0][1].shape[1]
    turns = pieces + 2 * SKEW * (mp_count - 1)
    each = dp_count // 4
    busy = count * dp_count // each
    feed_slices = 8
    feed_rows = width // feed_slices
    assert 1 + busy + feed_slices <= turns
    quarter, per_quarter, columns = rows // QUARTERS, pieces // QUARTERS, heads * HEAD_DIM
    group_rows = mp_count * rows
    offsets = sorted({2 * o for o in range(1, chips)} | {1} | {o * members for o in range(1, heads)})

    def kernel(part_ref, residual_ref, branch_ref, gain_ref, *refs):
        operands, down_ref, out_hbm, refs = refs[: 2 * count + 1], refs[2 * count + 1], refs[2 * count + 2], refs[2 * count + 3 :]
        (grad_ref, sums_ref, full_ref, feed_ref, heads_ref), terms, refs = refs[:5], refs[5 : 5 + count], refs[5 + count :]
        loaded, refs = refs[: 2 * count], refs[2 * count :]
        (credit, down_rows, down_sem, fed, fed_sem, out_rows, out_sem, gathered, gathered_sem, stage,
         stage_sem, head_send, head_recv, half_sem, total, low, kept, slices, from_partner, chip_sum, load_sem, keep_sem, pair_send, pair_recv, cross_send, cross_recv,
         flows, red_send, red_recv, line_send, line_recv, own_sem) = refs
        dp, mp = lax.axis_index("dp"), lax.axis_index("mp")
        partner = (dp ^ 1, mp)
        group, member = dp // members, dp % members
        greet_all([(dp ^ o, mp) for o in offsets], dp, mp, mp_count)
        reduce = LineReduce(part_ref, flows, rows, pieces, red_send, red_recv, dp, mp, mp_count)
        gather = LineGather(low, full_ref, rows, pieces, line_send, line_recv, dp, mp, mp_count)
        for piece in range(AHEAD):
            reduce.begin(piece)
        loads = [[] for _ in range(count)]
        for h in range(2):
            for b in range(mp_count):
                to = pl.ds(b * rows + h * half, half)
                loads[0].append(pltpu.make_async_copy(
                    operands[h].at[pl.ds(b * half, half)], loaded[0].at[to], half_sem.at[h, b]))
        for index in range(1, 2 * count):
            loads[index // 2].append(pltpu.make_async_copy(operands[index + 1], loaded[index], load_sem.at[index]))
        for copy in loads[0] + loads[1]:
            copy.start()
        sums_ref[...] = jnp.zeros_like(sums_ref)

        def pair(mat, o):
            return remote(slices.at[o], from_partner.at[o], pair_send.at[mat, o], pair_recv.at[mat, o], partner)

        def cross(mat, o, peer):
            return remote(chip_sum.at[mat, o - 1], terms[mat].at[o], cross_send.at[mat, o], cross_recv.at[mat, o],
                          (peer, mp))

        def weight_slice(mat, index):
            o = (index + 1) % chips
            mine = index >= chips
            owner = dp ^ (2 * o) ^ jnp.where(mine, 0, 1)
            left = loaded[2 * mat][:, pl.ds(pl.multiple_of(owner * depth, depth), depth)]
            value = contract_first(left, loaded[2 * mat + 1][...])

            @pl.when(jnp.logical_not(mine))
            def _():
                if mat:
                    pair(mat - 1, o).wait_send()
                    pl.semaphore_wait(credit, 1)
                slices[o] = value.astype(slices.dtype)
                pair(mat, o).start()

            @pl.when(mine)
            def _():
                pair(mat, o).wait_recv()
                both = (value + from_partner[o].astype(jnp.float32)).astype(slices.dtype)
                if mat < count - 1:
                    pl.semaphore_signal(credit, inc=1, device_id=partner, device_id_type=MESH)

                @pl.when(o == 0)
                def _():
                    kept[mat] = both
                    pltpu.make_async_copy(kept.at[mat], terms[mat].at[0], keep_sem.at[mat]).start()

                @pl.when(o != 0)
                def _():
                    chip_sum[mat, o - 1] = both
                    cross(mat, o, owner).start()

        def down_load(index):
            at = pl.ds(pl.multiple_of(index * feed_rows, feed_rows), feed_rows)
            return pltpu.make_async_copy(down_ref.at[at], down_rows.at[index % 2], down_sem.at[index % 2])

        def feed_store(index):
            at = pl.ds(pl.multiple_of(index * feed_rows, feed_rows), feed_rows)
            return pltpu.make_async_copy(fed.at[index % 2], feed_ref.at[:, at], fed_sem.at[index % 2])

        def feed_slice(index):
            down_load(index).wait()

            @pl.when(index + 1 < feed_slices)
            def _():
                down_load(index + 1).start()

            @pl.when(index >= 2)
            def _():
                feed_store(index - 2).wait()

            fed[index % 2] = contract_last(loaded[1][...], down_rows[index % 2]).astype(fed.dtype)
            feed_store(index).start()

        def rows_load(k, block, own):
            source = low.at[pl.ds(k * quarter, quarter)] if own else full_ref.at[
                pl.ds(pl.multiple_of(block * rows + k * quarter, quarter), quarter)]
            return pltpu.make_async_copy(source, gathered.at[block], gathered_sem.at[block])

        def head_copy(o, k):
            span = pl.ds(k * quarter, quarter)
            return remote(stage.at[:, span, lanes(group ^ o)], heads_ref.at[group, :, span], head_send.at[o, k],
                          head_recv.at[o, k], ((group ^ o) * members + member, mp))

        def local_copy(k):
            span = pl.ds(k * quarter, quarter)
            return pltpu.make_async_copy(stage.at[:, span, lanes(group)], heads_ref.at[group, :, span], stage_sem.at[k])

        def to_heads(k):
            for block in range(mp_count):
                for own in (True, False):

                    @pl.when((mp == block) if own else (mp != block))
                    def _():
                        rows_load(k, block, own).start()

            for block in range(mp_count):
                for own in (True, False):

                    @pl.when((mp == block) if own else (mp != block))
                    def _():
                        rows_load(k, block, own).wait()

            value = jnp.dot(gathered[...].reshape(mp_count * quarter, width), out_rows[...],
                            preferred_element_type=jnp.float32)
            stage[:, k * quarter : (k + 1) * quarter] = value.reshape(mp_count, quarter, columns).astype(stage.dtype)
            for o in range(1, heads):
                head_copy(o, k).start()
            local_copy(k).start()

        out_load = pltpu.make_async_copy(out_hbm, out_rows, out_sem)
        out_load.start()
        down_load(0).start()

        @pl.loop(0, turns)
        def _(turn):
            reduce.begin(jnp.minimum(turn + AHEAD, pieces - 1), turn + AHEAD < pieces)
            reduce.advance(turn)
            done = turn - SKEW * (mp_count - 1)

            @pl.when((done >= 0) & (done < pieces))
            def _():
                reduce.arrive(done)
                reduce.total(done, total)
                span = pl.ds(pl.multiple_of(done * size, size), size)
                unit, inverse = unit_rows(residual_ref[span])
                upstream = total[...]
                sums_ref[0:1] += jnp.sum(upstream * unit, axis=0, keepdims=True)
                sums_ref[1:2] += jnp.sum(upstream, axis=0, keepdims=True)
                grad = branch_ref[span].astype(jnp.float32) + norm_back(upstream, unit, inverse, gain_ref[...])
                grad_ref[span] = grad
                rounded = grad.astype(low.dtype)
                low[span] = rounded
                sums_ref[2:3] += jnp.sum(rounded.astype(jnp.float32), axis=0, keepdims=True)
                gather.advance(0, done)

            for step in range(1, mp_count):
                late = done - SKEW * step
                gather.advance(step, jnp.clip(late, 0, pieces - 1), (late >= 0) & (late < pieces))
            for mat in range(count):

                @pl.when(turn == 1 + mat * busy // count)
                def _():
                    for copy in loads[mat]:
                        copy.wait()

                first = turn - 1 - mat * busy // count

                @pl.when((first >= 0) & (first < busy // count))
                def _():
                    for i in range(each):
                        weight_slice(mat, first * each + i)

            @pl.when((turn >= 1 + busy) & (turn < 1 + busy + feed_slices))
            def _():
                feed_slice(turn - 1 - busy)

            for k in range(QUARTERS):

                @pl.when(turn == (k + 1) * per_quarter - 1 + 2 * SKEW * (mp_count - 1))
                def _():
                    if k == 0:
                        out_load.wait()
                    to_heads(k)

        own = pltpu.make_async_copy(low, full_ref.at[pl.ds(pl.multiple_of(mp * rows, rows), rows)], own_sem)
        own.start()
        reduce.finish()
        gather.finish()
        own.wait()
        for index in range(feed_slices - 2, feed_slices):
            feed_store(index).wait()
        for k in range(QUARTERS):
            local_copy(k).wait()
            for o in range(1, heads):
                head_copy(o, k).wait()
        for mat in range(count):
            pltpu.make_async_copy(kept.at[mat], terms[mat].at[0], keep_sem.at[mat]).wait()
            for o in range(chips):
                if mat == count - 1:
                    pair(mat, o).wait_send()
                if o:
                    cross(mat, o, dp ^ (2 * o)).wait()

    bf16, f32 = jnp.bfloat16, jnp.float32
    dma = pltpu.SemaphoreType.DMA
    flat = [array for two in pairs for array in two][1:]
    return pl.pallas_call(
        kernel,
        out_shape=[
            jax.ShapeDtypeStruct((rows, width), f32),
            jax.ShapeDtypeStruct((8, width), f32),
            jax.ShapeDtypeStruct((group_rows, width), bf16),
            jax.ShapeDtypeStruct((group_rows, width), bf16),
            jax.ShapeDtypeStruct((heads, mp_count, rows, HEAD_DIM), bf16),
        ]
        + [jax.ShapeDtypeStruct((chips, depth, units), bf16)] * count,
        in_specs=[VMEM] * 4 + [ANY] * (2 * count + 3),
        out_specs=[VMEM, VMEM] + [ANY] * (3 + count),
        scratch_shapes=[pltpu.VMEM((mp_count * rows, width), bf16)] + [pltpu.VMEM(a.shape, a.dtype) for a in flat]
        + [
            pltpu.SemaphoreType.REGULAR,
            pltpu.VMEM((2, feed_rows, units), bf16), dma((2,)),
            pltpu.VMEM((2, group_rows, feed_rows), bf16), dma((2,)),
            pltpu.VMEM((width, columns), bf16), dma(()),
            pltpu.VMEM((mp_count, quarter, width), bf16), dma((mp_count,)),
            pltpu.VMEM((mp_count, rows, columns), bf16), dma((QUARTERS,)),
            dma((heads, QUARTERS)), dma((heads, QUARTERS)),
            dma((2, mp_count)),
            pltpu.VMEM((size, width), f32),
            pltpu.VMEM((rows, width), bf16),
            pltpu.VMEM((count, depth, units), bf16),
            pltpu.VMEM((chips, depth, units), bf16),
            pltpu.VMEM((chips, depth, units), bf16),
            pltpu.VMEM((count, chips - 1, depth, units), bf16),
            dma((2 * count,)), dma((count,)),
        ]
        + [dma((count, chips)) for _ in range(4)]
        + LineReduce.scratch(mp_count, rows, width, pieces) + LineGather.semaphores(mp_count, pieces)
        + [dma(())],
        compiler_params=pltpu.CompilerParams(
            collective_id=collective_id, has_side_effects=True, vmem_limit_bytes=63 * MIB),
        cost_estimate=pl.CostEstimate(flops=40 << 30, bytes_accessed=300 * MIB, transcendentals=0),
    )(part, residual, branch_two, gain, *halves, *flat, down_weight, out_weight)


def finish_back(query_grad, key_part, value_part, weights, normed, residual_grad, hidden, gain, out_part, vectors, heads, members,
                collective_id):
    rows, width = hidden.shape
    dp_count, mp_count = lax.axis_size("dp"), lax.axis_size("mp")
    chips, pieces = dp_count // 2, pieces_of(rows)
    size, depth, columns = rows // pieces, width // dp_count, heads * HEAD_DIM
    kinds, quarter = 3, rows // QUARTERS
    per_quarter = pieces // QUARTERS
    slice_rows = width // per_quarter
    turns = pieces + SKEW * (mp_count - 1)
    slices_each = max(dp_count // 4, 1)
    group_rows = mp_count * rows
    slab, each = vectors.shape[1], width // dp_count // 128
    query_grad = query_grad.reshape(heads, mp_count, rows, HEAD_DIM)
    shared = [v.reshape(dp_count, mp_count, rows, HEAD_DIM) for v in (key_part, value_part)]

    def kernel(query_ref, key_ref, value_ref, weights_hbm, normed_hbm, residual_ref, hidden_ref, gain_ref, out_ref, vector_ref,
               grad_ref, weight_grad_ref, out_grad_ref, summed_ref,
               weights, normed, landed, own, parts, stage, part, total, flows, red_send, red_recv,
               slices, from_partner, chip_sum, from_chips, out_partner, out_sum, out_chips,
               load_sem, own_sem, part_send, part_recv, local_sem, head_send, head_recv,
               pair_send, pair_recv, cross_send, cross_recv,
               sums_ref, column_ref, packed, vector_parts, line_parts, vec_send, vec_recv, line_send, line_recv):
        dp, mp = lax.axis_index("dp"), lax.axis_index("mp")
        group, member = dp // members, dp % members
        partner = (dp ^ 1, mp)
        greet_all([(dp ^ o, mp) for o in range(1, dp_count)] + [(dp, mp ^ o) for o in range(1, mp_count)], dp, mp, mp_count)
        reduce = LineReduce(part, flows, rows, pieces, red_send, red_recv, dp, mp, mp_count)
        loads = [pltpu.make_async_copy(weights_hbm, weights, load_sem.at[0]),
                 pltpu.make_async_copy(normed_hbm, normed, load_sem.at[1])]
        shared_refs = (key_ref, value_ref)

        def rows_of(k):
            return pl.ds(k * quarter, quarter)

        def lane_span(kind, head):
            return pl.ds(pl.multiple_of(kind * columns + head * HEAD_DIM, HEAD_DIM), HEAD_DIM)

        def landing(kind, k, head):
            return landed.at[:, rows_of(k), lane_span(kind, head)]

        def own_copy(kind, o):
            return pltpu.make_async_copy(shared_refs[kind].at[(group ^ o) * members + member], own.at[kind, o],
                                         own_sem.at[kind, o])

        def part_copy(kind, o, p, k):
            return remote(shared_refs[kind].at[(group ^ o) * members + (member ^ p), :, rows_of(k)],
                          parts.at[kind, o, p - 1, :, rows_of(k)], part_send.at[kind, o, p - 1, k],
                          part_recv.at[kind, o, p - 1, k], (group * members + (member ^ p), mp))

        def head_copy(kind, o, k):
            source = query_ref.at[group ^ o, :, rows_of(k)] if kind == 2 else stage.at[kind, o, :, rows_of(k)]
            return remote(source, landing(kind, k, group), head_send.at[kind, o, k], head_recv.at[kind, o, k],
                          ((group ^ o) * members + member, mp))

        def local_copy(k):
            return pltpu.make_async_copy(query_ref.at[group, :, rows_of(k)], landing(2, k, group), local_sem.at[k])

        for k in range(QUARTERS):
            for kind in range(2):
                for o in range(heads):
                    for p in range(1, members):
                        part_copy(kind, o, p, k).start()
            if k == 0:
                for kind in range(2):
                    for o in range(heads):
                        own_copy(kind, o).start()
                for copy in loads:
                    copy.start()
            for o in range(1, heads):
                head_copy(2, o, k).start()
            local_copy(k).start()
        for k in range(QUARTERS):
            for kind in range(2):
                for o in list(range(1, heads)) + [0]:
                    if k == 0:
                        own_copy(kind, o).wait()
                    value = own[kind, o, :, k * quarter : (k + 1) * quarter].astype(jnp.float32)
                    for p in range(1, members):
                        part_copy(kind, o, p, k).wait_recv()
                        value = value + parts[kind, o, p - 1, :, k * quarter : (k + 1) * quarter].astype(jnp.float32)
                    if o:
                        stage[kind, o, :, k * quarter : (k + 1) * quarter] = value.astype(stage.dtype)
                        head_copy(kind, o, k).start()
                    else:
                        landed[:, k * quarter : (k + 1) * quarter, lane_span(kind, group)] = value.astype(landed.dtype)

        def arrived(k):
            for kind in range(kinds):
                for o in range(1, heads):
                    head_copy(kind, o, k).wait_recv()
            local_copy(k).wait()

        def project(k, first, count):
            span = pl.ds(pl.multiple_of(k * quarter, quarter), quarter)
            left = landed[:, span].reshape(mp_count * quarter, kinds * columns)
            features = pl.ds(pl.multiple_of(first, count), count)
            value = contract_last(left, weights[features]).astype(part.dtype)
            for block in range(mp_count):
                at = pl.ds(pl.multiple_of(block * rows + k * quarter, quarter), quarter)
                part[at, features] = value[block * quarter : (block + 1) * quarter]

        def slab(owner):
            return pl.ds(pl.multiple_of(owner * depth, depth), depth)

        def pair(o):
            return remote(slices.at[o], from_partner.at[o], pair_send.at[0, o], pair_recv.at[0, o], partner)

        def cross(o, peer):
            return remote(chip_sum.at[o], from_chips.at[o], cross_send.at[0, o], cross_recv.at[0, o], (peer, mp))

        def out_pair(o):
            return remote(out_ref.at[slab(dp ^ (2 * o) ^ 1)], out_partner.at[o], pair_send.at[1, o], pair_recv.at[1, o],
                          partner)

        def out_cross(o):
            return remote(out_sum.at[o], out_chips.at[o], cross_send.at[1, o], cross_recv.at[1, o], (dp ^ (2 * o), mp))

        def weight_slice(index):
            o = (index + 1) % chips
            mine = index >= chips
            owner = dp ^ (2 * o) ^ jnp.where(mine, 0, 1)
            rows_all = landed[...].reshape(group_rows, kinds * columns)
            value = contract_first(normed[:, slab(owner)], rows_all)

            @pl.when(jnp.logical_not(mine))
            def _():
                slices[o] = value.astype(slices.dtype)
                pair(o).start()

            @pl.when(mine)
            def _():
                pair(o).wait_recv()
                both = value + from_partner[o].astype(jnp.float32)

                @pl.when(o == 0)
                def _():
                    weight_grad_ref[...] = both

                @pl.when(o != 0)
                def _():
                    chip_sum[o] = both.astype(chip_sum.dtype)
                    cross(o, owner).start()

        for copy in loads:
            copy.wait()
        arrived(0)
        for part_index in range(per_quarter):
            project(0, part_index * slice_rows, slice_rows)
        for piece in range(AHEAD):
            reduce.begin(piece)
        for o in range(chips):
            out_pair(o).start()
        sums_ref[...] = jnp.zeros_like(sums_ref)

        @pl.loop(0, turns)
        def _(turn):
            for k in range(1, QUARTERS):

                @pl.when(turn == min(2, per_quarter) * (k - 1))
                def _():
                    arrived(k)

            @pl.when(turn < (QUARTERS - 1) * per_quarter)
            def _():
                k, portion = turn // per_quarter + 1, turn % per_quarter
                project(k, portion * slice_rows, slice_rows)

            reduce.begin(jnp.minimum(turn + AHEAD, pieces - 1), turn + AHEAD < pieces)
            reduce.advance(turn)
            done = turn - SKEW * (mp_count - 1)

            @pl.when(done >= 0)
            def _():
                reduce.arrive(done)
                reduce.total(done, total)
                span = pl.ds(pl.multiple_of(done * size, size), size)
                unit, inverse = unit_rows(hidden_ref[span].astype(jnp.float32))
                upstream = total[...]
                sums_ref[0:1] += jnp.sum(upstream * unit, axis=0, keepdims=True)
                sums_ref[1:2] += jnp.sum(upstream, axis=0, keepdims=True)
                grad_ref[span] = residual_ref[span] + norm_back(upstream, unit, inverse, gain_ref[...])

            @pl.when(turn == late_turn - 1)
            def _():
                for o in list(range(1, chips)) + [0]:
                    out_pair(o).wait_recv()
                    value = out_ref[slab(dp ^ (2 * o))].astype(jnp.float32) + out_partner[o].astype(jnp.float32)
                    if o:
                        out_sum[o] = value.astype(out_sum.dtype)
                        out_cross(o).start()
                    else:
                        out_grad_ref[...] = value

            @pl.when(turn == late_turn - 1)
            def _():
                column_ref[0:1] = jnp.sum(
                    landed[...].reshape(group_rows, kinds * columns).astype(jnp.float32), axis=0, keepdims=True)

            @pl.when((turn >= late_turn) & (turn < late_turn + dp_count // slices_each))
            def _():
                for i in range(slices_each):
                    weight_slice((turn - late_turn) * slices_each + i)

        reduce.finish()
        packed[...] = vector_ref[...]
        for owner in range(dp_count):
            for r in range(each):
                at = slice((owner * each + r) * 128, (owner * each + r + 1) * 128)
                for k in range(2):
                    packed[owner, k * each + r : k * each + r + 1] = sums_ref[k : k + 1, at]
        for head in range(heads):
            feature = mp * heads + head
            for k, kind in ((2, 2), (3, 1)):
                at = slice(kind * columns + head * HEAD_DIM, kind * columns + (head + 1) * HEAD_DIM)
                packed[feature // each, pl.ds(k * each + feature % each, 1)] = column_ref[0:1, at]

        def vector_copy(o):
            return remote(packed.at[dp ^ o], vector_parts.at[o], vec_send.at[o], vec_recv.at[o], (dp ^ o, mp))

        def line_copy(o):
            return remote(line_parts.at[mp], line_parts.at[mp], line_send.at[o], line_recv.at[o], (dp, mp ^ o))

        for o in range(1, dp_count):
            vector_copy(o).start()
        value = packed[dp]
        for o in range(1, dp_count):
            vector_copy(o).wait_recv()
            value = value + vector_parts[o]
        line_parts[mp] = value
        for o in range(1, mp_count):
            line_copy(o).start()
        for o in range(chips):
            pair(o).wait_send()
            out_pair(o).wait_send()
            if o:
                cross(o, dp ^ (2 * o)).wait()
                weight_grad_ref[...] += from_chips[o].astype(jnp.float32)
                out_cross(o).wait()
                out_grad_ref[...] += out_chips[o].astype(jnp.float32)
        for k in range(QUARTERS):
            for o in range(heads):
                for kind in range(2):
                    for p in range(1, members):
                        part_copy(kind, o, p, k).wait_send()
                if o:
                    for kind in range(kinds):
                        head_copy(kind, o, k).wait_send()
        for o in range(1, mp_count):
            line_copy(o).wait()
        value = line_parts[0]
        for index in range(1, mp_count):
            value = value + line_parts[index]
        summed_ref[...] = value
        for o in range(1, dp_count):
            vector_copy(o).wait_send()

    late_turn = min(2, per_quarter) * (QUARTERS - 2) + 1
    assert late_turn + dp_count // slices_each <= turns
    dma = pltpu.SemaphoreType.DMA
    bf16, f32 = jnp.bfloat16, jnp.float32
    own_columns = out_part.shape[1]
    return pl.pallas_call(
        kernel,
        out_shape=[
            jax.ShapeDtypeStruct((rows, width), f32),
            jax.ShapeDtypeStruct((depth, kinds * columns), f32),
            jax.ShapeDtypeStruct((depth, own_columns), f32),
            jax.ShapeDtypeStruct((slab, 128), f32),
        ],
        in_specs=[ANY] * 5 + [VMEM] * 5,
        out_specs=[VMEM] * 4,
        scratch_shapes=[
            pltpu.VMEM((width, kinds * columns), bf16),
            pltpu.VMEM((group_rows, width), bf16),
            pltpu.VMEM((mp_count, rows, kinds * columns), bf16),
            pltpu.VMEM((2, heads, mp_count, rows, HEAD_DIM), bf16),
            pltpu.VMEM((2, heads, members - 1, mp_count, rows, HEAD_DIM), bf16),
            pltpu.VMEM((2, heads, mp_count, rows, HEAD_DIM), bf16),
            pltpu.VMEM((group_rows, width), bf16),
            pltpu.VMEM((size, width), f32),
        ]
        + LineReduce.scratch(mp_count, rows, width, pieces)
        + [pltpu.VMEM((chips, depth, kinds * columns), bf16) for _ in range(4)]
        + [pltpu.VMEM((chips, depth, own_columns), bf16) for _ in range(3)]
        + [dma((2,)), dma((2, heads))]
        + [dma((2, heads, members - 1, QUARTERS)) for _ in range(2)]
        + [dma((QUARTERS,)), dma((kinds, heads, QUARTERS)), dma((kinds, heads, QUARTERS))]
        + [dma((2, chips)) for _ in range(4)]
        + [pltpu.VMEM((8, width), f32), pltpu.VMEM((8, kinds * columns), f32)]
        + [pltpu.VMEM((count, slab, 128), f32) for count in (dp_count, dp_count, mp_count)]
        + [dma((dp_count,)), dma((dp_count,)), dma((mp_count,)), dma((mp_count,))],
        compiler_params=pltpu.CompilerParams(
            collective_id=collective_id, has_side_effects=True, vmem_limit_bytes=63 * MIB),
        cost_estimate=pl.CostEstimate(flops=20 << 30, bytes_accessed=300 * MIB, transcendentals=0),
    )(query_grad, *shared, weights, normed, residual_grad, hidden, gain, out_part, vectors)


UNITS = 512
CHUNK = 1024


def feed_both_ways(rows_two, branch_halves, block, up_all, down_all, up_bias):
    rows, width = rows_two.shape
    units = up_all.shape[1]
    tile = min(UNITS, units)
    half = block // 2
    half_root = 1.0 / math.sqrt(2.0)
    density_scale = 1.0 / math.sqrt(2.0 * math.pi)

    def kernel(rows_ref, first_ref, second_ref, up_ref, down_ref, bias_ref, hidden_ref, grad_ref, column_ref, part_ref, total):
        step = pl.program_id(0)
        columns = jnp.zeros((1, tile), jnp.float32)
        up, down = up_ref[...], down_ref[...]
        for first in range(0, rows, CHUNK):
            span = slice(first, first + CHUNK)
            pre = jnp.dot(rows_ref[span], up, preferred_element_type=jnp.float32) + bias_ref[...]
            upstream = jnp.concatenate([
                jnp.dot(ref[b * half : (b + 1) * half], down, preferred_element_type=jnp.float32)
                for b in range(first // block, (first + CHUNK) // block) for ref in (first_ref, second_ref)
            ], axis=0)
            share = 0.5 + 0.5 * lax.erf(pre * half_root)
            hidden_ref[span] = (pre * share).astype(hidden_ref.dtype)
            slope = share + pre * (density_scale * jnp.exp(-0.5 * pre * pre))
            grad = (upstream * slope).astype(grad_ref.dtype)
            grad_ref[span] = grad
            columns = columns + jnp.sum(grad.astype(jnp.float32), axis=0, keepdims=True)
            back = contract_last(grad, up)

            @pl.when(step == 0)
            def _():
                total[span] = back

            @pl.when(step != 0)
            def _():
                total[span] += back

        column_ref[...] = columns

        @pl.when(step == units // tile - 1)
        def _():
            part_ref[...] = total[...].astype(part_ref.dtype)

    bf16 = jnp.bfloat16
    return pl.pallas_call(
        kernel,
        grid=(units // tile,),
        out_shape=[
            jax.ShapeDtypeStruct((rows, units), bf16),
            jax.ShapeDtypeStruct((rows, units), bf16),
            jax.ShapeDtypeStruct((1, units), jnp.float32),
            jax.ShapeDtypeStruct((rows, width), bf16),
        ],
        in_specs=[
            pl.BlockSpec((rows, width), lambda i: (0, 0)),
            pl.BlockSpec((rows // 2, width), lambda i: (0, 0)),
            pl.BlockSpec((rows // 2, width), lambda i: (0, 0)),
            pl.BlockSpec((width, tile), lambda i: (0, i)),
            pl.BlockSpec((width, tile), lambda i: (0, i)),
            pl.BlockSpec((1, tile), lambda i: (0, i)),
        ],
        out_specs=[
            pl.BlockSpec((rows, tile), lambda i: (0, i)),
            pl.BlockSpec((rows, tile), lambda i: (0, i)),
            pl.BlockSpec((1, tile), lambda i: (0, i)),
            pl.BlockSpec((rows, width), lambda i: (0, 0)),
        ],
        scratch_shapes=[pltpu.VMEM((rows, width), jnp.float32)],
        compiler_params=pltpu.CompilerParams(vmem_limit_bytes=60 * MIB),
        cost_estimate=pl.CostEstimate(
            flops=6 * rows * width * units, bytes_accessed=40 * MIB, transcendentals=2 * rows * units),
    )(rows_two, *branch_halves, up_all, down_all, up_bias)


def sum_terms(terms):
    return functools.reduce(jnp.add, [terms[k].astype(jnp.float32) for k in range(terms.shape[0])])


def per_device(
    hidden_in,
    output_grad,
    first_gain,
    first_shift,
    query_weight,
    query_bias,
    key_weight,
    value_weight,
    value_bias,
    out_weight,
    out_bias,
    second_gain,
    second_shift,
    up_weight,
    up_bias,
    down_weight,
    down_bias,
    seq_lengths,
    block_order,
    block_slot,
):
    local_rows, model_width = hidden_in.shape
    mp_count, dp_count = lax.axis_size("mp"), lax.axis_size("dp")
    mp_index, dp_index = lax.axis_index("mp"), lax.axis_index("dp")
    group_rows = local_rows * mp_count
    head_width = query_weight.shape[1]
    heads_local = head_width // HEAD_DIM
    hidden_width = up_weight.shape[1]
    members = dp_count // heads_local
    blocks_each = group_rows // BLOCK
    plan = (seq_lengths, block_order, block_slot)

    vectors = (first_gain, first_shift, query_bias, value_bias, out_bias, second_gain, second_shift, down_bias, up_bias)
    rows_one, vector_rows, projections, out_all, head_shared, head_queries, branch_two, branch_rest, live, branch_first = project_first(
        hidden_in, output_grad, seq_lengths, block_order, vectors,
        (key_weight, value_weight, query_weight), out_weight, heads_local, members, 0,
    )
    own_valid = live[:, :1] > 0
    vector_rows = vector_rows.reshape(dp_count, -1, 128)
    each = model_width // dp_count // 128
    gain_one, _, _, _, bias_out, gain_two, shift_two, bias_down = (
        vector_rows[:, k * each : (k + 1) * each].reshape(1, model_width) for k in range(8)
    )
    up_each = up_bias.shape[0] // 128
    bias_up = vector_rows[:, 8 * each : 8 * each + up_each].reshape(1, up_bias.shape[0] * dp_count)

    branch_second = whole_rows(branch_rest)
    head_mix, exact_mix, log_total = attend(head_queries, head_shared, *plan, members, blocks_each)
    residual, attended_low, rows_two, up_all, down_all = mix_norm_gather(
        head_mix, out_all, hidden_in, bias_out, gain_two, shift_two, (up_weight, down_weight), heads_local, members, 3
    )
    attended_low = attended_low.reshape(group_rows, head_width)

    bias_hidden = lax.dynamic_slice_in_dim(bias_up, mp_index * hidden_width, hidden_width, 1)
    hidden_low, pre_grad, pre_columns, up_part = feed_both_ways(
        rows_two, (branch_first, branch_second), local_rows, up_all, down_all, bias_hidden
    )
    residual_grad, sums_two, branch_rows_one, feed_part, head_grad, down_terms, up_terms = reduce_back_gather(
        up_part, residual, branch_two, gain_two, (branch_first, branch_second),
        ((None, hidden_low), (rows_two, pre_grad)), down_all, out_all, heads_local, members, 4,
    )
    down_weight_grad, up_weight_grad = (
        sum_terms(terms) for terms in (down_terms, up_terms)
    )
    residual_grad, down_weight_grad, up_weight_grad = lax.optimization_barrier(
        (residual_grad, down_weight_grad, up_weight_grad)
    )

    feed = row_share(feed_part)
    result = residual + feed + bias_down
    output = jnp.where(own_valid, result, 0.0).astype(jnp.bfloat16)

    head_grad = head_grad.reshape(heads_local * group_rows, HEAD_DIM)
    head_query_grad, head_key_grad, head_value_grad = attend_back(
        head_queries, head_shared, head_grad, exact_mix, log_total, *plan, members, blocks_each
    )

    def column_sums(values):
        return jnp.sum(values.astype(jnp.float32), axis=0)

    def placed(values):
        whole = jnp.zeros((values.shape[0] * mp_count,), jnp.float32)
        return lax.dynamic_update_slice_in_dim(whole, values, mp_index * values.shape[0], 0)

    none = jnp.zeros((model_width,), jnp.float32)
    sums = (
        none, none, none, none, sums_two[2], sums_two[0], sums_two[1], column_sums(branch_two), placed(pre_columns[0]),
    )
    packed = jnp.concatenate([v.reshape(dp_count, -1, 128) for v in sums], axis=1)
    packed = jnp.pad(packed, ((0, 0), (0, -packed.shape[1] % 8), (0, 0)))
    out_weight_part = contract_first(branch_rows_one, attended_low).astype(jnp.bfloat16)
    input_grad, weight_grads, out_weight_grad, summed = finish_back(
        head_query_grad, head_key_grad, head_value_grad, projections, rows_one, residual_grad, hidden_in, gain_one,
        out_weight_part, packed, heads_local, members, 7,
    )
    key_weight_grad, value_weight_grad, query_weight_grad = (
        weight_grads[:, k * head_width : (k + 1) * head_width] for k in range(3)
    )
    vector_grads = [summed[k * each : (k + 1) * each].reshape(-1) for k in range(8)]
    up_bias_grad = summed[8 * each : 8 * each + up_each].reshape(-1)
    return (
        output,
        input_grad,
        vector_grads[0],
        vector_grads[1],
        query_weight_grad,
        vector_grads[2],
        key_weight_grad,
        value_weight_grad,
        vector_grads[3],
        out_weight_grad,
        vector_grads[4],
        vector_grads[5],
        vector_grads[6],
        up_weight_grad,
        up_bias_grad,
        down_weight_grad,
        vector_grads[7],
    )


def solution(mesh):
    return jax.shard_map(
        per_device,
        mesh=mesh,
        in_specs=(
            P(("dp", "mp"), None),
            P(("dp", "mp"), None),
            P("dp"),
            P("dp"),
            P("dp", "mp"),
            P("dp"),
            P("dp", "mp"),
            P("dp", "mp"),
            P("dp"),
            P("dp", "mp"),
            P("dp"),
            P("dp"),
            P("dp"),
            P("dp", "mp"),
            P("dp"),
            P("dp", "mp"),
            P("dp"),
            P(),
            P(),
            P(),
        ),
        out_specs=(
            P(("dp", "mp"), None),
            P(("dp", "mp"), None),
            P("dp"),
            P("dp"),
            P("dp", "mp"),
            P("dp"),
            P("dp", "mp"),
            P("dp", "mp"),
            P("dp"),
            P("dp", "mp"),
            P("dp"),
            P("dp"),
            P("dp"),
            P("dp", "mp"),
            P("dp"),
            P("dp", "mp"),
            P("dp"),
        ),
        check_vma=False,
    )
```
